32 devices in a mesh: fsdp: 4 (over y, core), ctx: 8 (over z, x).
Axes of the slice: x: 2, y: 2, z: 4, core: 2. Of those that a mesh axis runs over, the one named last changes fastest.
Arguments:
- tokens: bfloat16 [4, 8192, 1024], P('fsdp', 'ctx'), may hold values from -6 to 6
- cotangent: bfloat16 [4, 8192, 1024], P('fsdp', 'ctx'), may hold values from -6 to 6
- order: int32 [4, 8192], P('fsdp'), may hold values from 0 to 8191, as said below
- lengths: int32 [4, 3], P('fsdp'), may hold values from 1024 to 6144, as said below
- adapter_ids: int32 [4, 3], P('fsdp'), may hold values from 0 to 7
- in_weight: bfloat16 [1024, 4384], P('fsdp'), may hold values from -0.1875 to 0.1875
- out_weight: bfloat16 [2048, 1024], P('fsdp'), may hold values from -0.125 to 0.125
- in_down: bfloat16 [1024, 128], P(None, 'fsdp'), may hold values from -0.1875 to 0.1875
- in_up: bfloat16 [128, 4384], P('fsdp'), may hold values from -0.75 to 0.75
- out_down: bfloat16 [2048, 128], P(None, 'fsdp'), may hold values from -0.125 to 0.125
- out_up: bfloat16 [128, 1024], P('fsdp'), may hold values from -0.75 to 0.75
- norm_gain: float32 [1024], replicated, may hold values from 0.25 to 1.75
- conv_weight: float32 [4, 2304], replicated, may hold values from -0.5 to 0.5
- conv_bias: float32 [2304], replicated, may hold values from -0.5 to 0.5
- dt_bias: float32 [32], replicated, may hold values from -6 to -1
- a_log: float32 [32], replicated, may hold values from -6 to 2
- skip_gain: float32 [32], replicated, may hold values from 0.5 to 1.5
- gate_gain: float32 [2048], replicated, may hold values from 0.25 to 1.75
Outputs:
- block_output: bfloat16 [4, 8192, 1024], P('fsdp', 'ctx')
- input_grad: bfloat16 [4, 8192, 1024], P('fsdp', 'ctx')
- in_down_grad: float32 [1024, 128], P(None, 'fsdp')
- in_up_grad: float32 [128, 4384], P('fsdp')
- out_down_grad: float32 [2048, 128], P(None, 'fsdp')
- out_up_grad: float32 [128, 1024], P('fsdp')
The draws below stay inside these ranges and needn't reach their ends.
Inputs may be any that keep to these rules, and one draw needn't show every extreme that they name: order[g] is a permutation of the group's slots; of the 1024 arrival positions of each block of 1024, exactly 128 land in each block of 1024 packed slots. Some sequence of each group has length exactly 6144; the lengths of a group sum to at most 8192, the remaining slots are padding at the group's end.
All inputs are finite; a program needn't handle non-finite values.
Results may differ from the reference program's by a relative error of at most 0.02.
The reference program's roundings to bfloat16 on the way count: a program that leaves them out, or rounds other values in their place, can miss the bound.
Values may be sent and summed in bfloat16 or wider, within the bound.
A program may use at most 256 MiB of HBM per device.

```python
from functools import partial
import jax
import jax.numpy as jnp
from jax import lax

D = 1024
HEADS = 32
HEAD = 64
STATE = 128
KERNEL = 4
SPAN = 256
RANK = 16
ADAPTERS = 8
SEQS = 3
MIN_LEN = 1024
MAX_LEN = 8192
TOK_DEV = 1024
INNER = 2048
CONV_CH = 2304
PROJ = 4384
GROUPS = 4
GROUP_TOK = 8192
N_CTX = 8


def draw_order(key, part):
    key = jax.random.fold_in(key, 23)
    share = TOK_DEV // N_CTX

    def one_group(group_key):
        send_key, land_key = jax.random.split(group_key)
        labels = jax.vmap(lambda k: jax.random.permutation(k, TOK_DEV))(jax.random.split(send_key, N_CTX))
        landing = jax.vmap(lambda k: jax.random.permutation(k, TOK_DEV))(jax.random.split(land_key, N_CTX))
        target = labels // share
        slot = labels % share
        source = jnp.arange(N_CTX, dtype=jnp.int32)[:, None]
        arrival = source * share + slot
        place = landing[target, arrival]
        return (target * TOK_DEV + place).reshape(-1).astype(jnp.int32)
    return jax.vmap(one_group)(jax.random.split(key, GROUPS))


def draw_lengths(key, part):
    key = jax.random.fold_in(key, 11)
    other_key, pick_key = jax.random.split(key)
    most = min(MAX_LEN, GROUP_TOK - (SEQS - 1) * MIN_LEN)
    room = min(MAX_LEN, (GROUP_TOK - most) // (SEQS - 1))
    others = jax.random.randint(other_key, (GROUPS, SEQS), MIN_LEN, room + 1)
    chosen = jax.random.randint(pick_key, (GROUPS, 1), 0, SEQS)
    column = jnp.arange(SEQS, dtype=jnp.int32)[None, :]
    return jnp.where(column == chosen, most, others).astype(jnp.int32)


def plant(drawn, stream_key, low, top_value):
    shape = drawn.shape
    index_at = [jax.random.randint(jax.random.fold_in(stream_key, axis), (), 0, shape[axis]) for axis in range(len(shape))]
    drawn = drawn.at[tuple(index_at)].set(low)
    longest = shape.index(max(shape))
    index_at[longest] = (index_at[longest] + 1) % shape[longest]
    return drawn.at[tuple(index_at)].set(top_value)


def levels(stream_key, dims, pieces, smallest, high):
    gain, own = 1.0, jax.random.fold_in(stream_key, 6)
    for dim, shards_of in pieces:
        draws = jnp.exp(jax.random.uniform(jax.random.fold_in(own, dim), (shards_of,), jnp.float32, smallest / len(pieces), high / len(pieces)))
        gain = gain * jnp.repeat(draws, dims[dim] // shards_of).reshape([-1 if axis == dim else 1 for axis in range(len(dims))])
    return gain


def normal_values(stream_key, shape, deviation, most, pieces=(), kind=jnp.bfloat16):
    values = deviation * jax.random.normal(stream_key, shape, jnp.float32)
    if pieces:
        values = values * levels(stream_key, shape, pieces, -0.22, 0.18)
    return jnp.clip(values, -most, most).astype(kind)


def setup_inputs(seed: int = 0) -> dict:
    keys = jax.random.split(jax.random.key(seed), 19)
    return {
        "tokens": normal_values(keys[0], (GROUPS, GROUP_TOK, D), 1.0, 6.0, ((0, 4), (1, 8))),
        "cotangent": normal_values(keys[1], (GROUPS, GROUP_TOK, D), 1.0, 6.0, ((0, 4), (1, 8))),
        "order": draw_order(jax.random.fold_in(keys[18], 71), 0),
        "lengths": draw_lengths(jax.random.fold_in(keys[18], 71), 0),
        "adapter_ids": plant(jax.random.randint(keys[4], (GROUPS, SEQS), 0, ADAPTERS), jax.random.fold_in(keys[4], 1), 0, ADAPTERS - 1).astype(jnp.int32),
        "in_weight": normal_values(keys[5], (D, PROJ), D ** -0.5, 0.1875, ((0, 4),)),
        "out_weight": normal_values(keys[6], (INNER, D), INNER ** -0.5, 0.125, ((0, 4),)),
        "in_down": normal_values(keys[7], (D, ADAPTERS * RANK), D ** -0.5, 0.1875, ((1, 4),)),
        "in_up": normal_values(keys[8], (ADAPTERS * RANK, PROJ), (4 * RANK) ** -0.5, 0.75, ((0, 4),)),
        "out_down": normal_values(keys[9], (INNER, ADAPTERS * RANK), INNER ** -0.5, 0.125, ((1, 4),)),
        "out_up": normal_values(keys[10], (ADAPTERS * RANK, D), (4 * RANK) ** -0.5, 0.75, ((0, 4),)),
        "norm_gain": jnp.clip(1.0 + 0.15 * jax.random.normal(keys[11], (D,), jnp.float32), 0.25, 1.75),
        "conv_weight": jnp.clip(jax.random.uniform(keys[12], (KERNEL, CONV_CH), jnp.float32, -0.5, 0.5), -0.5, 0.5),
        "conv_bias": jnp.clip(jax.random.uniform(keys[13], (CONV_CH,), jnp.float32, -0.5, 0.5), -0.5, 0.5),
        "dt_bias": jnp.clip(jax.random.uniform(keys[14], (HEADS,), jnp.float32, -6.0, -1.0), -6.0, -1.0),
        "a_log": jnp.clip(jax.random.uniform(keys[15], (HEADS,), jnp.float32, -6.0, 2.0), -6.0, 2.0),
        "skip_gain": jnp.clip(jax.random.uniform(keys[16], (HEADS,), jnp.float32, 0.5, 1.5), 0.5, 1.5),
        "gate_gain": jnp.clip(1.0 + 0.15 * jax.random.normal(keys[17], (INNER,), jnp.float32), 0.25, 1.75),
    }


epsilon = 1e-05
highest = lax.Precision.HIGHEST

@jax.custom_vjp
def low(v):
    return lax.optimization_barrier(v.astype(jnp.bfloat16)).astype(jnp.float32)

@jax.custom_vjp
def low_back(v):
    return v

def low_keep(v):
    return (low(v), None)

def low_pass(kept, grad):
    return (grad,)

def back_keep(v):
    return (v, None)

def back_low(kept, grad):
    return (low(grad),)
low.defvjp(low_keep, low_pass)
low_back.defvjp(back_keep, back_low)

def product(left, right):
    return jnp.dot(left, right, precision=highest, preferred_element_type=jnp.float32)

def seq_index(positions, ends):
    found = lax.optimization_barrier(jnp.sum((positions[:, None] >= ends[None, :]).astype(jnp.int32), 1))
    return jnp.where(positions >= 0, found, -1).astype(jnp.int32)

def block_work(rates, item):
    steps_b, seq_b, prev_id, c_b, b_b, xs_b = item
    steps_t = steps_b.T
    cumul = jnp.cumsum(steps_t * rates[:, None], axis=1)
    causal = jnp.arange(SPAN)[:, None] >= jnp.arange(SPAN)[None, :]
    same_mask = causal & (seq_b[:, None] == seq_b[None, :])
    spread = cumul[:, :, None] - cumul[:, None, :]
    kernel = jnp.where(same_mask[None], jnp.exp(jnp.minimum(spread, 0.0)), 0.0) * steps_t[:, None, :]
    end_same = (seq_b == seq_b[-1]).astype(jnp.float32)
    weights = jnp.exp(cumul[:, -1:] - cumul) * end_same[None, :] * steps_t
    passing = (seq_b == prev_id).astype(jnp.float32)
    reach = passing[None, :] * jnp.exp(cumul)
    carry = passing[-1] * jnp.exp(cumul[:, -1])
    scores = low_back(jnp.einsum('tn,sn->ts', c_b, b_b, precision=highest))
    mixing = low(scores[None] * kernel)
    within = jnp.einsum('hts,shp->thp', mixing, xs_b, precision=highest)
    weighted = low(xs_b * weights.T[..., None])
    local_state = low_back(jnp.einsum('shp,sn->hpn', weighted, b_b, precision=highest))
    return (within, local_state, reach, carry)

def forward(packed, in_down, in_up, out_down, out_up, fixed):
    valid, seq_ids, select, span_prev, in_weight, out_weight, norm_gain, conv_weight, conv_bias, dt_bias, a_log, skip_gain, gate_gain = fixed
    length = packed.shape[0]
    inner = HEADS * HEAD
    blocks = length // SPAN
    x_in = packed * valid[:, None]
    normed = x_in * lax.rsqrt(lax.optimization_barrier(jnp.mean(x_in * x_in, -1, keepdims=True)) + epsilon) * norm_gain
    normed_low = low(normed)
    lowrank = low(low_back(product(normed_low, in_down) * select))
    proj = low_back(product(normed_low, in_weight) + product(lowrank, in_up))
    gate_in = proj[:, :inner]
    raw = low(proj[:, inner:inner + CONV_CH])
    dt_raw = proj[:, inner + CONV_CH:]
    padded = jnp.concatenate([jnp.zeros((KERNEL - 1, CONV_CH), jnp.float32), raw], 0)
    seq_pad = jnp.concatenate([jnp.full((KERNEL - 1,), -1, jnp.int32), seq_ids], 0)
    accum = jnp.zeros((length, CONV_CH), jnp.float32) + conv_bias
    for tap in range(KERNEL):
        same = (seq_pad[tap:tap + length] == seq_ids)[:, None]
        accum = accum + jnp.where(same, padded[tap:tap + length] * conv_weight[tap], 0.0)
    active = jax.nn.silu(accum)
    x_state = low(active[:, :inner])
    b_mat = low(active[:, inner:inner + STATE])
    c_mat = low(active[:, inner + STATE:])
    step_size = jax.nn.softplus(dt_raw + dt_bias)
    rates = -jnp.exp(a_log)
    c_blocks = c_mat.reshape(blocks, SPAN, STATE)
    b_blocks = b_mat.reshape(blocks, SPAN, STATE)
    xs_blocks = x_state.reshape(blocks, SPAN, HEADS, HEAD)
    items = (step_size.reshape(blocks, SPAN, HEADS), seq_ids.reshape(blocks, SPAN), span_prev, c_blocks, b_blocks, xs_blocks)
    within, local_state, reach, carry = lax.map(jax.checkpoint(partial(block_work, rates)), items)

    def advance(state, item):
        decay, addend = item
        return (decay[:, None, None] * state + addend, state)
    _, starts = lax.scan(advance, jnp.zeros((HEADS, HEAD, STATE), jnp.float32), (carry, local_state))
    starts_low = low(starts)
    projected = low_back(jnp.einsum('ctn,chpn->cthp', c_blocks, starts_low, precision=highest))
    mixed = within + reach.transpose(0, 2, 1)[..., None] * projected + skip_gain[:, None] * xs_blocks
    mixed = low_back(mixed.reshape(length, inner))
    gated = mixed * jax.nn.silu(gate_in)
    norm_out = low(gated * lax.rsqrt(lax.optimization_barrier(jnp.mean(gated * gated, -1, keepdims=True)) + epsilon) * gate_gain)
    lowrank_out = low(low_back(product(norm_out, out_down) * select))
    branch = product(norm_out, out_weight) + product(lowrank_out, out_up)
    return (x_in + branch) * valid[:, None]

def reference(tokens, cotangent, order, lengths, adapter_ids, in_weight, out_weight, in_down, in_up, out_down, out_up, norm_gain, conv_weight, conv_bias, dt_bias, a_log, skip_gain, gate_gain):
    widen = lambda value: value.astype(jnp.float32)
    w_in = widen(in_weight)
    w_out = widen(out_weight)
    a_in = widen(in_down)
    b_in = widen(in_up)
    a_out = widen(out_down)
    b_out = widen(out_up)
    blocks = GROUP_TOK // SPAN
    grad_sums = [jnp.zeros_like(a_in), jnp.zeros_like(b_in), jnp.zeros_like(a_out), jnp.zeros_like(b_out)]
    outputs = []
    input_grads = []
    for group in range(GROUPS):
        perm = order[group].astype(jnp.int32)
        packed = jnp.zeros((GROUP_TOK, D), jnp.float32).at[perm].set(widen(tokens[group]))
        packed_cot = jnp.zeros((GROUP_TOK, D), jnp.float32).at[perm].set(widen(cotangent[group]))
        positions = jnp.arange(GROUP_TOK, dtype=jnp.int32)
        ends = jnp.cumsum(lengths[group]).astype(jnp.int32)
        seq_ids = seq_index(positions, ends)
        valid = (positions < ends[-1]).astype(jnp.float32)
        adapter_tok = lax.optimization_barrier(jnp.sum(jnp.where(seq_ids[:, None] == jnp.arange(SEQS, dtype=jnp.int32)[None, :], adapter_ids[group][None, :], 0), 1))
        select = ((jnp.arange(ADAPTERS * RANK, dtype=jnp.int32) // RANK)[None, :] == adapter_tok[:, None]).astype(jnp.float32) * valid[:, None]
        span_prev = seq_index(jnp.arange(blocks, dtype=jnp.int32) * SPAN - 1, ends)
        fixed = (valid, seq_ids, select, span_prev, w_in, w_out, norm_gain, conv_weight, conv_bias, dt_bias, a_log, skip_gain, gate_gain)
        result, pullback = jax.vjp(partial(forward, fixed=fixed), packed, a_in, b_in, a_out, b_out)
        grads = pullback(packed_cot)
        outputs.append(result[perm].astype(jnp.bfloat16))
        input_grads.append(grads[0][perm].astype(jnp.bfloat16))
        grad_sums = [total + piece for total, piece in zip(grad_sums, grads[1:])]
    return (jnp.stack(outputs), jnp.stack(input_grads), grad_sums[0], grad_sums[1], grad_sums[2], grad_sums[3])
```

```python
from functools import partial

import jax
import jax.numpy as jnp
from jax import lax
from jax.experimental import pallas as pl
from jax.experimental.pallas import tpu as pltpu
from jax.sharding import PartitionSpec as P

HEADS = 32
HEAD = 64
STATE = 128
KERNEL = 4
SPAN = 256
RANK = 16
ADAPTERS = 8
SEQS = 3
CONV_CH = 2304
INNER = HEADS * HEAD
LOW = ADAPTERS * RANK
LANES = 128
HALF = SPAN // 2
EPS = 1e-05
LOG2E = 1.4426950408889634

F32 = jnp.float32
BF16 = jnp.bfloat16
MIB = 1 << 20


def nn(a, b):
    return jnp.dot(a, b, preferred_element_type=F32)


def nt(a, b):
    return lax.dot_general(a, b, (((1,), (1,)), ((), ())), preferred_element_type=F32)


def tn(a, b):
    return lax.dot_general(a, b, (((0,), (0,)), ((), ())), preferred_element_type=F32)


def iota(shape, dim):
    return lax.broadcasted_iota(jnp.int32, shape, dim)


def one_hot(cond):
    return jnp.where(cond, 1.0, 0.0).astype(BF16)


def split(v, parts):
    out = []
    for _ in range(parts):
        piece = v.astype(BF16)
        out.append(piece)
        v = v - piece.astype(F32)
    return out


def expand(v, e, parts=2):
    return sum(nn(p, e) for p in split(v, parts))


def seq_of(pos, meta):
    found = sum((pos >= meta[k]).astype(jnp.int32) for k in (1, 2, 3))
    return jnp.where(pos >= 0, found, -1)


def valid_of(pos, meta):
    return (pos < meta[3]).astype(F32)


def select_of(pos, meta):
    seq = seq_of(pos, meta)
    ids = jnp.where(seq == 0, meta[4], 0) + jnp.where(seq == 1, meta[5], 0) + jnp.where(seq == 2, meta[6], 0)
    shape = (pos.shape[0], LOW)
    return jnp.where(iota(shape, 1) // RANK == ids, 1.0, 0.0) * valid_of(pos, meta)


def sigmoid(v):
    return 1.0 / (1.0 + jnp.exp(-v))


def col_pos(meta, block, rows=SPAN):
    return meta[0] + block * SPAN + iota((rows, 1), 0)


def running_count(mask):
    width = mask.shape[1]
    tri = one_hot(iota((SPAN, SPAN), 0) <= iota((SPAN, SPAN), 1))
    pieces, before = [], jnp.zeros((mask.shape[0], 1), F32)
    for c in range(0, width, SPAN):
        part = mask[:, c : c + SPAN]
        pieces.append(nn(part.astype(BF16), tri) + before)
        before = before + jnp.sum(part, 1, keepdims=True)
    return jnp.concatenate(pieces, 1)


def two_rows(v):
    first = jnp.broadcast_to(v >> 5, (16, v.shape[1]))
    second = jnp.broadcast_to(v & 31, (16, v.shape[1]))
    row = iota((16, v.shape[1]), 0)
    return jnp.where(row == 0, first, jnp.where(row == 1, second, 0)).astype(F32).astype(BF16)


def from_two(r):
    return (r[0:1] * 32.0 + r[1:2]).astype(jnp.int32)


def send_kernel(shift, share, meta, order_ref, x_ref, out_ref, spos_ref):
    rows = x_ref.shape[0]
    own = order_ref[pl.ds(meta[7], 1), :]
    dest = own >> shift
    hot = jnp.where(iota((order_ref.shape[0], rows), 0) == dest, 1.0, 0.0)
    rank = jnp.sum(hot * (running_count(hot) - 1.0), axis=0, keepdims=True)
    spos = dest * share + rank.astype(jnp.int32)
    spos_ref[...] = spos
    x = x_ref[...]
    for t in range(0, rows, SPAN):
        hit = one_hot(iota((SPAN, rows), 0) + t == spos)
        out_ref[t : t + SPAN, :] = nn(hit, x).astype(BF16)


def invert(idx):
    width = idx.shape[1]
    values = two_rows(iota((1, width), 1))
    pieces = []
    for t in range(0, width, SPAN):
        hit = one_hot(iota((SPAN, width), 0) + t == idx)
        pieces.append(from_two(nt(values, hit)))
    return jnp.concatenate(pieces, 1)


def route_kernel(shift, share, n, meta, order_ref, spos_ref, slot_ref, where_ref, tok_ref):
    rows = spos_ref.shape[1]
    order = order_ref[...]
    mine = jnp.where(order >> shift == meta[7], 1.0, 0.0)
    slot = order & (rows - 1)
    mark = jnp.where(mine > 0.0, running_count(mine) - 1.0, -1.0).astype(jnp.int32)
    for s in range(n):
        hit = one_hot(iota((share, rows), 0) == mark[s : s + 1, :])
        slot_ref[:, s * share : (s + 1) * share] = from_two(nt(two_rows(slot[s : s + 1, :]), hit))
    where_ref[...] = invert(slot_ref[...])
    tok_ref[...] = invert(spos_ref[...])


def permute_kernel(idx_ref, x_ref, out_ref):
    hit = one_hot(iota((out_ref.shape[0], x_ref.shape[0]), 0) + pl.program_id(0) * out_ref.shape[0] == idx_ref[...])
    out_ref[...] = nn(hit, x_ref[...]).astype(BF16)


def in_kernel(meta, slot_ref, got_ref, w_ref, a_ref, b_ref, gain_ref, x_ref, hb_ref, u_ref, z_ref, raw_ref, dtr_ref):
    i = pl.program_id(0)
    rows = got_ref.shape[0]
    pos = col_pos(meta, i)
    hit = one_hot(iota((SPAN, rows), 0) + i * SPAN == slot_ref[...])
    x = nn(hit, got_ref[...]) * valid_of(pos, meta)
    x_ref[...] = x.astype(BF16)
    h = x * lax.rsqrt(jnp.mean(x * x, 1, keepdims=True) + EPS) * gain_ref[...]
    hb = h.astype(BF16)
    hb_ref[...] = hb
    u = (nn(hb, a_ref[...]) * select_of(pos, meta)).astype(BF16)
    u_ref[...] = u

    def part(lo, hi):
        return nn(hb, w_ref[:, lo:hi]) + nn(u, b_ref[:, lo:hi])

    for c in range(0, INNER, 512):
        z_ref[:, c : c + 512] = part(c, c + 512)
    for c in range(0, CONV_CH, 256):
        raw_ref[:, c : c + 256] = part(INNER + c, INNER + c + 256).astype(BF16)
    last = part(INNER + CONV_CH, INNER + CONV_CH + HEADS)
    dtr_ref[...] = jnp.concatenate([last, jnp.zeros((SPAN, LANES - HEADS), F32)], 1)


def softplus(v):
    e = jnp.exp(-jnp.abs(v))
    series = e * (1.0 - e * (0.5 - e * (1.0 / 3.0 - 0.25 * e)))
    return jnp.maximum(v, 0.0) + jnp.where(e < 0.01, series, jnp.log(1.0 + e))


def conv_kernel(
    meta, raw_ref, halo_ref, dtr_ref, cw_ref, cb_ref, bias_ref, rate_ref, e_ref,
    xs_ref, bm_ref, cm_ref, dact_ref, dt_ref, c2_ref, c2t_ref, wts_ref, reach_ref, ls_ref, carry_ref, send_ref,
    tail, state, through,
):
    i = pl.program_id(0)

    @pl.when(i == 0)
    def _():
        tail[...] = halo_ref[8:16, :].astype(F32)
        state[...] = jnp.zeros_like(state)
        through[...] = jnp.ones_like(through)

    pos = col_pos(meta, i)
    seq = seq_of(pos, meta)
    masks = [(seq_of(pos - j, meta) == seq).astype(F32) for j in range(KERNEL)]
    for c in range(0, CONV_CH, 256):
        cur = raw_ref[:, c : c + 256].astype(F32)
        ext = jnp.concatenate([tail[:, c : c + 256], cur], 0)
        acc = cb_ref[:, c : c + 256] + cw_ref[3:4, c : c + 256] * cur
        for j in range(1, KERNEL):
            moved = pltpu.roll(ext, j, 0)[8:]
            acc = acc + (cw_ref[3 - j : 4 - j, c : c + 256] * moved) * masks[j]
        sg = sigmoid(acc)
        act = acc * sg
        dact_ref[:, c : c + 256] = (sg + act * (1.0 - sg)).astype(BF16)
        act = act.astype(BF16)
        if c < INNER:
            xs_ref[:, c : c + 256] = act
        else:
            bm_ref[...] = act[:, :STATE]
            cm_ref[...] = act[:, STATE:]
        tail[:, c : c + 256] = cur[SPAN - 8 :]
    dt = softplus(dtr_ref[...] + bias_ref[...])
    dt_ref[...] = dt
    tri = one_hot(iota((SPAN, SPAN), 0) >= iota((SPAN, SPAN), 1))
    cum = sum(nn(tri, p) for p in split(dt * rate_ref[...], 3))
    cum_end = cum[SPAN - 1 : SPAN, :]
    end = meta[0] + i * SPAN + SPAN - 1
    end_same = (seq == seq_of(end, meta)).astype(F32)
    passing = (seq == seq_of(meta[0] + i * SPAN - 1, meta)).astype(F32)
    wts = jnp.exp(cum_end - cum) * dt * end_same
    wts_ref[...] = wts
    reach = jnp.exp(cum) * passing
    reach_ref[...] = reach
    c2 = cum * LOG2E
    c2_ref[...] = c2
    c2t_ref[0] = c2.T[:HEADS]
    weighted = (xs_ref[...].astype(F32) * expand(wts, e_ref[...])).astype(BF16)
    ls = tn(bm_ref[...], weighted)
    ls_ref[0] = ls
    carry = expand(jnp.broadcast_to(reach[SPAN - 1 : SPAN, :], (16, LANES)), e_ref[...], 3)[:8]
    carry_ref[0] = carry
    state[...] = state[...] * carry[0:1] + ls
    through[...] = through[...] * carry

    @pl.when(i == pl.num_programs(0) - 1)
    def _():
        send_ref[:STATE] = state[...].astype(BF16)
        send_ref[STATE:] = jnp.broadcast_to(through[0:1], (16, INNER)).astype(BF16)


def block_mask(meta, i, transposed):
    col = col_pos(meta, i)
    row = meta[0] + i * SPAN + iota((1, SPAN), 1)
    same = seq_of(col, meta) == seq_of(row, meta)
    return same & ((row >= col) if transposed else (col >= row))


def halves(x):
    lane = iota(x.shape, 1)
    zero = jnp.zeros_like(x)
    return jnp.where(lane < HEAD, x, zero), jnp.where(lane >= HEAD, x, zero)


def within_kernel(meta, xs_ref, bm_ref, cm_ref, dt_ref, c2_ref, c2t_ref, e_ref, y_ref, xdt, sc):
    i = pl.program_id(0)
    sc[...] = jnp.where(block_mask(meta, i, False), nt(cm_ref[...], bm_ref[...]), 0.0)
    xdt[...] = (xs_ref[...].astype(F32) * expand(dt_ref[...], e_ref[...])).astype(BF16)
    c2 = c2_ref[...]

    def group(g, _):
        cols = pltpu.roll(c2, LANES - 8 * g, 1)
        rows = c2t_ref[0, pl.ds(pl.multiple_of(8 * g, 8), 8), :]
        for q in range(4):
            at = pl.ds(pl.multiple_of(g * 512 + q * 128, 128), 128)
            xa, xb = halves(xdt[:, at])
            mixes = []
            for h in (2 * q, 2 * q + 1):
                col, row = cols[:, h : h + 1], rows[h : h + 1, :]

                def mix(t, s):
                    decay = jnp.exp2(jnp.minimum(col[t : t + HALF] - row[:, s : s + HALF], 0.0))
                    return (sc[t : t + HALF, s : s + HALF] * decay).astype(BF16)

                mixes.append((mix(0, 0), mix(HALF, 0), mix(HALF, HALF)))
            (a00, a10, a11), (b00, b10, b11) = mixes
            y_ref[:HALF, at] = nn(jnp.concatenate([a00, b00], 1), jnp.concatenate([xa[:HALF], xb[:HALF]], 0))
            y_ref[HALF:, at] = nn(jnp.concatenate([a10, a11, b10, b11], 1), jnp.concatenate([xa, xb], 0))
        return 0

    lax.fori_loop(0, HEADS // 8, group, 0)


CHUNK = 32


def fold_kernel(reverse, meta, part_ref, through_ref, out_ref):
    k = pl.program_id(0)
    j = pl.num_programs(0) - 1 - k if reverse else k
    reached = j > meta[7] if reverse else j < meta[7]

    @pl.when(k == 0)
    def _():
        out_ref[...] = jnp.zeros_like(out_ref)

    @pl.when(reached)
    def _():
        out_ref[...] = out_ref[...] * through_ref[0].astype(F32)[0:1] + part_ref[0].astype(F32)


def out_kernel(
    meta, y_ref, z_ref, xs_ref, cm_ref, reach_ref, x_ref, ls_ref, carry_ref, all_ref, e_ref, skip_ref, gain_ref,
    w_ref, a_ref, b_ref, where_ref,
    start_ref, next_ref, mixed_ref, nout_ref, v_ref, rstd_ref, sorted_ref,
    run, acc, proj, wide,
):
    i = pl.program_id(0)

    @pl.when(i == 0)
    def _():
        run[...] = all_ref[...]
        acc[...] = jnp.zeros_like(acc)

    start = run[...].astype(BF16)
    start_ref[0] = start
    later = run[...] * carry_ref[0, 0:1, :] + ls_ref[0]
    run[...] = later
    next_ref[0] = later.astype(BF16)
    proj[...] = nn(cm_ref[...], start)
    wide[...] = expand(reach_ref[...], e_ref[...])

    def rows_step(k, _):
        at = pl.ds(pl.multiple_of(k * CHUNK, CHUNK), CHUNK)
        total = jnp.zeros((CHUNK, LANES), F32)
        for c in range(0, INNER, 256):
            cs = slice(c, c + 256)
            mixed = y_ref[at, cs] + wide[at, cs] * proj[at, cs] + skip_ref[:, cs] * xs_ref[at, cs].astype(F32)
            mixed_ref[at, cs] = mixed
            z = z_ref[at, cs]
            gated = mixed * (z * sigmoid(z))
            wide[at, cs] = gated
            sq = gated * gated
            total = total + sq[:, :LANES] + sq[:, LANES:]
        rstd = lax.rsqrt(jnp.sum(total, 1, keepdims=True) * (1.0 / INNER) + EPS)
        rstd_ref[at, :] = jnp.broadcast_to(rstd, (CHUNK, LANES))
        for c in range(0, INNER, 256):
            cs = slice(c, c + 256)
            nout_ref[at, cs] = (wide[at, cs] * rstd * gain_ref[:, cs]).astype(BF16)
        return 0

    lax.fori_loop(0, SPAN // CHUNK, rows_step, 0)
    pos = col_pos(meta, i)
    nout = nout_ref[...]
    v = (nn(nout, a_ref[...]) * select_of(pos, meta)).astype(BF16)
    v_ref[...] = v
    branch = nn(nout, w_ref[...]) + nn(v, b_ref[...])
    result = ((x_ref[...].astype(F32) + branch) * valid_of(pos, meta)).astype(BF16)
    hit = one_hot(iota((acc.shape[0], SPAN), 0) == where_ref[...])
    acc[...] += nn(hit, result)

    @pl.when(i == pl.num_programs(0) - 1)
    def _():
        sorted_ref[...] = acc[...].astype(BF16)


def gate_back_kernel(
    meta, mixed_ref, z_ref, nout_ref, v_ref, rstd_ref, xs_ref, cm_ref, reach_ref, start_ref, carry_ref, cot_ref, slot_ref,
    e_ref, skip_ref, gain_ref, w_ref, a_ref, b_ref,
    dout_ref, dm_ref, dz_ref, rs_ref, dcm_ref, dst_ref, own_ref, gup_ref, gdown_ref,
    own, through, gup, gdown, dn, wide, hi_s, lo_s, dproj,
):
    i = pl.program_id(0)

    @pl.when(i == 0)
    def _():
        own[...] = jnp.zeros_like(own)
        through[...] = jnp.ones_like(through)
        gup[...] = jnp.zeros_like(gup)
        gdown[...] = jnp.zeros_like(gdown)

    pos = col_pos(meta, i)
    rows = cot_ref.shape[0]
    hit = one_hot(iota((SPAN, rows), 0) + i * SPAN == slot_ref[...])
    dout = (nn(hit, cot_ref[...]) * valid_of(pos, meta)).astype(BF16)
    dout_ref[...] = dout
    gup[...] += tn(v_ref[...], dout)
    dv = nt(dout, b_ref[...]).astype(BF16) * select_of(pos, meta).astype(BF16)
    gdown[...] += tn(dv, nout_ref[...])
    dn[...] = nt(dout, w_ref[...]) + nt(dv, a_ref[...])
    wide[...] = expand(reach_ref[...], e_ref[...])

    def rows_step(k, _):
        at = pl.ds(pl.multiple_of(k * CHUNK, CHUNK), CHUNK)
        rstd = rstd_ref[at, :][:, 0:1]
        total = jnp.zeros((CHUNK, LANES), F32)
        for c in range(0, INNER, 256):
            cs = slice(c, c + 256)
            z = z_ref[at, cs]
            d = dn[at, cs] * gain_ref[:, cs]
            dn[at, cs] = d
            g = d * (mixed_ref[at, cs] * (z * sigmoid(z)))
            total = total + g[:, :LANES] + g[:, LANES:]
        back = jnp.sum(total, 1, keepdims=True) * (1.0 / INNER) * rstd * rstd
        for c in range(0, INNER, 256):
            cs = slice(c, c + 256)
            z = z_ref[at, cs]
            sg = sigmoid(z)
            silu = z * sg
            mixed = mixed_ref[at, cs]
            dg = rstd * (dn[at, cs] - mixed * silu * back)
            dm = (dg * silu).astype(BF16)
            dm_ref[at, cs] = dm
            dz_ref[at, cs] = (dg * mixed * (sg + silu * (1.0 - sg))).astype(BF16)
            dm = dm.astype(F32)
            dproj[at, cs] = (dm * wide[at, cs]).astype(BF16)
            hi, lo = split(dm * (mixed - skip_ref[:, cs] * xs_ref[at, cs].astype(F32)), 2)
            hi_s[at, cs] = hi
            lo_s[at, cs] = lo
        return 0

    lax.fori_loop(0, SPAN // CHUNK, rows_step, 0)
    rs_ref[...] = nt(hi_s[...], e_ref[...]) + nt(lo_s[...], e_ref[...])
    dcm_ref[...] = nt(dproj[...], start_ref[0])
    dst = tn(cm_ref[...], dproj[...])
    dst_ref[0] = dst
    own[...] += dst * through[0:1]
    through[...] = through[...] * carry_ref[0]

    @pl.when(i == pl.num_programs(0) - 1)
    def _():
        own_ref[...] = own[...].astype(BF16)
        gup_ref[...] = gup[...].astype(BF16)
        gdown_ref[...] = gdown[...].astype(BF16)


def mix_back_kernel(
    meta, xs_ref, bm_ref, cm_ref, dm_ref, dt_ref, c2_ref, c2t_ref, dcm1_ref, e_ref,
    dxk_ref, dbm_ref, dcm_ref,
    xdt, dte, sct, dsc,
):
    i = pl.program_id(0)
    mask = block_mask(meta, i, True)
    sct[...] = jnp.where(mask, nt(bm_ref[...], cm_ref[...]), 0.0)
    dsc[...] = jnp.zeros_like(dsc)
    dte[...] = expand(dt_ref[...], e_ref[...])
    xdt[...] = (xs_ref[...].astype(F32) * dte[...]).astype(BF16)
    c2 = c2_ref[...]

    def group(g, _):
        cols = pltpu.roll(c2, LANES - 8 * g, 1)
        rows = c2t_ref[0, pl.ds(pl.multiple_of(8 * g, 8), 8), :]
        for q in range(4):
            at = pl.ds(pl.multiple_of(g * 512 + q * 128, 128), 128)
            dm = dm_ref[:, at]
            da, db = halves(dm)
            mixes = []
            for h, x in zip((2 * q, 2 * q + 1), halves(xdt[:, at])):
                col, row = cols[:, h : h + 1], rows[h : h + 1, :]
                top = nt(x[:HALF], dm)
                low = nt(x[HALF:], dm[HALF:])

                def mix(s, t, d):
                    decay = jnp.exp2(jnp.minimum(row[:, t : t + HALF] - col[s : s + HALF], 0.0))
                    dsc[s : s + HALF, t : t + HALF] += d * decay
                    return (sct[s : s + HALF, t : t + HALF] * decay).astype(BF16)

                mixes.append((mix(0, 0, top[:, :HALF]), mix(0, HALF, top[:, HALF:]), mix(HALF, HALF, low)))
            (a00, a01, a11), (b00, b01, b11) = mixes
            g_top = nn(jnp.concatenate([a00, a01, b00, b01], 1), jnp.concatenate([da, db], 0))
            g_low = nn(jnp.concatenate([a11, b11], 1), jnp.concatenate([da[HALF:], db[HALF:]], 0))
            dxk_ref[:HALF, at] = g_top * dte[:HALF, at]
            dxk_ref[HALF:, at] = g_low * dte[HALF:, at]
        return 0

    lax.fori_loop(0, HEADS // 8, group, 0)
    ds = jnp.where(mask, dsc[...], 0.0).astype(BF16)
    dbm_ref[...] = nn(ds, cm_ref[...])
    dcm_ref[...] = dcm1_ref[...] + tn(ds, bm_ref[...])


def later_kernel(
    all_ref, dst_ref, carry_ref, next_ref, e_ref, skip_ref,
    xs_ref, bm_ref, dm_ref, dxk_ref, dbm_ref, dcm_ref, wts_ref, dact_ref,
    dl_ref, dend_ref, head_ref,
    acc,
):
    i = pl.program_id(0)

    @pl.when(i == 0)
    def _():
        acc[...] = all_ref[...]

    a = acc[...]
    dl = a.astype(BF16)
    dl_ref[0] = dl
    total = jnp.sum(a * next_ref[0].astype(F32), 0, keepdims=True)
    total = jnp.broadcast_to(total, (16, INNER))
    dend_ref[0] = sum(nt(p, e_ref[...]) for p in split(total, 3))[:8]
    acc[...] = dst_ref[0] + carry_ref[0, 0:1, :] * a

    @pl.when(i == pl.num_programs(0) - 1)
    def _():
        wide = expand(wts_ref[...], e_ref[...])
        weighted = (xs_ref[...].astype(F32) * wide).astype(BF16)
        dxs = dxk_ref[...] + nn(bm_ref[...], dl) * wide + skip_ref[...] * dm_ref[...].astype(F32)
        head_ref[:, :INNER] = dxs * dact_ref[:, :INNER].astype(F32)
        dbm = dbm_ref[...] + nt(weighted, dl)
        head_ref[:, INNER : INNER + STATE] = dbm * dact_ref[:, INNER : INNER + STATE].astype(F32)
        head_ref[:, INNER + STATE :] = dcm_ref[...] * dact_ref[:, INNER + STATE :].astype(F32)


def in_back_kernel(
    meta, dl_ref, dend_ref, xs_ref, bm_ref, dm_ref, dz_ref, dxk_ref, dbm_ref, dcm_ref, wts_ref, dtr_ref, rs_ref, dact_ref,
    halo_ref, cw_ref, e_ref, skip_ref, bias_ref, rate_ref, w_ref, a_ref, b_ref, u_ref, hb_ref, x_ref, dout_ref, gain_ref,
    where_ref,
    sorted_ref, gup_ref, gdown_ref,
    head, acc, gup, gdown, wide, dacc, hi_s, lo_s, draw,
):
    k = pl.program_id(0)
    i = pl.num_programs(0) - 1 - k

    @pl.when(k == 0)
    def _():
        head[...] = halo_ref[:8, :]
        acc[...] = jnp.zeros_like(acc)
        gup[...] = jnp.zeros_like(gup)
        gdown[...] = jnp.zeros_like(gdown)

    wide[...] = expand(wts_ref[...], e_ref[...])
    dacc[:, :INNER] = nn(bm_ref[...], dl_ref[0])

    def rows_step(r, _):
        at = pl.ds(pl.multiple_of(r * CHUNK, CHUNK), CHUNK)
        for c in range(0, INNER, 256):
            cs = slice(c, c + 256)
            w = wide[at, cs]
            xs = xs_ref[at, cs].astype(F32)
            dx = dxk_ref[at, cs] + dacc[at, cs] * w
            hi, lo = split(xs * dx, 2)
            hi_s[at, cs] = hi
            lo_s[at, cs] = lo
            dx = dx + skip_ref[:, cs] * dm_ref[at, cs].astype(F32)
            dacc[at, cs] = dx * dact_ref[at, cs].astype(F32)
            draw[at, cs] = (xs * w).astype(BF16)
        return 0

    lax.fori_loop(0, SPAN // CHUNK, rows_step, 0)
    dbm = dbm_ref[...] + nt(draw[:, :INNER], dl_ref[0])
    dacc[:, INNER : INNER + STATE] = dbm * dact_ref[:, INNER : INNER + STATE].astype(F32)
    dacc[:, INNER + STATE :] = dcm_ref[...] * dact_ref[:, INNER + STATE :].astype(F32)
    csum = nt(hi_s[...], e_ref[...]) + nt(lo_s[...], e_ref[...])

    pos = col_pos(meta, i)
    seq = seq_of(pos, meta)
    masks = [(seq_of(pos + j, meta) == seq).astype(F32) for j in range(KERNEL)]
    for c in range(0, CONV_CH, 256):
        cs = slice(c, c + 256)
        cur = dacc[:, cs]
        ext = jnp.concatenate([cur, head[:, cs]], 0)
        total = cw_ref[3:4, cs] * cur
        for j in range(1, KERNEL):
            moved = pltpu.roll(ext, SPAN + 8 - j, 0)[:SPAN]
            total = total + (cw_ref[3 - j : 4 - j, cs] * moved) * masks[j]
        draw[:, cs] = total.astype(BF16)
        head[:, cs] = cur[:8]

    last = iota((SPAN, 1), 0) == SPAN - 1
    dcum = rs_ref[...] - csum + jnp.where(last, dend_ref[0, 0:1, :], 0.0)
    tri = one_hot(iota((SPAN, SPAN), 0) <= iota((SPAN, SPAN), 1))
    dsteps = sum(nn(tri, p) for p in split(dcum, 3))
    v = dtr_ref[...] + bias_ref[...]
    sg = sigmoid(v)
    e = jnp.exp(jnp.minimum(v, 0.0))
    ratio = jnp.where(v < -12.0, 1.0 - 0.5 * e, sg / jnp.maximum(softplus(v), 1e-7))
    ddt = (csum * ratio + dsteps * rate_ref[...] * sg).astype(BF16)[:, :HEADS]

    dz = dz_ref[...]
    dr = draw[...]
    u, hb = u_ref[...], hb_ref[...]
    mid, end = INNER + CONV_CH, INNER + CONV_CH + HEADS
    gup[:, :INNER] += tn(u, dz)
    gup[:, INNER:mid] += tn(u, dr)
    gup[:, mid:end] += tn(u, ddt)
    du = nt(dz, b_ref[:, :INNER]) + nt(dr, b_ref[:, INNER:mid]) + nt(ddt, b_ref[:, mid:end])
    du = du.astype(BF16) * select_of(pos, meta).astype(BF16)
    gdown[...] += tn(du, hb)
    dh = nt(dz, w_ref[:, :INNER]) + nt(dr, w_ref[:, INNER:mid]) + nt(ddt, w_ref[:, mid:end]) + nt(du, a_ref[...])
    x = x_ref[...].astype(F32)
    rstd = lax.rsqrt(jnp.mean(x * x, 1, keepdims=True) + EPS)
    g = dh * gain_ref[...]
    back = jnp.mean(g * x, 1, keepdims=True) * rstd * rstd
    dx = rstd * (g - x * back)
    dx = ((dout_ref[...].astype(F32) + dx) * valid_of(pos, meta)).astype(BF16)
    hit = one_hot(iota((acc.shape[0], SPAN), 0) == where_ref[...])
    acc[...] += nn(hit, dx)

    @pl.when(k == pl.num_programs(0) - 1)
    def _():
        sorted_ref[...] = acc[...].astype(BF16)
        gup_ref[...] = gup[...].astype(BF16)
        gdown_ref[...] = gdown[...].astype(BF16)


def shape(*dims, dtype=F32):
    return jax.ShapeDtypeStruct(dims, dtype)


def params(mib=56):
    return pltpu.CompilerParams(vmem_limit_bytes=mib * MIB)


SMEM = pl.BlockSpec(memory_space=pltpu.SMEM)


def fixed(*dims):
    return pl.BlockSpec(dims, lambda i: (0,) * len(dims), pipeline_mode=pl.Buffered(1))


def kept(*dims):
    return pl.BlockSpec(dims, lambda i: (0,) * len(dims))


def row_tile(width):
    return pl.BlockSpec((SPAN, width), lambda i: (i, 0))


def blocked(*dims):
    return pl.BlockSpec((1,) + dims, lambda i: (i,) + (0,) * len(dims))


def permute(idx, x):
    rows, width = x.shape
    return pl.pallas_call(
        permute_kernel,
        grid=(rows // SPAN,),
        in_specs=[fixed(1, rows), fixed(rows, width)],
        out_specs=row_tile(width),
        out_shape=shape(rows, width, dtype=BF16),
        compiler_params=params(),
        name="permute",
    )(idx, x)


def a2a(x):
    return lax.all_to_all(x, "ctx", split_axis=0, concat_axis=0, tiled=True)


def shift_ctx(x, by):
    n = lax.axis_size("ctx")
    return lax.ppermute(x, "ctx", [(i, i + by) for i in range(n) if 0 <= i + by < n])


def local(
    tokens, cotangent, order, lengths, adapter_ids, in_weight, out_weight, in_down, in_up, out_down, out_up,
    norm_gain, conv_weight, conv_bias, dt_bias, a_log, skip_gain, gate_gain,
):
    n = lax.axis_size("ctx")
    me = lax.axis_index("ctx")
    rows, width = tokens.shape[1:]
    nb = rows // SPAN
    share = rows // n
    log_rows = rows.bit_length() - 1
    assert rows == 1 << log_rows and rows <= 1024 and rows % SPAN == 0
    proj_w = in_weight.shape[1]

    ends = jnp.cumsum(lengths[0])
    meta = jnp.concatenate([(me * rows)[None], ends, adapter_ids[0], me[None]]).astype(jnp.int32)
    by_source = order[0].reshape(n, rows)
    by_source = jnp.pad(by_source, ((0, -n % 16), (0, 0)), constant_values=-1)

    sent, spos = pl.pallas_call(
        partial(send_kernel, log_rows, share),
        in_specs=[SMEM] + [pl.BlockSpec(memory_space=pltpu.VMEM)] * 2,
        out_shape=(shape(rows, width, dtype=BF16), shape(1, rows, dtype=jnp.int32)),
        compiler_params=params(),
        name="send_tokens",
    )(meta, by_source, tokens[0])
    got = a2a(sent)
    got_cot = a2a(permute(spos, cotangent[0]))

    w_in = lax.all_gather(in_weight, "fsdp", axis=0, tiled=True)
    a_in = lax.all_gather(in_down, "fsdp", axis=1, tiled=True)
    b_in = lax.all_gather(in_up, "fsdp", axis=0, tiled=True)
    w_out = lax.all_gather(out_weight, "fsdp", axis=0, tiled=True)
    a_out = lax.all_gather(out_down, "fsdp", axis=1, tiled=True)
    b_out = lax.all_gather(out_up, "fsdp", axis=0, tiled=True)

    slot, where, tok = pl.pallas_call(
        partial(route_kernel, log_rows, share, n),
        in_specs=[SMEM] + [pl.BlockSpec(memory_space=pltpu.VMEM)] * 2,
        out_shape=(shape(1, rows, dtype=jnp.int32),) * 3,
        compiler_params=params(),
        name="route",
    )(meta, by_source, spos)

    heads_pad = lambda v: jnp.pad(v, (0, LANES - HEADS))[None]
    e = (jnp.arange(LANES)[:, None] == jnp.arange(INNER)[None, :] // HEAD).astype(BF16)
    bias = heads_pad(dt_bias)
    rate = heads_pad(-jnp.exp(a_log))
    skip = jnp.repeat(skip_gain, HEAD)[None]
    gain = norm_gain[None]
    gate = gate_gain[None]
    cb = conv_bias[None]

    x, hb, u, z, raw, dtr = pl.pallas_call(
        in_kernel,
        grid=(nb,),
        in_specs=[
            SMEM, fixed(1, rows), fixed(rows, width), fixed(width, proj_w), fixed(width, LOW), fixed(LOW, proj_w),
            fixed(1, width),
        ],
        out_specs=[row_tile(width), row_tile(width), row_tile(LOW), row_tile(INNER), row_tile(CONV_CH), row_tile(LANES)],
        out_shape=(
            shape(rows, width, dtype=BF16), shape(rows, width, dtype=BF16), shape(rows, LOW, dtype=BF16),
            shape(rows, INNER), shape(rows, CONV_CH, dtype=BF16), shape(rows, LANES),
        ),
        compiler_params=params(),
        name="in_proj",
    )(meta, slot, got, w_in, a_in, b_in, gain)

    halo = shift_ctx(raw[rows - 16 :], 1)

    xs, bm, cm, dact, dt, c2, c2t, wts, reach, ls, carry, send = pl.pallas_call(
        conv_kernel,
        grid=(nb,),
        in_specs=[
            SMEM, row_tile(CONV_CH), fixed(16, CONV_CH), row_tile(LANES), fixed(KERNEL, CONV_CH), fixed(1, CONV_CH),
            fixed(1, LANES), fixed(1, LANES), fixed(LANES, INNER),
        ],
        out_specs=[
            row_tile(INNER), row_tile(STATE), row_tile(STATE), row_tile(CONV_CH), row_tile(LANES), row_tile(LANES),
            blocked(HEADS, SPAN), row_tile(LANES), row_tile(LANES), blocked(STATE, INNER), blocked(8, INNER),
            kept(STATE + 16, INNER),
        ],
        out_shape=(
            shape(rows, INNER, dtype=BF16), shape(rows, STATE, dtype=BF16), shape(rows, STATE, dtype=BF16),
            shape(rows, CONV_CH, dtype=BF16), shape(rows, LANES), shape(rows, LANES),
            shape(nb, HEADS, SPAN), shape(rows, LANES), shape(rows, LANES), shape(nb, STATE, INNER), shape(nb, 8, INNER),
            shape(STATE + 16, INNER, dtype=BF16),
        ),
        scratch_shapes=[pltpu.VMEM((8, CONV_CH), F32), pltpu.VMEM((STATE, INNER), F32), pltpu.VMEM((8, INNER), F32)],
        compiler_params=params(),
        name="conv_state",
    )(meta, raw, halo, dtr, conv_weight, cb, bias, rate, e)

    states = lax.all_gather(send, "ctx")

    y = pl.pallas_call(
        within_kernel,
        grid=(nb,),
        in_specs=[
            SMEM, row_tile(INNER), row_tile(STATE), row_tile(STATE), row_tile(LANES), row_tile(LANES), blocked(HEADS, SPAN),
            fixed(LANES, INNER),
        ],
        out_specs=row_tile(INNER),
        out_shape=shape(rows, INNER),
        scratch_shapes=[pltpu.VMEM((SPAN, INNER), BF16), pltpu.VMEM((SPAN, SPAN), F32)],
        compiler_params=params(),
        name="within",
    )(meta, xs, bm, cm, dt, c2, c2t, e)

    def fold(parts, reverse):
        at = (lambda k: n - 1 - k) if reverse else (lambda k: k)
        return pl.pallas_call(
            partial(fold_kernel, reverse),
            grid=(n,),
            in_specs=[
                SMEM,
                pl.BlockSpec((1, STATE, INNER), lambda k: (at(k), 0, 0)),
                pl.BlockSpec((1, 16, INNER), lambda k: (at(k), STATE // 16, 0)),
            ],
            out_specs=kept(STATE, INNER),
            out_shape=shape(STATE, INNER),
            compiler_params=params(),
            name="fold",
        )(meta, parts, states)

    start_in = fold(states, False)

    start, after, mixed, nout, v, rstd, result = pl.pallas_call(
        out_kernel,
        grid=(nb,),
        in_specs=[
            SMEM, row_tile(INNER), row_tile(INNER), row_tile(INNER), row_tile(STATE), row_tile(LANES), row_tile(width),
            blocked(STATE, INNER), blocked(8, INNER), fixed(STATE, INNER), fixed(LANES, INNER), fixed(1, INNER),
            fixed(1, INNER), fixed(INNER, width), fixed(INNER, LOW), fixed(LOW, width),
            pl.BlockSpec((1, SPAN), lambda i: (0, i)),
        ],
        out_specs=[
            blocked(STATE, INNER), blocked(STATE, INNER), row_tile(INNER), row_tile(INNER), row_tile(LOW), row_tile(LANES),
            kept(rows, width),
        ],
        out_shape=(
            shape(nb, STATE, INNER, dtype=BF16), shape(nb, STATE, INNER, dtype=BF16), shape(rows, INNER),
            shape(rows, INNER, dtype=BF16), shape(rows, LOW, dtype=BF16), shape(rows, LANES), shape(rows, width, dtype=BF16),
        ),
        scratch_shapes=[
            pltpu.VMEM((STATE, INNER), F32), pltpu.VMEM((rows, width), F32), pltpu.VMEM((SPAN, INNER), F32),
            pltpu.VMEM((SPAN, INNER), F32),
        ],
        compiler_params=params(),
        name="gate_out",
    )(meta, y, z, xs, cm, reach, x, ls, carry, start_in, e, skip, gate, w_out, a_out, b_out, where)

    back_out = a2a(result)

    dout, dm, dz, rs, dcm1, dst, own, g_up_out, g_down_out = pl.pallas_call(
        gate_back_kernel,
        grid=(nb,),
        in_specs=[
            SMEM, row_tile(INNER), row_tile(INNER), row_tile(INNER), row_tile(LOW), row_tile(LANES), row_tile(INNER),
            row_tile(STATE), row_tile(LANES), blocked(STATE, INNER), blocked(8, INNER), fixed(rows, width), fixed(1, rows),
            fixed(LANES, INNER), fixed(1, INNER), fixed(1, INNER), fixed(INNER, width), fixed(INNER, LOW), fixed(LOW, width),
        ],
        out_specs=[
            row_tile(width), row_tile(INNER), row_tile(INNER), row_tile(LANES), row_tile(STATE), blocked(STATE, INNER),
            kept(STATE, INNER), kept(LOW, width), kept(LOW, INNER),
        ],
        out_shape=(
            shape(rows, width, dtype=BF16), shape(rows, INNER, dtype=BF16), shape(rows, INNER, dtype=BF16),
            shape(rows, LANES), shape(rows, STATE), shape(nb, STATE, INNER), shape(STATE, INNER, dtype=BF16),
            shape(LOW, width, dtype=BF16), shape(LOW, INNER, dtype=BF16),
        ),
        scratch_shapes=[
            pltpu.VMEM((STATE, INNER), F32), pltpu.VMEM((8, INNER), F32), pltpu.VMEM((LOW, width), F32),
            pltpu.VMEM((LOW, INNER), F32), pltpu.VMEM((SPAN, INNER), F32), pltpu.VMEM((SPAN, INNER), F32),
            pltpu.VMEM((SPAN, INNER), BF16), pltpu.VMEM((SPAN, INNER), BF16), pltpu.VMEM((SPAN, INNER), BF16),
        ],
        compiler_params=params(),
        name="gate_back",
    )(meta, mixed, z, nout, v, rstd, xs, cm, reach, start, carry, got_cot, slot, e, skip, gate, w_out, a_out, b_out)

    states_back = lax.all_gather(own, "ctx")
    later_in = fold(states_back, True)

    dxk, dbm, dcm = pl.pallas_call(
        mix_back_kernel,
        grid=(nb,),
        in_specs=[
            SMEM, row_tile(INNER), row_tile(STATE), row_tile(STATE), row_tile(INNER), row_tile(LANES), row_tile(LANES),
            blocked(HEADS, SPAN), row_tile(STATE), fixed(LANES, INNER),
        ],
        out_specs=[row_tile(INNER), row_tile(STATE), row_tile(STATE)],
        out_shape=(shape(rows, INNER), shape(rows, STATE), shape(rows, STATE)),
        scratch_shapes=[
            pltpu.VMEM((SPAN, INNER), BF16), pltpu.VMEM((SPAN, INNER), F32), pltpu.VMEM((SPAN, SPAN), F32),
            pltpu.VMEM((SPAN, SPAN), F32),
        ],
        compiler_params=params(),
        name="mix_back",
    )(meta, xs, bm, cm, dm, dt, c2, c2t, dcm1, e)

    back = lambda *dims: pl.BlockSpec((1,) + dims, lambda i: (nb - 1 - i,) + (0,) * len(dims))
    dl, dend, head = pl.pallas_call(
        later_kernel,
        grid=(nb,),
        in_specs=[
            fixed(STATE, INNER), back(STATE, INNER), back(8, INNER), back(STATE, INNER),
            fixed(LANES, INNER), fixed(1, INNER), fixed(16, INNER), fixed(16, STATE), fixed(16, INNER), fixed(16, INNER),
            fixed(16, STATE), fixed(16, STATE), fixed(16, LANES), fixed(16, CONV_CH),
        ],
        out_specs=[back(STATE, INNER), back(8, LANES), kept(16, CONV_CH)],
        out_shape=(shape(nb, STATE, INNER, dtype=BF16), shape(nb, 8, LANES), shape(16, CONV_CH)),
        scratch_shapes=[pltpu.VMEM((STATE, INNER), F32)],
        compiler_params=params(),
        name="later_state",
    )(later_in, dst, carry, after, e, skip, xs, bm, dm, dxk, dbm, dcm, wts, dact)

    from_next = shift_ctx(head, -1)

    tile = lambda w: pl.BlockSpec((SPAN, w), lambda i: (nb - 1 - i, 0))
    grad, g_up_in, g_down_in = pl.pallas_call(
        in_back_kernel,
        grid=(nb,),
        in_specs=[
            SMEM, back(STATE, INNER), back(8, LANES), tile(INNER), tile(STATE), tile(INNER), tile(INNER), tile(INNER),
            tile(STATE), tile(STATE), tile(LANES), tile(LANES), tile(LANES), tile(CONV_CH), fixed(16, CONV_CH),
            fixed(KERNEL, CONV_CH), fixed(LANES, INNER), fixed(1, INNER), fixed(1, LANES), fixed(1, LANES),
            fixed(width, proj_w), fixed(width, LOW), fixed(LOW, proj_w), tile(LOW), tile(width), tile(width), tile(width),
            fixed(1, width), pl.BlockSpec((1, SPAN), lambda i: (0, nb - 1 - i)),
        ],
        out_specs=[kept(rows, width), kept(LOW, proj_w), kept(LOW, width)],
        out_shape=(
            shape(rows, width, dtype=BF16), shape(LOW, proj_w, dtype=BF16), shape(LOW, width, dtype=BF16),
        ),
        scratch_shapes=[
            pltpu.VMEM((8, CONV_CH), F32), pltpu.VMEM((rows, width), F32), pltpu.VMEM((LOW, proj_w), F32),
            pltpu.VMEM((LOW, width), F32), pltpu.VMEM((SPAN, INNER), F32), pltpu.VMEM((SPAN, CONV_CH), F32),
            pltpu.VMEM((SPAN, INNER), BF16), pltpu.VMEM((SPAN, INNER), BF16), pltpu.VMEM((SPAN, CONV_CH), BF16),
        ],
        compiler_params=params(60),
        name="in_back",
    )(
        meta, dl, dend, xs, bm, dm, dz, dxk, dbm, dcm, wts, dtr, rs, dact, from_next, conv_weight, e, skip, bias, rate,
        w_in, a_in, b_in, u, hb, x, dout, gain, where,
    )

    back_grad = a2a(grad)

    def reduced(g):
        part = lax.psum_scatter(g, "fsdp", scatter_dimension=0, tiled=True)
        return lax.psum(part, "ctx").astype(F32)

    g_out = reduced(jnp.concatenate([g_down_out, g_up_out], 1))
    g_in = reduced(jnp.concatenate([g_down_in, g_up_in], 1))
    block_output = permute(tok, back_out)[None]
    input_grad = permute(tok, back_grad)[None]
    return (block_output, input_grad, g_in[:, :width].T, g_in[:, width:], g_out[:, :INNER].T, g_out[:, INNER:])


def solution(mesh):
    placed = (
        P("fsdp", "ctx", None),
        P("fsdp", "ctx", None),
        P("fsdp", None),
        P("fsdp", None),
        P("fsdp", None),
        P("fsdp", None),
        P("fsdp", None),
        P(None, "fsdp"),
        P("fsdp", None),
        P(None, "fsdp"),
        P("fsdp", None),
        P(),
        P(),
        P(),
        P(),
        P(),
        P(),
        P(),
    )
    return jax.shard_map(
        local,
        mesh=mesh,
        in_specs=placed,
        out_specs=(
            P("fsdp", "ctx", None),
            P("fsdp", "ctx", None),
            P(None, "fsdp"),
            P("fsdp", None),
            P(None, "fsdp"),
            P("fsdp", None),
        ),
        check_vma=False,
    )
```

```python
from functools import partial

import jax
import jax.numpy as jnp
from jax import lax
from jax.experimental import pallas as pl
from jax.experimental.pallas import tpu as pltpu
from jax.sharding import PartitionSpec as P

HEADS = 32
HEAD = 64
STATE = 128
KERNEL = 4
SPAN = 256
RANK = 16
ADAPTERS = 8
SEQS = 3
CONV_CH = 2304
INNER = HEADS * HEAD
LOW = ADAPTERS * RANK
LANES = 128
HALF = SPAN // 2
EPS = 1e-05
LOG2E = 1.4426950408889634

F32 = jnp.float32
BF16 = jnp.bfloat16
MIB = 1 << 20
MESH = pl.DeviceIdType.MESH


def nn(a, b):
    return jnp.dot(a, b, preferred_element_type=F32)


def nt(a, b):
    return lax.dot_general(a, b, (((1,), (1,)), ((), ())), preferred_element_type=F32)


def tn(a, b):
    return lax.dot_general(a, b, (((0,), (0,)), ((), ())), preferred_element_type=F32)


def iota(shape, dim):
    return lax.broadcasted_iota(jnp.int32, shape, dim)


def one_hot(cond):
    return jnp.where(cond, 1.0, 0.0).astype(BF16)


def split(v, parts):
    out = []
    for _ in range(parts):
        piece = v.astype(BF16)
        out.append(piece)
        v = v - piece.astype(F32)
    return out


def expand(v, e, parts=2):
    return sum(nn(p, e) for p in split(v, parts))


def seq_of(pos, meta):
    found = sum((pos >= meta[k]).astype(jnp.int32) for k in (1, 2, 3))
    return jnp.where(pos >= 0, found, -1)


def valid_of(pos, meta):
    return (pos < meta[3]).astype(F32)


def select_of(pos, meta):
    seq = seq_of(pos, meta)
    ids = jnp.where(seq == 0, meta[4], 0) + jnp.where(seq == 1, meta[5], 0) + jnp.where(seq == 2, meta[6], 0)
    shape = (pos.shape[0], LOW)
    return jnp.where(iota(shape, 1) // RANK == ids, 1.0, 0.0) * valid_of(pos, meta)


def sigmoid(v):
    return 1.0 / (1.0 + jnp.exp(-v))


def col_pos(meta, block, rows=SPAN):
    return meta[0] + block * SPAN + iota((rows, 1), 0)


def running_count(mask):
    width = mask.shape[1]
    tri = one_hot(iota((SPAN, SPAN), 0) <= iota((SPAN, SPAN), 1))
    pieces, before = [], jnp.zeros((mask.shape[0], 1), F32)
    for c in range(0, width, SPAN):
        part = mask[:, c : c + SPAN]
        pieces.append(nn(part.astype(BF16), tri) + before)
        before = before + jnp.sum(part, 1, keepdims=True)
    return jnp.concatenate(pieces, 1)


def two_rows(v):
    first = jnp.broadcast_to(v >> 5, (16, v.shape[1]))
    second = jnp.broadcast_to(v & 31, (16, v.shape[1]))
    row = iota((16, v.shape[1]), 0)
    return jnp.where(row == 0, first, jnp.where(row == 1, second, 0)).astype(F32).astype(BF16)


def from_two(r):
    return (r[0:1] * 32.0 + r[1:2]).astype(jnp.int32)


def invert(idx):
    width = idx.shape[1]
    values = two_rows(iota((1, width), 1))
    pieces = []
    for t in range(0, width, SPAN):
        hit = one_hot(iota((SPAN, width), 0) + t == idx)
        pieces.append(from_two(nt(values, hit)))
    return jnp.concatenate(pieces, 1)


def peers(axis):
    n, me = lax.axis_size(axis), lax.axis_index(axis)
    return [(k, lax.rem(me + k, n), lax.rem(me + n - k, n)) for k in range(1, n)]


def send(src, dst, send_sem, recv_sem, **where):
    return pltpu.make_async_remote_copy(
        src_ref=src, dst_ref=dst, send_sem=send_sem, recv_sem=recv_sem, device_id=where, device_id_type=MESH
    )


def greet(targets):
    barrier = pltpu.get_barrier_semaphore()
    for where in targets:
        pl.semaphore_signal(barrier, inc=1, device_id=where, device_id_type=MESH)
    pl.semaphore_wait(barrier, len(targets))


def arrive_kernel(
    log_rows, share, order_ref, x_ref, cot_ref, w_ref, ad_ref,
    got_ref, cots_ref, slot_ref, where_ref, tok_ref, wall_ref, adall_ref,
    sorted_ref, s_tok, r_tok, s_w, r_w, s_c, r_c, local_sem,
):
    n, me = lax.axis_size("ctx"), lax.axis_index("ctx")
    nf, f = lax.axis_size("fsdp"), lax.axis_index("fsdp")
    pair = f + 1 - 2 * lax.rem(f, 2)
    sides = [lax.rem(f + 2 * k, nf) for k in range(1, nf // 2)]
    backs = [lax.rem(f + nf - 2 * k, nf) for k in range(1, nf // 2)]
    rows = x_ref.shape[0]
    kw, ka = w_ref.shape[0], ad_ref.shape[0]

    greet([{"ctx": p} for _, p, _ in peers("ctx")] + [{"fsdp": p} for p in sides + [pair]])

    def shard(ref, which, k):
        return ref.at[pl.ds(pl.multiple_of(which * k, k), k), :]

    own = [(ad_ref, adall_ref, ka), (w_ref, wall_ref, kw)]
    across = []
    for k, side in enumerate(sides):
        across.append([send(src, shard(dst, f, h), s_w.at[k, m], r_w.at[k, m], fsdp=side) for m, (src, dst, h) in enumerate(own)])
        for c in across[-1]:
            c.start()
    inside = []
    for m, (src, dst, h) in enumerate(own):
        c = send(src, shard(dst, f, h), s_c.at[0, m], r_c.at[0, m], fsdp=pair)
        c.start()
        inside.append(c)
    keep = [pltpu.make_async_copy(src, shard(dst, f, h), local_sem.at[m]) for m, (src, dst, h) in enumerate(own)]
    for c in keep:
        c.start()

    own_order = order_ref[pl.ds(me, 1), :]
    dest = own_order >> log_rows
    hot = jnp.where(iota((order_ref.shape[0], rows), 0) == dest, 1.0, 0.0)
    rank = jnp.sum(hot * (running_count(hot) - 1.0), axis=0, keepdims=True)
    spos = dest * share + rank.astype(jnp.int32)
    x = x_ref[...]

    def place(which):
        return pl.ds(pl.multiple_of(which * share, share), share)

    tokens = []
    for k, to, _ in peers("ctx"):
        hit = one_hot(iota((share, rows), 0) + to * share == spos)
        sorted_ref[place(to), :] = nn(hit, x).astype(BF16)
        c = send(sorted_ref.at[place(to), :], got_ref.at[place(me), :], s_tok.at[k - 1], r_tok.at[k - 1], ctx=to)
        c.start()
        tokens.append(c)
    hit = one_hot(iota((share, rows), 0) + me * share == spos)
    sorted_ref[place(me), :] = nn(hit, x).astype(BF16)
    mine_copy = pltpu.make_async_copy(sorted_ref.at[place(me), :], got_ref.at[place(me), :], local_sem.at[2])
    mine_copy.start()

    cot = cot_ref[...]
    for t in range(0, rows, SPAN):
        cots_ref[t : t + SPAN, :] = nn(one_hot(iota((SPAN, rows), 0) + t == spos), cot).astype(BF16)
    order = order_ref[...]
    mine = jnp.where(order >> log_rows == me, 1.0, 0.0)
    slot = order & (rows - 1)
    mark = jnp.where(mine > 0.0, running_count(mine) - 1.0, -1.0).astype(jnp.int32)
    for s in range(n):
        hit = one_hot(iota((share, rows), 0) == mark[s : s + 1, :])
        slot_ref[:, s * share : (s + 1) * share] = from_two(nt(two_rows(slot[s : s + 1, :]), hit))
    where_ref[...] = invert(slot_ref[...])
    tok_ref[...] = invert(spos)

    for k, back in enumerate(backs):
        for m, (src, dst, h) in enumerate(own):
            across[k][m].wait_recv()
            c = send(shard(dst, back, h), shard(dst, back, h), s_c.at[k + 1, m], r_c.at[k + 1, m], fsdp=pair)
            c.start()
            inside.append(c)
    for c in inside:
        c.wait()
    for group in across:
        for c in group:
            c.wait_send()
    for c in tokens:
        c.wait()
    for c in keep + [mine_copy]:
        c.wait()


def owners_of(n):
    return min(n, INNER // LANES)


def each_owner(n, which, act):
    if owners_of(n) == n:
        act()
    else:
        pl.when(which < owners_of(n))(act)


class Exchange:
    def __init__(self, parts, through, first, starts, landed, sems, reverse):
        self.parts, self.through, self.first, self.starts, self.landed = parts, through, first, starts, landed
        self.s1, self.r1, self.s2, self.r2 = sems
        self.reverse = reverse
        self.n, self.me = lax.axis_size("ctx"), lax.axis_index("ctx")

    def out(self, k, to):
        return send(self.parts.at[to], self.first.at[self.me], self.s1.at[k - 1], self.r1.at[k - 1], ctx=to)

    def back(self, k, to):
        return send(self.starts.at[to], self.landed.at[self.me], self.s2.at[k - 1], self.r2.at[k - 1], ctx=to)

    def begin(self):
        greet([{"ctx": p} for _, p, _ in peers("ctx")])
        for k, to, _ in peers("ctx"):
            each_owner(self.n, to, lambda: self.out(k, to).start())

    def middle(self):
        n, me = self.n, self.me

        def act():
            self.first[me] = self.parts[me]
            for k, to, _ in peers("ctx"):
                self.out(k, to).wait_recv()

            def lap(t, running):
                j = n - 1 - t if self.reverse else t
                self.starts[j] = running.astype(BF16)
                part = self.first[j].astype(F32)
                through = self.through(self.first, j)
                return running * through + part[:STATE]

            lax.fori_loop(0, n, lap, jnp.zeros((STATE, self.first.shape[2]), F32))
            self.landed[me] = self.starts[me]
            for k, to, _ in peers("ctx"):
                self.back(k, to).start()

        each_owner(n, me, act)

    def finish(self, result):
        n, me = self.n, self.me
        for k, to, back in peers("ctx"):
            each_owner(n, back, lambda: self.back(k, to).wait_recv())
        w = self.landed.shape[2]
        for j in range(owners_of(n)):
            result[:, j * w : (j + 1) * w] = self.landed[j]
        for k, to, _ in peers("ctx"):
            each_owner(n, to, lambda: self.out(k, to).wait_send())

        def act():
            for k, to, _ in peers("ctx"):
                self.back(k, to).wait_send()

        each_owner(n, me, act)


def reduce_kernel(g_ref, out_ref, pair_in, pair_sum, side_in, total, ctx_in, piece, all_in, sems):
    n, me = lax.axis_size("ctx"), lax.axis_index("ctx")
    nf, f = lax.axis_size("fsdp"), lax.axis_index("fsdp")
    core = lax.rem(f, 2)
    pair = f + 1 - 2 * core
    sides = [lax.rem(f + 2 * k, nf) for k in range(1, nf // 2)]
    h = g_ref.shape[0] // nf
    cw = g_ref.shape[1] // n
    greet([{"ctx": p} for _, p, _ in peers("ctx")] + [{"fsdp": p} for p in sides + [pair]])

    def rows(which):
        return pl.ds(pl.multiple_of(which * h, h), h)

    first = []
    for y in range(nf // 2):
        c = send(g_ref.at[rows(2 * y + 1 - core), :], pair_in.at[y], sems.at[0, y], sems.at[1, y], fsdp=pair)
        c.start()
        first.append(c)
    for y in range(nf // 2):
        first[y].wait_recv()
        both = g_ref[rows(2 * y + core), :].astype(F32) + pair_in[y].astype(F32)
        pair_sum[y] = both.astype(BF16)
    second = []
    for k, side in enumerate(sides):
        c = send(pair_sum.at[side // 2], side_in.at[k], sems.at[2, k], sems.at[3, k], fsdp=side)
        c.start()
        second.append(c)
    mine = pair_sum[f // 2].astype(F32)
    for k, c in enumerate(second):
        c.wait_recv()
        mine = mine + side_in[k].astype(F32)
    for j in range(n):
        total[j] = mine[:, j * cw : (j + 1) * cw].astype(BF16)
    third = []
    for k, to, _ in peers("ctx"):
        c = send(total.at[to], ctx_in.at[k - 1], sems.at[4, k - 1], sems.at[5, k - 1], ctx=to)
        c.start()
        third.append(c)
    mine = total[me].astype(F32)
    for k, c in enumerate(third):
        c.wait_recv()
        mine = mine + ctx_in[k].astype(F32)
    piece[...] = mine.astype(BF16)
    fourth = []
    for k, to, _ in peers("ctx"):
        c = send(piece, all_in.at[me], sems.at[6, k - 1], sems.at[7, k - 1], ctx=to)
        c.start()
        fourth.append(c)
    all_in[me] = piece[...]
    for c in fourth:
        c.wait_recv()
    for j in range(n):
        out_ref[:, j * cw : (j + 1) * cw] = all_in[j].astype(F32)
    for c in first + second + third + fourth:
        c.wait_send()


def permute_kernel(idx_ref, x_ref, out_ref):
    hit = one_hot(iota((out_ref.shape[0], x_ref.shape[0]), 0) + pl.program_id(0) * out_ref.shape[0] == idx_ref[...])
    out_ref[...] = nn(hit, x_ref[...]).astype(BF16)


def in_kernel(meta, slot_ref, got_ref, w_ref, ad_ref, gain_ref, x_ref, hb_ref, u_ref, z_ref, raw_ref, dtr_ref):
    i = pl.program_id(0)
    rows = got_ref.shape[0]
    pos = col_pos(meta, i)
    hit = one_hot(iota((SPAN, rows), 0) + i * SPAN == slot_ref[...])
    x = nn(hit, got_ref[...]) * valid_of(pos, meta)
    x_ref[...] = x.astype(BF16)
    h = x * lax.rsqrt(jnp.mean(x * x, 1, keepdims=True) + EPS) * gain_ref[...]
    hb = h.astype(BF16)
    hb_ref[...] = hb
    d = hb.shape[1]
    u = (nt(hb, ad_ref[:, :d]) * select_of(pos, meta)).astype(BF16)
    u_ref[...] = u
    base = 2 * d + INNER

    def part(lo, hi):
        return nn(hb, w_ref[:, lo:hi]) + nn(u, ad_ref[:, base + lo : base + hi])

    for c in range(0, INNER, 512):
        z_ref[:, c : c + 512] = part(c, c + 512)
    for c in range(0, CONV_CH, 256):
        raw_ref[:, c : c + 256] = part(INNER + c, INNER + c + 256).astype(BF16)
    last = part(INNER + CONV_CH, INNER + CONV_CH + HEADS)
    dtr_ref[...] = jnp.concatenate([last, jnp.zeros((SPAN, LANES - HEADS), F32)], 1)


def softplus(v):
    e = jnp.exp(-jnp.abs(v))
    series = e * (1.0 - e * (0.5 - e * (1.0 / 3.0 - 0.25 * e)))
    return jnp.maximum(v, 0.0) + jnp.where(e < 0.01, series, jnp.log(1.0 + e))


def conv_kernel(
    meta, raw_ref, halo_ref, dtr_ref, cw_ref, cb_ref, bias_ref, rate_ref, e_ref,
    xs_ref, bm_ref, cm_ref, dact_ref, dt_ref, c2_ref, c2t_ref, wts_ref, reach_ref, ls_ref, carry_ref, send_ref,
    tail, state, through,
):
    i = pl.program_id(0)

    @pl.when(i == 0)
    def _():
        tail[...] = halo_ref[8:16, :].astype(F32)
        state[...] = jnp.zeros_like(state)
        through[...] = jnp.ones_like(through)

    pos = col_pos(meta, i)
    seq = seq_of(pos, meta)
    masks = [(seq_of(pos - j, meta) == seq).astype(F32) for j in range(KERNEL)]
    for c in range(0, CONV_CH, 256):
        cur = raw_ref[:, c : c + 256].astype(F32)
        ext = jnp.concatenate([tail[:, c : c + 256], cur], 0)
        acc = cb_ref[:, c : c + 256] + cw_ref[3:4, c : c + 256] * cur
        for j in range(1, KERNEL):
            moved = pltpu.roll(ext, j, 0)[8:]
            acc = acc + (cw_ref[3 - j : 4 - j, c : c + 256] * moved) * masks[j]
        sg = sigmoid(acc)
        act = acc * sg
        dact_ref[:, c : c + 256] = (sg + act * (1.0 - sg)).astype(BF16)
        act = act.astype(BF16)
        if c < INNER:
            xs_ref[:, c : c + 256] = act
        else:
            bm_ref[...] = act[:, :STATE]
            cm_ref[...] = act[:, STATE:]
        tail[:, c : c + 256] = cur[SPAN - 8 :]
    dt = softplus(dtr_ref[...] + bias_ref[...])
    dt_ref[...] = dt
    tri = one_hot(iota((SPAN, SPAN), 0) >= iota((SPAN, SPAN), 1))
    cum = sum(nn(tri, p) for p in split(dt * rate_ref[...], 3))
    cum_end = cum[SPAN - 1 : SPAN, :]
    end = meta[0] + i * SPAN + SPAN - 1
    end_same = (seq == seq_of(end, meta)).astype(F32)
    passing = (seq == seq_of(meta[0] + i * SPAN - 1, meta)).astype(F32)
    wts = jnp.exp(cum_end - cum) * dt * end_same
    wts_ref[...] = wts
    reach = jnp.exp(cum) * passing
    reach_ref[...] = reach
    c2 = cum * LOG2E
    c2_ref[...] = c2
    c2t_ref[0] = c2.T[:HEADS]
    weighted = (xs_ref[...].astype(F32) * expand(wts, e_ref[...])).astype(BF16)
    ls = tn(bm_ref[...], weighted)
    ls_ref[0] = ls
    carry = expand(jnp.broadcast_to(reach[SPAN - 1 : SPAN, :], (16, LANES)), e_ref[...], 3)[:8]
    carry_ref[0] = carry
    state[...] = state[...] * carry[0:1] + ls
    through[...] = through[...] * carry

    @pl.when(i == pl.num_programs(0) - 1)
    def _():
        w = send_ref.shape[2]
        for j in range(send_ref.shape[0]):
            at = slice(j * w, (j + 1) * w)
            send_ref[j, :STATE] = state[:, at].astype(BF16)
            send_ref[j, STATE:] = jnp.broadcast_to(through[0:1, at], (16, w)).astype(BF16)


def block_mask(meta, i, transposed):
    col = col_pos(meta, i)
    row = meta[0] + i * SPAN + iota((1, SPAN), 1)
    same = seq_of(col, meta) == seq_of(row, meta)
    return same & ((row >= col) if transposed else (col >= row))


def halves(x):
    lane = iota(x.shape, 1)
    zero = jnp.zeros_like(x)
    return jnp.where(lane < HEAD, x, zero), jnp.where(lane >= HEAD, x, zero)


def within_kernel(
    meta, xs_ref, bm_ref, cm_ref, dt_ref, c2_ref, c2t_ref, e_ref, parts_ref, pin_ref,
    y_ref, start_ref, thr_ref,
    xdt, sc, first, starts, landed, *sems,
):
    i = pl.program_id(0)
    exchange = Exchange(
        parts_ref, lambda first, j: first[j, STATE:].astype(F32)[0:1], first, starts, landed, sems, False
    )
    pl.when(i == 0)(exchange.begin)
    sc[...] = jnp.where(block_mask(meta, i, False), nt(cm_ref[...], bm_ref[...]), 0.0)
    xdt[...] = (xs_ref[...].astype(F32) * expand(dt_ref[...], e_ref[...])).astype(BF16)
    c2 = c2_ref[...]

    def group(g, _):
        cols = pltpu.roll(c2, LANES - 8 * g, 1)
        rows = c2t_ref[0, pl.ds(pl.multiple_of(8 * g, 8), 8), :]
        for q in range(4):
            at = pl.ds(pl.multiple_of(g * 512 + q * 128, 128), 128)
            xa, xb = halves(xdt[:, at])
            mixes = []
            for h in (2 * q, 2 * q + 1):
                col, row = cols[:, h : h + 1], rows[h : h + 1, :]

                def mix(t, s):
                    decay = jnp.exp2(jnp.minimum(col[t : t + HALF] - row[:, s : s + HALF], 0.0))
                    return (sc[t : t + HALF, s : s + HALF] * decay).astype(BF16)

                mixes.append((mix(0, 0), mix(HALF, 0), mix(HALF, HALF)))
            (a00, a10, a11), (b00, b10, b11) = mixes
            y_ref[:HALF, at] = nn(jnp.concatenate([a00, b00], 1), jnp.concatenate([xa[:HALF], xb[:HALF]], 0))
            y_ref[HALF:, at] = nn(jnp.concatenate([a10, a11, b10, b11], 1), jnp.concatenate([xa, xb], 0))
        return 0

    lax.fori_loop(0, HEADS // 8, group, 0)
    steps = pl.num_programs(0)
    pl.when(i == steps - 2)(exchange.middle)

    @pl.when(i == steps - 1)
    def _():
        exchange.finish(start_ref)
        for j in range(thr_ref.shape[0]):
            thr_ref[j] = first[j, STATE:]


CHUNK = 32


def out_kernel(
    meta, y_ref, z_ref, xs_ref, cm_ref, reach_ref, x_ref, ls_ref, carry_ref, all_ref, e_ref, skip_ref, gain_ref,
    w_ref, ad_ref, where_ref,
    start_ref, next_ref, mixed_ref, nout_ref, v_ref, rstd_ref, sorted_ref,
    run, acc, proj, wide,
):
    i = pl.program_id(0)

    @pl.when(i == 0)
    def _():
        run[...] = all_ref[...].astype(F32)
        acc[...] = jnp.zeros_like(acc)

    start = run[...].astype(BF16)
    start_ref[0] = start
    later = run[...] * carry_ref[0, 0:1, :] + ls_ref[0]
    run[...] = later
    next_ref[0] = later.astype(BF16)
    proj[...] = nn(cm_ref[...], start)
    wide[...] = expand(reach_ref[...], e_ref[...])

    def rows_step(k, _):
        at = pl.ds(pl.multiple_of(k * CHUNK, CHUNK), CHUNK)
        total = jnp.zeros((CHUNK, LANES), F32)
        for c in range(0, INNER, 256):
            cs = slice(c, c + 256)
            mixed = y_ref[at, cs] + wide[at, cs] * proj[at, cs] + skip_ref[:, cs] * xs_ref[at, cs].astype(F32)
            mixed_ref[at, cs] = mixed
            z = z_ref[at, cs]
            gated = mixed * (z * sigmoid(z))
            wide[at, cs] = gated
            sq = gated * gated
            total = total + sq[:, :LANES] + sq[:, LANES:]
        rstd = lax.rsqrt(jnp.sum(total, 1, keepdims=True) * (1.0 / INNER) + EPS)
        rstd_ref[at, :] = jnp.broadcast_to(rstd, (CHUNK, LANES))
        for c in range(0, INNER, 256):
            cs = slice(c, c + 256)
            nout_ref[at, cs] = (wide[at, cs] * rstd * gain_ref[:, cs]).astype(BF16)
        return 0

    lax.fori_loop(0, SPAN // CHUNK, rows_step, 0)
    pos = col_pos(meta, i)
    nout = nout_ref[...]
    d = x_ref.shape[1]
    v = (nt(nout, ad_ref[:, d : d + INNER]) * select_of(pos, meta)).astype(BF16)
    v_ref[...] = v
    branch = nn(nout, w_ref[...]) + nn(v, ad_ref[:, d + INNER : 2 * d + INNER])
    result = ((x_ref[...].astype(F32) + branch) * valid_of(pos, meta)).astype(BF16)
    hit = one_hot(iota((acc.shape[0], SPAN), 0) == where_ref[...])
    acc[...] += nn(hit, result)

    @pl.when(i == pl.num_programs(0) - 1)
    def _():
        sorted_ref[...] = acc[...].astype(BF16)


def gate_back_kernel(
    meta, mixed_ref, z_ref, nout_ref, v_ref, rstd_ref, xs_ref, cm_ref, reach_ref, start_ref, carry_ref, cot_ref, slot_ref,
    e_ref, skip_ref, gain_ref, w_ref, ad_ref,
    dout_ref, dm_ref, dz_ref, rs_ref, dcm_ref, dst_ref, own_ref, g_ref,
    own, through, gup, gdown, dn, wide, hi_s, lo_s, dproj,
):
    i = pl.program_id(0)

    @pl.when(i == 0)
    def _():
        own[...] = jnp.zeros_like(own)
        through[...] = jnp.ones_like(through)
        gup[...] = jnp.zeros_like(gup)
        gdown[...] = jnp.zeros_like(gdown)

    pos = col_pos(meta, i)
    rows = cot_ref.shape[0]
    hit = one_hot(iota((SPAN, rows), 0) + i * SPAN == slot_ref[...])
    dout = (nn(hit, cot_ref[...]) * valid_of(pos, meta)).astype(BF16)
    dout_ref[...] = dout
    gup[...] += tn(v_ref[...], dout)
    d = dout_ref.shape[1]
    dv = nt(dout, ad_ref[:, d + INNER : 2 * d + INNER]).astype(BF16) * select_of(pos, meta).astype(BF16)
    gdown[...] += tn(dv, nout_ref[...])
    dn[...] = nt(dout, w_ref[...]) + nn(dv, ad_ref[:, d : d + INNER])
    wide[...] = expand(reach_ref[...], e_ref[...])

    def rows_step(k, _):
        at = pl.ds(pl.multiple_of(k * CHUNK, CHUNK), CHUNK)
        rstd = rstd_ref[at, :][:, 0:1]
        total = jnp.zeros((CHUNK, LANES), F32)
        for c in range(0, INNER, 256):
            cs = slice(c, c + 256)
            z = z_ref[at, cs]
            d = dn[at, cs] * gain_ref[:, cs]
            dn[at, cs] = d
            g = d * (mixed_ref[at, cs] * (z * sigmoid(z)))
            total = total + g[:, :LANES] + g[:, LANES:]
        back = jnp.sum(total, 1, keepdims=True) * (1.0 / INNER) * rstd * rstd
        for c in range(0, INNER, 256):
            cs = slice(c, c + 256)
            z = z_ref[at, cs]
            sg = sigmoid(z)
            silu = z * sg
            mixed = mixed_ref[at, cs]
            dg = rstd * (dn[at, cs] - mixed * silu * back)
            dm = (dg * silu).astype(BF16)
            dm_ref[at, cs] = dm
            dz_ref[at, cs] = (dg * mixed * (sg + silu * (1.0 - sg))).astype(BF16)
            dm = dm.astype(F32)
            dproj[at, cs] = (dm * wide[at, cs]).astype(BF16)
            hi, lo = split(dm * (mixed - skip_ref[:, cs] * xs_ref[at, cs].astype(F32)), 2)
            hi_s[at, cs] = hi
            lo_s[at, cs] = lo
        return 0

    lax.fori_loop(0, SPAN // CHUNK, rows_step, 0)
    rs_ref[...] = nt(hi_s[...], e_ref[...]) + nt(lo_s[...], e_ref[...])
    dcm_ref[...] = nt(dproj[...], start_ref[0])
    dst = tn(cm_ref[...], dproj[...])
    dst_ref[0] = dst
    own[...] += dst * through[0:1]
    through[...] = through[...] * carry_ref[0]

    @pl.when(i == pl.num_programs(0) - 1)
    def _():
        w = own_ref.shape[2]
        for j in range(own_ref.shape[0]):
            own_ref[j] = own[:, j * w : (j + 1) * w].astype(BF16)
        g_ref[:, :INNER] = gdown[...].astype(BF16)
        g_ref[:, INNER:] = gup[...].astype(BF16)


def mix_back_kernel(
    meta, xs_ref, bm_ref, cm_ref, dm_ref, dt_ref, c2_ref, c2t_ref, dcm1_ref, e_ref, parts_ref, thr_ref,
    dxk_ref, dbm_ref, dcm_ref, later_ref,
    xdt, dte, sct, dsc, first, starts, landed, *sems,
):
    i = pl.program_id(0)
    exchange = Exchange(parts_ref, lambda first, j: thr_ref[j].astype(F32)[0:1], first, starts, landed, sems, True)
    pl.when(i == 0)(exchange.begin)
    mask = block_mask(meta, i, True)
    sct[...] = jnp.where(mask, nt(bm_ref[...], cm_ref[...]), 0.0)
    dsc[...] = jnp.zeros_like(dsc)
    dte[...] = expand(dt_ref[...], e_ref[...])
    xdt[...] = (xs_ref[...].astype(F32) * dte[...]).astype(BF16)
    c2 = c2_ref[...]

    def group(g, _):
        cols = pltpu.roll(c2, LANES - 8 * g, 1)
        rows = c2t_ref[0, pl.ds(pl.multiple_of(8 * g, 8), 8), :]
        for q in range(4):
            at = pl.ds(pl.multiple_of(g * 512 + q * 128, 128), 128)
            dm = dm_ref[:, at]
            da, db = halves(dm)
            mixes = []
            for h, x in zip((2 * q, 2 * q + 1), halves(xdt[:, at])):
                col, row = cols[:, h : h + 1], rows[h : h + 1, :]
                top = nt(x[:HALF], dm)
                low = nt(x[HALF:], dm[HALF:])

                def mix(s, t, d):
                    decay = jnp.exp2(jnp.minimum(row[:, t : t + HALF] - col[s : s + HALF], 0.0))
                    dsc[s : s + HALF, t : t + HALF] += d * decay
                    return (sct[s : s + HALF, t : t + HALF] * decay).astype(BF16)

                mixes.append((mix(0, 0, top[:, :HALF]), mix(0, HALF, top[:, HALF:]), mix(HALF, HALF, low)))
            (a00, a01, a11), (b00, b01, b11) = mixes
            g_top = nn(jnp.concatenate([a00, a01, b00, b01], 1), jnp.concatenate([da, db], 0))
            g_low = nn(jnp.concatenate([a11, b11], 1), jnp.concatenate([da[HALF:], db[HALF:]], 0))
            dxk_ref[:HALF, at] = g_top * dte[:HALF, at]
            dxk_ref[HALF:, at] = g_low * dte[HALF:, at]
        return 0

    lax.fori_loop(0, HEADS // 8, group, 0)
    ds = jnp.where(mask, dsc[...], 0.0).astype(BF16)
    dbm_ref[...] = nn(ds, cm_ref[...])
    dcm_ref[...] = dcm1_ref[...] + tn(ds, bm_ref[...])
    steps = pl.num_programs(0)
    pl.when(i == steps - 2)(exchange.middle)
    pl.when(i == steps - 1)(lambda: exchange.finish(later_ref))


def later_kernel(
    all_ref, dst_ref, carry_ref, next_ref, e_ref, skip_ref,
    xs_ref, bm_ref, dm_ref, dxk_ref, dbm_ref, dcm_ref, wts_ref, dact_ref, pin_ref,
    dl_ref, dend_ref, head_ref,
    acc,
):
    i = pl.program_id(0)

    @pl.when(i == 0)
    def _():
        acc[...] = all_ref[...].astype(F32)

    a = acc[...]
    dl = a.astype(BF16)
    dl_ref[0] = dl
    total = jnp.sum(a * next_ref[0].astype(F32), 0, keepdims=True)
    total = jnp.broadcast_to(total, (16, INNER))
    dend_ref[0] = sum(nt(p, e_ref[...]) for p in split(total, 3))[:8]
    acc[...] = dst_ref[0] + carry_ref[0, 0:1, :] * a

    @pl.when(i == pl.num_programs(0) - 1)
    def _():
        wide = expand(wts_ref[...], e_ref[...])
        weighted = (xs_ref[...].astype(F32) * wide).astype(BF16)
        dxs = dxk_ref[...] + nn(bm_ref[...], dl) * wide + skip_ref[...] * dm_ref[...].astype(F32)
        head_ref[:, :INNER] = dxs * dact_ref[:, :INNER].astype(F32)
        dbm = dbm_ref[...] + nt(weighted, dl)
        head_ref[:, INNER : INNER + STATE] = dbm * dact_ref[:, INNER : INNER + STATE].astype(F32)
        head_ref[:, INNER + STATE :] = dcm_ref[...] * dact_ref[:, INNER + STATE :].astype(F32)


def in_back_kernel(
    meta, dl_ref, dend_ref, xs_ref, bm_ref, dm_ref, dz_ref, dxk_ref, dbm_ref, dcm_ref, wts_ref, dtr_ref, rs_ref, dact_ref,
    halo_ref, cw_ref, e_ref, skip_ref, bias_ref, rate_ref, w_ref, ad_ref, u_ref, hb_ref, x_ref, dout_ref, gain_ref,
    where_ref, gout_ref,
    sorted_ref, g_ref,
    head, acc, gup, gdown, wide, dacc, hi_s, lo_s, draw,
):
    k = pl.program_id(0)
    i = pl.num_programs(0) - 1 - k

    @pl.when(k == 0)
    def _():
        head[...] = halo_ref[:8, :]
        acc[...] = jnp.zeros_like(acc)
        gup[...] = jnp.zeros_like(gup)
        gdown[...] = jnp.zeros_like(gdown)

    wide[...] = expand(wts_ref[...], e_ref[...])
    dacc[:, :INNER] = nn(bm_ref[...], dl_ref[0])

    def rows_step(r, _):
        at = pl.ds(pl.multiple_of(r * CHUNK, CHUNK), CHUNK)
        for c in range(0, INNER, 256):
            cs = slice(c, c + 256)
            w = wide[at, cs]
            xs = xs_ref[at, cs].astype(F32)
            dx = dxk_ref[at, cs] + dacc[at, cs] * w
            hi, lo = split(xs * dx, 2)
            hi_s[at, cs] = hi
            lo_s[at, cs] = lo
            dx = dx + skip_ref[:, cs] * dm_ref[at, cs].astype(F32)
            dacc[at, cs] = dx * dact_ref[at, cs].astype(F32)
            draw[at, cs] = (xs * w).astype(BF16)
        return 0

    lax.fori_loop(0, SPAN // CHUNK, rows_step, 0)
    dbm = dbm_ref[...] + nt(draw[:, :INNER], dl_ref[0])
    dacc[:, INNER : INNER + STATE] = dbm * dact_ref[:, INNER : INNER + STATE].astype(F32)
    dacc[:, INNER + STATE :] = dcm_ref[...] * dact_ref[:, INNER + STATE :].astype(F32)
    csum = nt(hi_s[...], e_ref[...]) + nt(lo_s[...], e_ref[...])

    pos = col_pos(meta, i)
    seq = seq_of(pos, meta)
    masks = [(seq_of(pos + j, meta) == seq).astype(F32) for j in range(KERNEL)]
    for c in range(0, CONV_CH, 256):
        cs = slice(c, c + 256)
        cur = dacc[:, cs]
        ext = jnp.concatenate([cur, head[:, cs]], 0)
        total = cw_ref[3:4, cs] * cur
        for j in range(1, KERNEL):
            moved = pltpu.roll(ext, SPAN + 8 - j, 0)[:SPAN]
            total = total + (cw_ref[3 - j : 4 - j, cs] * moved) * masks[j]
        draw[:, cs] = total.astype(BF16)
        head[:, cs] = cur[:8]

    last = iota((SPAN, 1), 0) == SPAN - 1
    dcum = rs_ref[...] - csum + jnp.where(last, dend_ref[0, 0:1, :], 0.0)
    tri = one_hot(iota((SPAN, SPAN), 0) <= iota((SPAN, SPAN), 1))
    dsteps = sum(nn(tri, p) for p in split(dcum, 3))
    v = dtr_ref[...] + bias_ref[...]
    sg = sigmoid(v)
    e = jnp.exp(jnp.minimum(v, 0.0))
    ratio = jnp.where(v < -12.0, 1.0 - 0.5 * e, sg / jnp.maximum(softplus(v), 1e-7))
    ddt = (csum * ratio + dsteps * rate_ref[...] * sg).astype(BF16)[:, :HEADS]

    dz = dz_ref[...]
    dr = draw[...]
    u, hb = u_ref[...], hb_ref[...]
    mid, end = INNER + CONV_CH, INNER + CONV_CH + HEADS
    gup[:, :INNER] += tn(u, dz)
    gup[:, INNER:mid] += tn(u, dr)
    gup[:, mid:end] += tn(u, ddt)
    d = hb.shape[1]
    base = 2 * d + INNER
    du = (
        nt(dz, ad_ref[:, base : base + INNER])
        + nt(dr, ad_ref[:, base + INNER : base + mid])
        + nt(ddt, ad_ref[:, base + mid : base + end])
    )
    du = du.astype(BF16) * select_of(pos, meta).astype(BF16)
    gdown[...] += tn(du, hb)
    dh = nt(dz, w_ref[:, :INNER]) + nt(dr, w_ref[:, INNER:mid]) + nt(ddt, w_ref[:, mid:end]) + nn(du, ad_ref[:, :d])
    x = x_ref[...].astype(F32)
    rstd = lax.rsqrt(jnp.mean(x * x, 1, keepdims=True) + EPS)
    g = dh * gain_ref[...]
    back = jnp.mean(g * x, 1, keepdims=True) * rstd * rstd
    dx = rstd * (g - x * back)
    dx = ((dout_ref[...].astype(F32) + dx) * valid_of(pos, meta)).astype(BF16)
    hit = one_hot(iota((acc.shape[0], SPAN), 0) == where_ref[...])
    acc[...] += nn(hit, dx)

    @pl.when(k == pl.num_programs(0) - 1)
    def _():
        sorted_ref[...] = acc[...].astype(BF16)
        g_ref[:, :d] = gdown[...].astype(BF16)
        g_ref[:, d:base] = gout_ref[...]
        g_ref[:, base : base + end] = gup[...].astype(BF16)
        rest = g_ref.shape[1] - base - end
        g_ref[:, base + end :] = jnp.zeros((LOW, rest), BF16)


def shape(*dims, dtype=F32):
    return jax.ShapeDtypeStruct(dims, dtype)


def params(mib=56, remote=None):
    if remote is None:
        return pltpu.CompilerParams(vmem_limit_bytes=mib * MIB)
    return pltpu.CompilerParams(vmem_limit_bytes=mib * MIB, collective_id=remote, has_side_effects=True)


SMEM = pl.BlockSpec(memory_space=pltpu.SMEM)
VMEM = pl.BlockSpec(memory_space=pltpu.VMEM)
ANY = pl.BlockSpec(memory_space=pl.ANY)


def exchange_scratch(n, rows):
    owners = owners_of(n)
    w = INNER // owners
    return [
        pltpu.VMEM((n, rows, w), BF16), pltpu.VMEM((n, STATE, w), BF16), pltpu.VMEM((owners, STATE, w), BF16),
    ] + [pltpu.SemaphoreType.DMA((n - 1,))] * 4


def fixed(*dims):
    return pl.BlockSpec(dims, lambda i: (0,) * len(dims), pipeline_mode=pl.Buffered(1))


def kept(*dims):
    return pl.BlockSpec(dims, lambda i: (0,) * len(dims))


def row_tile(width):
    return pl.BlockSpec((SPAN, width), lambda i: (i, 0))


def blocked(*dims):
    return pl.BlockSpec((1,) + dims, lambda i: (i,) + (0,) * len(dims))


def permute(idx, x):
    rows, width = x.shape
    return pl.pallas_call(
        permute_kernel,
        grid=(rows // SPAN,),
        in_specs=[fixed(1, rows), fixed(rows, width)],
        out_specs=row_tile(width),
        out_shape=shape(rows, width, dtype=BF16),
        compiler_params=params(),
        name="permute",
    )(idx, x)


def a2a(x):
    return lax.all_to_all(x, "ctx", split_axis=0, concat_axis=0, tiled=True)


def shift_ctx(x, by):
    n = lax.axis_size("ctx")
    return lax.ppermute(x, "ctx", [(i, i + by) for i in range(n) if 0 <= i + by < n])


def local(
    tokens, cotangent, order, lengths, adapter_ids, in_weight, out_weight, in_down, in_up, out_down, out_up,
    norm_gain, conv_weight, conv_bias, dt_bias, a_log, skip_gain, gate_gain,
):
    n = lax.axis_size("ctx")
    me = lax.axis_index("ctx")
    rows, width = tokens.shape[1:]
    nb = rows // SPAN
    share = rows // n
    log_rows = rows.bit_length() - 1
    assert rows == 1 << log_rows and rows <= 1024 and rows % SPAN == 0
    proj_w = in_weight.shape[1]

    ends = jnp.cumsum(lengths[0])
    meta = jnp.concatenate([(me * rows)[None], ends, adapter_ids[0], me[None]]).astype(jnp.int32)
    by_source = order[0].reshape(n, rows)
    by_source = jnp.pad(by_source, ((0, -n % 16), (0, 0)), constant_values=-1)

    nf = lax.axis_size("fsdp")
    assert nf % 2 == 0 and share % 16 == 0
    adapters = jnp.concatenate([in_down.T, out_down.T, out_up, in_up], 1)
    kw, ka, cols = in_weight.shape[0], adapters.shape[0], adapters.shape[1]
    dma = pltpu.SemaphoreType.DMA
    got, cot_sorted, slot, where, tok, w_in, ad = pl.pallas_call(
        partial(arrive_kernel, log_rows, share),
        in_specs=[VMEM, VMEM, VMEM, ANY, ANY],
        out_specs=[ANY, VMEM, VMEM, VMEM, VMEM, ANY, ANY],
        out_shape=(
            shape(rows, width, dtype=BF16), shape(rows, width, dtype=BF16), shape(1, rows, dtype=jnp.int32),
            shape(1, rows, dtype=jnp.int32), shape(1, rows, dtype=jnp.int32), shape(kw * nf, proj_w, dtype=BF16),
            shape(ka * nf, cols, dtype=BF16),
        ),
        scratch_shapes=[
            pltpu.VMEM((rows, width), BF16), dma((n - 1,)), dma((n - 1,)), dma((nf // 2 - 1, 2)), dma((nf // 2 - 1, 2)),
            dma((nf // 2, 2)), dma((nf // 2, 2)), dma((3,)),
        ],
        compiler_params=params(remote=1),
        name="arrive",
    )(by_source, tokens[0], cotangent[0], in_weight, adapters)
    got_cot = a2a(cot_sorted)
    w_out = lax.all_gather(out_weight, "fsdp", axis=0, tiled=True)

    owners = owners_of(n)
    cw = -(-cols // (n * LANES)) * LANES
    heads_pad = lambda v: jnp.pad(v, (0, LANES - HEADS))[None]
    e = (jnp.arange(LANES)[:, None] == jnp.arange(INNER)[None, :] // HEAD).astype(BF16)
    bias = heads_pad(dt_bias)
    rate = heads_pad(-jnp.exp(a_log))
    skip = jnp.repeat(skip_gain, HEAD)[None]
    gain = norm_gain[None]
    gate = gate_gain[None]
    cb = conv_bias[None]

    x, hb, u, z, raw, dtr = pl.pallas_call(
        in_kernel,
        grid=(nb,),
        in_specs=[
            SMEM, fixed(1, rows), fixed(rows, width), fixed(width, proj_w), fixed(LOW, cols), fixed(1, width),
        ],
        out_specs=[row_tile(width), row_tile(width), row_tile(LOW), row_tile(INNER), row_tile(CONV_CH), row_tile(LANES)],
        out_shape=(
            shape(rows, width, dtype=BF16), shape(rows, width, dtype=BF16), shape(rows, LOW, dtype=BF16),
            shape(rows, INNER), shape(rows, CONV_CH, dtype=BF16), shape(rows, LANES),
        ),
        compiler_params=params(),
        name="in_proj",
    )(meta, slot, got, w_in, ad, gain)

    halo = shift_ctx(raw[rows - 16 :], 1)

    xs, bm, cm, dact, dt, c2, c2t, wts, reach, ls, carry, parts = pl.pallas_call(
        conv_kernel,
        grid=(nb,),
        in_specs=[
            SMEM, row_tile(CONV_CH), fixed(16, CONV_CH), row_tile(LANES), fixed(KERNEL, CONV_CH), fixed(1, CONV_CH),
            fixed(1, LANES), fixed(1, LANES), fixed(LANES, INNER),
        ],
        out_specs=[
            row_tile(INNER), row_tile(STATE), row_tile(STATE), row_tile(CONV_CH), row_tile(LANES), row_tile(LANES),
            blocked(HEADS, SPAN), row_tile(LANES), row_tile(LANES), blocked(STATE, INNER), blocked(8, INNER),
            kept(owners, STATE + 16, INNER // owners),
        ],
        out_shape=(
            shape(rows, INNER, dtype=BF16), shape(rows, STATE, dtype=BF16), shape(rows, STATE, dtype=BF16),
            shape(rows, CONV_CH, dtype=BF16), shape(rows, LANES), shape(rows, LANES),
            shape(nb, HEADS, SPAN), shape(rows, LANES), shape(rows, LANES), shape(nb, STATE, INNER), shape(nb, 8, INNER),
            shape(owners, STATE + 16, INNER // owners, dtype=BF16),
        ),
        scratch_shapes=[pltpu.VMEM((8, CONV_CH), F32), pltpu.VMEM((STATE, INNER), F32), pltpu.VMEM((8, INNER), F32)],
        compiler_params=params(),
        name="conv_state",
    )(meta, raw, halo, dtr, conv_weight, cb, bias, rate, e)

    y, start_in, thr = pl.pallas_call(
        within_kernel,
        grid=(nb,),
        in_specs=[
            SMEM, row_tile(INNER), row_tile(STATE), row_tile(STATE), row_tile(LANES), row_tile(LANES), blocked(HEADS, SPAN),
            fixed(LANES, INNER), VMEM, ANY,
        ],
        out_specs=[row_tile(INNER), kept(STATE, INNER), kept(n, 16, INNER // owners)],
        out_shape=(shape(rows, INNER), shape(STATE, INNER, dtype=BF16), shape(n, 16, INNER // owners, dtype=BF16)),
        scratch_shapes=[pltpu.VMEM((SPAN, INNER), BF16), pltpu.VMEM((SPAN, SPAN), F32)] + exchange_scratch(n, STATE + 16),
        compiler_params=params(remote=2),
        name="within",
    )(meta, xs, bm, cm, dt, c2, c2t, e, parts, got_cot)

    start, after, mixed, nout, v, rstd, result = pl.pallas_call(
        out_kernel,
        grid=(nb,),
        in_specs=[
            SMEM, row_tile(INNER), row_tile(INNER), row_tile(INNER), row_tile(STATE), row_tile(LANES), row_tile(width),
            blocked(STATE, INNER), blocked(8, INNER), fixed(STATE, INNER), fixed(LANES, INNER), fixed(1, INNER),
            fixed(1, INNER), fixed(INNER, width), fixed(LOW, cols),
            pl.BlockSpec((1, SPAN), lambda i: (0, i)),
        ],
        out_specs=[
            blocked(STATE, INNER), blocked(STATE, INNER), row_tile(INNER), row_tile(INNER), row_tile(LOW), row_tile(LANES),
            kept(rows, width),
        ],
        out_shape=(
            shape(nb, STATE, INNER, dtype=BF16), shape(nb, STATE, INNER, dtype=BF16), shape(rows, INNER),
            shape(rows, INNER, dtype=BF16), shape(rows, LOW, dtype=BF16), shape(rows, LANES), shape(rows, width, dtype=BF16),
        ),
        scratch_shapes=[
            pltpu.VMEM((STATE, INNER), F32), pltpu.VMEM((rows, width), F32), pltpu.VMEM((SPAN, INNER), F32),
            pltpu.VMEM((SPAN, INNER), F32),
        ],
        compiler_params=params(),
        name="gate_out",
    )(meta, y, z, xs, cm, reach, x, ls, carry, start_in, e, skip, gate, w_out, ad, where)

    back_out = a2a(result)

    dout, dm, dz, rs, dcm1, dst, own, g_out = pl.pallas_call(
        gate_back_kernel,
        grid=(nb,),
        in_specs=[
            SMEM, row_tile(INNER), row_tile(INNER), row_tile(INNER), row_tile(LOW), row_tile(LANES), row_tile(INNER),
            row_tile(STATE), row_tile(LANES), blocked(STATE, INNER), blocked(8, INNER), fixed(rows, width), fixed(1, rows),
            fixed(LANES, INNER), fixed(1, INNER), fixed(1, INNER), fixed(INNER, width), fixed(LOW, cols),
        ],
        out_specs=[
            row_tile(width), row_tile(INNER), row_tile(INNER), row_tile(LANES), row_tile(STATE), blocked(STATE, INNER),
            kept(owners, STATE, INNER // owners), kept(LOW, INNER + width),
        ],
        out_shape=(
            shape(rows, width, dtype=BF16), shape(rows, INNER, dtype=BF16), shape(rows, INNER, dtype=BF16),
            shape(rows, LANES), shape(rows, STATE), shape(nb, STATE, INNER), shape(owners, STATE, INNER // owners, dtype=BF16),
            shape(LOW, INNER + width, dtype=BF16),
        ),
        scratch_shapes=[
            pltpu.VMEM((STATE, INNER), F32), pltpu.VMEM((8, INNER), F32), pltpu.VMEM((LOW, width), F32),
            pltpu.VMEM((LOW, INNER), F32), pltpu.VMEM((SPAN, INNER), F32), pltpu.VMEM((SPAN, INNER), F32),
            pltpu.VMEM((SPAN, INNER), BF16), pltpu.VMEM((SPAN, INNER), BF16), pltpu.VMEM((SPAN, INNER), BF16),
        ],
        compiler_params=params(),
        name="gate_back",
    )(meta, mixed, z, nout, v, rstd, xs, cm, reach, start, carry, got_cot, slot, e, skip, gate, w_out, ad)

    dxk, dbm, dcm, later_in = pl.pallas_call(
        mix_back_kernel,
        grid=(nb,),
        in_specs=[
            SMEM, row_tile(INNER), row_tile(STATE), row_tile(STATE), row_tile(INNER), row_tile(LANES), row_tile(LANES),
            blocked(HEADS, SPAN), row_tile(STATE), fixed(LANES, INNER), VMEM, VMEM,
        ],
        out_specs=[row_tile(INNER), row_tile(STATE), row_tile(STATE), kept(STATE, INNER)],
        out_shape=(shape(rows, INNER), shape(rows, STATE), shape(rows, STATE), shape(STATE, INNER, dtype=BF16)),
        scratch_shapes=[
            pltpu.VMEM((SPAN, INNER), BF16), pltpu.VMEM((SPAN, INNER), F32), pltpu.VMEM((SPAN, SPAN), F32),
            pltpu.VMEM((SPAN, SPAN), F32),
        ] + exchange_scratch(n, STATE),
        compiler_params=params(remote=3),
        name="mix_back",
    )(meta, xs, bm, cm, dm, dt, c2, c2t, dcm1, e, own, thr)

    back = lambda *dims: pl.BlockSpec((1,) + dims, lambda i: (nb - 1 - i,) + (0,) * len(dims))
    dl, dend, head = pl.pallas_call(
        later_kernel,
        grid=(nb,),
        in_specs=[
            fixed(STATE, INNER), back(STATE, INNER), back(8, INNER), back(STATE, INNER),
            fixed(LANES, INNER), fixed(1, INNER), fixed(16, INNER), fixed(16, STATE), fixed(16, INNER), fixed(16, INNER),
            fixed(16, STATE), fixed(16, STATE), fixed(16, LANES), fixed(16, CONV_CH), ANY,
        ],
        out_specs=[back(STATE, INNER), back(8, LANES), kept(16, CONV_CH)],
        out_shape=(shape(nb, STATE, INNER, dtype=BF16), shape(nb, 8, LANES), shape(16, CONV_CH)),
        scratch_shapes=[pltpu.VMEM((STATE, INNER), F32)],
        compiler_params=params(),
        name="later_state",
    )(later_in, dst, carry, after, e, skip, xs, bm, dm, dxk, dbm, dcm, wts, dact, back_out)

    from_next = shift_ctx(head, -1)

    tile = lambda w: pl.BlockSpec((SPAN, w), lambda i: (nb - 1 - i, 0))
    grad, g_all = pl.pallas_call(
        in_back_kernel,
        grid=(nb,),
        in_specs=[
            SMEM, back(STATE, INNER), back(8, LANES), tile(INNER), tile(STATE), tile(INNER), tile(INNER), tile(INNER),
            tile(STATE), tile(STATE), tile(LANES), tile(LANES), tile(LANES), tile(CONV_CH), fixed(16, CONV_CH),
            fixed(KERNEL, CONV_CH), fixed(LANES, INNER), fixed(1, INNER), fixed(1, LANES), fixed(1, LANES),
            fixed(width, proj_w), fixed(LOW, cols), tile(LOW), tile(width), tile(width), tile(width),
            fixed(1, width), pl.BlockSpec((1, SPAN), lambda i: (0, nb - 1 - i)), fixed(LOW, INNER + width),
        ],
        out_specs=[kept(rows, width), kept(LOW, n * cw)],
        out_shape=(shape(rows, width, dtype=BF16), shape(LOW, n * cw, dtype=BF16)),
        scratch_shapes=[
            pltpu.VMEM((8, CONV_CH), F32), pltpu.VMEM((rows, width), F32), pltpu.VMEM((LOW, proj_w), F32),
            pltpu.VMEM((LOW, width), F32), pltpu.VMEM((SPAN, INNER), F32), pltpu.VMEM((SPAN, CONV_CH), F32),
            pltpu.VMEM((SPAN, INNER), BF16), pltpu.VMEM((SPAN, INNER), BF16), pltpu.VMEM((SPAN, CONV_CH), BF16),
        ],
        compiler_params=params(60),
        name="in_back",
    )(
        meta, dl, dend, xs, bm, dm, dz, dxk, dbm, dcm, wts, dtr, rs, dact, from_next, conv_weight, e, skip, bias, rate,
        w_in, ad, u, hb, x, dout, gain, where, g_out,
    )

    back_grad = a2a(grad)

    half, low = nf // 2, LOW // nf
    sums = pl.pallas_call(
        reduce_kernel,
        in_specs=[VMEM],
        out_specs=VMEM,
        out_shape=shape(low, n * cw),
        scratch_shapes=[
            pltpu.VMEM((half, low, n * cw), BF16), pltpu.VMEM((half, low, n * cw), BF16),
            pltpu.VMEM((max(half - 1, 1), low, n * cw), BF16), pltpu.VMEM((n, low, cw), BF16),
            pltpu.VMEM((n - 1, low, cw), BF16), pltpu.VMEM((low, cw), BF16), pltpu.VMEM((n, low, cw), BF16),
            dma((8, max(n, half))),
        ],
        compiler_params=params(remote=4),
        name="reduce",
    )(g_all)
    block_output = permute(tok, back_out)[None]
    input_grad = permute(tok, back_grad)[None]
    base = 2 * width + INNER
    return (
        block_output, input_grad, sums[:, :width].T, sums[:, base : base + proj_w], sums[:, width : width + INNER].T,
        sums[:, width + INNER : base],
    )


def solution(mesh):
    placed = (
        P("fsdp", "ctx", None),
        P("fsdp", "ctx", None),
        P("fsdp", None),
        P("fsdp", None),
        P("fsdp", None),
        P("fsdp", None),
        P("fsdp", None),
        P(None, "fsdp"),
        P("fsdp", None),
        P(None, "fsdp"),
        P("fsdp", None),
        P(),
        P(),
        P(),
        P(),
        P(),
        P(),
        P(),
    )
    return jax.shard_map(
        local,
        mesh=mesh,
        in_specs=placed,
        out_specs=(
            P("fsdp", "ctx", None),
            P("fsdp", "ctx", None),
            P(None, "fsdp"),
            P("fsdp", None),
            P(None, "fsdp"),
            P("fsdp", None),
        ),
        check_vma=False,
    )
```

```python
from functools import partial

import jax
import jax.numpy as jnp
from jax import lax
from jax.experimental import pallas as pl
from jax.experimental.pallas import tpu as pltpu
from jax.sharding import PartitionSpec as P

HEADS = 32
HEAD = 64
STATE = 128
KERNEL = 4
SPAN = 256
RANK = 16
ADAPTERS = 8
SEQS = 3
CONV_CH = 2304
INNER = HEADS * HEAD
LOW = ADAPTERS * RANK
LANES = 128
HALF = SPAN // 2
EPS = 1e-05
LOG2E = 1.4426950408889634

F32 = jnp.float32
BF16 = jnp.bfloat16
MIB = 1 << 20
MESH = pl.DeviceIdType.MESH


def nn(a, b):
    return jnp.dot(a, b, preferred_element_type=F32)


def nt(a, b):
    return lax.dot_general(a, b, (((1,), (1,)), ((), ())), preferred_element_type=F32)


def tn(a, b):
    return lax.dot_general(a, b, (((0,), (0,)), ((), ())), preferred_element_type=F32)


def iota(shape, dim):
    return lax.broadcasted_iota(jnp.int32, shape, dim)


def one_hot(cond):
    return jnp.where(cond, 1.0, 0.0).astype(BF16)


def split(v, parts):
    out = []
    for _ in range(parts):
        piece = v.astype(BF16)
        out.append(piece)
        v = v - piece.astype(F32)
    return out


def pairs(v):
    return jnp.concatenate(split(v, 2), 1)


class Meta:
    def __init__(self, len_ref, id_ref, rows):
        self.start = lax.axis_index("ctx") * rows
        self.ends = []
        for k in range(SEQS):
            self.ends.append(len_ref[0, k] + (self.ends[-1] if k else 0))
        self.ids = [id_ref[0, k] for k in range(SEQS)]

    def seq(self, pos):
        found = sum((pos >= end).astype(jnp.int32) for end in self.ends)
        return jnp.where(pos >= 0, found, -1)

    def valid(self, pos):
        return (pos < self.ends[-1]).astype(F32)

    def select(self, pos):
        seq = self.seq(pos)
        ids = sum(jnp.where(seq == k, self.ids[k], 0) for k in range(SEQS))
        shape = (pos.shape[0], LOW)
        return jnp.where(iota(shape, 1) // RANK == ids, 1.0, 0.0) * self.valid(pos)

    def cols(self, tile):
        return self.start + tile * SPAN + iota((SPAN, 1), 0)

    def rows(self, tile):
        return self.start + tile * SPAN + iota((1, SPAN), 1)


def sigmoid(v):
    return 0.5 * jnp.tanh(0.5 * v) + 0.5


def running_count(mask):
    width = mask.shape[1]
    tri = one_hot(iota((SPAN, SPAN), 0) <= iota((SPAN, SPAN), 1))
    pieces, before = [], jnp.zeros((mask.shape[0], 1), F32)
    for c in range(0, width, SPAN):
        part = mask[:, c : c + SPAN]
        pieces.append(nn(part.astype(BF16), tri) + before)
        before = before + jnp.sum(part, 1, keepdims=True)
    return jnp.concatenate(pieces, 1)


def two_rows(v):
    first = jnp.broadcast_to(v >> 5, (16, v.shape[1]))
    second = jnp.broadcast_to(v & 31, (16, v.shape[1]))
    row = iota((16, v.shape[1]), 0)
    return jnp.where(row == 0, first, jnp.where(row == 1, second, 0)).astype(F32).astype(BF16)


def from_two(r):
    return (r[0:1] * 32.0 + r[1:2]).astype(jnp.int32)


def invert(idx):
    width = idx.shape[1]
    values = two_rows(iota((1, width), 1))
    pieces = []
    for t in range(0, width, SPAN):
        hit = one_hot(iota((SPAN, width), 0) + t == idx)
        pieces.append(from_two(nt(values, hit)))
    return jnp.concatenate(pieces, 1)


def peers(axis):
    n, me = lax.axis_size(axis), lax.axis_index(axis)
    return [(k, lax.rem(me + k, n), lax.rem(me + n - k, n)) for k in range(1, n)]


def send(src, dst, send_sem, recv_sem, **where):
    return pltpu.make_async_remote_copy(
        src_ref=src, dst_ref=dst, send_sem=send_sem, recv_sem=recv_sem, device_id=where, device_id_type=MESH
    )


def hail(targets):
    barrier = pltpu.get_barrier_semaphore()
    for where in targets:
        pl.semaphore_signal(barrier, inc=1, device_id=where, device_id_type=MESH)


def hailed(targets):
    pl.semaphore_wait(pltpu.get_barrier_semaphore(), len(targets))


def place(which, share):
    return pl.ds(pl.multiple_of(which * share, share), share)


def spread_sems(n):
    return [pltpu.SemaphoreType.DMA((n - 1,)), pltpu.SemaphoreType.DMA((n - 1,)), pltpu.SemaphoreType.DMA]


def ring_targets():
    n, me = lax.axis_size("ctx"), lax.axis_index("ctx")
    return [{"ctx": lax.rem(me + 1, n)}, {"ctx": lax.rem(me + n - 1, n)}]


def ctx_targets():
    return [{"ctx": p} for _, p, _ in peers("ctx")]


def fsdp_sides():
    nf, f = lax.axis_size("fsdp"), lax.axis_index("fsdp")
    sides = [lax.rem(f + 2 * k, nf) for k in range(1, nf // 2)]
    backs = [lax.rem(f + nf - 2 * k, nf) for k in range(1, nf // 2)]
    return f, f + 1 - 2 * lax.rem(f, 2), sides, backs


def fsdp_targets():
    _, pair, sides, _ = fsdp_sides()
    return [{"fsdp": p} for p in sides + [pair]]


class Gather:
    def __init__(self, pieces, sems):
        s_y, r_y, s_c, r_c, keep = sems
        f, pair, sides, backs = fsdp_sides()
        self.across = [
            [send(src, dst(f), s_y.at[k, m], r_y.at[k, m], fsdp=side) for m, (src, dst) in enumerate(pieces)]
            for k, side in enumerate(sides)
        ]
        self.inside = [[send(src, dst(f), s_c.at[0, m], r_c.at[0, m], fsdp=pair) for m, (src, dst) in enumerate(pieces)]]
        self.inside += [
            [send(dst(back), dst(back), s_c.at[k + 1, m], r_c.at[k + 1, m], fsdp=pair) for m, (src, dst) in enumerate(pieces)]
            for k, back in enumerate(backs)
        ]
        self.keep = [pltpu.make_async_copy(src, dst(f), keep.at[m]) for m, (src, dst) in enumerate(pieces)]

    def begin(self):
        for group in self.across:
            for c in group:
                c.start()
        for c in self.inside[0] + self.keep:
            c.start()

    def relay(self, lo=0, hi=None):
        for k, group in enumerate(self.across):
            for c, forward in list(zip(group, self.inside[k + 1]))[lo:hi]:
                c.wait_recv()
                forward.start()

    def finish(self):
        for group in self.inside:
            for c in group:
                c.wait()
        for group in self.across:
            for c in group:
                c.wait_send()
        for c in self.keep:
            c.wait()


def gather_sems(nf, pieces):
    dma = pltpu.SemaphoreType.DMA
    side = max(nf // 2 - 1, 1)
    return [dma((side, pieces)), dma((side, pieces)), dma((nf // 2, pieces)), dma((nf // 2, pieces)), dma((pieces,))]


def stacked(ref, h):
    return lambda which: ref.at[place(which, h), :]


def chunks_of(total, parts):
    step = -(-total // (16 * parts)) * 16
    return [(lo, min(lo + step, total)) for lo in range(0, total, step)]


WEIGHT_PARTS = 4


def arrive_kernel(
    log_rows, share, order_ref, x_ref, cot_ref, wt_ref, down_ref, up_ref, bias_in, log_in, skip_in,
    got_ref, cots_ref, slot_ref, where_ref, tok_ref, wall_ref, dall_ref, uall_ref, e_ref, skip_ref, bias_ref, rate_ref,
    sorted_ref, s_tok, r_tok, own_sem, *sems,
):
    n, me = lax.axis_size("ctx"), lax.axis_index("ctx")
    rows = x_ref.shape[0]
    targets = ctx_targets() + fsdp_targets()
    hail(targets)
    pieces = [(down_ref, stacked(dall_ref, down_ref.shape[0])), (up_ref, stacked(uall_ref, up_ref.shape[0]))]
    for lo, hi in chunks_of(wt_ref.shape[0], WEIGHT_PARTS):
        pieces.append((wt_ref.at[lo:hi, :], lambda which, lo=lo, hi=hi: wall_ref.at[which, lo:hi, :]))
    gather = Gather(pieces, sems)

    own_order = order_ref[:, pl.ds(pl.multiple_of(me * rows, rows), rows)]
    dest = own_order >> log_rows
    hot = jnp.where(iota((max(n, 16), rows), 0) == dest, 1.0, 0.0)
    rank = jnp.sum(hot * (running_count(hot) - 1.0), axis=0, keepdims=True)
    spos = dest * share + rank.astype(jnp.int32)
    sort_rows(spos, x_ref, sorted_ref)
    hailed(targets)
    gather.begin()
    tokens = [
        send(
            sorted_ref.at[place(to, share), :], got_ref.at[place(me, share), :], s_tok.at[k - 1], r_tok.at[k - 1], ctx=to
        )
        for k, to, _ in peers("ctx")
    ]
    for c in tokens:
        c.start()
    own = pltpu.make_async_copy(sorted_ref.at[place(me, share), :], got_ref.at[place(me, share), :], own_sem)
    own.start()

    sort_rows(spos, cot_ref, cots_ref)
    by_source = [order_ref[:, s * rows : (s + 1) * rows] for s in range(n)]
    order = jnp.concatenate(by_source + [jnp.full((1, rows), -1, jnp.int32)] * (-n % 16), 0)
    mine = jnp.where(order >> log_rows == me, 1.0, 0.0)
    mark = jnp.where(mine > 0.0, running_count(mine) - 1.0, -1.0).astype(jnp.int32)
    for s in range(n):
        hit = one_hot(iota((share, rows), 0) == mark[s : s + 1, :])
        slot = by_source[s] & (rows - 1)
        slot_ref[:, s * share : (s + 1) * share] = from_two(nt(two_rows(slot), hit))
    where_ref[...] = invert(slot_ref[...])
    tok_ref[...] = invert(spos)
    e_ref[...] = one_hot((iota((2 * LANES, INNER), 0) & (LANES - 1)) == iota((2 * LANES, INNER), 1) // HEAD)
    pad = jnp.zeros((1, LANES - HEADS), F32)
    wide = jnp.broadcast_to(jnp.concatenate([skip_in[...], pad], 1), (16, LANES))
    skip_ref[...] = sum(nn(p, e_ref[:LANES, :]) for p in split(wide, 3))[0:1]
    bias_ref[...] = jnp.concatenate([bias_in[...], pad], 1)
    rate_ref[...] = jnp.concatenate([-jnp.exp(log_in[...]), pad], 1)

    gather.relay()
    gather.finish()
    for c in tokens:
        c.wait()
    own.wait()


def sort_rows(idx, src, dst):
    rows = src.shape[0]
    for t in range(0, rows, SPAN):
        hit = one_hot(iota((SPAN, rows), 0) + t == idx)
        dst[t : t + SPAN, :] = nn(hit, src[...]).astype(BF16)


def owners_of(n):
    return min(n, INNER // LANES)


def each_owner(n, which, act):
    if owners_of(n) == n:
        act()
    else:
        pl.when(which < owners_of(n))(act)


class Exchange:
    def __init__(self, parts, through, first, starts, landed, sems, reverse):
        self.parts, self.through, self.first, self.starts, self.landed = parts, through, first, starts, landed
        self.s1, self.r1, self.s2, self.r2 = sems
        self.reverse = reverse
        self.n, self.me = lax.axis_size("ctx"), lax.axis_index("ctx")

    def out(self, k, to):
        return send(self.parts.at[to], self.first.at[self.me], self.s1.at[k - 1], self.r1.at[k - 1], ctx=to)

    def back(self, k, to):
        return send(self.starts.at[to], self.landed.at[self.me], self.s2.at[k - 1], self.r2.at[k - 1], ctx=to)

    def begin(self):
        for k, to, _ in peers("ctx"):
            each_owner(self.n, to, lambda: self.out(k, to).start())

    def middle(self):
        n, me = self.n, self.me

        def act():
            self.first[me] = self.parts[me]
            for k, to, _ in peers("ctx"):
                self.out(k, to).wait_recv()

            def lap(t, running):
                j = n - 1 - t if self.reverse else t
                self.starts[j] = running.astype(BF16)
                part = self.first[j].astype(F32)
                through = self.through(self.first, j)
                return running * through + part[:STATE]

            lax.fori_loop(0, n, lap, jnp.zeros((STATE, self.first.shape[2]), F32))
            self.landed[me] = self.starts[me]
            for k, to, _ in peers("ctx"):
                self.back(k, to).start()

        each_owner(n, me, act)

    def finish(self, result):
        n, me = self.n, self.me
        for k, to, back in peers("ctx"):
            each_owner(n, back, lambda: self.back(k, to).wait_recv())
        w = self.landed.shape[2]
        for j in range(owners_of(n)):
            result[:, j * w : (j + 1) * w] = self.landed[j].astype(result.dtype)
        for k, to, _ in peers("ctx"):
            each_owner(n, to, lambda: self.out(k, to).wait_send())

        def act():
            for k, to, _ in peers("ctx"):
                self.back(k, to).wait_send()

        each_owner(n, me, act)


class Reduce:
    def __init__(self, g_ref, out_ref, bufs):
        self.g, self.out = g_ref, out_ref
        self.pair_in, self.pair_sum, self.side_in, self.total, self.ctx_in, self.piece, self.all_in, sems = bufs
        self.n, self.me = lax.axis_size("ctx"), lax.axis_index("ctx")
        nf = lax.axis_size("fsdp")
        self.f, pair, sides, _ = fsdp_sides()
        self.core = lax.rem(self.f, 2)
        self.h, self.cw = g_ref.shape[0] // nf, g_ref.shape[1] // self.n
        self.first = [
            send(g_ref.at[place(2 * y + 1 - self.core, self.h), :], self.pair_in.at[y], sems.at[0, y], sems.at[1, y], fsdp=pair)
            for y in range(nf // 2)
        ]
        self.second = [
            send(self.pair_sum.at[side // 2], self.side_in.at[k], sems.at[2, k], sems.at[3, k], fsdp=side)
            for k, side in enumerate(sides)
        ]
        self.third = [
            send(self.total.at[to], self.ctx_in.at[k - 1], sems.at[4, k - 1], sems.at[5, k - 1], ctx=to)
            for k, to, _ in peers("ctx")
        ]
        self.fourth = [
            send(self.piece, self.all_in.at[self.me], sems.at[6, k - 1], sems.at[7, k - 1], ctx=to)
            for k, to, _ in peers("ctx")
        ]

    def begin(self):
        for c in self.first:
            c.start()

    def over_y(self):
        for y, c in enumerate(self.first):
            c.wait_recv()
            both = self.g[place(2 * y + self.core, self.h), :].astype(F32) + self.pair_in[y].astype(F32)
            self.pair_sum[y] = both.astype(BF16)
        for c in self.second:
            c.start()

    def scatter(self):
        mine = self.pair_sum[self.f // 2].astype(F32)
        for k, c in enumerate(self.second):
            c.wait_recv()
            mine = mine + self.side_in[k].astype(F32)
        for j in range(self.n):
            self.total[j] = mine[:, j * self.cw : (j + 1) * self.cw].astype(BF16)
        for c in self.third:
            c.start()

    def gather(self):
        mine = self.total[self.me].astype(F32)
        for k, c in enumerate(self.third):
            c.wait_recv()
            mine = mine + self.ctx_in[k].astype(F32)
        self.piece[...] = mine.astype(BF16)
        for c in self.fourth:
            c.start()
        self.all_in[self.me] = self.piece[...]

    def finish(self):
        for c in self.fourth:
            c.wait_recv()
        for j in range(self.n):
            self.out[:, j * self.cw : (j + 1) * self.cw] = self.all_in[j].astype(F32)
        for c in self.first + self.second + self.third + self.fourth:
            c.wait_send()


def reduce_scratch(n, nf, cw):
    half, low = nf // 2, LOW // nf
    return [
        pltpu.VMEM((half, low, n * cw), BF16), pltpu.VMEM((half, low, n * cw), BF16),
        pltpu.VMEM((max(half - 1, 1), low, n * cw), BF16), pltpu.VMEM((n, low, cw), BF16),
        pltpu.VMEM((n - 1, low, cw), BF16), pltpu.VMEM((low, cw), BF16), pltpu.VMEM((n, low, cw), BF16),
        pltpu.SemaphoreType.DMA((8, max(n, half))),
    ]


class Resident:
    def __init__(self, wall_ref, dst, sems, lo, hi):
        nf, _, kw = wall_ref.shape
        self.copies = [
            pltpu.make_async_copy(wall_ref.at[f, lo:hi, :], dst.at[:, f * kw : (f + 1) * kw], sems.at[f]) for f in range(nf)
        ]

    def begin(self):
        for c in self.copies:
            c.start()

    def finish(self):
        for c in self.copies:
            c.wait()


def softplus(v):
    e = jnp.exp(-jnp.abs(v))
    series = e * (1.0 - e * (0.5 - e * (1.0 / 3.0 - 0.25 * e)))
    return jnp.maximum(v, 0.0) + jnp.where(e < 0.01, series, jnp.log(1.0 + e))


def in_conv_kernel(
    len_ref, id_ref, slot_ref, got_ref, wall_ref, down_ref, up_ref, gain_ref, cw_ref, cb_ref, bias_ref, rate_ref, e_ref,
    wo_ref, od_ref, ou_ref,
    x_ref, hb_ref, u_ref, dtr_ref, xs_ref, bm_ref, cm_ref, dact_ref, dt_ref, c2_ref, c2t_ref, wts_ref, reach_ref, ls_ref,
    carry_ref, send_ref, woall_ref, odall_ref, ouall_ref,
    wv, raw_s, dtr_s, ls_s, carry_s, tail, edge, landed, w_sem, s_halo, r_halo, *sems,
):
    s = pl.program_id(0)
    nb = pl.num_programs(0) // 2
    n, me = lax.axis_size("ctx"), lax.axis_index("ctx")
    rows = got_ref.shape[0]
    meta = Meta(len_ref, id_ref, rows)
    mid = INNER + CONV_CH
    weights = Resident(wall_ref, wv, w_sem, INNER, wall_ref.shape[1])
    targets = ring_targets() + fsdp_targets()
    halo = send(edge.at[5:8, :], landed.at[5:8, :], s_halo, r_halo, ctx=lax.rem(me + 1, n))
    pieces = [(od_ref, stacked(odall_ref, od_ref.shape[0])), (ou_ref, stacked(ouall_ref, ou_ref.shape[0]))]
    kw = wo_ref.shape[0]
    for lo, hi in chunks_of(kw, 2):
        at = lambda which, lo=lo, hi=hi: woall_ref.at[pl.ds(pl.multiple_of(which * kw + lo, 16), hi - lo), :]
        pieces.append((wo_ref.at[lo:hi, :], at))
    gather = Gather(pieces, sems)

    @pl.when(s == 0)
    def _():
        weights.begin()
        landed[...] = jnp.zeros_like(landed)
        hail(targets)

    @pl.when(s < nb)
    def _():
        t = lax.rem(s + nb - 1, nb)
        pos = meta.cols(t)
        hit = one_hot(iota((SPAN, rows), 0) + t * SPAN == slot_ref[...])
        x = nn(hit, got_ref[...]) * meta.valid(pos)
        x_ref[...] = x.astype(BF16)
        h = x * lax.rsqrt(jnp.mean(x * x, 1, keepdims=True) + EPS) * gain_ref[...]
        hb = h.astype(BF16)
        hb_ref[...] = hb
        u = (nt(hb, down_ref[...]) * meta.select(pos)).astype(BF16)
        u_ref[...] = u
        pl.when(s == 0)(weights.finish)
        for c in range(0, CONV_CH, 256):
            part = nt(hb, wv[c : c + 256, :]) + nn(u, up_ref[:, INNER + c : INNER + c + 256])
            raw_s[t, :, c : c + 256] = part.astype(BF16)
        last = nt(hb, wv[CONV_CH:, :]) + nn(u, up_ref[:, mid:])
        last = jnp.concatenate([last, jnp.zeros((SPAN, LANES - HEADS), F32)], 1)
        dtr_s[t] = last
        dtr_ref[...] = last

    @pl.when(s == 0)
    def _():
        edge[...] = raw_s[nb - 1, SPAN - 16 :, :].astype(F32)[8:]
        hailed(targets)
        pl.when(me < n - 1)(halo.start)
        gather.begin()

    @pl.when(s >= nb)
    def _():
        t = lax.rem(s - nb + 1, nb)

        @pl.when(t > 0)
        def _():
            tail[...] = raw_s[t - 1, SPAN - 16 :, :].astype(F32)[8:]

        pos = meta.cols(t)
        seq = meta.seq(pos)
        masks = [(meta.seq(pos - j) == seq).astype(F32) for j in range(KERNEL)]
        for c in range(0, CONV_CH, 256):
            cur = raw_s[t, :, c : c + 256].astype(F32)
            ext = jnp.concatenate([tail[:, c : c + 256], cur], 0)
            acc = cb_ref[:, c : c + 256] + cw_ref[3:4, c : c + 256] * cur
            for j in range(1, KERNEL):
                moved = pltpu.roll(ext, j, 0)[8:]
                acc = acc + (cw_ref[3 - j : 4 - j, c : c + 256] * moved) * masks[j]
            sg = sigmoid(acc)
            act = acc * sg
            dact_ref[:, c : c + 256] = (sg + act * (1.0 - sg)).astype(BF16)
            act = act.astype(BF16)
            if c < INNER:
                xs_ref[:, c : c + 256] = act
            else:
                bm_ref[...] = act[:, :STATE]
                cm_ref[...] = act[:, STATE:]
        dt = softplus(dtr_s[t] + bias_ref[...])
        dt_ref[...] = dt
        tri = one_hot(iota((SPAN, SPAN), 0) >= iota((SPAN, SPAN), 1))
        cum = sum(nn(tri, p) for p in split(dt * rate_ref[...], 3))
        cum_end = cum[SPAN - 1 : SPAN, :]
        first = meta.start + t * SPAN
        end_same = (seq == meta.seq(first + SPAN - 1)).astype(F32)
        passing = (seq == meta.seq(first - 1)).astype(F32)
        wts = jnp.exp(cum_end - cum) * dt * end_same
        wts_ref[...] = wts
        reach = jnp.exp(cum) * passing
        reach_ref[...] = reach
        c2 = cum * LOG2E
        c2_ref[...] = c2
        c2t_ref[0] = c2.T[:HEADS]
        both = pairs(wts)
        ends = [p for p in split(jnp.broadcast_to(reach[SPAN - 1 : SPAN, :], (16, LANES)), 3)]
        for c in range(0, INNER, 256):
            cs = slice(c, c + 256)
            weighted = (xs_ref[:, cs].astype(F32) * nn(both, e_ref[:, cs])).astype(BF16)
            ls = tn(bm_ref[...], weighted)
            ls_ref[0, :, cs] = ls
            ls_s[t, :, cs] = ls
        carry = sum(nn(p, e_ref[:LANES, :]) for p in ends)[:8]
        carry_ref[0] = carry
        carry_s[t] = carry

    @pl.when(s == nb + 1)
    def _():
        gather.relay(0, 3)

    @pl.when(s == 2 * nb - 2)
    def _():
        pl.when(me < n - 1)(halo.wait_send)
        pl.when(me > 0)(halo.wait_recv)
        tail[...] = jnp.where(me > 0, landed[...], 0.0)

    @pl.when(s == 2 * nb - 1)
    def _():
        w = send_ref.shape[2]
        for j in range(send_ref.shape[0]):
            at = slice(j * w, (j + 1) * w)
            state, through = ls_s[0, :, at], carry_s[0, 0:1, at]
            for b in range(1, ls_s.shape[0]):
                state = state * carry_s[b, 0:1, at] + ls_s[b, :, at]
                through = through * carry_s[b, 0:1, at]
            send_ref[j, :STATE] = state.astype(BF16)
            send_ref[j, STATE:] = jnp.broadcast_to(through, (16, w)).astype(BF16)
        gather.relay(3)
        gather.finish()


def block_mask(meta, t, transposed):
    col, row = meta.cols(t), meta.rows(t)
    return (meta.seq(col) == meta.seq(row)) & ((row >= col) if transposed else (col >= row))


def halves(x):
    lane = iota(x.shape, 1)
    zero = jnp.zeros_like(x)
    return jnp.where(lane < HEAD, x, zero), jnp.where(lane >= HEAD, x, zero)


def within_kernel(
    len_ref, id_ref, xs_ref, bm_ref, cm_ref, dt_ref, c2_ref, c2t_ref, e_ref, parts_ref, hb_ref, u_ref, up_ref, wall_ref,
    y_ref, z_ref, start_ref, thr_ref,
    xdt, sc, wv, first, starts, landed, s1, r1, s2, r2, w_sem,
):
    s = pl.program_id(0)
    nb = pl.num_programs(0) // 2
    meta = Meta(len_ref, id_ref, nb * SPAN)
    exchange = Exchange(
        parts_ref, lambda first, j: first[j, STATE:].astype(F32)[0:1], first, starts, landed, (s1, r1, s2, r2), False
    )
    weights = Resident(wall_ref, wv, w_sem, 0, INNER)

    @pl.when(s == 0)
    def _():
        hail(ctx_targets())
        weights.begin()

    @pl.when(s < nb)
    def _():
        sc[...] = jnp.where(block_mask(meta, s, False), nt(cm_ref[...], bm_ref[...]), 0.0)
        both = pairs(dt_ref[...])
        for c in range(0, INNER, 256):
            cs = slice(c, c + 256)
            xdt[:, cs] = (xs_ref[:, cs].astype(F32) * nn(both, e_ref[:, cs])).astype(BF16)
        c2 = c2_ref[...]

        def group(g, _):
            cols = pltpu.roll(c2, LANES - 8 * g, 1)
            rows = c2t_ref[0, pl.ds(pl.multiple_of(8 * g, 8), 8), :]
            for q in range(4):
                at = pl.ds(pl.multiple_of(g * 512 + q * 128, 128), 128)
                xa, xb = halves(xdt[:, at])
                mixes = []
                for h in (2 * q, 2 * q + 1):
                    col, row = cols[:, h : h + 1], rows[h : h + 1, :]

                    def mix(t, r):
                        decay = jnp.exp2(jnp.minimum(col[t : t + HALF] - row[:, r : r + HALF], 0.0))
                        return (sc[t : t + HALF, r : r + HALF] * decay).astype(BF16)

                    mixes.append((mix(0, 0), mix(HALF, 0), mix(HALF, HALF)))
                (a00, a10, a11), (b00, b10, b11) = mixes
                top = nn(jnp.concatenate([a00, b00], 1), jnp.concatenate([xa[:HALF], xb[:HALF]], 0))
                low = nn(jnp.concatenate([a10, a11, b10, b11], 1), jnp.concatenate([xa, xb], 0))
                y_ref[:HALF, at] = top.astype(BF16)
                y_ref[HALF:, at] = low.astype(BF16)
            return 0

        lax.fori_loop(0, HEADS // 8, group, 0)

    @pl.when(s == 0)
    def _():
        hailed(ctx_targets())
        exchange.begin()

    pl.when(s == nb)(weights.finish)

    @pl.when(s >= nb)
    def _():
        for c in range(0, INNER, 256):
            z_ref[:, c : c + 256] = (nt(hb_ref[...], wv[c : c + 256, :]) + nn(u_ref[...], up_ref[:, c : c + 256])).astype(BF16)

    pl.when(s == nb)(exchange.middle)

    @pl.when(s == 2 * nb - 1)
    def _():
        exchange.finish(start_ref)
        for j in range(thr_ref.shape[0]):
            thr_ref[j] = first[j, STATE:]


def out_kernel(
    len_ref, id_ref, y_ref, z_ref, xs_ref, cm_ref, reach_ref, x_ref, ls_ref, carry_ref, all_ref, e_ref, skip_ref, gain_ref,
    w_ref, down_ref, up_ref, where_ref,
    start_ref, next_ref, mixed_ref, nout_ref, v_ref, rstd_ref, sorted_ref,
    run, kept_rows, wide,
):
    i = pl.program_id(0)
    meta = Meta(len_ref, id_ref, kept_rows.shape[0])

    @pl.when(i == 0)
    def _():
        run[...] = all_ref[...].astype(F32)

    both = pairs(reach_ref[...])
    total = jnp.zeros((SPAN, LANES), F32)
    for c in range(0, INNER, 256):
        cs = slice(c, c + 256)
        now = run[:, cs]
        start = now.astype(BF16)
        start_ref[0, :, cs] = start
        later = now * carry_ref[0, 0:1, cs] + ls_ref[0, :, cs]
        run[:, cs] = later
        next_ref[0, :, cs] = later.astype(BF16)
        mixed = y_ref[:, cs].astype(F32) + nn(both, e_ref[:, cs]) * nn(cm_ref[...], start)
        mixed = mixed + skip_ref[:, cs] * xs_ref[:, cs].astype(F32)
        mixed_ref[:, cs] = mixed.astype(BF16)
        z = z_ref[:, cs].astype(F32)
        gated = mixed * (z * sigmoid(z))
        wide[:, cs] = gated
        sq = gated * gated
        total = total + sq[:, :LANES] + sq[:, LANES:]
    rstd = lax.rsqrt(jnp.sum(total, 1, keepdims=True) * (1.0 / INNER) + EPS)
    rstd_ref[...] = jnp.broadcast_to(rstd, (SPAN, LANES))
    for c in range(0, INNER, 256):
        cs = slice(c, c + 256)
        nout_ref[:, cs] = (wide[:, cs] * rstd * gain_ref[:, cs]).astype(BF16)
    pos = meta.cols(i)
    v = (nt(nout_ref[...], down_ref[...]) * meta.select(pos)).astype(BF16)
    v_ref[...] = v
    valid = meta.valid(pos)
    at = pl.ds(pl.multiple_of(i * SPAN, SPAN), SPAN)
    for c in range(0, w_ref.shape[1], 256):
        cs = slice(c, c + 256)
        branch = nn(nout_ref[...], w_ref[:, cs]) + nn(v, up_ref[:, cs])
        kept_rows[at, cs] = ((x_ref[:, cs].astype(F32) + branch) * valid).astype(BF16)

    @pl.when(i == pl.num_programs(0) - 1)
    def _():
        sort_rows(where_ref[...], kept_rows, sorted_ref)


def gate_back_kernel(
    len_ref, id_ref, mixed_ref, z_ref, nout_ref, v_ref, rstd_ref, xs_ref, cm_ref, reach_ref, start_ref, carry_ref, cot_ref,
    slot_ref, e_ref, skip_ref, gain_ref, w_ref, down_ref, up_ref,
    dout_ref, dm_ref, dz_ref, rs_ref, dcm_ref, dst_ref, own_ref, g_ref,
    own, through, gup, gdown, dn, prods, dproj,
):
    i = pl.program_id(0)
    rows = cot_ref.shape[0]
    meta = Meta(len_ref, id_ref, rows)

    @pl.when(i == 0)
    def _():
        own[...] = jnp.zeros_like(own)
        through[...] = jnp.ones_like(through)
        gup[...] = jnp.zeros_like(gup)
        gdown[...] = jnp.zeros_like(gdown)

    pos = meta.cols(i)
    hit = one_hot(iota((SPAN, rows), 0) + i * SPAN == slot_ref[...])
    valid = meta.valid(pos)
    for c in range(0, cot_ref.shape[1], 256):
        cs = slice(c, c + 256)
        dout_ref[:, cs] = (nn(hit, cot_ref[:, cs]) * valid).astype(BF16)
    dout = dout_ref[...]
    gup[...] += tn(v_ref[...], dout)
    dv = nt(dout, up_ref[...]).astype(BF16) * meta.select(pos).astype(BF16)
    rstd = rstd_ref[:, 0:1]
    total = jnp.zeros((SPAN, LANES), F32)
    for c in range(0, INNER, 256):
        cs = slice(c, c + 256)
        z = z_ref[:, cs].astype(F32)
        d = (nt(dout, w_ref[cs, :]) + nn(dv, down_ref[:, cs])) * gain_ref[:, cs]
        dn[:, cs] = d
        g = d * (mixed_ref[:, cs].astype(F32) * (z * sigmoid(z)))
        total = total + g[:, :LANES] + g[:, LANES:]
        gdown[:, cs] += tn(dv, nout_ref[:, cs])
    back = jnp.sum(total, 1, keepdims=True) * (1.0 / INNER) * rstd * rstd
    both = pairs(reach_ref[...])
    for c in range(0, INNER, 256):
        cs = slice(c, c + 256)
        z = z_ref[:, cs].astype(F32)
        sg = sigmoid(z)
        silu = z * sg
        mixed = mixed_ref[:, cs].astype(F32)
        dg = rstd * (dn[:, cs] - mixed * silu * back)
        dm = (dg * silu).astype(BF16)
        dm_ref[:, cs] = dm
        dz_ref[:, cs] = (dg * mixed * (sg + silu * (1.0 - sg))).astype(BF16)
        dm = dm.astype(F32)
        dp = (dm * nn(both, e_ref[:, cs])).astype(BF16)
        dproj[:, cs] = dp
        prods[:, cs] = (dm * (mixed - skip_ref[:, cs] * xs_ref[:, cs].astype(F32))).astype(BF16)
        dst = tn(cm_ref[...], dp)
        dst_ref[0, :, cs] = dst
        own[:, cs] += dst * through[0:1, cs]
    rs_ref[...] = nt(prods[...], e_ref[:LANES, :])
    dcm_ref[...] = nt(dproj[...], start_ref[0])
    through[...] = through[...] * carry_ref[0]

    @pl.when(i == pl.num_programs(0) - 1)
    def _():
        w = own_ref.shape[2]
        for j in range(own_ref.shape[0]):
            own_ref[j] = own[:, j * w : (j + 1) * w].astype(BF16)
        g_ref[:, :INNER] = gdown[...].astype(BF16)
        g_ref[:, INNER:] = gup[...].astype(BF16)


def mix_back_kernel(
    len_ref, id_ref, xs_ref, bm_ref, cm_ref, dm_ref, dt_ref, c2_ref, c2t_ref, dcm1_ref, e_ref, parts_ref, thr_ref,
    dst_ref, carry_ref, next_ref, dz_ref, u_ref, up_ref, wall_ref, g_ref,
    dxk_ref, dbm_ref, dcm_ref, dl_ref, dend_ref, dhz_ref, duz_ref, ga_ref,
    xdt, dte, sct, dsc, later, wv, gup, first, starts, landed, s1, r1, s2, r2, w_sem,
):
    s = pl.program_id(0)
    nb = pl.num_programs(0) // 2
    meta = Meta(len_ref, id_ref, nb * SPAN)
    exchange = Exchange(
        parts_ref, lambda first, j: thr_ref[j].astype(F32)[0:1], first, starts, landed, (s1, r1, s2, r2), True
    )
    weights = Resident(wall_ref, wv, w_sem, 0, INNER)

    @pl.when(s == 0)
    def _():
        hail(ctx_targets())
        weights.begin()
        gup[...] = jnp.zeros_like(gup)

    @pl.when(s < nb)
    def _():
        mask = block_mask(meta, s, True)
        sct[...] = jnp.where(mask, nt(bm_ref[...], cm_ref[...]), 0.0)
        dsc[...] = jnp.zeros_like(dsc)
        both = pairs(dt_ref[...])
        for c in range(0, INNER, 256):
            cs = slice(c, c + 256)
            wide = nn(both, e_ref[:, cs])
            dte[:, cs] = wide
            xdt[:, cs] = (xs_ref[:, cs].astype(F32) * wide).astype(BF16)
        c2 = c2_ref[...]

        def group(g, _):
            cols = pltpu.roll(c2, LANES - 8 * g, 1)
            rows = c2t_ref[0, pl.ds(pl.multiple_of(8 * g, 8), 8), :]
            for q in range(4):
                at = pl.ds(pl.multiple_of(g * 512 + q * 128, 128), 128)
                dm = dm_ref[:, at]
                da, db = halves(dm)
                mixes = []
                for h, x in zip((2 * q, 2 * q + 1), halves(xdt[:, at])):
                    col, row = cols[:, h : h + 1], rows[h : h + 1, :]
                    top = nt(x[:HALF], dm)
                    low = nt(x[HALF:], dm[HALF:])

                    def mix(r, t, d):
                        decay = jnp.exp2(jnp.minimum(row[:, t : t + HALF] - col[r : r + HALF], 0.0))
                        dsc[r : r + HALF, t : t + HALF] += d * decay
                        return (sct[r : r + HALF, t : t + HALF] * decay).astype(BF16)

                    mixes.append((mix(0, 0, top[:, :HALF]), mix(0, HALF, top[:, HALF:]), mix(HALF, HALF, low)))
                (a00, a01, a11), (b00, b01, b11) = mixes
                g_top = nn(jnp.concatenate([a00, a01, b00, b01], 1), jnp.concatenate([da, db], 0))
                g_low = nn(jnp.concatenate([a11, b11], 1), jnp.concatenate([da[HALF:], db[HALF:]], 0))
                dxk_ref[:HALF, at] = (g_top * dte[:HALF, at]).astype(BF16)
                dxk_ref[HALF:, at] = (g_low * dte[HALF:, at]).astype(BF16)
            return 0

        lax.fori_loop(0, HEADS // 8, group, 0)
        ds = jnp.where(mask, dsc[...], 0.0).astype(BF16)
        dbm_ref[...] = nn(ds, cm_ref[...])
        dcm_ref[...] = dcm1_ref[...] + tn(ds, bm_ref[...])

    @pl.when(s == 0)
    def _():
        hailed(ctx_targets())
        exchange.begin()

    pl.when(s == nb)(weights.finish)

    @pl.when(s >= nb)
    def _():
        dz = dz_ref[...]
        for c in range(0, dhz_ref.shape[1], 256):
            dhz_ref[:, c : c + 256] = nn(dz, wv[:, c : c + 256]).astype(BF16)
        duz_ref[...] = nt(dz, up_ref[:, :INNER])
        for c in range(0, INNER, 512):
            gup[:, c : c + 512] += tn(u_ref[...], dz_ref[:, c : c + 512])

    pl.when(s == nb)(exchange.middle)

    @pl.when(s == 2 * nb - 1)
    def _():
        base = g_ref.shape[1]
        ga_ref[:, :base] = g_ref[...]
        ga_ref[:, base : base + INNER] = gup[...].astype(BF16)
        if ga_ref.shape[1] > base + INNER:
            ga_ref[:, base + INNER :] = jnp.zeros((LOW, ga_ref.shape[1] - base - INNER), BF16)
        exchange.finish(later)
        for b in reversed(range(dl_ref.shape[0])):
            sums = []
            for c in range(0, INNER, 256):
                cs = slice(c, c + 256)
                a = later[:, cs]
                dl_ref[b, :, cs] = a.astype(BF16)
                sums.append(jnp.sum(a * next_ref[b, :, cs].astype(F32), 0, keepdims=True))
                later[:, cs] = dst_ref[b, :, cs] + carry_ref[b, 0:1, cs] * a
            total = jnp.broadcast_to(jnp.concatenate(sums, 1), (16, INNER))
            dend_ref[b] = sum(nt(p, e_ref[:LANES, :]) for p in split(total, 3))[:8]


def scan_back_kernel(
    len_ref, id_ref, dl_ref, dend_ref, xs_ref, bm_ref, dm_ref, dxk_ref, dbm_ref, dcm_ref, wts_ref, dtr_ref, rs_ref, dact_ref,
    cw_ref, e_ref, skip_ref, bias_ref, rate_ref, up_ref, u_ref, hb_ref, duz_ref, g_ref, pin_ref,
    dr_ref, du_ref, gin_ref, gout_ref,
    dacc, ddts, head, edge, landed, gup, gdown, prods, weighted, s_head, r_head, *bufs,
):
    s = pl.program_id(0)
    tiles = pl.num_programs(0) - 1
    n, me = lax.axis_size("ctx"), lax.axis_index("ctx")
    meta = Meta(len_ref, id_ref, tiles * SPAN)
    reduce = Reduce(g_ref, gout_ref, bufs)
    edge_copy = send(edge.at[0:3, :], landed.at[0:3, :], s_head, r_head, ctx=lax.rem(me + n - 1, n))
    targets = ctx_targets() + fsdp_targets()

    @pl.when(s == 0)
    def _():
        gup[...] = jnp.zeros_like(gup)
        gdown[...] = jnp.zeros_like(gdown)
        landed[...] = jnp.zeros_like(landed)
        hail(targets)

    now, before = lax.rem(s, 2), lax.rem(s + 1, 2)

    @pl.when(s < tiles)
    def _():
        both = pairs(wts_ref[...])
        for c in range(0, INNER, 256):
            cs = slice(c, c + 256)
            w = nn(both, e_ref[:, cs])
            xs = xs_ref[:, cs].astype(F32)
            dx = dxk_ref[:, cs].astype(F32) + nn(bm_ref[...], dl_ref[0, :, cs]) * w
            prods[:, cs] = (xs * dx).astype(BF16)
            dx = dx + skip_ref[:, cs] * dm_ref[:, cs].astype(F32)
            dacc[now, :, cs] = dx * dact_ref[:, cs].astype(F32)
            weighted[:, cs] = (xs * w).astype(BF16)
        dbm = dbm_ref[...] + nt(weighted[...], dl_ref[0])
        dacc[now, :, INNER : INNER + STATE] = dbm * dact_ref[:, INNER : INNER + STATE].astype(F32)
        dacc[now, :, INNER + STATE :] = dcm_ref[...] * dact_ref[:, INNER + STATE :].astype(F32)
        csum = nt(prods[...], e_ref[:LANES, :])
        last = iota((SPAN, 1), 0) == SPAN - 1
        dcum = rs_ref[...] - csum + jnp.where(last, dend_ref[0, 0:1, :], 0.0)
        tri = one_hot(iota((SPAN, SPAN), 0) <= iota((SPAN, SPAN), 1))
        dsteps = sum(nn(tri, p) for p in split(dcum, 3))
        v = dtr_ref[...] + bias_ref[...]
        sg = 1.0 / (1.0 + jnp.exp(-v))
        e = jnp.exp(jnp.minimum(v, 0.0))
        ratio = jnp.where(v < -12.0, 1.0 - 0.5 * e, sg / jnp.maximum(softplus(v), 1e-7))
        ddt = jnp.where(iota((SPAN, LANES), 1) < HEADS, csum * ratio + dsteps * rate_ref[...] * sg, 0.0).astype(BF16)
        ddts[now] = ddt
        head[...] = dacc[now, :8, :]

    @pl.when(s == 0)
    def _():
        edge[...] = dacc[0, :8, :]
        hailed(targets)
        pl.when(me > 0)(edge_copy.start)
        reduce.begin()

    @pl.when(s == tiles)
    def _():
        pl.when(me > 0)(edge_copy.wait_send)
        pl.when(me < n - 1)(edge_copy.wait_recv)
        head[...] = jnp.where(me < n - 1, landed[...], 0.0)

    @pl.when(s > 0)
    def _():
        pos = meta.cols(s - 1)
        seq = meta.seq(pos)
        masks = [(meta.seq(pos + j) == seq).astype(F32) for j in range(KERNEL)]
        for c in range(0, CONV_CH, 256):
            cs = slice(c, c + 256)
            cur = dacc[before, :, cs]
            ext = jnp.concatenate([cur, head[:, cs]], 0)
            total = cw_ref[3:4, cs] * cur
            for j in range(1, KERNEL):
                moved = pltpu.roll(ext, SPAN + 8 - j, 0)[:SPAN]
                total = total + (cw_ref[3 - j : 4 - j, cs] * moved) * masks[j]
            dr_ref[:, cs] = total.astype(BF16)
        dr_ref[:, CONV_CH:] = ddts[before][:, :HEADS]
        u, hb = u_ref[...], hb_ref[...]
        width = dr_ref.shape[1]
        for lo in range(0, width, 512):
            hi = min(lo + 512, width)
            gup[:, lo:hi] += tn(u, dr_ref[:, lo:hi])
        du = duz_ref[...] + nt(dr_ref[...], up_ref[:, INNER:])
        du = du.astype(BF16) * meta.select(pos).astype(BF16)
        du_ref[...] = du
        gdown[...] += tn(du, hb)

    pl.when(s == 1)(reduce.over_y)
    pl.when(s == 2)(reduce.scatter)
    pl.when(s == 3)(reduce.gather)

    @pl.when(s == tiles)
    def _():
        d, end = gdown.shape[1], gup.shape[1]
        gin_ref[:, :d] = gdown[...].astype(BF16)
        gin_ref[:, d : d + end] = gup[...].astype(BF16)
        if gin_ref.shape[1] > d + end:
            gin_ref[:, d + end :] = jnp.zeros((LOW, gin_ref.shape[1] - d - end), BF16)
        reduce.finish()


def tail_kernel(
    len_ref, id_ref, dhz_ref, dr_ref, du_ref, x_ref, dout_ref, wall_ref, down_ref, gain_ref, where_ref, g_ref, back_ref, tok_ref,
    out_ref, grad_ref, gsum_ref,
    wv, kept_rows, sorted_ref, got, dh, w_sem, s_sem, r_sem, own_sem, *bufs,
):
    s = pl.program_id(0)
    tiles = pl.num_programs(0) - 1
    n, me = lax.axis_size("ctx"), lax.axis_index("ctx")
    rows = kept_rows.shape[0]
    share = rows // n
    meta = Meta(len_ref, id_ref, rows)
    reduce = Reduce(g_ref, gsum_ref, bufs)
    weights = Resident(wall_ref, wv, w_sem, INNER, wall_ref.shape[1])
    targets = ctx_targets() + fsdp_targets()

    @pl.when(s == 0)
    def _():
        weights.begin()
        hail(targets)
        weights.finish()

    @pl.when(s < tiles)
    def _():
        pos = meta.cols(s)
        du = du_ref[...]
        for c in range(0, dh.shape[1], 256):
            cs = slice(c, c + 256)
            dh[:, cs] = dhz_ref[:, cs].astype(F32) + nn(dr_ref[...], wv[:, cs]) + nn(du, down_ref[:, cs])
        x = x_ref[...].astype(F32)
        rstd = lax.rsqrt(jnp.mean(x * x, 1, keepdims=True) + EPS)
        g = dh[...] * gain_ref[...]
        back = jnp.mean(g * x, 1, keepdims=True) * rstd * rstd
        dx = rstd * (g - x * back)
        dx = ((dout_ref[...].astype(F32) + dx) * meta.valid(pos)).astype(BF16)
        kept_rows[pl.ds(pl.multiple_of(s * SPAN, SPAN), SPAN), :] = dx

    @pl.when(s == 0)
    def _():
        hailed(targets)
        reduce.begin()

    pl.when(s == 1)(reduce.over_y)
    pl.when(s == 2)(reduce.scatter)

    @pl.when(s == tiles)
    def _():
        copies = [
            send(sorted_ref.at[place(to, share), :], got.at[place(me, share), :], s_sem.at[k - 1], r_sem.at[k - 1], ctx=to)
            for k, to, _ in peers("ctx")
        ]
        reduce.gather()
        sort_rows(where_ref[...], kept_rows, sorted_ref)
        for c in copies:
            c.start()
        got[place(me, share), :] = sorted_ref[place(me, share), :]
        sort_rows(tok_ref[...], back_ref, out_ref)
        reduce.finish()
        for c in copies:
            c.wait()
        sort_rows(tok_ref[...], got, grad_ref)


def shape(*dims, dtype=F32):
    return jax.ShapeDtypeStruct(dims, dtype)


def params(mib=56, remote=None):
    if remote is None:
        return pltpu.CompilerParams(vmem_limit_bytes=mib * MIB)
    return pltpu.CompilerParams(vmem_limit_bytes=mib * MIB, collective_id=remote, has_side_effects=True)


SMEM = pl.BlockSpec(memory_space=pltpu.SMEM)
VMEM = pl.BlockSpec(memory_space=pltpu.VMEM)
ANY = pl.BlockSpec(memory_space=pl.ANY)


def exchange_scratch(n, rows):
    owners = owners_of(n)
    w = INNER // owners
    return [
        pltpu.VMEM((n, rows, w), BF16), pltpu.VMEM((n, STATE, w), BF16), pltpu.VMEM((owners, STATE, w), BF16),
    ] + [pltpu.SemaphoreType.DMA((n - 1,))] * 4


def fixed(*dims):
    return pl.BlockSpec(dims, lambda i: (0,) * len(dims), pipeline_mode=pl.Buffered(1))


def kept(*dims):
    return pl.BlockSpec(dims, lambda i: (0,) * len(dims))


def row_tile(width, at=lambda i: i):
    return pl.BlockSpec((SPAN, width), lambda i: (at(i), 0))


def blocked(*dims, at=lambda i: i):
    return pl.BlockSpec((1,) + dims, lambda i: (at(i),) + (0,) * len(dims))


def a2a(x):
    return lax.all_to_all(x, "ctx", split_axis=0, concat_axis=0, tiled=True)


def local(
    tokens, cotangent, order, lengths, adapter_ids, in_weight, out_weight, in_down, in_up, out_down, out_up,
    norm_gain, conv_weight, conv_bias, dt_bias, a_log, skip_gain, gate_gain,
):
    n, nf = lax.axis_size("ctx"), lax.axis_size("fsdp")
    rows, width = tokens.shape[1:]
    nb = rows // SPAN
    share = rows // n
    log_rows = rows.bit_length() - 1
    assert rows == 1 << log_rows and rows <= 1024 and rows % SPAN == 0 and nb >= 4
    assert nf % 2 == 0 and share % 16 == 0
    proj_w = in_weight.shape[1]
    rest = proj_w - INNER
    bf = lambda *dims: shape(*dims, dtype=BF16)
    vm = pltpu.VMEM
    dma = pltpu.SemaphoreType.DMA
    padded = lambda c: -(-c // (n * LANES)) * LANES * n
    owners = owners_of(n)
    ow = INNER // owners
    wt, in_down_t, out_down_t = in_weight.T, in_down.T, out_down.T
    kw, ko, ka = wt.shape[1], out_weight.shape[0], in_down_t.shape[0]
    idx = shape(1, rows, dtype=jnp.int32)
    gain, gate, cb = norm_gain[None], gate_gain[None], conv_bias[None]
    seqs = (lengths, adapter_ids)

    parts_w = len(chunks_of(proj_w, WEIGHT_PARTS))
    got, cot_sorted, slot, where, tok, w_in, a_in, b_in, e, skip, bias, rate = pl.pallas_call(
        partial(arrive_kernel, log_rows, share),
        in_specs=[VMEM] * 9,
        out_specs=[ANY, VMEM, VMEM, VMEM, VMEM, ANY, ANY, ANY, VMEM, VMEM, VMEM, VMEM],
        out_shape=(
            bf(rows, width), bf(rows, width), idx, idx, idx, bf(nf, proj_w, kw), bf(LOW, width), bf(LOW, proj_w),
            bf(2 * LANES, INNER), shape(1, INNER), shape(1, LANES), shape(1, LANES),
        ),
        scratch_shapes=[vm((rows, width), BF16)] + spread_sems(n) + gather_sems(nf, 2 + parts_w),
        compiler_params=params(remote=1),
        name="arrive",
    )(order, tokens[0], cotangent[0], wt, in_down_t, in_up, dt_bias[None], a_log[None], skip_gain[None])
    got_cot = a2a(cot_sorted)

    lead = lambda s: (jnp.minimum(s, nb - 1) + nb - 1) % nb
    conv = lambda s: (jnp.maximum(s - nb, 0) + 1) % nb
    parts_o = 2 + len(chunks_of(ko, 2))
    (
        x, hb, u, dtr, xs, bm, cm, dact, dt, c2, c2t, wts, reach, ls, carry, parts, w_out, a_out, b_out,
    ) = pl.pallas_call(
        in_conv_kernel,
        grid=(2 * nb,),
        in_specs=[
            SMEM, SMEM, fixed(1, rows), fixed(rows, width), ANY, fixed(LOW, width), fixed(LOW, proj_w), fixed(1, width),
            fixed(KERNEL, CONV_CH), fixed(1, CONV_CH), fixed(1, LANES), fixed(1, LANES), fixed(2 * LANES, INNER),
            fixed(ko, width), fixed(ka, INNER), fixed(ka, width),
        ],
        out_specs=[
            row_tile(width, lead), row_tile(width, lead), row_tile(LOW, lead), row_tile(LANES, lead),
            row_tile(INNER, conv), row_tile(STATE, conv), row_tile(STATE, conv), row_tile(CONV_CH, conv),
            row_tile(LANES, conv), row_tile(LANES, conv), blocked(HEADS, SPAN, at=conv), row_tile(LANES, conv),
            row_tile(LANES, conv), blocked(STATE, INNER, at=conv), blocked(8, INNER, at=conv),
            kept(owners, STATE + 16, ow), ANY, ANY, ANY,
        ],
        out_shape=(
            bf(rows, width), bf(rows, width), bf(rows, LOW), shape(rows, LANES),
            bf(rows, INNER), bf(rows, STATE), bf(rows, STATE), bf(rows, CONV_CH),
            shape(rows, LANES), shape(rows, LANES), shape(nb, HEADS, SPAN), shape(rows, LANES),
            shape(rows, LANES), shape(nb, STATE, INNER), shape(nb, 8, INNER),
            bf(owners, STATE + 16, ow), bf(INNER, width), bf(LOW, INNER), bf(LOW, width),
        ),
        scratch_shapes=[
            vm((rest, width), BF16), vm((nb, SPAN, CONV_CH), BF16), vm((nb, SPAN, LANES), F32), vm((nb, STATE, INNER), F32),
            vm((nb, 8, INNER), F32), vm((8, CONV_CH), F32), vm((8, CONV_CH), F32), vm((8, CONV_CH), F32), dma((nf,)), dma, dma,
        ] + gather_sems(nf, parts_o),
        compiler_params=params(remote=2),
        name="in_conv",
    )(*seqs, slot, got, w_in, a_in, b_in, gain, conv_weight, cb, bias, rate, e, out_weight, out_down_t, out_up)

    early = lambda s: jnp.minimum(s, nb - 1)
    late = lambda s: jnp.maximum(s - nb, 0)
    y, z, start_in, thr = pl.pallas_call(
        within_kernel,
        grid=(2 * nb,),
        in_specs=[
            SMEM, SMEM, row_tile(INNER, early), row_tile(STATE, early), row_tile(STATE, early), row_tile(LANES, early),
            row_tile(LANES, early), blocked(HEADS, SPAN, at=early), fixed(2 * LANES, INNER), VMEM, row_tile(width, late),
            row_tile(LOW, late), fixed(LOW, proj_w), ANY,
        ],
        out_specs=[row_tile(INNER, early), row_tile(INNER, late), kept(STATE, INNER), kept(n, 16, ow)],
        out_shape=(bf(rows, INNER), bf(rows, INNER), bf(STATE, INNER), bf(n, 16, ow)),
        scratch_shapes=[vm((SPAN, INNER), BF16), vm((SPAN, SPAN), F32), vm((INNER, width), BF16)]
        + exchange_scratch(n, STATE + 16) + [dma((nf,))],
        compiler_params=params(remote=3),
        name="within",
    )(*seqs, xs, bm, cm, dt, c2, c2t, e, parts, hb, u, b_in, w_in)

    start, after, mixed, nout, v, rstd, result = pl.pallas_call(
        out_kernel,
        grid=(nb,),
        in_specs=[
            SMEM, SMEM, row_tile(INNER), row_tile(INNER), row_tile(INNER), row_tile(STATE), row_tile(LANES), row_tile(width),
            blocked(STATE, INNER), blocked(8, INNER), fixed(STATE, INNER), fixed(2 * LANES, INNER), fixed(1, INNER),
            fixed(1, INNER), fixed(INNER, width), fixed(LOW, INNER), fixed(LOW, width), fixed(1, rows),
        ],
        out_specs=[
            blocked(STATE, INNER), blocked(STATE, INNER), row_tile(INNER), row_tile(INNER), row_tile(LOW), row_tile(LANES),
            kept(rows, width),
        ],
        out_shape=(
            bf(nb, STATE, INNER), bf(nb, STATE, INNER), bf(rows, INNER), bf(rows, INNER), bf(rows, LOW),
            shape(rows, LANES), bf(rows, width),
        ),
        scratch_shapes=[vm((STATE, INNER), F32), vm((rows, width), BF16), vm((SPAN, INNER), F32)],
        compiler_params=params(),
        name="gate_out",
    )(*seqs, y, z, xs, cm, reach, x, ls, carry, start_in, e, skip, gate, w_out, a_out, b_out, where)
    back_out = a2a(result)

    dout, dm, dz, rs, dcm1, dst, own, g_out = pl.pallas_call(
        gate_back_kernel,
        grid=(nb,),
        in_specs=[
            SMEM, SMEM, row_tile(INNER), row_tile(INNER), row_tile(INNER), row_tile(LOW), row_tile(LANES), row_tile(INNER),
            row_tile(STATE), row_tile(LANES), blocked(STATE, INNER), blocked(8, INNER), fixed(rows, width), fixed(1, rows),
            fixed(2 * LANES, INNER), fixed(1, INNER), fixed(1, INNER), fixed(INNER, width), fixed(LOW, INNER),
            fixed(LOW, width),
        ],
        out_specs=[
            row_tile(width), row_tile(INNER), row_tile(INNER), row_tile(LANES), row_tile(STATE), blocked(STATE, INNER),
            kept(owners, STATE, ow), kept(LOW, INNER + width),
        ],
        out_shape=(
            bf(rows, width), bf(rows, INNER), bf(rows, INNER), shape(rows, LANES), shape(rows, STATE),
            shape(nb, STATE, INNER), bf(owners, STATE, ow), bf(LOW, INNER + width),
        ),
        scratch_shapes=[
            vm((STATE, INNER), F32), vm((8, INNER), F32), vm((LOW, width), F32), vm((LOW, INNER), F32),
            vm((SPAN, INNER), F32), vm((SPAN, INNER), BF16), vm((SPAN, INNER), BF16),
        ],
        compiler_params=params(),
        name="gate_back",
    )(*seqs, mixed, z, nout, v, rstd, xs, cm, reach, start, carry, got_cot, slot, e, skip, gate, w_out, a_out, b_out)

    cols_a = padded(2 * INNER + width)
    dxk, dbm, dcm, dl, dend, dhz, duz, g_a = pl.pallas_call(
        mix_back_kernel,
        grid=(2 * nb,),
        in_specs=[
            SMEM, SMEM, row_tile(INNER, early), row_tile(STATE, early), row_tile(STATE, early), row_tile(INNER, early),
            row_tile(LANES, early), row_tile(LANES, early), blocked(HEADS, SPAN, at=early), row_tile(STATE, early),
            fixed(2 * LANES, INNER), VMEM, VMEM, fixed(nb, STATE, INNER), fixed(nb, 8, INNER), fixed(nb, STATE, INNER),
            row_tile(INNER, late), row_tile(LOW, late), fixed(LOW, proj_w), ANY, fixed(LOW, INNER + width),
        ],
        out_specs=[
            row_tile(INNER, early), row_tile(STATE, early), row_tile(STATE, early), kept(nb, STATE, INNER),
            kept(nb, 8, LANES), row_tile(width, late), row_tile(LOW, late), kept(LOW, cols_a),
        ],
        out_shape=(
            bf(rows, INNER), shape(rows, STATE), shape(rows, STATE), bf(nb, STATE, INNER), shape(nb, 8, LANES),
            bf(rows, width), shape(rows, LOW), bf(LOW, cols_a),
        ),
        scratch_shapes=[
            vm((SPAN, INNER), BF16), vm((SPAN, INNER), F32), vm((SPAN, SPAN), F32), vm((SPAN, SPAN), F32),
            vm((STATE, INNER), F32), vm((INNER, width), BF16), vm((LOW, INNER), F32),
        ] + exchange_scratch(n, STATE) + [dma((nf,))],
        compiler_params=params(remote=4),
        name="mix_back",
    )(*seqs, xs, bm, cm, dm, dt, c2, c2t, dcm1, e, own, thr, dst, carry, after, dz, u, b_in, w_in, g_out)

    cols_b = padded(width + rest)
    behind = lambda s: jnp.maximum(s - 1, 0)
    dr, du, g_b, sums_a = pl.pallas_call(
        scan_back_kernel,
        grid=(nb + 1,),
        in_specs=[
            SMEM, SMEM, blocked(STATE, INNER, at=early), blocked(8, LANES, at=early), row_tile(INNER, early),
            row_tile(STATE, early), row_tile(INNER, early), row_tile(INNER, early), row_tile(STATE, early),
            row_tile(STATE, early), row_tile(LANES, early), row_tile(LANES, early), row_tile(LANES, early),
            row_tile(CONV_CH, early), fixed(KERNEL, CONV_CH), fixed(2 * LANES, INNER), fixed(1, INNER), fixed(1, LANES),
            fixed(1, LANES), fixed(LOW, proj_w), row_tile(LOW, behind), row_tile(width, behind), row_tile(LOW, behind),
            fixed(LOW, cols_a), ANY,
        ],
        out_specs=[row_tile(rest, behind), row_tile(LOW, behind), kept(LOW, cols_b), kept(LOW // nf, cols_a)],
        out_shape=(bf(rows, rest), bf(rows, LOW), bf(LOW, cols_b), shape(LOW // nf, cols_a)),
        scratch_shapes=[
            vm((2, SPAN, CONV_CH), F32), vm((2, SPAN, LANES), BF16), vm((8, CONV_CH), F32), vm((8, CONV_CH), F32),
            vm((8, CONV_CH), F32), vm((LOW, rest), F32), vm((LOW, width), F32), vm((SPAN, INNER), BF16),
            vm((SPAN, INNER), BF16), dma, dma,
        ] + reduce_scratch(n, nf, cols_a // n),
        compiler_params=params(remote=5),
        name="scan_back",
    )(
        *seqs, dl, dend, xs, bm, dm, dxk, dbm, dcm, wts, dtr, rs, dact, conv_weight, e, skip, bias, rate, b_in, u, hb, duz,
        g_a, back_out,
    )

    block_output, input_grad, sums_b = pl.pallas_call(
        tail_kernel,
        grid=(nb + 1,),
        in_specs=[
            SMEM, SMEM, row_tile(width, early), row_tile(rest, early), row_tile(LOW, early), row_tile(width, early),
            row_tile(width, early), ANY, fixed(LOW, width), fixed(1, width), fixed(1, rows), fixed(LOW, cols_b),
            fixed(rows, width), fixed(1, rows),
        ],
        out_specs=[kept(rows, width), kept(rows, width), kept(LOW // nf, cols_b)],
        out_shape=(bf(rows, width), bf(rows, width), shape(LOW // nf, cols_b)),
        scratch_shapes=[
            vm((rest, width), BF16), vm((rows, width), BF16), vm((rows, width), BF16), vm((rows, width), BF16),
            vm((SPAN, width), F32), dma((nf,)),
        ] + spread_sems(n) + reduce_scratch(n, nf, cols_b // n),
        compiler_params=params(remote=6),
        name="tail",
    )(*seqs, dhz, dr, du, x, dout, w_in, a_in, gain, where, g_b, back_out, tok)
    up_a = INNER + width
    return (
        block_output[None], input_grad[None], sums_b[:, :width].T,
        jnp.concatenate([sums_a[:, up_a : up_a + INNER], sums_b[:, width : width + rest]], 1),
        sums_a[:, :INNER].T, sums_a[:, INNER:up_a],
    )


def solution(mesh):
    placed = (
        P("fsdp", "ctx", None),
        P("fsdp", "ctx", None),
        P("fsdp", None),
        P("fsdp", None),
        P("fsdp", None),
        P("fsdp", None),
        P("fsdp", None),
        P(None, "fsdp"),
        P("fsdp", None),
        P(None, "fsdp"),
        P("fsdp", None),
        P(),
        P(),
        P(),
        P(),
        P(),
        P(),
        P(),
    )
    return jax.shard_map(
        local,
        mesh=mesh,
        in_specs=placed,
        out_specs=(
            P("fsdp", "ctx", None),
            P("fsdp", "ctx", None),
            P(None, "fsdp"),
            P("fsdp", None),
            P(None, "fsdp"),
            P("fsdp", None),
        ),
        check_vma=False,
    )
```

```python
from functools import partial

import jax
import jax.numpy as jnp
from jax import lax
from jax.experimental import pallas as pl
from jax.experimental.pallas import tpu as pltpu
from jax.sharding import PartitionSpec as P

HEADS = 32
HEAD = 64
STATE = 128
KERNEL = 4
SPAN = 256
RANK = 16
ADAPTERS = 8
SEQS = 3
CONV_CH = 2304
INNER = HEADS * HEAD
LOW = ADAPTERS * RANK
LANES = 128
HALF = SPAN // 2
EPS = 1e-05
LOG2E = 1.4426950408889634

F32 = jnp.float32
BF16 = jnp.bfloat16
MIB = 1 << 20
MESH = pl.DeviceIdType.MESH


def nn(a, b):
    return jnp.dot(a, b, preferred_element_type=F32)


def nt(a, b):
    return lax.dot_general(a, b, (((1,), (1,)), ((), ())), preferred_element_type=F32)


def tn(a, b):
    return lax.dot_general(a, b, (((0,), (0,)), ((), ())), preferred_element_type=F32)


def iota(shape, dim):
    return lax.broadcasted_iota(jnp.int32, shape, dim)


def one_hot(cond):
    return jnp.where(cond, 1.0, 0.0).astype(BF16)


def split(v, parts):
    out = []
    for _ in range(parts):
        piece = v.astype(BF16)
        out.append(piece)
        v = v - piece.astype(F32)
    return out


def pairs(v):
    return jnp.concatenate(split(v, 2), 1)


class Meta:
    def __init__(self, len_ref, id_ref, rows):
        self.start = lax.axis_index("ctx") * rows
        self.ends = []
        for k in range(SEQS):
            self.ends.append(len_ref[0, k] + (self.ends[-1] if k else 0))
        self.ids = [id_ref[0, k] for k in range(SEQS)]

    def seq(self, pos):
        found = sum((pos >= end).astype(jnp.int32) for end in self.ends)
        return jnp.where(pos >= 0, found, -1)

    def valid(self, pos):
        return (pos < self.ends[-1]).astype(F32)

    def select(self, pos):
        seq = self.seq(pos)
        ids = sum(jnp.where(seq == k, self.ids[k], 0) for k in range(SEQS))
        shape = (pos.shape[0], LOW)
        return jnp.where(iota(shape, 1) // RANK == ids, 1.0, 0.0) * self.valid(pos)

    def cols(self, tile):
        return self.start + tile * SPAN + iota((SPAN, 1), 0)

    def rows(self, tile):
        return self.start + tile * SPAN + iota((1, SPAN), 1)


def sigmoid(v):
    return 0.5 * jnp.tanh(0.5 * v) + 0.5


def running_count(mask):
    width = mask.shape[1]
    tri = one_hot(iota((SPAN, SPAN), 0) <= iota((SPAN, SPAN), 1))
    pieces, before = [], jnp.zeros((mask.shape[0], 1), F32)
    for c in range(0, width, SPAN):
        part = mask[:, c : c + SPAN]
        pieces.append(nn(part.astype(BF16), tri) + before)
        before = before + jnp.sum(part, 1, keepdims=True)
    return jnp.concatenate(pieces, 1)


def two_rows(v):
    first = jnp.broadcast_to(v >> 5, (16, v.shape[1]))
    second = jnp.broadcast_to(v & 31, (16, v.shape[1]))
    row = iota((16, v.shape[1]), 0)
    return jnp.where(row == 0, first, jnp.where(row == 1, second, 0)).astype(F32).astype(BF16)


def from_two(r):
    return (r[0:1] * 32.0 + r[1:2]).astype(jnp.int32)


def invert(idx):
    width = idx.shape[1]
    values = two_rows(iota((1, width), 1))
    pieces = []
    for t in range(0, width, SPAN):
        hit = one_hot(iota((SPAN, width), 0) + t == idx)
        pieces.append(from_two(nt(values, hit)))
    return jnp.concatenate(pieces, 1)


def peers(axis):
    n, me = lax.axis_size(axis), lax.axis_index(axis)
    return [(k, lax.rem(me + k, n), lax.rem(me + n - k, n)) for k in range(1, n)]


def send(src, dst, send_sem, recv_sem, **where):
    return pltpu.make_async_remote_copy(
        src_ref=src, dst_ref=dst, send_sem=send_sem, recv_sem=recv_sem, device_id=where, device_id_type=MESH
    )


def hail(targets):
    barrier = pltpu.get_barrier_semaphore()
    for where in targets:
        pl.semaphore_signal(barrier, inc=1, device_id=where, device_id_type=MESH)


def hailed(targets):
    pl.semaphore_wait(pltpu.get_barrier_semaphore(), len(targets))


def place(which, share):
    return pl.ds(pl.multiple_of(which * share, share), share)


def halves_of(n):
    near = [k for k in range(1, n) if k <= n // 2 and (k % 2 == 1 or k == n // 2)]
    return near, [k for k in range(1, n) if k not in near]


class Spread:
    def __init__(self, src, dst, send_sem, recv_sem, own_sem, steps):
        n, me = lax.axis_size("ctx"), lax.axis_index("ctx")
        share = src.shape[0] // n
        self.copies = [
            send(src.at[place(to, share), :], dst.at[place(me, share), :], send_sem.at[k - 1], recv_sem.at[k - 1], ctx=to)
            for k, to, _ in peers("ctx") if k in steps
        ]
        self.own = None
        if own_sem is not None:
            self.own = pltpu.make_async_copy(src.at[place(me, share), :], dst.at[place(me, share), :], own_sem)

    def begin(self):
        for c in self.copies:
            c.start()
        if self.own is not None:
            self.own.start()

    def finish(self):
        for c in self.copies:
            c.wait()
        if self.own is not None:
            self.own.wait()


def spread_sems(n):
    return [pltpu.SemaphoreType.DMA((n - 1,)), pltpu.SemaphoreType.DMA((n - 1,)), pltpu.SemaphoreType.DMA]


def ring_targets():
    n, me = lax.axis_size("ctx"), lax.axis_index("ctx")
    return [{"ctx": lax.rem(me + 1, n)}, {"ctx": lax.rem(me + n - 1, n)}]


def ctx_targets():
    return [{"ctx": p} for _, p, _ in peers("ctx")]


def fsdp_sides():
    nf, f = lax.axis_size("fsdp"), lax.axis_index("fsdp")
    sides = [lax.rem(f + 2 * k, nf) for k in range(1, nf // 2)]
    backs = [lax.rem(f + nf - 2 * k, nf) for k in range(1, nf // 2)]
    return f, f + 1 - 2 * lax.rem(f, 2), sides, backs


def fsdp_targets():
    _, pair, sides, _ = fsdp_sides()
    return [{"fsdp": p} for p in sides + [pair]]


class Gather:
    def __init__(self, pieces, sems, kept=None):
        s_y, r_y, s_c, r_c, keep = sems
        f, pair, sides, backs = fsdp_sides()
        self.across = [
            [send(src, dst(f), s_y.at[k, m], r_y.at[k, m], fsdp=side) for m, (src, dst) in enumerate(pieces)]
            for k, side in enumerate(sides)
        ]
        self.inside = [[send(src, dst(f), s_c.at[0, m], r_c.at[0, m], fsdp=pair) for m, (src, dst) in enumerate(pieces)]]
        self.inside += [
            [send(dst(back), dst(back), s_c.at[k + 1, m], r_c.at[k + 1, m], fsdp=pair) for m, (src, dst) in enumerate(pieces)]
            for k, back in enumerate(backs)
        ]
        self.keep = [pltpu.make_async_copy(src, dst(f), keep.at[m]) for m, (src, dst) in enumerate(pieces[:kept])]

    def begin(self):
        for group in self.across:
            for c in group:
                c.start()
        for c in self.inside[0] + self.keep:
            c.start()

    def relay(self, lo=0, hi=None):
        for k, group in enumerate(self.across):
            for c, forward in list(zip(group, self.inside[k + 1]))[lo:hi]:
                c.wait_recv()
                forward.start()

    def finish(self, lo=0, hi=None):
        for group in self.inside:
            for c in group[lo:hi]:
                c.wait()
        for group in self.across:
            for c in group[lo:hi]:
                c.wait_send()
        for c in self.keep[lo:hi]:
            c.wait()


def gather_sems(nf, pieces):
    dma = pltpu.SemaphoreType.DMA
    side = max(nf // 2 - 1, 1)
    return [dma((side, pieces)), dma((side, pieces)), dma((nf // 2, pieces)), dma((nf // 2, pieces)), dma((pieces,))]


def stacked(ref, h):
    return lambda which: ref.at[place(which, h), :]


def chunks_of(total, parts):
    step = -(-total // (16 * parts)) * 16
    return [(lo, min(lo + step, total)) for lo in range(0, total, step)]


WEIGHT_PARTS = 4
SPLIT = 1024


def arrive_kernel(
    log_rows, share, order_ref, x_ref, cot_ref, wt_ref, down_ref, up_ref, bias_in, log_in, skip_in,
    got_ref, cots_ref, slot_ref, where_ref, tok_ref, wall_ref, dall_ref, uall_ref, e_ref, skip_ref, bias_ref, rate_ref,
    sorted_ref, s_tok, r_tok, own_sem, *sems,
):
    n, me = lax.axis_size("ctx"), lax.axis_index("ctx")
    rows = x_ref.shape[0]
    targets = ctx_targets() + fsdp_targets()
    hail(targets)
    pieces = [(down_ref, stacked(dall_ref, down_ref.shape[0])), (up_ref, stacked(uall_ref, up_ref.shape[0]))]
    for lo, hi in chunks_of(wt_ref.shape[0] - SPLIT, WEIGHT_PARTS):
        pieces.append((wt_ref.at[SPLIT + lo : SPLIT + hi, :], lambda which, lo=lo, hi=hi: wall_ref.at[which, lo:hi, :]))
    gather = Gather(pieces, sems)

    own_order = order_ref[:, pl.ds(pl.multiple_of(me * rows, rows), rows)]
    dest = own_order >> log_rows
    hot = jnp.where(iota((max(n, 16), rows), 0) == dest, 1.0, 0.0)
    rank = jnp.sum(hot * (running_count(hot) - 1.0), axis=0, keepdims=True)
    spos = dest * share + rank.astype(jnp.int32)
    sort_rows(spos, x_ref, sorted_ref)
    hailed(targets)
    gather.begin()
    tokens = [
        send(
            sorted_ref.at[place(to, share), :], got_ref.at[place(me, share), :], s_tok.at[k - 1], r_tok.at[k - 1], ctx=to
        )
        for k, to, _ in peers("ctx")
    ]
    for c in tokens:
        c.start()
    own = pltpu.make_async_copy(sorted_ref.at[place(me, share), :], got_ref.at[place(me, share), :], own_sem)
    own.start()

    sort_rows(spos, cot_ref, cots_ref)
    by_source = [order_ref[:, s * rows : (s + 1) * rows] for s in range(n)]
    order = jnp.concatenate(by_source + [jnp.full((1, rows), -1, jnp.int32)] * (-n % 16), 0)
    mine = jnp.where(order >> log_rows == me, 1.0, 0.0)
    mark = jnp.where(mine > 0.0, running_count(mine) - 1.0, -1.0).astype(jnp.int32)
    for s in range(n):
        hit = one_hot(iota((share, rows), 0) == mark[s : s + 1, :])
        slot = by_source[s] & (rows - 1)
        slot_ref[:, s * share : (s + 1) * share] = from_two(nt(two_rows(slot), hit))
    where_ref[...] = invert(slot_ref[...])
    tok_ref[...] = invert(spos)
    e_ref[...] = one_hot((iota((2 * LANES, INNER), 0) & (LANES - 1)) == iota((2 * LANES, INNER), 1) // HEAD)
    pad = jnp.zeros((1, LANES - HEADS), F32)
    wide = jnp.broadcast_to(jnp.concatenate([skip_in[...], pad], 1), (16, LANES))
    skip_ref[...] = sum(nn(p, e_ref[:LANES, :]) for p in split(wide, 3))[0:1]
    bias_ref[...] = jnp.concatenate([bias_in[...], pad], 1)
    rate_ref[...] = jnp.concatenate([-jnp.exp(log_in[...]), pad], 1)

    gather.relay()
    gather.finish()
    for c in tokens:
        c.wait()
    own.wait()


def sort_rows(idx, src, dst):
    rows = src.shape[0]

    def body(t):
        hit = one_hot(iota((SPAN, rows), 0) + t * SPAN == idx)
        for cs in wide_chunks(src.shape[1]):
            dst[tile_rows(t), cs] = nn(hit, src[:, cs]).astype(BF16)

    each_tile(rows // SPAN, body)


def owners_of(n):
    return min(n, INNER // LANES)


def each_owner(n, which, act):
    if owners_of(n) == n:
        act()
    else:
        pl.when(which < owners_of(n))(act)


class Exchange:
    def __init__(self, parts, through, first, starts, landed, sems, reverse):
        self.parts, self.through, self.first, self.starts, self.landed = parts, through, first, starts, landed
        self.s1, self.r1, self.s2, self.r2 = sems
        self.reverse = reverse
        self.n, self.me = lax.axis_size("ctx"), lax.axis_index("ctx")

    def out(self, k, to):
        return send(self.parts.at[to], self.first.at[self.me], self.s1.at[k - 1], self.r1.at[k - 1], ctx=to)

    def back(self, k, to):
        return send(self.starts.at[to], self.landed.at[self.me], self.s2.at[k - 1], self.r2.at[k - 1], ctx=to)

    def begin(self):
        for k, to, _ in peers("ctx"):
            each_owner(self.n, to, lambda: self.out(k, to).start())

    def middle(self):
        n, me = self.n, self.me

        def act():
            self.first[me] = self.parts[me]
            for k, to, _ in peers("ctx"):
                self.out(k, to).wait_recv()

            def lap(t, running):
                j = n - 1 - t if self.reverse else t
                self.starts[j] = running.astype(BF16)
                part = self.first[j].astype(F32)
                through = self.through(self.first, j)
                return running * through + part[:STATE]

            lax.fori_loop(0, n, lap, jnp.zeros((STATE, self.first.shape[2]), F32))
            self.landed[me] = self.starts[me]
            for k, to, _ in peers("ctx"):
                self.back(k, to).start()

        each_owner(n, me, act)

    def finish(self, result):
        n, me = self.n, self.me
        for k, to, back in peers("ctx"):
            each_owner(n, back, lambda: self.back(k, to).wait_recv())
        w = self.landed.shape[2]
        for j in range(owners_of(n)):
            result[:, j * w : (j + 1) * w] = self.landed[j].astype(result.dtype)
        for k, to, _ in peers("ctx"):
            each_owner(n, to, lambda: self.out(k, to).wait_send())

        def act():
            for k, to, _ in peers("ctx"):
                self.back(k, to).wait_send()

        each_owner(n, me, act)


class Reduce:
    def __init__(self, g_ref, outs, bufs):
        self.g, self.outs = g_ref, outs
        self.pair_in, self.pair_sum, self.side_in, self.total, self.ctx_in, self.piece, self.all_in, sems = bufs
        self.n, self.me = lax.axis_size("ctx"), lax.axis_index("ctx")
        nf = lax.axis_size("fsdp")
        self.f, pair, sides, _ = fsdp_sides()
        self.core = lax.rem(self.f, 2)
        self.h, self.cw = g_ref.shape[0] // nf, g_ref.shape[1] // self.n
        self.first = [
            send(g_ref.at[place(2 * y + 1 - self.core, self.h), :], self.pair_in.at[y], sems.at[0, y], sems.at[1, y], fsdp=pair)
            for y in range(nf // 2)
        ]
        self.second = [
            send(self.pair_sum.at[side // 2], self.side_in.at[k], sems.at[2, k], sems.at[3, k], fsdp=side)
            for k, side in enumerate(sides)
        ]
        self.third = [
            send(self.total.at[to], self.ctx_in.at[k - 1], sems.at[4, k - 1], sems.at[5, k - 1], ctx=to)
            for k, to, _ in peers("ctx")
        ]
        self.fourth = [
            send(self.piece, self.all_in.at[self.me], sems.at[6, k - 1], sems.at[7, k - 1], ctx=to)
            for k, to, _ in peers("ctx")
        ]

    def parts(self, body):
        def step(j, _):
            body(pl.ds(pl.multiple_of(j * self.cw, LANES), self.cw), j)
            return 0

        lax.fori_loop(0, self.n, step, 0)

    def begin(self):
        for c in self.first:
            c.start()

    def over_y(self):
        for y, c in enumerate(self.first):
            c.wait_recv()

            def add(cs, j, y=y):
                both = self.g[place(2 * y + self.core, self.h), cs].astype(F32) + self.pair_in[y, :, cs].astype(F32)
                self.pair_sum[y, :, cs] = both.astype(BF16)

            self.parts(add)
        for c in self.second:
            c.start()

    def scatter(self):
        for c in self.second:
            c.wait_recv()

        def add(cs, j):
            mine = self.pair_sum[self.f // 2, :, cs].astype(F32)
            for k in range(len(self.second)):
                mine = mine + self.side_in[k, :, cs].astype(F32)
            self.total[j] = mine.astype(BF16)

        self.parts(add)
        for c in self.third:
            c.start()

    def gather(self):
        mine = self.total[self.me].astype(F32)
        for k, c in enumerate(self.third):
            c.wait_recv()
            mine = mine + self.ctx_in[k].astype(F32)
        self.piece[...] = mine.astype(BF16)
        for c in self.fourth:
            c.start()
        self.all_in[self.me] = self.piece[...]

    def finish(self):
        for c in self.fourth:
            c.wait_recv()

        for j in range(self.n):
            for ref, at, lo, hi in self.outs:
                a, b = max(lo, j * self.cw), min(hi, (j + 1) * self.cw)
                if a < b:
                    part = self.all_in[j, :, a - j * self.cw : b - j * self.cw]
                    ref[:, at + a - lo : at + b - lo] = part.astype(F32)
        for c in self.first + self.second + self.third + self.fourth:
            c.wait_send()


def reduce_scratch(n, nf, cw):
    half, low = nf // 2, LOW // nf
    return [
        pltpu.VMEM((half, low, n * cw), BF16), pltpu.VMEM((half, low, n * cw), BF16),
        pltpu.VMEM((max(half - 1, 1), low, n * cw), BF16), pltpu.VMEM((n, low, cw), BF16),
        pltpu.VMEM((n - 1, low, cw), BF16), pltpu.VMEM((low, cw), BF16), pltpu.VMEM((n, low, cw), BF16),
        pltpu.SemaphoreType.DMA((8, max(n, half))),
    ]


class Mover:
    def __init__(self, sems):
        self.sems, self.used = sems, 0

    def go(self, src, dst):
        c = pltpu.make_async_copy(src, dst, self.sems.at[self.used])
        self.used += 1
        c.start()
        return c

    def tiles(self, src, dst):
        return [self.go(src.at[t : t + SPAN, :], dst.at[t : t + SPAN, :]) for t in range(0, dst.shape[0], SPAN)]


MOVES = 64


def each_tile(n, body):
    def step(t, _):
        body(t)
        return 0

    lax.fori_loop(0, n, step, 0)


def tile_rows(t):
    return pl.ds(pl.multiple_of(t * SPAN, SPAN), SPAN)


def each_chunk(width, body, step=256):
    def run(c, _):
        body(lambda base=0: pl.ds(pl.multiple_of(base + c * step, LANES), step))
        return 0

    lax.fori_loop(0, width // step, run, 0)


def wide_chunks(width, step=256):
    return [slice(c, min(c + step, width)) for c in range(0, width, step)]


class Resident:
    def __init__(self, wall_ref, dst, sems, lo, hi, early=None):
        nf, _, kw = wall_ref.shape
        f = lax.axis_index("fsdp")
        self.copies, at = [], 0
        for j in range(nf):
            which = lax.rem(f + j, nf)
            cols = pl.ds(pl.multiple_of(which * kw, LANES), kw)
            if early is not None:
                own, others = early
                src = own.at[0:SPLIT, :] if j == 0 else others.at[which]
                self.copies.append(pltpu.make_async_copy(src, dst.at[0:SPLIT, cols], sems.at[nf + j]))
            start = max(lo, SPLIT)
            src = wall_ref.at[which, start - SPLIT : hi - SPLIT, :]
            self.copies.append(pltpu.make_async_copy(src, dst.at[start - lo : hi - lo, cols], sems.at[j]))

    def begin(self):
        for c in self.copies:
            c.start()

    def finish(self):
        for c in self.copies:
            c.wait()


def softplus(v):
    e = jnp.exp(-jnp.abs(v))
    series = e * (1.0 - e * (0.5 - e * (1.0 / 3.0 - 0.25 * e)))
    return jnp.maximum(v, 0.0) + jnp.where(e < 0.01, series, jnp.log(1.0 + e))


def block_mask(meta, t, transposed):
    col, row = meta.cols(t), meta.rows(t)
    return (meta.seq(col) == meta.seq(row)) & ((row >= col) if transposed else (col >= row))


def halves(x):
    lane = iota(x.shape, 1)
    zero = jnp.zeros_like(x)
    return jnp.where(lane < HEAD, x, zero), jnp.where(lane >= HEAD, x, zero)


DTR, DT, C2, WTS, RS, DCM = (slice(k * LANES, (k + 1) * LANES) for k in range(6))
SMALL = 6 * LANES


def front_kernel(
    len_ref, id_ref, slot_ref, where_ref, gain_ref, cw_ref, cb_ref, bias_ref, rate_ref, skip_ref, gate_ref, od_ref, ou_ref,
    got_h, wall_h, dall_h, uall_h, e_h, cots_h, wo_h, wt_h,
    x_h, hb_h, u_h, act_h, dact_h, small_h, c2t_h, carry_h, next_h, thr_h, dout_h, dm_h, dz_h, dst_h, own_ref, g_ref,
    back_h, woall_h, wzall_h,
    wv, down, up, odown, oup, e, got, x, hb, u, v, dv, raw, act, ls, y, nout, states, sorted_ref, cot, small, reaches, c2t, carry,
    wide, prods, low, run, through, sc, tails, landed, parts, first, starts, slices,
    move_sems, w_sem, s_halo, r_halo, s_cot, r_cot, own_cot, s_out, r_out, own_out, s1, r1, s2, r2, *g_sems,
):
    n, me = lax.axis_size("ctx"), lax.axis_index("ctx")
    nf, f = lax.axis_size("fsdp"), lax.axis_index("fsdp")
    rows, width = x.shape
    nb = rows // SPAN
    mid = INNER + CONV_CH
    meta = Meta(len_ref, id_ref, rows)
    targets = ctx_targets() + fsdp_targets()
    landed[...] = jnp.zeros_like(landed)
    hail(targets)
    mover = Mover(move_sems)
    in_got = mover.go(got_h, got)
    in_down = mover.go(dall_h, down)
    proj_w = wt_h.shape[0]
    first_weights = Resident(wall_h, wv, w_sem.at[0], INNER, proj_w)
    first_weights.begin()
    in_up = mover.go(uall_h, up)
    in_e = mover.go(e_h, e)
    halo = send(tails.at[nb, 5:8, :], landed.at[5:8, :], s_halo, r_halo, ctx=lax.rem(me + 1, n))
    cots = Spread(cots_h, cot, s_cot, r_cot, own_cot, halves_of(n)[0])
    late_cots = Spread(cots_h, cot, s_cot, r_cot, None, halves_of(n)[1])
    kw = wo_h.shape[0]
    pieces = [
        (od_ref, stacked(odown, od_ref.shape[0])), (ou_ref, stacked(oup, ou_ref.shape[0])),
        (wt_h.at[0:SPLIT, :], lambda which: wzall_h.at[which]), (wo_h, stacked(woall_h, kw)),
    ]
    gather = Gather(pieces, g_sems, kept=2)
    exchange = Exchange(
        parts, lambda first, j: first[j, STATE:].astype(F32)[0:1], first, starts, slices, (s1, r1, s2, r2), False
    )
    in_got.wait()
    in_down.wait()

    def norm(t):
        at = tile_rows(t)
        pos = meta.cols(t)
        hit = one_hot(iota((SPAN, rows), 0) + t * SPAN == slot_ref[...])
        valid = meta.valid(pos)
        total = jnp.zeros((SPAN, LANES), F32)
        for cs in wide_chunks(width):
            xt = nn(hit, got[:, cs]) * valid
            x[at, cs] = xt.astype(BF16)
            sq = xt * xt
            total = total + sq[:, :LANES] + sq[:, LANES:]
        rstd = lax.rsqrt(jnp.sum(total, 1, keepdims=True) * (1.0 / width) + EPS)
        for cs in wide_chunks(width):
            hb[at, cs] = (x[at, cs].astype(F32) * rstd * gain_ref[:, cs]).astype(BF16)
        u[at, :] = (nt(hb[at, :], down[...]) * meta.select(pos)).astype(BF16)

    in_up.wait()
    first_weights.finish()

    def project(s):
        t = nb - 1 - s
        norm(t)
        at = tile_rows(t)
        for cs in wide_chunks(CONV_CH):
            raw[at, cs] = (nt(hb[at, :], wv[cs, :]) + nn(u[at, :], up[:, INNER + cs.start : INNER + cs.stop])).astype(BF16)
        last = nt(hb[at, :], wv[CONV_CH:, :]) + nn(u[at, :], up[:, mid:])
        small[at, DTR] = jnp.concatenate([last, jnp.zeros((SPAN, LANES - HEADS), F32)], 1)
        tails[t + 1] = raw[pl.ds(pl.multiple_of(t * SPAN + SPAN - 16, 16), 16), :].astype(F32)[8:]

        @pl.when(t == nb - 1)
        def _():
            hailed(targets)
            pl.when(me < n - 1)(halo.start)
            gather.begin()
            cots.begin()

    each_tile(nb, project)
    done = [mover.go(x, x_h), mover.go(hb, hb_h), mover.go(u, u_h)]
    hb_out = done[1]
    in_e.wait()

    def conv(s):
        t = lax.rem(s + 1, nb)
        at = tile_rows(t)

        @pl.when(t == 0)
        def _():
            pl.when(me > 0)(halo.wait_recv)
            tails[0] = jnp.where(me > 0, landed[...], 0.0)

        pos = meta.cols(t)
        seq = meta.seq(pos)
        masks = [(meta.seq(pos - j) == seq).astype(F32) for j in range(KERNEL)]
        for cs in wide_chunks(CONV_CH):
            cur = raw[at, cs].astype(F32)
            ext = jnp.concatenate([tails[t, :, cs], cur], 0)
            acc = cb_ref[:, cs] + cw_ref[3:4, cs] * cur
            for j in range(1, KERNEL):
                moved = pltpu.roll(ext, j, 0)[8:]
                acc = acc + (cw_ref[3 - j : 4 - j, cs] * moved) * masks[j]
            sg = sigmoid(acc)
            val = acc * sg
            raw[at, cs] = (sg + val * (1.0 - sg)).astype(BF16)
            act[at, cs] = val.astype(BF16)
        dt = softplus(small[at, DTR] + bias_ref[...])
        small[at, DT] = dt
        tri = one_hot(iota((SPAN, SPAN), 0) >= iota((SPAN, SPAN), 1))
        cum = sum(nn(tri, p) for p in split(dt * rate_ref[...], 3))
        start = meta.start + t * SPAN
        end_same = (seq == meta.seq(start + SPAN - 1)).astype(F32)
        passing = (seq == meta.seq(start - 1)).astype(F32)
        wts = jnp.exp(cum[SPAN - 1 : SPAN, :] - cum) * dt * end_same
        small[at, WTS] = wts
        reach = jnp.exp(cum) * passing
        reaches[at, :] = reach
        c2 = cum * LOG2E
        small[at, C2] = c2
        c2t[t] = c2.T[:HEADS]
        both = pairs(wts)
        bm = act[at, INNER : INNER + STATE]
        for cs in wide_chunks(INNER):
            weighted = (act[at, cs].astype(F32) * nn(both, e[:, cs])).astype(BF16)
            ls[t, :, cs] = tn(bm, weighted)
        ends = split(jnp.broadcast_to(reach[SPAN - 1 : SPAN, :], (16, LANES)), 3)
        carry[t] = sum(nn(p, e[:LANES, :]) for p in ends)[:8]

    each_tile(nb, conv)
    dact_out = mover.go(raw, dact_h)
    done += [mover.go(act, act_h), mover.go(c2t, c2t_h), mover.go(carry, carry_h)]
    ow = parts.shape[2]
    for j in range(parts.shape[0]):
        at = slice(j * ow, (j + 1) * ow)
        state, reached = ls[0, :, at], carry[0, 0:1, at]
        for b in range(1, nb):
            state = state * carry[b, 0:1, at] + ls[b, :, at]
            reached = reached * carry[b, 0:1, at]
        parts[j, :STATE] = state.astype(BF16)
        parts[j, STATE:] = jnp.broadcast_to(reached, (16, ow)).astype(BF16)
    exchange.begin()

    def mix_tile(t):
        at = tile_rows(t)
        bm, cm = act[at, INNER : INNER + STATE], act[at, INNER + STATE :]
        sc[...] = jnp.where(block_mask(meta, t, False), nt(cm, bm), 0.0)
        both = pairs(small[at, DT])
        for cs in wide_chunks(INNER):
            low[:, cs] = (act[at, cs].astype(F32) * nn(both, e[:, cs])).astype(BF16)
        c2 = small[at, C2]
        top_rows, low_rows = pl.ds(pl.multiple_of(t * SPAN, HALF), HALF), pl.ds(pl.multiple_of(t * SPAN + HALF, HALF), HALF)

        def group(g, _):
            cols = pltpu.roll(c2, LANES - 4 * g, 1)
            rws = c2t[t, pl.ds(pl.multiple_of(8 * (g // 2), 8), 8), :]
            rws = pltpu.roll(rws, 4 * lax.rem(g, 2), 0)
            for q in range(2):
                lanes = pl.ds(pl.multiple_of(g * 256 + q * 128, 128), 128)
                xa, xb = halves(low[:, lanes])
                mixes = []
                for h in (2 * q, 2 * q + 1):
                    col, row = cols[:, h : h + 1], rws[h : h + 1, :]

                    def mix(i, j):
                        decay = jnp.exp2(jnp.minimum(col[i : i + HALF] - row[:, j : j + HALF], 0.0))
                        return (sc[i : i + HALF, j : j + HALF] * decay).astype(BF16)

                    mixes.append((mix(0, 0), mix(HALF, 0), mix(HALF, HALF)))
                (a00, a10, a11), (b00, b10, b11) = mixes
                top = nn(jnp.concatenate([a00, b00], 1), jnp.concatenate([xa[:HALF], xb[:HALF]], 0))
                bot = nn(jnp.concatenate([a10, a11, b10, b11], 1), jnp.concatenate([xa, xb], 0))
                y[top_rows, lanes] = top.astype(BF16)
                y[low_rows, lanes] = bot.astype(BF16)
            return 0

        lax.fori_loop(0, HEADS // 4, group, 0)

    each_tile(nb, mix_tile)
    gather.relay(0, 3)
    gather.finish(0, 3)
    second_weights = Resident(wall_h, wv, w_sem.at[1], 0, INNER, (wt_h, wzall_h))
    second_weights.begin()
    dact_out.wait()
    gather.relay(3)
    second_weights.finish()

    def gate_tile(t):
        at = tile_rows(t)
        for cs in wide_chunks(INNER):
            raw[at, cs] = (nt(hb[at, :], wv[cs, :]) + nn(u[at, :], up[:, cs])).astype(BF16)
        pl.when(t == nb // 2)(exchange.middle)

    each_tile(nb, gate_tile)
    late_cots.begin()
    gather.finish(3)
    out_weights = [mover.go(wo_h, wv.at[place(f, kw), :])]
    for j in range(1, nf):
        which = lax.rem(f + j, nf)
        out_weights.append(mover.go(woall_h.at[place(which, kw), :], wv.at[place(which, kw), :]))
    exchange.finish(run)
    for j in range(thr_h.shape[0]):
        thr_h[j] = first[j, STATE:]
    for c in out_weights:
        c.wait()

    def out_tile(t):
        at = tile_rows(t)
        both = pairs(reaches[at, :])
        cm = act[at, INNER + STATE :]
        total = jnp.zeros((SPAN, LANES), F32)
        for cs in wide_chunks(INNER):
            now = run[:, cs]
            start = now.astype(BF16)
            states[t, :, cs] = start
            later = now * carry[t, 0:1, cs] + ls[t, :, cs]
            run[:, cs] = later
            mixed = y[at, cs].astype(F32) + nn(both, e[:, cs]) * nn(cm, start)
            mixed = mixed + skip_ref[:, cs] * act[at, cs].astype(F32)
            y[at, cs] = mixed.astype(BF16)
            z = raw[at, cs].astype(F32)
            gated = mixed * (z * sigmoid(z))
            wide[:, cs] = gated
            sq = gated * gated
            total = total + sq[:, :LANES] + sq[:, LANES:]
        rstd = lax.rsqrt(jnp.sum(total, 1, keepdims=True) * (1.0 / INNER) + EPS)
        small[at, RS] = jnp.broadcast_to(rstd, (SPAN, LANES))
        for cs in wide_chunks(INNER):
            nout[at, cs] = (wide[:, cs] * rstd * gate_ref[:, cs]).astype(BF16)
        pos = meta.cols(t)
        vt = (nt(nout[at, :], odown[...]) * meta.select(pos)).astype(BF16)
        v[at, :] = vt
        valid = meta.valid(pos)
        for cs in wide_chunks(width):
            branch = nn(nout[at, :], wv[:INNER, cs]) + nn(vt, oup[:, cs])
            got[at, cs] = ((x[at, cs].astype(F32) + branch) * valid).astype(BF16)

    each_tile(nb, out_tile)
    states[nb] = run[...].astype(BF16)
    next_out = mover.go(states.at[1 : nb + 1], next_h)
    sort_rows(where_ref[...], got, sorted_ref)
    results = Spread(sorted_ref, back_h, s_out, r_out, own_out, range(1, n))
    results.begin()
    cots.finish()
    late_cots.finish()
    hb_out.wait()

    def dout_tile(t):
        at = tile_rows(t)
        pos = meta.cols(t)
        hit = one_hot(iota((SPAN, rows), 0) + t * SPAN == slot_ref[...])
        valid = meta.valid(pos)
        for cs in wide_chunks(width):
            hb[at, cs] = (nn(hit, cot[:, cs]) * valid).astype(BF16)
        dv[at, :] = nt(hb[at, :], oup[...]).astype(BF16) * meta.select(pos).astype(BF16)

    each_tile(nb, dout_tile)
    done.append(mover.go(hb, dout_h))

    def down_grad(at):
        g_ref[:, at()] = tn(dv[...], nout[:, at()]).astype(BF16)

    def up_grad(at):
        g_ref[:, at(INNER)] = tn(v[...], hb[:, at()]).astype(BF16)

    each_chunk(INNER, down_grad)
    each_chunk(width, up_grad)
    run[...] = jnp.zeros_like(run)
    through[...] = jnp.ones_like(through)
    next_out.wait()

    def back_tile(t):
        at = tile_rows(t)
        dout, dvt = hb[at, :], dv[at, :]
        rstd = small[at, RS][:, 0:1]
        cm = act[at, INNER + STATE :]
        total = jnp.zeros((SPAN, LANES), F32)
        for cs in wide_chunks(INNER):
            z = raw[at, cs].astype(F32)
            d = (nt(dout, wv[cs, :]) + nn(dvt, odown[:, cs])) * gate_ref[:, cs]
            wide[:, cs] = d
            g = d * (y[at, cs].astype(F32) * (z * sigmoid(z)))
            total = total + g[:, :LANES] + g[:, LANES:]
        back = jnp.sum(total, 1, keepdims=True) * (1.0 / INNER) * rstd * rstd
        both = pairs(reaches[at, :])
        dcm = jnp.zeros((SPAN, STATE), F32)
        for cs in wide_chunks(INNER):
            z = raw[at, cs].astype(F32)
            sg = sigmoid(z)
            silu = z * sg
            mixed = y[at, cs].astype(F32)
            dg = rstd * (wide[:, cs] - mixed * silu * back)
            dm = (dg * silu).astype(BF16)
            nout[at, cs] = dm
            raw[at, cs] = (dg * mixed * (sg + silu * (1.0 - sg))).astype(BF16)
            dm = dm.astype(F32)
            dp = (dm * nn(both, e[:, cs])).astype(BF16)
            prods[:, cs] = (dm * (mixed - skip_ref[:, cs] * act[at, cs].astype(F32))).astype(BF16)
            dcm = dcm + nt(dp, states[t, :, cs])
            dst = tn(cm, dp)
            states[t, :, cs] = dst.astype(BF16)
            run[:, cs] += dst * through[0:1, cs]
        small[at, RS] = nt(prods[...], e[:LANES, :])
        small[at, DCM] = dcm
        through[...] = through[...] * carry[t]

    each_tile(nb, back_tile)
    for j in range(own_ref.shape[0]):
        own_ref[j] = run[:, j * ow : (j + 1) * ow].astype(BF16)
    done += [mover.go(nout, dm_h), mover.go(raw.at[:, 0:INNER], dz_h), mover.go(states.at[0:nb], dst_h), mover.go(small, small_h)]
    pl.when(me < n - 1)(halo.wait_send)
    results.finish()
    for k, c in enumerate(done):
        if k != 1:
            c.wait()


def back_kernel(
    len_ref, id_ref, where_ref, tok_ref, gain_ref, cw_ref, bias_ref, rate_ref, skip_ref, thr_ref, parts,
    g_out, wall_h, dall_h, uall_h, e_h, act_h, dact_h, small_h, c2t_h, carry_h, next_h, dm_h, dz_h, dst_h, hb_h, u_h, x_h, dout_h, back_h,
    wt_h, wzall_h,
    out_h, grad_h, indown_ref, inup_ref, outdown_ref, outup_ref, land_h,
    wv, down, up, e, act, dact, ddt, small, c2t, carry, states, dm, dz, dst, hb, u, du, duz, dhz, dbm, ga, gb,
    wide, low, prods, sct, dsc, later, head, edge, landed, first, starts, slices,
    move_sems, w_sem, s_head, r_head, s_grad, r_grad, s1, r1, s2, r2, *bufs,
):
    n, me = lax.axis_size("ctx"), lax.axis_index("ctx")
    rows, width = hb.shape
    nb = rows // SPAN
    mid, end = INNER + CONV_CH, INNER + CONV_CH + HEADS
    meta = Meta(len_ref, id_ref, rows)
    targets = ctx_targets() + fsdp_targets()
    landed[...] = jnp.zeros_like(landed)
    hail(targets)
    mover = Mover(move_sems)
    proj_w = wt_h.shape[0]
    second_weights = Resident(wall_h, wv, w_sem.at[0], 0, INNER, (wt_h, wzall_h))
    second_weights.begin()
    in_dz = mover.tiles(dz_h, dz)
    in_up = mover.go(uall_h, up)
    in_u = mover.go(u_h, u)
    base = g_out.shape[1]
    in_g = mover.go(g_out, ga.at[:, 0:base])
    for_mix = [mover.go(e_h, e), mover.go(small_h, small), mover.go(c2t_h, c2t), mover.go(act_h, act), mover.go(dm_h, dm)]
    for_chain = [mover.go(next_h, states), mover.go(dst_h, dst), mover.go(carry_h, carry)]
    for_scan = [mover.go(dact_h, dact), mover.go(hb_h, hb), mover.go(dall_h, down)]
    exchange = Exchange(parts, lambda first, j: thr_ref[j].astype(F32)[0:1], first, starts, slices, (s1, r1, s2, r2), True)
    count = len(bufs) // 2
    up_a, up_b = INNER + width, width + proj_w - INNER
    sum_a = Reduce(
        ga, [(outdown_ref, 0, 0, INNER), (outup_ref, 0, INNER, up_a), (inup_ref, 0, up_a, up_a + INNER)], bufs[:count]
    )
    sum_b = Reduce(gb, [(indown_ref, 0, 0, width), (inup_ref, INNER, width, up_b)], bufs[count:])
    second_weights.finish()
    in_up.wait()
    for c in in_dz:
        c.wait()

    def gate_tile(t):
        at = tile_rows(t)
        for cs in wide_chunks(width):
            dhz[at, cs] = nn(dz[at, :], wv[:INNER, cs]).astype(BF16)
        duz[at, :] = nt(dz[at, :], up[:, :INNER])

        @pl.when(t == 0)
        def _():
            hailed(targets)
            exchange.begin()

    each_tile(nb, gate_tile)
    first_weights = Resident(wall_h, wv, w_sem.at[1], INNER, proj_w)
    first_weights.begin()
    in_u.wait()

    def gate_grad(at):
        ga[:, at(base)] = tn(u[...], dz[:, at()]).astype(BF16)

    each_chunk(INNER, gate_grad)
    if ga.shape[1] > base + INNER:
        ga[:, base + INNER :] = jnp.zeros((LOW, ga.shape[1] - base - INNER), BF16)
    for c in for_mix:
        c.wait()

    def mix_tile(t):
        at = tile_rows(t)
        bm, cm = act[at, INNER : INNER + STATE], act[at, INNER + STATE :]
        mask = block_mask(meta, t, True)
        sct[...] = jnp.where(mask, nt(bm, cm), 0.0)
        dsc[...] = jnp.zeros_like(dsc)
        both = pairs(small[at, DT])
        for cs in wide_chunks(INNER):
            dt = nn(both, e[:, cs])
            wide[:, cs] = dt
            low[:, cs] = (act[at, cs].astype(F32) * dt).astype(BF16)
        c2 = small[at, C2]
        top_rows, low_rows = pl.ds(pl.multiple_of(t * SPAN, HALF), HALF), pl.ds(pl.multiple_of(t * SPAN + HALF, HALF), HALF)

        def group(g, _):
            cols = pltpu.roll(c2, LANES - 4 * g, 1)
            rws = c2t[t, pl.ds(pl.multiple_of(8 * (g // 2), 8), 8), :]
            rws = pltpu.roll(rws, 4 * lax.rem(g, 2), 0)
            for q in range(2):
                lanes = pl.ds(pl.multiple_of(g * 256 + q * 128, 128), 128)
                dmt = dm[at, lanes]
                da, db = halves(dmt)
                mixes = []
                for h, xh in zip((2 * q, 2 * q + 1), halves(low[:, lanes])):
                    col, row = cols[:, h : h + 1], rws[h : h + 1, :]
                    top = nt(xh[:HALF], dmt)
                    bot = nt(xh[HALF:], dmt[HALF:])

                    def mix(i, j, d):
                        decay = jnp.exp2(jnp.minimum(row[:, j : j + HALF] - col[i : i + HALF], 0.0))
                        dsc[i : i + HALF, j : j + HALF] += d * decay
                        return (sct[i : i + HALF, j : j + HALF] * decay).astype(BF16)

                    mixes.append((mix(0, 0, top[:, :HALF]), mix(0, HALF, top[:, HALF:]), mix(HALF, HALF, bot)))
                (a00, a01, a11), (b00, b01, b11) = mixes
                g_top = nn(jnp.concatenate([a00, a01, b00, b01], 1), jnp.concatenate([da, db], 0))
                g_low = nn(jnp.concatenate([a11, b11], 1), jnp.concatenate([da[HALF:], db[HALF:]], 0))
                dz[top_rows, lanes] = (g_top * wide[:HALF, lanes]).astype(BF16)
                dz[low_rows, lanes] = (g_low * wide[HALF:, lanes]).astype(BF16)
            return 0

        lax.fori_loop(0, HEADS // 4, group, 0)
        ds = jnp.where(mask, dsc[...], 0.0).astype(BF16)
        dbm[at, :] = nn(ds, cm)
        small[at, DCM] += tn(ds, bm)
        pl.when(t == nb // 2)(exchange.middle)

    each_tile(nb, mix_tile)
    in_g.wait()
    sum_a.begin()
    for c in for_chain:
        c.wait()
    exchange.finish(later)
    dend = []
    for b in reversed(range(nb)):
        sums = []
        for cs in wide_chunks(INNER):
            a = later[:, cs]
            sums.append(jnp.sum(a * states[b, :, cs].astype(F32), 0, keepdims=True))
            states[b, :, cs] = a.astype(BF16)
            later[:, cs] = dst[b, :, cs].astype(F32) + carry[b, 0:1, cs] * a
        total = jnp.broadcast_to(jnp.concatenate(sums, 1), (16, INNER))
        head[b : b + 1, :LANES] = sum(nt(p, e[:LANES, :]) for p in split(total, 3))[:1]
    for c in for_scan:
        c.wait()

    def edge_rows(k, t):
        at = pl.ds(pl.multiple_of(t * SPAN, SPAN), k)
        both = pairs(small[at, WTS])
        bm = act[at, INNER : INNER + STATE]
        for cs in wide_chunks(INNER):
            w = nn(both, e[:, cs])
            xs = act[at, cs].astype(F32)
            dx = dz[at, cs].astype(F32) + nn(bm, states[t, :, cs]) * w
            prods[:k, cs] = (xs * dx).astype(BF16)
            dx = dx + skip_ref[:, cs] * dm[at, cs].astype(F32)
            wide[:k, cs] = dx * dact[at, cs].astype(F32)
            low[:k, cs] = (xs * w).astype(BF16)
        bcols, ccols = slice(INNER, INNER + STATE), slice(INNER + STATE, CONV_CH)
        wide[:k, bcols] = (dbm[at, :] + nt(low[:k, :], states[t])) * dact[at, bcols].astype(F32)
        wide[:k, ccols] = small[at, DCM] * dact[at, ccols].astype(F32)

    edge_rows(16, 0)
    edge[...] = wide[:8, :]
    edge_copy = send(edge.at[0:3, :], landed.at[0:3, :], s_head, r_head, ctx=lax.rem(me + n - 1, n))
    pl.when(me > 0)(edge_copy.start)
    sum_a.over_y()

    def scan_tile(s):
        t = nb - 1 - s
        at = tile_rows(t)
        ends = head[pl.ds(t, 1), :LANES]
        edge_rows(SPAN, t)
        csum = nt(prods[...], e[:LANES, :])
        last = iota((SPAN, 1), 0) == SPAN - 1
        dcum = small[at, RS] - csum + jnp.where(last, ends, 0.0)
        tri = one_hot(iota((SPAN, SPAN), 0) <= iota((SPAN, SPAN), 1))
        dsteps = sum(nn(tri, p) for p in split(dcum, 3))
        val = small[at, DTR] + bias_ref[...]
        sg = 1.0 / (1.0 + jnp.exp(-val))
        ex = jnp.exp(jnp.minimum(val, 0.0))
        ratio = jnp.where(val < -12.0, 1.0 - 0.5 * ex, sg / jnp.maximum(softplus(val), 1e-7))
        steps = csum * ratio + dsteps * rate_ref[...] * sg
        ddt[at, :] = jnp.where(iota((SPAN, LANES), 1) < HEADS, steps, 0.0).astype(BF16)
        pos = meta.cols(t)
        seq = meta.seq(pos)
        masks = [(meta.seq(pos + j) == seq).astype(F32) for j in range(KERNEL)]
        for cs in wide_chunks(CONV_CH):
            cur = wide[:, cs]
            ext = jnp.concatenate([cur, edge[:, cs]], 0)
            total = cw_ref[3:4, cs] * cur
            for j in range(1, KERNEL):
                moved = pltpu.roll(ext, SPAN + 8 - j, 0)[:SPAN]
                total = total + (cw_ref[3 - j : 4 - j, cs] * moved) * masks[j]
            dact[at, cs] = total.astype(BF16)
        edge[...] = wide[:8, :]
        dut = duz[at, :] + nt(dact[at, :], up[:, INNER:mid]) + nt(ddt[at, :HEADS], up[:, mid:end])
        du[at, :] = dut.astype(BF16) * meta.select(pos).astype(BF16)
        pl.when(s == 0)(sum_a.scatter)
        pl.when(s == 2)(sum_a.gather)

    pl.when(me > 0)(edge_copy.wait_send)
    pl.when(me < n - 1)(edge_copy.wait_recv)
    edge[...] = jnp.where(me < n - 1, landed[...], 0.0)
    each_tile(nb, scan_tile)

    def down_grad(at):
        gb[:, at()] = tn(du[...], hb[:, at()]).astype(BF16)

    def conv_grad(at):
        gb[:, at(width)] = tn(u[...], dact[:, at()]).astype(BF16)

    each_chunk(width, down_grad)
    each_chunk(CONV_CH, conv_grad)
    gb[:, width + CONV_CH :] = jnp.zeros((LOW, gb.shape[1] - width - CONV_CH), BF16)
    gb[:, width + CONV_CH : width + CONV_CH + HEADS] = tn(u[...], ddt[:, :HEADS]).astype(BF16)
    sum_b.begin()
    xs, douts = dm.at[:, 0:width], dm.at[:, width : 2 * width]
    for_last = [mover.go(x_h, xs), mover.go(dout_h, douts)]
    first_weights.finish()
    sum_a.finish()
    for c in for_last:
        c.wait()

    def last_tile(t):
        at = tile_rows(t)
        squares, crosses = jnp.zeros((SPAN, LANES), F32), jnp.zeros((SPAN, LANES), F32)
        for cs in wide_chunks(width):
            dh = (
                dhz[at, cs].astype(F32) + nn(dact[at, :], wv[:CONV_CH, cs]) + nn(ddt[at, :HEADS], wv[CONV_CH:, cs])
                + nn(du[at, :], down[:, cs])
            )
            g = dh * gain_ref[:, cs]
            wide[:, cs] = g
            xt = dm[at, cs].astype(F32)
            sq, cross = xt * xt, g * xt
            squares = squares + sq[:, :LANES] + sq[:, LANES:]
            crosses = crosses + cross[:, :LANES] + cross[:, LANES:]
        rstd = lax.rsqrt(jnp.sum(squares, 1, keepdims=True) * (1.0 / width) + EPS)
        back = jnp.sum(crosses, 1, keepdims=True) * (1.0 / width) * rstd * rstd
        valid = meta.valid(meta.cols(t))
        for cs in wide_chunks(width):
            dx = rstd * (wide[:, cs] - dm[at, cs].astype(F32) * back)
            dout = dm[at, width + cs.start : width + cs.stop].astype(F32)
            hb[at, cs] = ((dout + dx) * valid).astype(BF16)
        pl.when(t == 0)(sum_b.over_y)
        pl.when(t == nb - 1)(sum_b.scatter)

    each_tile(nb, last_tile)
    share = rows // n
    sort_rows(where_ref[...], hb, act.at[:, 0:width])
    copies = [
        send(
            act.at[place(to, share), 0:width], land_h.at[place(me, share), :], s_grad.at[k - 1], r_grad.at[k - 1], ctx=to
        )
        for k, to, _ in peers("ctx")
    ]
    for c in copies:
        c.start()
    dhz[place(me, share), :] = act[place(me, share), 0:width]
    mover.go(back_h, dm.at[:, 0:width]).wait()
    sort_rows(tok_ref[...], dm.at[:, 0:width], dz.at[:, 0:width])
    out_done = mover.go(dz.at[:, 0:width], out_h)
    sum_b.gather()
    sum_b.finish()
    arrived = []
    for c, (_, _, back) in zip(copies, peers("ctx")):
        c.wait_recv()
        arrived.append(mover.go(land_h.at[place(back, share), :], dhz.at[place(back, share), :]))
    for c in arrived:
        c.wait()
    for c in copies:
        c.wait_send()
    tok, grads = tok_ref[...], []
    for t in range(0, rows, SPAN):
        hit = one_hot(iota((SPAN, rows), 0) + t == tok)
        for cs in wide_chunks(width):
            hb[t : t + SPAN, cs] = nn(hit, dhz[:, cs]).astype(BF16)
        grads.append(mover.go(hb.at[t : t + SPAN, :], grad_h.at[t : t + SPAN, :]))
    for c in grads + [out_done]:
        c.wait()


def shape(*dims, dtype=F32):
    return jax.ShapeDtypeStruct(dims, dtype)


def params(mib=60, remote=None):
    if remote is None:
        return pltpu.CompilerParams(vmem_limit_bytes=mib * MIB)
    return pltpu.CompilerParams(vmem_limit_bytes=mib * MIB, collective_id=remote, has_side_effects=True)


SMEM = pl.BlockSpec(memory_space=pltpu.SMEM)
VMEM = pl.BlockSpec(memory_space=pltpu.VMEM)
ANY = pl.BlockSpec(memory_space=pl.ANY)


def exchange_scratch(n, rows):
    owners = owners_of(n)
    w = INNER // owners
    return [
        pltpu.VMEM((n, rows, w), BF16), pltpu.VMEM((n, STATE, w), BF16), pltpu.VMEM((owners, STATE, w), BF16),
    ] + [pltpu.SemaphoreType.DMA((n - 1,))] * 4


def local(
    tokens, cotangent, order, lengths, adapter_ids, in_weight, out_weight, in_down, in_up, out_down, out_up,
    norm_gain, conv_weight, conv_bias, dt_bias, a_log, skip_gain, gate_gain,
):
    n, nf = lax.axis_size("ctx"), lax.axis_size("fsdp")
    rows, width = tokens.shape[1:]
    nb = rows // SPAN
    share = rows // n
    log_rows = rows.bit_length() - 1
    assert rows == 1 << log_rows and rows <= 1024 and rows % SPAN == 0 and nb >= 4
    assert nf % 2 == 0 and share % 16 == 0
    proj_w = in_weight.shape[1]
    rest = proj_w - INNER
    bf = lambda *dims: shape(*dims, dtype=BF16)
    vm = pltpu.VMEM
    dma = pltpu.SemaphoreType.DMA
    padded = lambda c: -(-c // (n * LANES)) * LANES * n
    owners = owners_of(n)
    ow = INNER // owners
    wt, in_down_t, out_down_t = in_weight.T, in_down.T, out_down.T
    kw, ko, ka = wt.shape[1], out_weight.shape[0], in_down_t.shape[0]
    idx = shape(1, rows, dtype=jnp.int32)
    gain, gate, cb = norm_gain[None], gate_gain[None], conv_bias[None]
    seqs = (lengths, adapter_ids)

    parts_w = len(chunks_of(proj_w - SPLIT, WEIGHT_PARTS))
    got, cot_sorted, slot, where, tok, w_in, a_in, b_in, e, skip, bias, rate = pl.pallas_call(
        partial(arrive_kernel, log_rows, share),
        in_specs=[VMEM] * 9,
        out_specs=[ANY, VMEM, VMEM, VMEM, VMEM, ANY, ANY, ANY, VMEM, VMEM, VMEM, VMEM],
        out_shape=(
            bf(rows, width), bf(rows, width), idx, idx, idx, bf(nf, proj_w - SPLIT, kw), bf(LOW, width), bf(LOW, proj_w),
            bf(2 * LANES, INNER), shape(1, INNER), shape(1, LANES), shape(1, LANES),
        ),
        scratch_shapes=[vm((rows, width), BF16)] + spread_sems(n) + gather_sems(nf, 2 + parts_w),
        compiler_params=params(remote=1),
        name="arrive",
    )(order, tokens[0], cotangent[0], wt, in_down_t, in_up, dt_bias[None], a_log[None], skip_gain[None])

    f32 = shape
    front_out = [
        bf(rows, width), bf(rows, width), bf(rows, LOW), bf(rows, CONV_CH), bf(rows, CONV_CH), f32(rows, SMALL),
        f32(nb, HEADS, SPAN), f32(nb, 8, INNER), bf(nb, STATE, INNER), bf(n, 16, ow), bf(rows, width), bf(rows, INNER),
        bf(rows, INNER), bf(nb, STATE, INNER), bf(owners, STATE, ow), bf(LOW, INNER + width), bf(rows, width),
        bf(INNER, width), bf(nf, SPLIT, kw),
    ]
    x, hb, u, act, dact, small, c2t, carry, after, thr, dout, dm, dz, dst, own, g_out, back_out, _, w_early = pl.pallas_call(
        front_kernel,
        in_specs=[SMEM, SMEM] + [VMEM] * 11 + [ANY] * 8,
        out_specs=[ANY] * 9 + [VMEM] + [ANY] * 4 + [VMEM, VMEM] + [ANY] * 3,
        out_shape=front_out,
        scratch_shapes=[
            vm((rest, width), BF16), vm((LOW, width), BF16), vm((LOW, proj_w), BF16), vm((LOW, INNER), BF16),
            vm((LOW, width), BF16), vm((2 * LANES, INNER), BF16), vm((rows, width), BF16), vm((rows, width), BF16),
            vm((rows, width), BF16), vm((rows, LOW), BF16), vm((rows, LOW), BF16), vm((rows, LOW), BF16),
            vm((rows, CONV_CH), BF16), vm((rows, CONV_CH), BF16), vm((nb, STATE, INNER), F32), vm((rows, INNER), BF16),
            vm((rows, INNER), BF16), vm((nb + 1, STATE, INNER), BF16), vm((rows, width), BF16), vm((rows, width), BF16),
            vm((rows, SMALL), F32), vm((rows, LANES), F32), vm((nb, HEADS, SPAN), F32), vm((nb, 8, INNER), F32),
            vm((SPAN, INNER), F32), vm((SPAN, INNER), BF16), vm((SPAN, INNER), BF16), vm((STATE, INNER), F32),
            vm((8, INNER), F32),
            vm((SPAN, SPAN), F32), vm((nb + 1, 8, CONV_CH), F32), vm((8, CONV_CH), F32),
            vm((owners, STATE + 16, ow), BF16), vm((n, STATE + 16, ow), BF16), vm((n, STATE, ow), BF16),
            vm((owners, STATE, ow), BF16), dma((MOVES,)), dma((2, 2 * nf)), dma, dma,
        ] + spread_sems(n) + spread_sems(n) + [dma((n - 1,))] * 4 + gather_sems(nf, 4),
        compiler_params=params(remote=2),
        name="front",
    )(
        *seqs, slot, where, gain, conv_weight, cb, bias, rate, skip, gate, out_down_t, out_up, got, w_in, a_in, b_in, e,
        cot_sorted, out_weight, wt,
    )

    cols_a, cols_b = padded(2 * INNER + width), padded(width + rest)
    low = LOW // nf
    block_output, input_grad, g_in_down, g_in_up, g_out_down, g_out_up, _ = pl.pallas_call(
        back_kernel,
        in_specs=[SMEM, SMEM] + [VMEM] * 9 + [ANY] * 21,
        out_specs=[ANY, ANY, VMEM, VMEM, VMEM, VMEM, ANY],
        out_shape=(
            bf(rows, width), bf(rows, width), f32(low, width), f32(low, proj_w), f32(low, INNER), f32(low, width),
            bf(rows, width),
        ),
        scratch_shapes=[
            vm((rest, width), BF16), vm((LOW, width), BF16), vm((LOW, proj_w), BF16), vm((2 * LANES, INNER), BF16),
            vm((rows, CONV_CH), BF16), vm((rows, CONV_CH), BF16), vm((rows, LANES), BF16), vm((rows, SMALL), F32),
            vm((nb, HEADS, SPAN), F32), vm((nb, 8, INNER), F32), vm((nb, STATE, INNER), BF16), vm((rows, INNER), BF16),
            vm((rows, INNER), BF16), vm((nb, STATE, INNER), BF16), vm((rows, width), BF16), vm((rows, LOW), BF16),
            vm((rows, LOW), BF16), vm((rows, LOW), F32), vm((rows, width), BF16), vm((rows, STATE), F32), vm((LOW, cols_a), BF16), vm((LOW, cols_b), BF16), vm((SPAN, CONV_CH), F32),
            vm((SPAN, INNER), BF16), vm((SPAN, INNER), BF16), vm((SPAN, SPAN), F32), vm((SPAN, SPAN), F32),
            vm((STATE, INNER), F32), vm((8, LANES), F32), vm((8, CONV_CH), F32), vm((8, CONV_CH), F32),
            vm((n, STATE, ow), BF16), vm((n, STATE, ow), BF16), vm((owners, STATE, ow), BF16),
            dma((MOVES,)), dma((2, 2 * nf)), dma, dma,
        ] + [dma((n - 1,))] * 6 + reduce_scratch(n, nf, cols_a // n) + reduce_scratch(n, nf, cols_b // n),
        compiler_params=params(62, remote=3),
        name="back",
    )(
        *seqs, where, tok, gain, conv_weight, bias, rate, skip, thr, own, g_out, w_in, a_in, b_in, e, act, dact, small, c2t,
        carry, after, dm, dz, dst, hb, u, x, dout, back_out, wt, w_early,
    )
    return block_output[None], input_grad[None], g_in_down.T, g_in_up, g_out_down.T, g_out_up


def solution(mesh):
    placed = (
        P("fsdp", "ctx", None),
        P("fsdp", "ctx", None),
        P("fsdp", None),
        P("fsdp", None),
        P("fsdp", None),
        P("fsdp", None),
        P("fsdp", None),
        P(None, "fsdp"),
        P("fsdp", None),
        P(None, "fsdp"),
        P("fsdp", None),
        P(),
        P(),
        P(),
        P(),
        P(),
        P(),
        P(),
    )
    return jax.shard_map(
        local,
        mesh=mesh,
        in_specs=placed,
        out_specs=(
            P("fsdp", "ctx", None),
            P("fsdp", "ctx", None),
            P(None, "fsdp"),
            P("fsdp", None),
            P(None, "fsdp"),
            P("fsdp", None),
        ),
        check_vma=False,
    )
```

```python
from functools import partial

import jax
import jax.numpy as jnp
from jax import lax
from jax.experimental import pallas as pl
from jax.experimental.pallas import tpu as pltpu
from jax.sharding import PartitionSpec as P

HEADS = 32
HEAD = 64
STATE = 128
KERNEL = 4
SPAN = 256
RANK = 16
ADAPTERS = 8
SEQS = 3
CONV_CH = 2304
INNER = HEADS * HEAD
LOW = ADAPTERS * RANK
LANES = 128
HALF = SPAN // 2
EPS = 1e-05
LOG2E = 1.4426950408889634

F32 = jnp.float32
BF16 = jnp.bfloat16
MIB = 1 << 20
MESH = pl.DeviceIdType.MESH


def nn(a, b):
    return jnp.dot(a, b, preferred_element_type=F32)


def nt(a, b):
    return lax.dot_general(a, b, (((1,), (1,)), ((), ())), preferred_element_type=F32)


def tn(a, b):
    return lax.dot_general(a, b, (((0,), (0,)), ((), ())), preferred_element_type=F32)


def iota(shape, dim):
    return lax.broadcasted_iota(jnp.int32, shape, dim)


def one_hot(cond):
    return jnp.where(cond, 1.0, 0.0).astype(BF16)


def split(v, parts):
    out = []
    for _ in range(parts):
        piece = v.astype(BF16)
        out.append(piece)
        v = v - piece.astype(F32)
    return out


def pairs(v):
    return jnp.concatenate(split(v, 2), 1)


class Meta:
    def __init__(self, len_ref, id_ref, rows):
        self.start = lax.axis_index("ctx") * rows
        self.ends = []
        for k in range(SEQS):
            self.ends.append(len_ref[0, k] + (self.ends[-1] if k else 0))
        self.ids = [id_ref[0, k] for k in range(SEQS)]

    def seq(self, pos):
        found = sum((pos >= end).astype(jnp.int32) for end in self.ends)
        return jnp.where(pos >= 0, found, -1)

    def valid(self, pos):
        return (pos < self.ends[-1]).astype(F32)

    def select(self, pos):
        seq = self.seq(pos)
        ids = sum(jnp.where(seq == k, self.ids[k], 0) for k in range(SEQS))
        shape = (pos.shape[0], LOW)
        return jnp.where(iota(shape, 1) // RANK == ids, 1.0, 0.0) * self.valid(pos)

    def cols(self, tile):
        return self.start + tile * SPAN + iota((SPAN, 1), 0)

    def rows(self, tile):
        return self.start + tile * SPAN + iota((1, SPAN), 1)


def sigmoid(v):
    return 0.5 * jnp.tanh(0.5 * v) + 0.5


def running_count(mask):
    width = mask.shape[1]
    tri = one_hot(iota((SPAN, SPAN), 0) <= iota((SPAN, SPAN), 1))
    pieces, before = [], jnp.zeros((mask.shape[0], 1), F32)
    for c in range(0, width, SPAN):
        part = mask[:, c : c + SPAN]
        pieces.append(nn(part.astype(BF16), tri) + before)
        before = before + jnp.sum(part, 1, keepdims=True)
    return jnp.concatenate(pieces, 1)


def two_rows(v):
    first = jnp.broadcast_to(v >> 5, (16, v.shape[1]))
    second = jnp.broadcast_to(v & 31, (16, v.shape[1]))
    row = iota((16, v.shape[1]), 0)
    return jnp.where(row == 0, first, jnp.where(row == 1, second, 0)).astype(F32).astype(BF16)


def from_two(r):
    return (r[0:1] * 32.0 + r[1:2]).astype(jnp.int32)


def invert(idx):
    width = idx.shape[1]
    values = two_rows(iota((1, width), 1))
    pieces = []
    for t in range(0, width, SPAN):
        hit = one_hot(iota((SPAN, width), 0) + t == idx)
        pieces.append(from_two(nt(values, hit)))
    return jnp.concatenate(pieces, 1)


def peers(axis):
    n, me = lax.axis_size(axis), lax.axis_index(axis)
    return [(k, lax.rem(me + k, n), lax.rem(me + n - k, n)) for k in range(1, n)]


def send(src, dst, send_sem, recv_sem, **where):
    return pltpu.make_async_remote_copy(
        src_ref=src, dst_ref=dst, send_sem=send_sem, recv_sem=recv_sem, device_id=where, device_id_type=MESH
    )


def hail(targets):
    barrier = pltpu.get_barrier_semaphore()
    for where in targets:
        pl.semaphore_signal(barrier, inc=1, device_id=where, device_id_type=MESH)


def hailed(targets):
    pl.semaphore_wait(pltpu.get_barrier_semaphore(), len(targets))


def place(which, share):
    return pl.ds(pl.multiple_of(which * share, share), share)


def sets_of(n, late):
    second = [k for k in range(1, n) if k % 8 in late]
    return [k for k in range(1, n) if k not in second], second


COT_LATE, OUT_LATE = (2, 6), (2, 5, 6)


class Spread:
    def __init__(self, src, dst, send_sem, recv_sem, own_sem, steps):
        n, me = lax.axis_size("ctx"), lax.axis_index("ctx")
        share = src.shape[0] // n
        self.copies = [
            send(src.at[place(to, share), :], dst.at[place(me, share), :], send_sem.at[k - 1], recv_sem.at[k - 1], ctx=to)
            for k, to, _ in peers("ctx") if k in steps
        ]
        self.own = None
        if own_sem is not None:
            self.own = pltpu.make_async_copy(src.at[place(me, share), :], dst.at[place(me, share), :], own_sem)

    def begin(self):
        for c in self.copies:
            c.start()
        if self.own is not None:
            self.own.start()

    def finish(self):
        for c in self.copies:
            c.wait()
        if self.own is not None:
            self.own.wait()


def spread_sems(n):
    return [pltpu.SemaphoreType.DMA((n - 1,)), pltpu.SemaphoreType.DMA((n - 1,)), pltpu.SemaphoreType.DMA]


def ring_targets():
    n, me = lax.axis_size("ctx"), lax.axis_index("ctx")
    return [{"ctx": lax.rem(me + 1, n)}, {"ctx": lax.rem(me + n - 1, n)}]


def ctx_targets():
    return [{"ctx": p} for _, p, _ in peers("ctx")]


def fsdp_sides():
    nf, f = lax.axis_size("fsdp"), lax.axis_index("fsdp")
    sides = [lax.rem(f + 2 * k, nf) for k in range(1, nf // 2)]
    backs = [lax.rem(f + nf - 2 * k, nf) for k in range(1, nf // 2)]
    return f, f + 1 - 2 * lax.rem(f, 2), sides, backs


def fsdp_targets():
    _, pair, sides, _ = fsdp_sides()
    return [{"fsdp": p} for p in sides + [pair]]


class Gather:
    def __init__(self, pieces, sems, kept=None):
        s_y, r_y, s_c, r_c, keep = sems
        f, pair, sides, backs = fsdp_sides()
        self.across = [
            [send(src, dst(f), s_y.at[k, m], r_y.at[k, m], fsdp=side) for m, (src, dst) in enumerate(pieces)]
            for k, side in enumerate(sides)
        ]
        self.inside = [[send(src, dst(f), s_c.at[0, m], r_c.at[0, m], fsdp=pair) for m, (src, dst) in enumerate(pieces)]]
        self.inside += [
            [send(dst(back), dst(back), s_c.at[k + 1, m], r_c.at[k + 1, m], fsdp=pair) for m, (src, dst) in enumerate(pieces)]
            for k, back in enumerate(backs)
        ]
        self.keep = [pltpu.make_async_copy(src, dst(f), keep.at[m]) for m, (src, dst) in enumerate(pieces[:kept])]

    def begin(self):
        for group in self.across:
            for c in group:
                c.start()
        for c in self.inside[0] + self.keep:
            c.start()

    def relay(self, lo=0, hi=None):
        for k, group in enumerate(self.across):
            for c, forward in list(zip(group, self.inside[k + 1]))[lo:hi]:
                c.wait_recv()
                forward.start()

    def finish(self, lo=0, hi=None):
        for group in self.inside:
            for c in group[lo:hi]:
                c.wait()
        for group in self.across:
            for c in group[lo:hi]:
                c.wait_send()
        for c in self.keep[lo:hi]:
            c.wait()


def gather_sems(nf, pieces):
    dma = pltpu.SemaphoreType.DMA
    side = max(nf // 2 - 1, 1)
    return [dma((side, pieces)), dma((side, pieces)), dma((nf // 2, pieces)), dma((nf // 2, pieces)), dma((pieces,))]


def stacked(ref, h):
    return lambda which: ref.at[place(which, h), :]


def chunks_of(total, parts):
    step = -(-total // (16 * parts)) * 16
    return [(lo, min(lo + step, total)) for lo in range(0, total, step)]


WEIGHT_PARTS = 4
SPLIT = 1024


def arrive_kernel(
    log_rows, share, order_ref, x_ref, cot_ref, wt_ref, down_ref, up_ref, bias_in, log_in, skip_in,
    got_ref, cots_ref, slot_ref, where_ref, tok_ref, wall_ref, dall_ref, uall_ref, e_ref, skip_ref, bias_ref, rate_ref,
    sorted_ref, s_tok, r_tok, own_sem, *sems,
):
    n, me = lax.axis_size("ctx"), lax.axis_index("ctx")
    rows = x_ref.shape[0]
    targets = ctx_targets() + fsdp_targets()
    hail(targets)
    pieces = [(down_ref, stacked(dall_ref, down_ref.shape[0])), (up_ref, stacked(uall_ref, up_ref.shape[0]))]
    for lo, hi in chunks_of(wt_ref.shape[0] - SPLIT, WEIGHT_PARTS):
        pieces.append((wt_ref.at[SPLIT + lo : SPLIT + hi, :], lambda which, lo=lo, hi=hi: wall_ref.at[which, lo:hi, :]))
    gather = Gather(pieces, sems)

    own_order = order_ref[:, pl.ds(pl.multiple_of(me * rows, rows), rows)]
    dest = own_order >> log_rows
    hot = jnp.where(iota((max(n, 16), rows), 0) == dest, 1.0, 0.0)
    rank = jnp.sum(hot * (running_count(hot) - 1.0), axis=0, keepdims=True)
    spos = dest * share + rank.astype(jnp.int32)
    sort_rows(spos, x_ref, sorted_ref)
    hailed(targets)
    gather.begin()
    tokens = [
        send(
            sorted_ref.at[place(to, share), :], got_ref.at[place(me, share), :], s_tok.at[k - 1], r_tok.at[k - 1], ctx=to
        )
        for k, to, _ in peers("ctx")
    ]
    for c in tokens:
        c.start()
    own = pltpu.make_async_copy(sorted_ref.at[place(me, share), :], got_ref.at[place(me, share), :], own_sem)
    own.start()

    sort_rows(spos, cot_ref, cots_ref)
    by_source = [order_ref[:, s * rows : (s + 1) * rows] for s in range(n)]
    order = jnp.concatenate(by_source + [jnp.full((1, rows), -1, jnp.int32)] * (-n % 16), 0)
    mine = jnp.where(order >> log_rows == me, 1.0, 0.0)
    mark = jnp.where(mine > 0.0, running_count(mine) - 1.0, -1.0).astype(jnp.int32)
    for s in range(n):
        hit = one_hot(iota((share, rows), 0) == mark[s : s + 1, :])
        slot = by_source[s] & (rows - 1)
        slot_ref[:, s * share : (s + 1) * share] = from_two(nt(two_rows(slot), hit))
    where_ref[...] = invert(slot_ref[...])
    tok_ref[...] = invert(spos)
    e_ref[...] = one_hot((iota((2 * LANES, INNER), 0) & (LANES - 1)) == iota((2 * LANES, INNER), 1) // HEAD)
    pad = jnp.zeros((1, LANES - HEADS), F32)
    wide = jnp.broadcast_to(jnp.concatenate([skip_in[...], pad], 1), (16, LANES))
    skip_ref[...] = sum(nn(p, e_ref[:LANES, :]) for p in split(wide, 3))[0:1]
    bias_ref[...] = jnp.concatenate([bias_in[...], pad], 1)
    rate_ref[...] = jnp.concatenate([-jnp.exp(log_in[...]), pad], 1)

    gather.relay()
    gather.finish()
    for c in tokens:
        c.wait()
    own.wait()


def sort_rows(idx, src, dst):
    rows = src.shape[0]

    def body(t):
        hit = one_hot(iota((SPAN, rows), 0) + t * SPAN == idx)
        for cs in wide_chunks(src.shape[1]):
            dst[tile_rows(t), cs] = nn(hit, src[:, cs]).astype(BF16)

    each_tile(rows // SPAN, body)


def owners_of(n):
    return min(n, INNER // LANES)


def each_owner(n, which, act):
    if owners_of(n) == n:
        act()
    else:
        pl.when(which < owners_of(n))(act)


class Exchange:
    def __init__(self, parts, through, first, starts, landed, sems, reverse):
        self.parts, self.through, self.first, self.starts, self.landed = parts, through, first, starts, landed
        self.s1, self.r1, self.s2, self.r2 = sems
        self.reverse = reverse
        self.n, self.me = lax.axis_size("ctx"), lax.axis_index("ctx")

    def out(self, k, to):
        return send(self.parts.at[to], self.first.at[self.me], self.s1.at[k - 1], self.r1.at[k - 1], ctx=to)

    def back(self, k, to):
        return send(self.starts.at[to], self.landed.at[self.me], self.s2.at[k - 1], self.r2.at[k - 1], ctx=to)

    def begin(self):
        for k, to, _ in peers("ctx"):
            each_owner(self.n, to, lambda: self.out(k, to).start())

    def middle(self):
        n, me = self.n, self.me

        def act():
            self.first[me] = self.parts[me]
            for k, to, _ in peers("ctx"):
                self.out(k, to).wait_recv()

            def lap(t, running):
                j = n - 1 - t if self.reverse else t
                self.starts[j] = running.astype(BF16)
                part = self.first[j].astype(F32)
                through = self.through(self.first, j)
                return running * through + part[:STATE]

            lax.fori_loop(0, n, lap, jnp.zeros((STATE, self.first.shape[2]), F32))
            self.landed[me] = self.starts[me]
            for k, to, _ in peers("ctx"):
                self.back(k, to).start()

        each_owner(n, me, act)

    def finish(self, result):
        n, me = self.n, self.me
        for k, to, back in peers("ctx"):
            each_owner(n, back, lambda: self.back(k, to).wait_recv())
        w = self.landed.shape[2]
        for j in range(owners_of(n)):
            result[:, j * w : (j + 1) * w] = self.landed[j].astype(result.dtype)
        for k, to, _ in peers("ctx"):
            each_owner(n, to, lambda: self.out(k, to).wait_send())

        def act():
            for k, to, _ in peers("ctx"):
                self.back(k, to).wait_send()

        each_owner(n, me, act)


class Reduce:
    def __init__(self, g_ref, outs, bufs):
        self.g, self.outs = g_ref, outs
        self.pair_in, self.pair_sum, self.side_in, self.total, self.ctx_in, self.piece, self.all_in, sems = bufs
        self.n, self.me = lax.axis_size("ctx"), lax.axis_index("ctx")
        nf = lax.axis_size("fsdp")
        self.f, pair, sides, _ = fsdp_sides()
        self.core = lax.rem(self.f, 2)
        self.h, self.cw = g_ref.shape[0] // nf, g_ref.shape[1] // self.n
        self.first = [
            send(g_ref.at[place(2 * y + 1 - self.core, self.h), :], self.pair_in.at[y], sems.at[0, y], sems.at[1, y], fsdp=pair)
            for y in range(nf // 2)
        ]
        self.second = [
            send(self.pair_sum.at[side // 2], self.side_in.at[k], sems.at[2, k], sems.at[3, k], fsdp=side)
            for k, side in enumerate(sides)
        ]
        self.third = [
            send(self.total.at[to], self.ctx_in.at[k - 1], sems.at[4, k - 1], sems.at[5, k - 1], ctx=to)
            for k, to, _ in peers("ctx")
        ]
        self.fourth = [
            send(self.piece, self.all_in.at[self.me], sems.at[6, k - 1], sems.at[7, k - 1], ctx=to)
            for k, to, _ in peers("ctx")
        ]

    def parts(self, body):
        def step(j, _):
            body(pl.ds(pl.multiple_of(j * self.cw, LANES), self.cw), j)
            return 0

        lax.fori_loop(0, self.n, step, 0)

    def begin(self):
        for c in self.first:
            c.start()

    def over_y(self):
        for y, c in enumerate(self.first):
            c.wait_recv()

            def add(cs, j, y=y):
                both = self.g[place(2 * y + self.core, self.h), cs].astype(F32) + self.pair_in[y, :, cs].astype(F32)
                self.pair_sum[y, :, cs] = both.astype(BF16)

            self.parts(add)
        for c in self.second:
            c.start()

    def scatter(self):
        for c in self.second:
            c.wait_recv()

        def add(cs, j):
            mine = self.pair_sum[self.f // 2, :, cs].astype(F32)
            for k in range(len(self.second)):
                mine = mine + self.side_in[k, :, cs].astype(F32)
            self.total[j] = mine.astype(BF16)

        self.parts(add)
        for c in self.third:
            c.start()

    def gather(self):
        mine = self.total[self.me].astype(F32)
        for k, c in enumerate(self.third):
            c.wait_recv()
            mine = mine + self.ctx_in[k].astype(F32)
        self.piece[...] = mine.astype(BF16)
        for c in self.fourth:
            c.start()
        self.all_in[self.me] = self.piece[...]

    def finish(self):
        for c in self.fourth:
            c.wait_recv()

        for j in range(self.n):
            for ref, at, lo, hi in self.outs:
                a, b = max(lo, j * self.cw), min(hi, (j + 1) * self.cw)
                if a < b:
                    part = self.all_in[j, :, a - j * self.cw : b - j * self.cw]
                    ref[:, at + a - lo : at + b - lo] = part.astype(F32)
        for c in self.first + self.second + self.third + self.fourth:
            c.wait_send()


def reduce_scratch(n, nf, cw):
    half, low = nf // 2, LOW // nf
    return [
        pltpu.VMEM((half, low, n * cw), BF16), pltpu.VMEM((half, low, n * cw), BF16),
        pltpu.VMEM((max(half - 1, 1), low, n * cw), BF16), pltpu.VMEM((n, low, cw), BF16),
        pltpu.VMEM((n - 1, low, cw), BF16), pltpu.VMEM((low, cw), BF16), pltpu.VMEM((n, low, cw), BF16),
        pltpu.SemaphoreType.DMA((8, max(n, half))),
    ]


class Mover:
    def __init__(self, sems):
        self.sems, self.used = sems, 0

    def go(self, src, dst):
        c = pltpu.make_async_copy(src, dst, self.sems.at[self.used])
        self.used += 1
        c.start()
        return c

    def tiles(self, src, dst):
        return [self.go(src.at[t : t + SPAN, :], dst.at[t : t + SPAN, :]) for t in range(0, dst.shape[0], SPAN)]


MOVES = 64


def each_tile(n, body):
    def step(t, _):
        body(t)
        return 0

    lax.fori_loop(0, n, step, 0)


def tile_rows(t):
    return pl.ds(pl.multiple_of(t * SPAN, SPAN), SPAN)


def each_chunk(width, body, step=256):
    def run(c, _):
        body(lambda base=0: pl.ds(pl.multiple_of(base + c * step, LANES), step))
        return 0

    lax.fori_loop(0, width // step, run, 0)


def wide_chunks(width, step=256):
    return [slice(c, min(c + step, width)) for c in range(0, width, step)]


class Resident:
    def __init__(self, wall_ref, dst, sems, lo, hi, early=None):
        nf, _, kw = wall_ref.shape
        f = lax.axis_index("fsdp")
        self.copies, at = [], 0
        for j in range(nf):
            which = lax.rem(f + j, nf)
            cols = pl.ds(pl.multiple_of(which * kw, LANES), kw)
            if early is not None:
                own, others = early
                src = own.at[0:SPLIT, :] if j == 0 else others.at[which]
                self.copies.append(pltpu.make_async_copy(src, dst.at[0:SPLIT, cols], sems.at[nf + j]))
            start = max(lo, SPLIT)
            src = wall_ref.at[which, start - SPLIT : hi - SPLIT, :]
            self.copies.append(pltpu.make_async_copy(src, dst.at[start - lo : hi - lo, cols], sems.at[j]))

    def begin(self):
        for c in self.copies:
            c.start()

    def finish(self):
        for c in self.copies:
            c.wait()


def softplus(v):
    e = jnp.exp(-jnp.abs(v))
    series = e * (1.0 - e * (0.5 - e * (1.0 / 3.0 - 0.25 * e)))
    return jnp.maximum(v, 0.0) + jnp.where(e < 0.01, series, jnp.log(1.0 + e))


def block_mask(meta, t, transposed):
    col, row = meta.cols(t), meta.rows(t)
    return (meta.seq(col) == meta.seq(row)) & ((row >= col) if transposed else (col >= row))


def halves(x):
    lane = iota(x.shape, 1)
    zero = jnp.zeros_like(x)
    return jnp.where(lane < HEAD, x, zero), jnp.where(lane >= HEAD, x, zero)


DTR, DT, C2, WTS, RS, DCM = (slice(k * LANES, (k + 1) * LANES) for k in range(6))
SMALL = 6 * LANES


def front_kernel(
    len_ref, id_ref, slot_ref, where_ref, gain_ref, cw_ref, cb_ref, bias_ref, rate_ref, skip_ref, gate_ref, od_ref, ou_ref,
    got_h, wall_h, dall_h, uall_h, e_h, cots_h, wo_h, wt_h,
    x_h, hb_h, u_h, act_h, dact_h, small_h, dl_h, dend_ref, edge_ref, dm_h, dxk_h, dhz_h, duz_h, dout_h, g_ref,
    back_h, woall_h, wzall_h,
    wv, down, up, odown, oup, e, got, x, hb, u, v, dv, raw, act, ls, y, nout, states, sorted_ref, cot, small, reaches, c2t, carry,
    wide, prods, low, run, through, sc, dsc, tails, landed, dact0, edge, landed2, parts, first, starts, slices, parts2, first2, starts2, slices2,
    move_sems, w_sem, s_halo, r_halo, s_cot, r_cot, own_cot, s_out, r_out, own_out, s_edge, r_edge,
    s1, r1, s2, r2, s3, r3, s4, r4, *g_sems,
):
    n, me = lax.axis_size("ctx"), lax.axis_index("ctx")
    nf, f = lax.axis_size("fsdp"), lax.axis_index("fsdp")
    rows, width = x.shape
    nb = rows // SPAN
    mid = INNER + CONV_CH
    meta = Meta(len_ref, id_ref, rows)
    targets = ctx_targets() + fsdp_targets()
    landed[...] = jnp.zeros_like(landed)
    landed2[...] = jnp.zeros_like(landed2)
    hail(targets)
    mover = Mover(move_sems)
    in_got = mover.go(got_h, got)
    in_down = mover.go(dall_h, down)
    proj_w = wt_h.shape[0]
    first_weights = Resident(wall_h, wv, w_sem.at[0], INNER, proj_w)
    first_weights.begin()
    in_up = mover.go(uall_h, up)
    in_e = mover.go(e_h, e)
    halo = send(tails.at[nb, 5:8, :], landed.at[5:8, :], s_halo, r_halo, ctx=lax.rem(me + 1, n))
    soon, late = sets_of(n, COT_LATE)
    cots = Spread(cots_h, cot, s_cot, r_cot, own_cot, soon)
    late_cots = Spread(cots_h, cot, s_cot, r_cot, None, late)
    kw = wo_h.shape[0]
    pieces = [
        (od_ref, stacked(odown, od_ref.shape[0])), (ou_ref, stacked(oup, ou_ref.shape[0])),
        (wt_h.at[0:SPLIT, :], lambda which: wzall_h.at[which]), (wo_h, stacked(woall_h, kw)),
    ]
    gather = Gather(pieces, g_sems, kept=2)
    exchange = Exchange(
        parts, lambda first, j: first[j, STATE:].astype(F32)[0:1], first, starts, slices, (s1, r1, s2, r2), False
    )
    later = Exchange(
        parts2, lambda _, j: first[j, STATE:].astype(F32)[0:1], first2, starts2, slices2, (s3, r3, s4, r4), True
    )
    edge_copy = send(edge.at[0:3, :], landed2.at[0:3, :], s_edge, r_edge, ctx=lax.rem(me + n - 1, n))
    in_got.wait()
    in_down.wait()

    def norm(t):
        at = tile_rows(t)
        pos = meta.cols(t)
        hit = one_hot(iota((SPAN, rows), 0) + t * SPAN == slot_ref[...])
        valid = meta.valid(pos)
        total = jnp.zeros((SPAN, LANES), F32)
        for cs in wide_chunks(width):
            xt = nn(hit, got[:, cs]) * valid
            x[at, cs] = xt.astype(BF16)
            sq = xt * xt
            total = total + sq[:, :LANES] + sq[:, LANES:]
        rstd = lax.rsqrt(jnp.sum(total, 1, keepdims=True) * (1.0 / width) + EPS)
        for cs in wide_chunks(width):
            hb[at, cs] = (x[at, cs].astype(F32) * rstd * gain_ref[:, cs]).astype(BF16)
        u[at, :] = (nt(hb[at, :], down[...]) * meta.select(pos)).astype(BF16)

    in_up.wait()
    first_weights.finish()

    def project(s):
        t = nb - 1 - s
        norm(t)
        at = tile_rows(t)
        for cs in wide_chunks(CONV_CH):
            raw[at, cs] = (nt(hb[at, :], wv[cs, :]) + nn(u[at, :], up[:, INNER + cs.start : INNER + cs.stop])).astype(BF16)
        last = nt(hb[at, :], wv[CONV_CH:, :]) + nn(u[at, :], up[:, mid:])
        small[at, DTR] = jnp.concatenate([last, jnp.zeros((SPAN, LANES - HEADS), F32)], 1)
        tails[t + 1] = raw[pl.ds(pl.multiple_of(t * SPAN + SPAN - 16, 16), 16), :].astype(F32)[8:]

        @pl.when(t == nb - 1)
        def _():
            hailed(targets)
            pl.when(me < n - 1)(halo.start)
            gather.begin()
            cots.begin()

    each_tile(nb, project)
    done = [mover.go(x, x_h), mover.go(hb, hb_h), mover.go(u, u_h)]
    hb_out = done[1]
    in_e.wait()

    def conv(s):
        t = lax.rem(s + 1, nb)
        at = tile_rows(t)

        @pl.when(t == 0)
        def _():
            pl.when(me > 0)(halo.wait_recv)
            tails[0] = jnp.where(me > 0, landed[...], 0.0)

        pos = meta.cols(t)
        seq = meta.seq(pos)
        around = meta.start + t * SPAN - 8 + iota((SPAN + 8, 1), 0)
        mask = (meta.seq(around - 1) == meta.seq(around)).astype(F32)
        for cs in wide_chunks(CONV_CH):
            ext = jnp.concatenate([tails[t, :, cs], raw[at, cs].astype(F32)], 0)
            acc = cw_ref[0:1, cs] * ext
            for j in range(1, KERNEL):
                acc = cw_ref[j : j + 1, cs] * ext + mask * pltpu.roll(acc, 1, 0)
            acc = cb_ref[:, cs] + acc[8:]
            sg = sigmoid(acc)
            val = acc * sg
            raw[at, cs] = (sg + val * (1.0 - sg)).astype(BF16)
            act[at, cs] = val.astype(BF16)
        dt = softplus(small[at, DTR] + bias_ref[...])
        small[at, DT] = dt
        tri = one_hot(iota((SPAN, SPAN), 0) >= iota((SPAN, SPAN), 1))
        cum = sum(nn(tri, p) for p in split(dt * rate_ref[...], 3))
        start = meta.start + t * SPAN
        end_same = (seq == meta.seq(start + SPAN - 1)).astype(F32)
        passing = (seq == meta.seq(start - 1)).astype(F32)
        wts = jnp.exp(cum[SPAN - 1 : SPAN, :] - cum) * dt * end_same
        small[at, WTS] = wts
        reach = jnp.exp(cum) * passing
        reaches[at, :] = reach
        c2 = cum * LOG2E
        small[at, C2] = c2
        c2t[t] = c2.T[:HEADS]
        both = pairs(wts)
        bm = act[at, INNER : INNER + STATE]
        for cs in wide_chunks(INNER):
            weighted = (act[at, cs].astype(F32) * nn(both, e[:, cs])).astype(BF16)
            ls[t, :, cs] = tn(bm, weighted)
        ends = split(jnp.broadcast_to(reach[SPAN - 1 : SPAN, :], (16, LANES)), 3)
        carry[t] = sum(nn(p, e[:LANES, :]) for p in ends)[:8]

    each_tile(nb, conv)
    dact0[...] = raw[0:16, :]
    dact_out = mover.go(raw, dact_h)
    done += [mover.go(act, act_h)]
    ow = parts.shape[2]
    for j in range(parts.shape[0]):
        at = slice(j * ow, (j + 1) * ow)
        state, reached = ls[0, :, at], carry[0, 0:1, at]
        for b in range(1, nb):
            state = state * carry[b, 0:1, at] + ls[b, :, at]
            reached = reached * carry[b, 0:1, at]
        parts[j, :STATE] = state.astype(BF16)
        parts[j, STATE:] = jnp.broadcast_to(reached, (16, ow)).astype(BF16)
    exchange.begin()

    def mix_tile(t):
        at = tile_rows(t)
        bm, cm = act[at, INNER : INNER + STATE], act[at, INNER + STATE :]
        sc[...] = jnp.where(block_mask(meta, t, False), nt(cm, bm), 0.0)
        both = pairs(small[at, DT])
        for cs in wide_chunks(INNER):
            low[:, cs] = (act[at, cs].astype(F32) * nn(both, e[:, cs])).astype(BF16)
        c2 = small[at, C2]
        top_rows, low_rows = pl.ds(pl.multiple_of(t * SPAN, HALF), HALF), pl.ds(pl.multiple_of(t * SPAN + HALF, HALF), HALF)

        def group(g, _):
            cols = pltpu.roll(c2, LANES - 4 * g, 1)
            rws = c2t[t, pl.ds(pl.multiple_of(8 * (g // 2), 8), 8), :]
            rws = pltpu.roll(rws, 4 * lax.rem(g, 2), 0)
            for q in range(2):
                lanes = pl.ds(pl.multiple_of(g * 256 + q * 128, 128), 128)
                xa, xb = halves(low[:, lanes])
                mixes = []
                for h in (2 * q, 2 * q + 1):
                    col, row = cols[:, h : h + 1], rws[h : h + 1, :]

                    def mix(i, j):
                        decay = jnp.exp2(jnp.minimum(col[i : i + HALF] - row[:, j : j + HALF], 0.0))
                        return (sc[i : i + HALF, j : j + HALF] * decay).astype(BF16)

                    mixes.append((mix(0, 0), mix(HALF, 0), mix(HALF, HALF)))
                (a00, a10, a11), (b00, b10, b11) = mixes
                top = nn(jnp.concatenate([a00, b00], 1), jnp.concatenate([xa[:HALF], xb[:HALF]], 0))
                bot = nn(jnp.concatenate([a10, a11, b10, b11], 1), jnp.concatenate([xa, xb], 0))
                y[top_rows, lanes] = top.astype(BF16)
                y[low_rows, lanes] = bot.astype(BF16)
            return 0

        lax.fori_loop(0, HEADS // 4, group, 0)

    each_tile(nb, mix_tile)
    gather.relay(0, 3)
    gather.finish(0, 3)
    second_weights = Resident(wall_h, wv, w_sem.at[1], 0, INNER, (wt_h, wzall_h))
    second_weights.begin()
    dact_out.wait()
    gather.relay(3)
    second_weights.finish()

    def gate_tile(t):
        at = tile_rows(t)
        for cs in wide_chunks(INNER):
            raw[at, cs] = (nt(hb[at, :], wv[cs, :]) + nn(u[at, :], up[:, cs])).astype(BF16)
        pl.when(t == nb // 2)(exchange.middle)
        pl.when(t == nb // 2)(late_cots.begin)

    each_tile(nb, gate_tile)
    gather.finish(3)
    out_weights = [mover.go(wo_h, wv.at[place(f, kw), :])]
    for j in range(1, nf):
        which = lax.rem(f + j, nf)
        out_weights.append(mover.go(woall_h.at[place(which, kw), :], wv.at[place(which, kw), :]))
    exchange.finish(run)
    for c in out_weights:
        c.wait()

    def out_tile(t):
        at = tile_rows(t)
        both = pairs(reaches[at, :])
        cm = act[at, INNER + STATE :]
        total = jnp.zeros((SPAN, LANES), F32)
        for cs in wide_chunks(INNER):
            now = run[:, cs]
            start = now.astype(BF16)
            states[t, :, cs] = start
            later = now * carry[t, 0:1, cs] + ls[t, :, cs]
            run[:, cs] = later
            mixed = y[at, cs].astype(F32) + nn(both, e[:, cs]) * nn(cm, start)
            mixed = mixed + skip_ref[:, cs] * act[at, cs].astype(F32)
            y[at, cs] = mixed.astype(BF16)
            z = raw[at, cs].astype(F32)
            gated = mixed * (z * sigmoid(z))
            wide[:, cs] = gated
            sq = gated * gated
            total = total + sq[:, :LANES] + sq[:, LANES:]
        rstd = lax.rsqrt(jnp.sum(total, 1, keepdims=True) * (1.0 / INNER) + EPS)
        small[at, RS] = jnp.broadcast_to(rstd, (SPAN, LANES))
        for cs in wide_chunks(INNER):
            nout[at, cs] = (wide[:, cs] * rstd * gate_ref[:, cs]).astype(BF16)
        pos = meta.cols(t)
        vt = (nt(nout[at, :], odown[...]) * meta.select(pos)).astype(BF16)
        v[at, :] = vt
        valid = meta.valid(pos)
        for cs in wide_chunks(width):
            branch = nn(nout[at, :], wv[:INNER, cs]) + nn(vt, oup[:, cs])
            got[at, cs] = ((x[at, cs].astype(F32) + branch) * valid).astype(BF16)

    each_tile(nb, out_tile)
    states[nb] = run[...].astype(BF16)
    sort_rows(where_ref[...], got, sorted_ref)
    soon, late = sets_of(n, OUT_LATE)
    results = Spread(sorted_ref, back_h, s_out, r_out, own_out, soon)
    late_results = Spread(sorted_ref, back_h, s_out, r_out, None, late)
    results.begin()
    cots.finish()
    late_cots.finish()
    hb_out.wait()

    def dout_tile(t):
        at = tile_rows(t)
        pos = meta.cols(t)
        hit = one_hot(iota((SPAN, rows), 0) + t * SPAN == slot_ref[...])
        valid = meta.valid(pos)
        for cs in wide_chunks(width):
            hb[at, cs] = (nn(hit, cot[:, cs]) * valid).astype(BF16)
        dv[at, :] = nt(hb[at, :], oup[...]).astype(BF16) * meta.select(pos).astype(BF16)

    each_tile(nb, dout_tile)
    done.append(mover.go(hb, dout_h))

    def down_grad(at):
        g_ref[:, at()] = tn(dv[...], nout[:, at()]).astype(BF16)

    def up_grad(at):
        g_ref[:, at(INNER)] = tn(v[...], hb[:, at()]).astype(BF16)

    each_chunk(INNER, down_grad)
    each_chunk(width, up_grad)
    run[...] = jnp.zeros_like(run)
    through[...] = jnp.ones_like(through)

    def back_tile(t):
        at = tile_rows(t)
        dout, dvt = hb[at, :], dv[at, :]
        rstd = small[at, RS][:, 0:1]
        cm = act[at, INNER + STATE :]
        total = jnp.zeros((SPAN, LANES), F32)
        for cs in wide_chunks(INNER):
            z = raw[at, cs].astype(F32)
            d = (nt(dout, wv[cs, :]) + nn(dvt, odown[:, cs])) * gate_ref[:, cs]
            wide[:, cs] = d
            g = d * (y[at, cs].astype(F32) * (z * sigmoid(z)))
            total = total + g[:, :LANES] + g[:, LANES:]
        back = jnp.sum(total, 1, keepdims=True) * (1.0 / INNER) * rstd * rstd
        both = pairs(reaches[at, :])
        dcm = jnp.zeros((SPAN, STATE), F32)
        for cs in wide_chunks(INNER):
            z = raw[at, cs].astype(F32)
            sg = sigmoid(z)
            silu = z * sg
            mixed = y[at, cs].astype(F32)
            dg = rstd * (wide[:, cs] - mixed * silu * back)
            dm = (dg * silu).astype(BF16)
            nout[at, cs] = dm
            raw[at, cs] = (dg * mixed * (sg + silu * (1.0 - sg))).astype(BF16)
            dm = dm.astype(F32)
            dp = (dm * nn(both, e[:, cs])).astype(BF16)
            prods[:, cs] = (dm * (mixed - skip_ref[:, cs] * act[at, cs].astype(F32))).astype(BF16)
            dcm = dcm + nt(dp, states[t, :, cs])
            dst = tn(cm, dp)
            ls[t, :, cs] = dst
            run[:, cs] += dst * through[0:1, cs]
        small[at, RS] = nt(prods[...], e[:LANES, :])
        small[at, DCM] = dcm
        through[...] = through[...] * carry[t]

    each_tile(nb, back_tile)
    third_weights = Resident(wall_h, wv, w_sem.at[2], 0, INNER, (wt_h, wzall_h))
    third_weights.begin()
    for j in range(parts2.shape[0]):
        parts2[j] = run[:, j * ow : (j + 1) * ow].astype(BF16)
    later.begin()
    done.append(mover.go(nout, dm_h))
    base = INNER + width

    def gate_grad(at):
        g_ref[:, at(base)] = tn(u[...], raw[:, at()]).astype(BF16)

    each_chunk(INNER, gate_grad)
    if g_ref.shape[1] > base + INNER:
        g_ref[:, base + INNER :] = jnp.zeros((LOW, g_ref.shape[1] - base - INNER), BF16)
    third_weights.finish()

    def dhz_tile(t):
        at = tile_rows(t)
        for cs in wide_chunks(width):
            cot[at, cs] = nn(raw[at, :INNER], wv[:INNER, cs]).astype(BF16)
        reaches[at, :] = nt(raw[at, :INNER], up[:, :INNER])

    each_tile(nb, dhz_tile)
    done += [mover.go(cot, dhz_h), mover.go(reaches, duz_h)]

    def mix_back_tile(t):
        at = tile_rows(t)
        bm, cm = act[at, INNER : INNER + STATE], act[at, INNER + STATE :]
        mask = block_mask(meta, t, True)
        sc[...] = jnp.where(mask, nt(bm, cm), 0.0)
        dsc[...] = jnp.zeros_like(dsc)
        both = pairs(small[at, DT])
        for cs in wide_chunks(INNER):
            dt = nn(both, e[:, cs])
            wide[:, cs] = dt
            low[:, cs] = (act[at, cs].astype(F32) * dt).astype(BF16)
        c2 = small[at, C2]
        top_rows, low_rows = pl.ds(pl.multiple_of(t * SPAN, HALF), HALF), pl.ds(pl.multiple_of(t * SPAN + HALF, HALF), HALF)

        def group(g, _):
            cols = pltpu.roll(c2, LANES - 4 * g, 1)
            rws = c2t[t, pl.ds(pl.multiple_of(8 * (g // 2), 8), 8), :]
            rws = pltpu.roll(rws, 4 * lax.rem(g, 2), 0)
            for q in range(2):
                lanes = pl.ds(pl.multiple_of(g * 256 + q * 128, 128), 128)
                dmt = nout[at, lanes]
                da, db = halves(dmt)
                mixes = []
                for h, xh in zip((2 * q, 2 * q + 1), halves(low[:, lanes])):
                    col, row = cols[:, h : h + 1], rws[h : h + 1, :]
                    top = nt(xh[:HALF], dmt)
                    bot = nt(xh[HALF:], dmt[HALF:])

                    def mix(i, j, d):
                        decay = jnp.exp2(jnp.minimum(row[:, j : j + HALF] - col[i : i + HALF], 0.0))
                        dsc[i : i + HALF, j : j + HALF] += d * decay
                        return (sc[i : i + HALF, j : j + HALF] * decay).astype(BF16)

                    mixes.append((mix(0, 0, top[:, :HALF]), mix(0, HALF, top[:, HALF:]), mix(HALF, HALF, bot)))
                (a00, a01, a11), (b00, b01, b11) = mixes
                g_top = nn(jnp.concatenate([a00, a01, b00, b01], 1), jnp.concatenate([da, db], 0))
                g_low = nn(jnp.concatenate([a11, b11], 1), jnp.concatenate([da[HALF:], db[HALF:]], 0))
                raw[top_rows, lanes] = (g_top * wide[:HALF, lanes]).astype(BF16)
                raw[low_rows, lanes] = (g_low * wide[HALF:, lanes]).astype(BF16)
            return 0

        lax.fori_loop(0, HEADS // 4, group, 0)
        ds = jnp.where(mask, dsc[...], 0.0).astype(BF16)
        small[at, DT] = nn(ds, cm)
        small[at, DCM] += tn(ds, bm)
        pl.when(t == nb // 2)(later.middle)
        pl.when(t == nb // 2)(late_results.begin)

    each_tile(nb, mix_back_tile)
    done += [mover.go(raw.at[:, 0:INNER], dxk_h), mover.go(small, small_h)]
    later.finish(run)
    for b in reversed(range(nb)):
        sums = []
        for cs in wide_chunks(INNER):
            a = run[:, cs]
            sums.append(jnp.sum(a * states[b + 1, :, cs].astype(F32), 0, keepdims=True))
            states[b + 1, :, cs] = a.astype(BF16)
            run[:, cs] = ls[b, :, cs] + carry[b, 0:1, cs] * a
        total = jnp.broadcast_to(jnp.concatenate(sums, 1), (16, INNER))
        dend_ref[b : b + 1, :] = sum(nt(p, e[:LANES, :]) for p in split(total, 3))[:1]
    done.append(mover.go(states.at[1 : nb + 1], dl_h))

    first_rows = slice(0, 16)
    both = pairs(small[first_rows, WTS])
    bm = act[first_rows, INNER : INNER + STATE]
    for cs in wide_chunks(INNER):
        w = nn(both, e[:, cs])
        dx = raw[first_rows, cs].astype(F32) + nn(bm, states[1, :, cs]) * w
        dx = dx + skip_ref[:, cs] * nout[first_rows, cs].astype(F32)
        edge[:, cs] = (dx * dact0[:, cs].astype(F32))[:8]
        low[first_rows, cs] = (act[first_rows, cs].astype(F32) * w).astype(BF16)
    bcols, ccols = slice(INNER, INNER + STATE), slice(INNER + STATE, CONV_CH)
    dbm = small[first_rows, DT] + nt(low[first_rows, :], states[1])
    edge[:, bcols] = (dbm * dact0[:, bcols].astype(F32))[:8]
    edge[:, ccols] = (small[first_rows, DCM] * dact0[:, ccols].astype(F32))[:8]
    pl.when(me > 0)(edge_copy.start)
    pl.when(me < n - 1)(halo.wait_send)
    results.finish()
    late_results.finish()
    pl.when(me > 0)(edge_copy.wait_send)
    pl.when(me < n - 1)(edge_copy.wait_recv)
    edge_ref[...] = landed2[...]
    for k, c in enumerate(done):
        if k != 1:
            c.wait()


def wait_all(copies):
    for c in copies:
        c.wait()


def back_kernel(
    len_ref, id_ref, where_ref, tok_ref, gain_ref, cw_ref, bias_ref, rate_ref, skip_ref, dend_ref, edge_ref, ga,
    wall_h, dall_h, uall_h, e_h, act_h, dact_h, small_h, dl_h, dm_h, dxk_h, hb_h, u_h, duz_h, dhz_h, x_h, dout_h, back_h,
    out_h, grad_h, indown_ref, inup_ref, outdown_ref, outup_ref, land_h,
    wv, down, up, e, act, dact, ddt, small, dl, dm, dxk, hb, u, du, duz, dhz, x, dout, gb, wide, low, prods, edge,
    move_sems, w_sem, s_grad, r_grad, *bufs,
):
    n, me = lax.axis_size("ctx"), lax.axis_index("ctx")
    rows, width = hb.shape
    nb = rows // SPAN
    mid, end = INNER + CONV_CH, INNER + CONV_CH + HEADS
    proj_w = uall_h.shape[1]
    meta = Meta(len_ref, id_ref, rows)
    targets = ctx_targets() + fsdp_targets()
    hail(targets)
    mover = Mover(move_sems)
    now = [mover.go(e_h, e), mover.go(dl_h, dl)]
    loads = {}
    for t in reversed(range(nb)):
        at = slice(t * SPAN, (t + 1) * SPAN)
        pairs_of = ((small_h, small), (act_h, act), (dxk_h, dxk), (dm_h, dm), (dact_h, dact))
        loads[t] = [mover.go(src.at[at, :], dst.at[at, :]) for src, dst in pairs_of]
        if t == nb - 1:
            now += [mover.go(uall_h, up), mover.go(duz_h, duz)]
    weights = Resident(wall_h, wv, w_sem, INNER, proj_w)
    weights.begin()
    for_grads = [mover.go(hb_h, hb), mover.go(u_h, u)]
    for_last = [mover.go(dall_h, down), mover.go(dhz_h, dhz), mover.go(x_h, x), mover.go(dout_h, dout)]
    count = len(bufs) // 2
    up_a, up_b = INNER + width, width + proj_w - INNER
    sum_a = Reduce(
        ga, [(outdown_ref, 0, 0, INNER), (outup_ref, 0, INNER, up_a), (inup_ref, 0, up_a, up_a + INNER)], bufs[:count]
    )
    sum_b = Reduce(gb, [(indown_ref, 0, 0, width), (inup_ref, INNER, width, up_b)], bufs[count:])
    edge[...] = edge_ref[...]
    wait_all(now)

    def edge_rows(k, t):
        at = pl.ds(pl.multiple_of(t * SPAN, SPAN), k)
        both = pairs(small[at, WTS])
        bm = act[at, INNER : INNER + STATE]
        for cs in wide_chunks(INNER):
            w = nn(both, e[:, cs])
            xs = act[at, cs].astype(F32)
            dx = dxk[at, cs].astype(F32) + nn(bm, dl[t, :, cs]) * w
            prods[:k, cs] = (xs * dx).astype(BF16)
            dx = dx + skip_ref[:, cs] * dm[at, cs].astype(F32)
            wide[:k, cs] = dx * dact[at, cs].astype(F32)
            low[:k, cs] = (xs * w).astype(BF16)
        bcols, ccols = slice(INNER, INNER + STATE), slice(INNER + STATE, CONV_CH)
        wide[:k, bcols] = (small[at, DT] + nt(low[:k, :], dl[t])) * dact[at, bcols].astype(F32)
        wide[:k, ccols] = small[at, DCM] * dact[at, ccols].astype(F32)

    def scan_tile(s):
        t = nb - 1 - s
        at = tile_rows(t)
        pl.when(s == 0)(lambda: wait_all(loads[nb - 1]))
        for k in range(1, nb):
            pl.when(s == k)(lambda k=k: wait_all(loads[nb - 1 - k]))
        ends = dend_ref[pl.ds(t, 1), :]
        edge_rows(SPAN, t)
        csum = nt(prods[...], e[:LANES, :])
        last = iota((SPAN, 1), 0) == SPAN - 1
        dcum = small[at, RS] - csum + jnp.where(last, ends, 0.0)
        tri = one_hot(iota((SPAN, SPAN), 0) <= iota((SPAN, SPAN), 1))
        dsteps = sum(nn(tri, p) for p in split(dcum, 3))
        val = small[at, DTR] + bias_ref[...]
        sg = 1.0 / (1.0 + jnp.exp(-val))
        ex = jnp.exp(jnp.minimum(val, 0.0))
        ratio = jnp.where(val < -12.0, 1.0 - 0.5 * ex, sg / jnp.maximum(softplus(val), 1e-7))
        steps = csum * ratio + dsteps * rate_ref[...] * sg
        ddt[at, :] = jnp.where(iota((SPAN, LANES), 1) < HEADS, steps, 0.0).astype(BF16)
        pos = meta.cols(t)
        around = meta.start + t * SPAN + iota((SPAN + 8, 1), 0)
        mask = (meta.seq(around + 1) == meta.seq(around)).astype(F32)
        for cs in wide_chunks(CONV_CH):
            ext = jnp.concatenate([wide[:, cs], edge[:, cs]], 0)
            total = cw_ref[0:1, cs] * ext
            for j in range(1, KERNEL):
                total = cw_ref[j : j + 1, cs] * ext + mask * pltpu.roll(total, SPAN + 7, 0)
            dact[at, cs] = total[:SPAN].astype(BF16)
        edge[...] = wide[:8, :]
        dut = duz[at, :] + nt(dact[at, :], up[:, INNER:mid]) + nt(ddt[at, :HEADS], up[:, mid:end])
        du[at, :] = dut.astype(BF16) * meta.select(pos).astype(BF16)

        @pl.when(s == 0)
        def _():
            hailed(targets)
            sum_a.begin()

        pl.when(s == 1)(sum_a.over_y)
        pl.when(s == nb - 1)(sum_a.scatter)

    each_tile(nb, scan_tile)
    wait_all(for_grads)

    def down_grad(at):
        gb[:, at()] = tn(du[...], hb[:, at()]).astype(BF16)

    def conv_grad(at):
        gb[:, at(width)] = tn(u[...], dact[:, at()]).astype(BF16)

    each_chunk(width, down_grad)
    each_chunk(CONV_CH, conv_grad)
    gb[:, width + CONV_CH :] = jnp.zeros((LOW, gb.shape[1] - width - CONV_CH), BF16)
    gb[:, width + CONV_CH : width + CONV_CH + HEADS] = tn(u[...], ddt[:, :HEADS]).astype(BF16)
    sum_b.begin()
    results = act.at[:, width : 2 * width]
    for_out = mover.go(back_h, results)
    weights.finish()
    wait_all(for_last)

    def last_tile(t):
        at = tile_rows(t)
        squares, crosses = jnp.zeros((SPAN, LANES), F32), jnp.zeros((SPAN, LANES), F32)
        for cs in wide_chunks(width):
            dh = (
                dhz[at, cs].astype(F32) + nn(dact[at, :], wv[:CONV_CH, cs]) + nn(ddt[at, :HEADS], wv[CONV_CH:, cs])
                + nn(du[at, :], down[:, cs])
            )
            g = dh * gain_ref[:, cs]
            wide[:, cs] = g
            xt = x[at, cs].astype(F32)
            sq, cross = xt * xt, g * xt
            squares = squares + sq[:, :LANES] + sq[:, LANES:]
            crosses = crosses + cross[:, :LANES] + cross[:, LANES:]
        rstd = lax.rsqrt(jnp.sum(squares, 1, keepdims=True) * (1.0 / width) + EPS)
        back = jnp.sum(crosses, 1, keepdims=True) * (1.0 / width) * rstd * rstd
        valid = meta.valid(meta.cols(t))
        for cs in wide_chunks(width):
            dx = rstd * (wide[:, cs] - x[at, cs].astype(F32) * back)
            douts = dout[at, cs].astype(F32)
            hb[at, cs] = ((douts + dx) * valid).astype(BF16)
        pl.when(t == 0)(sum_b.over_y)
        pl.when(t == nb - 2)(sum_a.gather)
        pl.when(t == nb - 1)(sum_b.scatter)

    each_tile(nb, last_tile)
    share = rows // n
    for_out.wait()
    sort_rows(where_ref[...], hb, act.at[:, 0:width])
    sum_b.gather()
    copies = [
        send(
            act.at[place(to, share), 0:width], land_h.at[place(me, share), :], s_grad.at[k - 1], r_grad.at[k - 1], ctx=to
        )
        for k, to, _ in peers("ctx")
    ]
    for c in copies:
        c.start()
    dhz[place(me, share), :] = act[place(me, share), 0:width]
    sort_rows(tok_ref[...], results, x)
    out_done = mover.go(x, out_h)
    sum_a.finish()
    sum_b.finish()
    arrived = []
    for c, (_, _, back) in zip(copies, peers("ctx")):
        c.wait_recv()
        arrived.append(mover.go(land_h.at[place(back, share), :], dhz.at[place(back, share), :]))
    wait_all(arrived)
    for c in copies:
        c.wait_send()
    tok, grads = tok_ref[...], []
    for t in range(0, rows, SPAN):
        hit = one_hot(iota((SPAN, rows), 0) + t == tok)
        for cs in wide_chunks(width):
            hb[t : t + SPAN, cs] = nn(hit, dhz[:, cs]).astype(BF16)
        grads.append(mover.go(hb.at[t : t + SPAN, :], grad_h.at[t : t + SPAN, :]))
    wait_all(grads + [out_done])


def shape(*dims, dtype=F32):
    return jax.ShapeDtypeStruct(dims, dtype)


def params(mib=60, remote=None):
    if remote is None:
        return pltpu.CompilerParams(vmem_limit_bytes=mib * MIB)
    return pltpu.CompilerParams(vmem_limit_bytes=mib * MIB, collective_id=remote, has_side_effects=True)


SMEM = pl.BlockSpec(memory_space=pltpu.SMEM)
VMEM = pl.BlockSpec(memory_space=pltpu.VMEM)
ANY = pl.BlockSpec(memory_space=pl.ANY)


def exchange_scratch(n, rows):
    owners = owners_of(n)
    w = INNER // owners
    return [
        pltpu.VMEM((n, rows, w), BF16), pltpu.VMEM((n, STATE, w), BF16), pltpu.VMEM((owners, STATE, w), BF16),
    ] + [pltpu.SemaphoreType.DMA((n - 1,))] * 4


def local(
    tokens, cotangent, order, lengths, adapter_ids, in_weight, out_weight, in_down, in_up, out_down, out_up,
    norm_gain, conv_weight, conv_bias, dt_bias, a_log, skip_gain, gate_gain,
):
    n, nf = lax.axis_size("ctx"), lax.axis_size("fsdp")
    rows, width = tokens.shape[1:]
    nb = rows // SPAN
    share = rows // n
    log_rows = rows.bit_length() - 1
    assert rows == 1 << log_rows and rows <= 1024 and rows % SPAN == 0 and nb >= 4
    assert nf % 2 == 0 and share % 16 == 0
    proj_w = in_weight.shape[1]
    rest = proj_w - INNER
    bf = lambda *dims: shape(*dims, dtype=BF16)
    vm = pltpu.VMEM
    dma = pltpu.SemaphoreType.DMA
    padded = lambda c: -(-c // (n * LANES)) * LANES * n
    owners = owners_of(n)
    ow = INNER // owners
    wt, in_down_t, out_down_t = in_weight.T, in_down.T, out_down.T
    kw, ko, ka = wt.shape[1], out_weight.shape[0], in_down_t.shape[0]
    idx = shape(1, rows, dtype=jnp.int32)
    gain, gate, cb = norm_gain[None], gate_gain[None], conv_bias[None]
    seqs = (lengths, adapter_ids)

    parts_w = len(chunks_of(proj_w - SPLIT, WEIGHT_PARTS))
    got, cot_sorted, slot, where, tok, w_in, a_in, b_in, e, skip, bias, rate = pl.pallas_call(
        partial(arrive_kernel, log_rows, share),
        in_specs=[VMEM] * 9,
        out_specs=[ANY, VMEM, VMEM, VMEM, VMEM, ANY, ANY, ANY, VMEM, VMEM, VMEM, VMEM],
        out_shape=(
            bf(rows, width), bf(rows, width), idx, idx, idx, bf(nf, proj_w - SPLIT, kw), bf(LOW, width), bf(LOW, proj_w),
            bf(2 * LANES, INNER), shape(1, INNER), shape(1, LANES), shape(1, LANES),
        ),
        scratch_shapes=[vm((rows, width), BF16)] + spread_sems(n) + gather_sems(nf, 2 + parts_w),
        compiler_params=params(remote=1),
        name="arrive",
    )(order, tokens[0], cotangent[0], wt, in_down_t, in_up, dt_bias[None], a_log[None], skip_gain[None])

    f32 = shape
    cols_a, cols_b = padded(2 * INNER + width), padded(width + rest)
    low = LOW // nf
    front_out = [
        bf(rows, width), bf(rows, width), bf(rows, LOW), bf(rows, CONV_CH), bf(rows, CONV_CH), f32(rows, SMALL),
        bf(nb, STATE, INNER), f32(nb, LANES), f32(8, CONV_CH), bf(rows, INNER), bf(rows, INNER), bf(rows, width),
        f32(rows, LOW), bf(rows, width), bf(LOW, cols_a), bf(rows, width), bf(INNER, width), bf(nf, SPLIT, kw),
    ]
    slot_buffers = [vm((n, STATE, ow), BF16), vm((n, STATE, ow), BF16), vm((owners, STATE, ow), BF16)]
    x, hb, u, act, dact, small, dl, dend, edge, dm, dxk, dhz, duz, dout, g_a, back_out, _, _ = pl.pallas_call(
        front_kernel,
        in_specs=[SMEM, SMEM] + [VMEM] * 11 + [ANY] * 8,
        out_specs=[ANY] * 7 + [VMEM, VMEM] + [ANY] * 5 + [VMEM] + [ANY] * 3,
        out_shape=front_out,
        scratch_shapes=[
            vm((rest, width), BF16), vm((LOW, width), BF16), vm((LOW, proj_w), BF16), vm((LOW, INNER), BF16),
            vm((LOW, width), BF16), vm((2 * LANES, INNER), BF16), vm((rows, width), BF16), vm((rows, width), BF16),
            vm((rows, width), BF16), vm((rows, LOW), BF16), vm((rows, LOW), BF16), vm((rows, LOW), BF16),
            vm((rows, CONV_CH), BF16), vm((rows, CONV_CH), BF16), vm((nb, STATE, INNER), F32), vm((rows, INNER), BF16),
            vm((rows, INNER), BF16), vm((nb + 1, STATE, INNER), BF16), vm((rows, width), BF16), vm((rows, width), BF16),
            vm((rows, SMALL), F32), vm((rows, LANES), F32), vm((nb, HEADS, SPAN), F32), vm((nb, 8, INNER), F32),
            vm((SPAN, INNER), F32), vm((SPAN, INNER), BF16), vm((SPAN, INNER), BF16), vm((STATE, INNER), F32),
            vm((8, INNER), F32), vm((SPAN, SPAN), F32), vm((SPAN, SPAN), F32), vm((nb + 1, 8, CONV_CH), F32),
            vm((8, CONV_CH), F32), vm((16, CONV_CH), BF16), vm((8, CONV_CH), F32), vm((8, CONV_CH), F32),
            vm((owners, STATE + 16, ow), BF16), vm((n, STATE + 16, ow), BF16), vm((n, STATE, ow), BF16),
            vm((owners, STATE, ow), BF16), vm((owners, STATE, ow), BF16),
        ] + slot_buffers + [dma((MOVES,)), dma((3, 2 * nf)), dma, dma] + spread_sems(n) + spread_sems(n) + [dma, dma]
        + [dma((n - 1,))] * 8 + gather_sems(nf, 4),
        compiler_params=params(63, remote=2),
        name="front",
    )(
        *seqs, slot, where, gain, conv_weight, cb, bias, rate, skip, gate, out_down_t, out_up, got, w_in, a_in, b_in, e,
        cot_sorted, out_weight, wt,
    )

    block_output, input_grad, g_in_down, g_in_up, g_out_down, g_out_up, _ = pl.pallas_call(
        back_kernel,
        in_specs=[SMEM, SMEM] + [VMEM] * 10 + [ANY] * 17,
        out_specs=[ANY, ANY, VMEM, VMEM, VMEM, VMEM, ANY],
        out_shape=(
            bf(rows, width), bf(rows, width), f32(low, width), f32(low, proj_w), f32(low, INNER), f32(low, width),
            bf(rows, width),
        ),
        scratch_shapes=[
            vm((rest, width), BF16), vm((LOW, width), BF16), vm((LOW, proj_w), BF16), vm((2 * LANES, INNER), BF16),
            vm((rows, CONV_CH), BF16), vm((rows, CONV_CH), BF16), vm((rows, LANES), BF16), vm((rows, SMALL), F32),
            vm((nb, STATE, INNER), BF16), vm((rows, INNER), BF16), vm((rows, INNER), BF16), vm((rows, width), BF16),
            vm((rows, LOW), BF16), vm((rows, LOW), BF16), vm((rows, LOW), F32), vm((rows, width), BF16),
            vm((rows, width), BF16), vm((rows, width), BF16), vm((LOW, cols_b), BF16),
            vm((SPAN, CONV_CH), F32), vm((SPAN, INNER), BF16), vm((SPAN, INNER), BF16), vm((8, CONV_CH), F32),
            dma((MOVES,)), dma((2 * nf,)),
        ] + [dma((n - 1,))] * 2 + reduce_scratch(n, nf, cols_a // n) + reduce_scratch(n, nf, cols_b // n),
        compiler_params=params(62, remote=3),
        name="back",
    )(
        *seqs, where, tok, gain, conv_weight, bias, rate, skip, dend, edge, g_a, w_in, a_in, b_in, e, act, dact, small, dl,
        dm, dxk, hb, u, duz, dhz, x, dout, back_out,
    )
    return block_output[None], input_grad[None], g_in_down.T, g_in_up, g_out_down.T, g_out_up


def solution(mesh):
    placed = (
        P("fsdp", "ctx", None),
        P("fsdp", "ctx", None),
        P("fsdp", None),
        P("fsdp", None),
        P("fsdp", None),
        P("fsdp", None),
        P("fsdp", None),
        P(None, "fsdp"),
        P("fsdp", None),
        P(None, "fsdp"),
        P("fsdp", None),
        P(),
        P(),
        P(),
        P(),
        P(),
        P(),
        P(),
    )
    return jax.shard_map(
        local,
        mesh=mesh,
        in_specs=placed,
        out_specs=(
            P("fsdp", "ctx", None),
            P("fsdp", "ctx", None),
            P(None, "fsdp"),
            P("fsdp", None),
            P(None, "fsdp"),
            P("fsdp", None),
        ),
        check_vma=False,
    )
```

```python
from functools import partial

import jax
import jax.numpy as jnp
from jax import lax
from jax.experimental import pallas as pl
from jax.experimental.pallas import tpu as pltpu
from jax.sharding import PartitionSpec as P

HEADS = 32
HEAD = 64
STATE = 128
KERNEL = 4
SPAN = 256
RANK = 16
ADAPTERS = 8
SEQS = 3
CONV_CH = 2304
INNER = HEADS * HEAD
LOW = ADAPTERS * RANK
LANES = 128
HALF = SPAN // 2
EPS = 1e-05
LOG2E = 1.4426950408889634

F32 = jnp.float32
BF16 = jnp.bfloat16
MIB = 1 << 20
MESH = pl.DeviceIdType.MESH


def nn(a, b):
    return jnp.dot(a, b, preferred_element_type=F32)


def nt(a, b):
    return lax.dot_general(a, b, (((1,), (1,)), ((), ())), preferred_element_type=F32)


def tn(a, b):
    return lax.dot_general(a, b, (((0,), (0,)), ((), ())), preferred_element_type=F32)


def iota(shape, dim):
    return lax.broadcasted_iota(jnp.int32, shape, dim)


def one_hot(cond):
    return jnp.where(cond, 1.0, 0.0).astype(BF16)


def split(v, parts):
    out = []
    for _ in range(parts):
        piece = v.astype(BF16)
        out.append(piece)
        v = v - piece.astype(F32)
    return out


def pairs(v):
    return jnp.concatenate(split(v, 2), 1)


class Meta:
    def __init__(self, len_ref, id_ref, rows):
        self.start = lax.axis_index("ctx") * rows
        self.ends = []
        for k in range(SEQS):
            self.ends.append(len_ref[0, k] + (self.ends[-1] if k else 0))
        self.ids = [id_ref[0, k] for k in range(SEQS)]

    def seq(self, pos):
        found = sum((pos >= end).astype(jnp.int32) for end in self.ends)
        return jnp.where(pos >= 0, found, -1)

    def valid(self, pos):
        return (pos < self.ends[-1]).astype(F32)

    def select(self, pos):
        seq = self.seq(pos)
        ids = sum(jnp.where(seq == k, self.ids[k], 0) for k in range(SEQS))
        shape = (pos.shape[0], LOW)
        return jnp.where(iota(shape, 1) // RANK == ids, 1.0, 0.0) * self.valid(pos)

    def cols(self, tile):
        return self.start + tile * SPAN + iota((SPAN, 1), 0)

    def rows(self, tile):
        return self.start + tile * SPAN + iota((1, SPAN), 1)


def sigmoid(v):
    return 0.5 * jnp.tanh(0.5 * v) + 0.5


def running_count(mask):
    width = mask.shape[1]
    tri = one_hot(iota((SPAN, SPAN), 0) <= iota((SPAN, SPAN), 1))
    pieces, before = [], jnp.zeros((mask.shape[0], 1), F32)
    for c in range(0, width, SPAN):
        part = mask[:, c : c + SPAN]
        pieces.append(nn(part.astype(BF16), tri) + before)
        before = before + jnp.sum(part, 1, keepdims=True)
    return jnp.concatenate(pieces, 1)


def two_rows(v):
    first = jnp.broadcast_to(v >> 5, (16, v.shape[1]))
    second = jnp.broadcast_to(v & 31, (16, v.shape[1]))
    row = iota((16, v.shape[1]), 0)
    return jnp.where(row == 0, first, jnp.where(row == 1, second, 0)).astype(F32).astype(BF16)


def from_two(r):
    return (r[0:1] * 32.0 + r[1:2]).astype(jnp.int32)


def invert(idx):
    width = idx.shape[1]
    values = two_rows(iota((1, width), 1))
    pieces = []
    for t in range(0, width, SPAN):
        hit = one_hot(iota((SPAN, width), 0) + t == idx)
        pieces.append(from_two(nt(values, hit)))
    return jnp.concatenate(pieces, 1)


def peers(axis):
    n, me = lax.axis_size(axis), lax.axis_index(axis)
    return [(k, lax.rem(me + k, n), lax.rem(me + n - k, n)) for k in range(1, n)]


def send(src, dst, send_sem, recv_sem, **where):
    return pltpu.make_async_remote_copy(
        src_ref=src, dst_ref=dst, send_sem=send_sem, recv_sem=recv_sem, device_id=where, device_id_type=MESH
    )


def hail(targets):
    barrier = pltpu.get_barrier_semaphore()
    for where in targets:
        pl.semaphore_signal(barrier, inc=1, device_id=where, device_id_type=MESH)


def hailed(targets):
    pl.semaphore_wait(pltpu.get_barrier_semaphore(), len(targets))


def place(which, share):
    return pl.ds(pl.multiple_of(which * share, share), share)


def sets_of(n, late):
    second = [k for k in range(1, n) if k % 8 in late]
    return [k for k in range(1, n) if k not in second], second


COT_LATE, OUT_LATE = (2, 6), (2, 6)


class Spread:
    def __init__(self, src, dst, send_sem, recv_sem, own_sem, steps):
        n, me = lax.axis_size("ctx"), lax.axis_index("ctx")
        share = src.shape[0] // n
        self.copies = [
            send(src.at[place(to, share), :], dst.at[place(me, share), :], send_sem.at[k - 1], recv_sem.at[k - 1], ctx=to)
            for k, to, _ in peers("ctx") if k in steps
        ]
        self.own = None
        if own_sem is not None:
            self.own = pltpu.make_async_copy(src.at[place(me, share), :], dst.at[place(me, share), :], own_sem)

    def begin(self):
        for c in self.copies:
            c.start()
        if self.own is not None:
            self.own.start()

    def finish(self):
        for c in self.copies:
            c.wait()
        if self.own is not None:
            self.own.wait()


def spread_sems(n):
    return [pltpu.SemaphoreType.DMA((n - 1,)), pltpu.SemaphoreType.DMA((n - 1,)), pltpu.SemaphoreType.DMA]


def ring_targets():
    n, me = lax.axis_size("ctx"), lax.axis_index("ctx")
    return [{"ctx": lax.rem(me + 1, n)}, {"ctx": lax.rem(me + n - 1, n)}]


def ctx_targets():
    return [{"ctx": p} for _, p, _ in peers("ctx")]


def fsdp_sides():
    nf, f = lax.axis_size("fsdp"), lax.axis_index("fsdp")
    sides = [lax.rem(f + 2 * k, nf) for k in range(1, nf // 2)]
    backs = [lax.rem(f + nf - 2 * k, nf) for k in range(1, nf // 2)]
    return f, f + 1 - 2 * lax.rem(f, 2), sides, backs


def fsdp_targets():
    _, pair, sides, _ = fsdp_sides()
    return [{"fsdp": p} for p in sides + [pair]]


class Gather:
    def __init__(self, pieces, sems, kept=None):
        s_y, r_y, s_c, r_c, keep = sems
        f, pair, sides, backs = fsdp_sides()
        self.across = [
            [send(src, dst(f), s_y.at[k, m], r_y.at[k, m], fsdp=side) for m, (src, dst) in enumerate(pieces)]
            for k, side in enumerate(sides)
        ]
        self.inside = [[send(src, dst(f), s_c.at[0, m], r_c.at[0, m], fsdp=pair) for m, (src, dst) in enumerate(pieces)]]
        self.inside += [
            [send(dst(back), dst(back), s_c.at[k + 1, m], r_c.at[k + 1, m], fsdp=pair) for m, (src, dst) in enumerate(pieces)]
            for k, back in enumerate(backs)
        ]
        self.keep = [pltpu.make_async_copy(src, dst(f), keep.at[m]) for m, (src, dst) in enumerate(pieces[:kept])]

    def begin(self):
        for group in self.across:
            for c in group:
                c.start()
        for c in self.inside[0] + self.keep:
            c.start()

    def relay(self, lo=0, hi=None):
        for k, group in enumerate(self.across):
            for c, forward in list(zip(group, self.inside[k + 1]))[lo:hi]:
                c.wait_recv()
                forward.start()

    def finish(self, lo=0, hi=None):
        for group in self.inside:
            for c in group[lo:hi]:
                c.wait()
        for group in self.across:
            for c in group[lo:hi]:
                c.wait_send()
        for c in self.keep[lo:hi]:
            c.wait()


def gather_sems(nf, pieces):
    dma = pltpu.SemaphoreType.DMA
    side = max(nf // 2 - 1, 1)
    return [dma((side, pieces)), dma((side, pieces)), dma((nf // 2, pieces)), dma((nf // 2, pieces)), dma((pieces,))]


def stacked(ref, h):
    return lambda which: ref.at[place(which, h), :]


def chunks_of(total, parts):
    step = -(-total // (16 * parts)) * 16
    return [(lo, min(lo + step, total)) for lo in range(0, total, step)]


WEIGHT_PARTS = 4
SPLIT = 1536


def arrive_kernel(
    log_rows, share, order_ref, x_ref, cot_ref, wt_ref, down_ref, up_ref, bias_in, log_in, skip_in,
    got_ref, cots_ref, slot_ref, where_ref, tok_ref, wall_ref, dall_ref, uall_ref, e_ref, skip_ref, bias_ref, rate_ref,
    sorted_ref, s_tok, r_tok, own_sem, *sems,
):
    n, me = lax.axis_size("ctx"), lax.axis_index("ctx")
    rows = x_ref.shape[0]
    targets = ctx_targets() + fsdp_targets()
    hail(targets)
    pieces = [(down_ref, stacked(dall_ref, down_ref.shape[0])), (up_ref, stacked(uall_ref, up_ref.shape[0]))]
    for lo, hi in chunks_of(wt_ref.shape[0] - SPLIT, WEIGHT_PARTS):
        pieces.append((wt_ref.at[SPLIT + lo : SPLIT + hi, :], lambda which, lo=lo, hi=hi: wall_ref.at[which, lo:hi, :]))
    gather = Gather(pieces, sems)

    own_order = order_ref[:, pl.ds(pl.multiple_of(me * rows, rows), rows)]
    dest = own_order >> log_rows
    hot = jnp.where(iota((max(n, 16), rows), 0) == dest, 1.0, 0.0)
    rank = jnp.sum(hot * (running_count(hot) - 1.0), axis=0, keepdims=True)
    spos = dest * share + rank.astype(jnp.int32)
    sort_rows(spos, x_ref, sorted_ref)
    hailed(targets)
    gather.begin()
    tokens = [
        send(
            sorted_ref.at[place(to, share), :], got_ref.at[place(me, share), :], s_tok.at[k - 1], r_tok.at[k - 1], ctx=to
        )
        for k, to, _ in peers("ctx")
    ]
    for c in tokens:
        c.start()
    own = pltpu.make_async_copy(sorted_ref.at[place(me, share), :], got_ref.at[place(me, share), :], own_sem)
    own.start()

    sort_rows(spos, cot_ref, cots_ref)
    by_source = [order_ref[:, s * rows : (s + 1) * rows] for s in range(n)]
    order = jnp.concatenate(by_source + [jnp.full((1, rows), -1, jnp.int32)] * (-n % 16), 0)
    mine = jnp.where(order >> log_rows == me, 1.0, 0.0)
    mark = jnp.where(mine > 0.0, running_count(mine) - 1.0, -1.0).astype(jnp.int32)
    for s in range(n):
        hit = one_hot(iota((share, rows), 0) == mark[s : s + 1, :])
        slot = by_source[s] & (rows - 1)
        slot_ref[:, s * share : (s + 1) * share] = from_two(nt(two_rows(slot), hit))
    where_ref[...] = invert(slot_ref[...])
    tok_ref[...] = invert(spos)
    e_ref[...] = one_hot((iota((2 * LANES, INNER), 0) & (LANES - 1)) == iota((2 * LANES, INNER), 1) // HEAD)
    pad = jnp.zeros((1, LANES - HEADS), F32)
    wide = jnp.broadcast_to(jnp.concatenate([skip_in[...], pad], 1), (16, LANES))
    skip_ref[...] = sum(nn(p, e_ref[:LANES, :]) for p in split(wide, 3))[0:1]
    bias_ref[...] = jnp.concatenate([bias_in[...], pad], 1)
    rate_ref[...] = jnp.concatenate([-jnp.exp(log_in[...]), pad], 1)

    gather.relay()
    gather.finish()
    for c in tokens:
        c.wait()
    own.wait()


def sort_rows(idx, src, dst):
    rows = src.shape[0]

    def body(t):
        hit = one_hot(iota((SPAN, rows), 0) + t * SPAN == idx)
        for cs in wide_chunks(src.shape[1]):
            dst[tile_rows(t), cs] = nn(hit, src[:, cs]).astype(BF16)

    each_tile(rows // SPAN, body)


def owners_of(n):
    return min(n, INNER // LANES)


def each_owner(n, which, act):
    if owners_of(n) == n:
        act()
    else:
        pl.when(which < owners_of(n))(act)


class Exchange:
    def __init__(self, parts, through, first, starts, landed, sems, reverse):
        self.parts, self.through, self.first, self.starts, self.landed = parts, through, first, starts, landed
        self.s1, self.r1, self.s2, self.r2 = sems
        self.reverse = reverse
        self.n, self.me = lax.axis_size("ctx"), lax.axis_index("ctx")

    def out(self, k, to):
        return send(self.parts.at[to], self.first.at[self.me], self.s1.at[k - 1], self.r1.at[k - 1], ctx=to)

    def back(self, k, to):
        return send(self.starts.at[to], self.landed.at[self.me], self.s2.at[k - 1], self.r2.at[k - 1], ctx=to)

    def begin(self):
        for k, to, _ in peers("ctx"):
            each_owner(self.n, to, lambda: self.out(k, to).start())

    def middle(self):
        n, me = self.n, self.me

        def act():
            self.first[me] = self.parts[me]
            for k, to, _ in peers("ctx"):
                self.out(k, to).wait_recv()

            def lap(t, running):
                j = n - 1 - t if self.reverse else t
                self.starts[j] = running.astype(BF16)
                part = self.first[j].astype(F32)
                through = self.through(self.first, j)
                return running * through + part[:STATE]

            lax.fori_loop(0, n, lap, jnp.zeros((STATE, self.first.shape[2]), F32))
            self.landed[me] = self.starts[me]
            for k, to, _ in peers("ctx"):
                self.back(k, to).start()

        each_owner(n, me, act)

    def finish(self, result):
        n, me = self.n, self.me
        for k, to, back in peers("ctx"):
            each_owner(n, back, lambda: self.back(k, to).wait_recv())
        w = self.landed.shape[2]
        for j in range(owners_of(n)):
            result[:, j * w : (j + 1) * w] = self.landed[j].astype(result.dtype)
        for k, to, _ in peers("ctx"):
            each_owner(n, to, lambda: self.out(k, to).wait_send())

        def act():
            for k, to, _ in peers("ctx"):
                self.back(k, to).wait_send()

        each_owner(n, me, act)


class Reduce:
    def __init__(self, g_ref, outs, bufs):
        self.g, self.outs = g_ref, outs
        self.pair_in, self.pair_sum, self.side_in, self.total, self.ctx_in, self.piece, self.all_in, sems = bufs
        self.n, self.me = lax.axis_size("ctx"), lax.axis_index("ctx")
        nf = lax.axis_size("fsdp")
        self.f, pair, sides, _ = fsdp_sides()
        self.core = lax.rem(self.f, 2)
        self.h, self.cw = g_ref.shape[0] // nf, g_ref.shape[1] // self.n
        self.first = [
            send(g_ref.at[place(2 * y + 1 - self.core, self.h), :], self.pair_in.at[y], sems.at[0, y], sems.at[1, y], fsdp=pair)
            for y in range(nf // 2)
        ]
        self.second = [
            send(self.pair_sum.at[side // 2], self.side_in.at[k], sems.at[2, k], sems.at[3, k], fsdp=side)
            for k, side in enumerate(sides)
        ]
        self.third = [
            send(self.total.at[to], self.ctx_in.at[k - 1], sems.at[4, k - 1], sems.at[5, k - 1], ctx=to)
            for k, to, _ in peers("ctx")
        ]
        self.fourth = [
            send(self.piece, self.all_in.at[self.me], sems.at[6, k - 1], sems.at[7, k - 1], ctx=to)
            for k, to, _ in peers("ctx")
        ]

    def parts(self, body):
        def step(j, _):
            body(pl.ds(pl.multiple_of(j * self.cw, LANES), self.cw), j)
            return 0

        lax.fori_loop(0, self.n, step, 0)

    def begin(self):
        for c in self.first:
            c.start()

    def over_y(self):
        for y, c in enumerate(self.first):
            c.wait_recv()

            def add(cs, j, y=y):
                both = self.g[place(2 * y + self.core, self.h), cs].astype(F32) + self.pair_in[y, :, cs].astype(F32)
                self.pair_sum[y, :, cs] = both.astype(BF16)

            self.parts(add)
        for c in self.second:
            c.start()

    def scatter(self):
        for c in self.second:
            c.wait_recv()

        def add(cs, j):
            mine = self.pair_sum[self.f // 2, :, cs].astype(F32)
            for k in range(len(self.second)):
                mine = mine + self.side_in[k, :, cs].astype(F32)
            self.total[j] = mine.astype(BF16)

        self.parts(add)
        for c in self.third:
            c.start()

    def gather(self):
        mine = self.total[self.me].astype(F32)
        for k, c in enumerate(self.third):
            c.wait_recv()
            mine = mine + self.ctx_in[k].astype(F32)
        self.piece[...] = mine.astype(BF16)
        for c in self.fourth:
            c.start()
        self.all_in[self.me] = self.piece[...]

    def finish(self):
        for c in self.fourth:
            c.wait_recv()

        for j in range(self.n):
            for ref, at, lo, hi in self.outs:
                a, b = max(lo, j * self.cw), min(hi, (j + 1) * self.cw)
                if a < b:
                    part = self.all_in[j, :, a - j * self.cw : b - j * self.cw]
                    ref[:, at + a - lo : at + b - lo] = part.astype(F32)
        for c in self.first + self.second + self.third + self.fourth:
            c.wait_send()


def reduce_scratch(n, nf, cw):
    half, low = nf // 2, LOW // nf
    return [
        pltpu.VMEM((half, low, n * cw), BF16), pltpu.VMEM((half, low, n * cw), BF16),
        pltpu.VMEM((max(half - 1, 1), low, n * cw), BF16), pltpu.VMEM((n, low, cw), BF16),
        pltpu.VMEM((n - 1, low, cw), BF16), pltpu.VMEM((low, cw), BF16), pltpu.VMEM((n, low, cw), BF16),
        pltpu.SemaphoreType.DMA((8, max(n, half))),
    ]


class Mover:
    def __init__(self, sems):
        self.sems, self.used = sems, 0

    def go(self, src, dst):
        c = pltpu.make_async_copy(src, dst, self.sems.at[self.used])
        self.used += 1
        c.start()
        return c

    def tiles(self, src, dst):
        return [self.go(src.at[t : t + SPAN, :], dst.at[t : t + SPAN, :]) for t in range(0, dst.shape[0], SPAN)]


MOVES = 64


def each_tile(n, body):
    def step(t, _):
        body(t)
        return 0

    lax.fori_loop(0, n, step, 0)


def tile_rows(t):
    return pl.ds(pl.multiple_of(t * SPAN, SPAN), SPAN)


def each_chunk(width, body, step=256):
    def run(c, _):
        body(lambda base=0: pl.ds(pl.multiple_of(base + c * step, LANES), step))
        return 0

    lax.fori_loop(0, width // step, run, 0)


def wide_chunks(width, step=256):
    return [slice(c, min(c + step, width)) for c in range(0, width, step)]


class Resident:
    def __init__(self, wall_ref, dst, sems, lo, hi, early=None):
        nf, _, kw = wall_ref.shape
        f = lax.axis_index("fsdp")
        self.copies, at = [], 0
        for j in range(nf):
            which = lax.rem(f + j, nf)
            cols = pl.ds(pl.multiple_of(which * kw, LANES), kw)
            if early is not None:
                own, others = early
                src = own.at[0:SPLIT, :] if j == 0 else others.at[which]
                self.copies.append(pltpu.make_async_copy(src, dst.at[0:SPLIT, cols], sems.at[nf + j]))
            start = max(lo, SPLIT)
            src = wall_ref.at[which, start - SPLIT : hi - SPLIT, :]
            self.copies.append(pltpu.make_async_copy(src, dst.at[start - lo : hi - lo, cols], sems.at[j]))

    def begin(self):
        for c in self.copies:
            c.start()

    def finish(self):
        for c in self.copies:
            c.wait()


def softplus(v):
    e = jnp.exp(-jnp.abs(v))
    series = e * (1.0 - e * (0.5 - e * (1.0 / 3.0 - 0.25 * e)))
    return jnp.maximum(v, 0.0) + jnp.where(e < 0.01, series, jnp.log(1.0 + e))


def block_mask(meta, t, transposed):
    col, row = meta.cols(t), meta.rows(t)
    return (meta.seq(col) == meta.seq(row)) & ((row >= col) if transposed else (col >= row))


def halves(x):
    lane = iota(x.shape, 1)
    zero = jnp.zeros_like(x)
    return jnp.where(lane < HEAD, x, zero), jnp.where(lane >= HEAD, x, zero)


DTR, DT, C2, WTS, RS, DCM = (slice(k * LANES, (k + 1) * LANES) for k in range(6))
SMALL = 6 * LANES


def front_kernel(
    len_ref, id_ref, slot_ref, where_ref, gain_ref, cw_ref, cb_ref, bias_ref, rate_ref, skip_ref, gate_ref, od_ref, ou_ref,
    got_h, wall_h, dall_h, uall_h, e_h, cots_h, wo_h, wt_h,
    x_h, hb_h, u_h, act_h, dact_h, small_h, dl_h, dend_ref, edge_ref, dm_h, dxk_h, dhz_h, duz_h, dout_h, g_ref,
    back_h, woall_h, wzall_h,
    wv, down, up, odown, oup, e, got, x, hb, u, v, dv, raw, act, ls, y, nout, states, sorted_ref, cot, small, reaches, c2t, carry,
    wide, prods, low, run, through, sc, dsc, tails, landed, dact0, edge, landed2, parts, first, starts, slices, parts2, first2, starts2, slices2,
    move_sems, w_sem, s_halo, r_halo, s_cot, r_cot, own_cot, s_out, r_out, own_out, s_edge, r_edge,
    s1, r1, s2, r2, s3, r3, s4, r4, *g_sems,
):
    n, me = lax.axis_size("ctx"), lax.axis_index("ctx")
    nf, f = lax.axis_size("fsdp"), lax.axis_index("fsdp")
    rows, width = x.shape
    nb = rows // SPAN
    mid = INNER + CONV_CH
    meta = Meta(len_ref, id_ref, rows)
    targets = ctx_targets() + fsdp_targets()
    landed[...] = jnp.zeros_like(landed)
    landed2[...] = jnp.zeros_like(landed2)
    hail(targets)
    mover = Mover(move_sems)
    in_got = mover.go(got_h, got)
    in_down = mover.go(dall_h, down)
    proj_w = wt_h.shape[0]
    first_weights = Resident(wall_h, wv, w_sem.at[0], INNER, proj_w)
    first_weights.begin()
    in_up = mover.go(uall_h, up)
    in_e = mover.go(e_h, e)
    halo = send(tails.at[nb, 5:8, :], landed.at[5:8, :], s_halo, r_halo, ctx=lax.rem(me + 1, n))
    soon, late = sets_of(n, COT_LATE)
    cots = Spread(cots_h, cot, s_cot, r_cot, own_cot, soon)
    late_cots = Spread(cots_h, cot, s_cot, r_cot, None, late)
    kw = wo_h.shape[0]
    pieces = [
        (od_ref, stacked(odown, od_ref.shape[0])), (ou_ref, stacked(oup, ou_ref.shape[0])),
        (wt_h.at[0:SPLIT, :], lambda which: wzall_h.at[which]), (wo_h, stacked(woall_h, kw)),
    ]
    gather = Gather(pieces, g_sems, kept=2)
    exchange = Exchange(
        parts, lambda first, j: first[j, STATE:].astype(F32)[0:1], first, starts, slices, (s1, r1, s2, r2), False
    )
    later = Exchange(
        parts2, lambda _, j: first[j, STATE:].astype(F32)[0:1], first2, starts2, slices2, (s3, r3, s4, r4), True
    )
    edge_copy = send(edge.at[0:3, :], landed2.at[0:3, :], s_edge, r_edge, ctx=lax.rem(me + n - 1, n))
    in_got.wait()
    in_down.wait()

    def norm(t):
        at = tile_rows(t)
        pos = meta.cols(t)
        hit = one_hot(iota((SPAN, rows), 0) + t * SPAN == slot_ref[...])
        valid = meta.valid(pos)
        total = jnp.zeros((SPAN, LANES), F32)
        for cs in wide_chunks(width):
            xt = nn(hit, got[:, cs]) * valid
            x[at, cs] = xt.astype(BF16)
            sq = xt * xt
            total = total + sq[:, :LANES] + sq[:, LANES:]
        rstd = lax.rsqrt(jnp.sum(total, 1, keepdims=True) * (1.0 / width) + EPS)
        for cs in wide_chunks(width):
            hb[at, cs] = (x[at, cs].astype(F32) * rstd * gain_ref[:, cs]).astype(BF16)
        u[at, :] = (nt(hb[at, :], down[...]) * meta.select(pos)).astype(BF16)

    in_up.wait()
    first_weights.finish()

    def project(s):
        t = nb - 1 - s
        norm(t)
        at = tile_rows(t)
        for cs in wide_chunks(CONV_CH):
            raw[at, cs] = (nt(hb[at, :], wv[cs, :]) + nn(u[at, :], up[:, INNER + cs.start : INNER + cs.stop])).astype(BF16)
        last = nt(hb[at, :], wv[CONV_CH:, :]) + nn(u[at, :], up[:, mid:])
        small[at, DTR] = jnp.concatenate([last, jnp.zeros((SPAN, LANES - HEADS), F32)], 1)
        tails[t + 1] = raw[pl.ds(pl.multiple_of(t * SPAN + SPAN - 16, 16), 16), :].astype(F32)[8:]

        @pl.when(t == nb - 1)
        def _():
            hailed(targets)
            pl.when(me < n - 1)(halo.start)
            gather.begin()
            cots.begin()

    each_tile(nb, project)
    done = [mover.go(x, x_h), mover.go(hb, hb_h), mover.go(u, u_h)]
    hb_out = done[1]
    in_e.wait()

    def conv(s):
        t = lax.rem(s + 1, nb)
        at = tile_rows(t)

        @pl.when(t == 0)
        def _():
            pl.when(me > 0)(halo.wait_recv)
            tails[0] = jnp.where(me > 0, landed[...], 0.0)

        pos = meta.cols(t)
        seq = meta.seq(pos)
        around = meta.start + t * SPAN - 8 + iota((SPAN + 8, 1), 0)
        mask = (meta.seq(around - 1) == meta.seq(around)).astype(F32)
        for cs in wide_chunks(CONV_CH):
            ext = jnp.concatenate([tails[t, :, cs], raw[at, cs].astype(F32)], 0)
            acc = cw_ref[0:1, cs] * ext
            for j in range(1, KERNEL):
                acc = cw_ref[j : j + 1, cs] * ext + mask * pltpu.roll(acc, 1, 0)
            acc = cb_ref[:, cs] + acc[8:]
            sg = sigmoid(acc)
            val = acc * sg
            raw[at, cs] = (sg + val * (1.0 - sg)).astype(BF16)
            act[at, cs] = val.astype(BF16)
        dt = softplus(small[at, DTR] + bias_ref[...])
        small[at, DT] = dt
        tri = one_hot(iota((SPAN, SPAN), 0) >= iota((SPAN, SPAN), 1))
        cum = sum(nn(tri, p) for p in split(dt * rate_ref[...], 3))
        start = meta.start + t * SPAN
        end_same = (seq == meta.seq(start + SPAN - 1)).astype(F32)
        passing = (seq == meta.seq(start - 1)).astype(F32)
        wts = jnp.exp(cum[SPAN - 1 : SPAN, :] - cum) * dt * end_same
        small[at, WTS] = wts
        reach = jnp.exp(cum) * passing
        reaches[at, :] = reach
        c2 = cum * LOG2E
        small[at, C2] = c2
        c2t[t] = c2.T[:HEADS]
        both = pairs(wts)
        bm = act[at, INNER : INNER + STATE]
        for cs in wide_chunks(INNER):
            weighted = (act[at, cs].astype(F32) * nn(both, e[:, cs])).astype(BF16)
            ls[t, :, cs] = tn(bm, weighted)
        ends = split(jnp.broadcast_to(reach[SPAN - 1 : SPAN, :], (16, LANES)), 3)
        carry[t] = sum(nn(p, e[:LANES, :]) for p in ends)[:8]

    each_tile(nb, conv)
    dact0[...] = raw[0:16, :]
    dact_out = mover.go(raw, dact_h)
    done += [mover.go(act, act_h)]
    ow = parts.shape[2]
    for j in range(parts.shape[0]):
        at = slice(j * ow, (j + 1) * ow)
        state, reached = ls[0, :, at], carry[0, 0:1, at]
        for b in range(1, nb):
            state = state * carry[b, 0:1, at] + ls[b, :, at]
            reached = reached * carry[b, 0:1, at]
        parts[j, :STATE] = state.astype(BF16)
        parts[j, STATE:] = jnp.broadcast_to(reached, (16, ow)).astype(BF16)
    exchange.begin()

    def mix_tile(t):
        at = tile_rows(t)
        bm, cm = act[at, INNER : INNER + STATE], act[at, INNER + STATE :]
        sc[...] = jnp.where(block_mask(meta, t, False), nt(cm, bm), 0.0)
        both = pairs(small[at, DT])
        for cs in wide_chunks(INNER):
            low[:, cs] = (act[at, cs].astype(F32) * nn(both, e[:, cs])).astype(BF16)
        c2 = small[at, C2]
        top_rows, low_rows = pl.ds(pl.multiple_of(t * SPAN, HALF), HALF), pl.ds(pl.multiple_of(t * SPAN + HALF, HALF), HALF)

        def group(g, _):
            cols = pltpu.roll(c2, LANES - 4 * g, 1)
            rws = c2t[t, pl.ds(pl.multiple_of(8 * (g // 2), 8), 8), :]
            rws = pltpu.roll(rws, 4 * lax.rem(g, 2), 0)
            for q in range(2):
                lanes = pl.ds(pl.multiple_of(g * 256 + q * 128, 128), 128)
                xa, xb = halves(low[:, lanes])
                mixes = []
                for h in (2 * q, 2 * q + 1):
                    col, row = cols[:, h : h + 1], rws[h : h + 1, :]

                    def mix(i, j):
                        decay = jnp.exp2(jnp.minimum(col[i : i + HALF] - row[:, j : j + HALF], 0.0))
                        return (sc[i : i + HALF, j : j + HALF] * decay).astype(BF16)

                    mixes.append((mix(0, 0), mix(HALF, 0), mix(HALF, HALF)))
                (a00, a10, a11), (b00, b10, b11) = mixes
                top = nn(jnp.concatenate([a00, b00], 1), jnp.concatenate([xa[:HALF], xb[:HALF]], 0))
                bot = nn(jnp.concatenate([a10, a11, b10, b11], 1), jnp.concatenate([xa, xb], 0))
                y[top_rows, lanes] = top.astype(BF16)
                y[low_rows, lanes] = bot.astype(BF16)
            return 0

        lax.fori_loop(0, HEADS // 4, group, 0)

    second_weights = Resident(wall_h, wv, w_sem.at[1], 0, INNER, (wt_h, wzall_h))

    def mix_and_load(t):
        mix_tile(t)
        pl.when(t == 0)(lambda: gather.relay(0, 3))

        @pl.when(t == nb // 2)
        def _():
            gather.finish(0, 3)
            second_weights.begin()

    each_tile(nb, mix_and_load)
    dact_out.wait()
    gather.relay(3)
    second_weights.finish()

    def gate_tile(t):
        at = tile_rows(t)
        for cs in wide_chunks(INNER):
            raw[at, cs] = (nt(hb[at, :], wv[cs, :]) + nn(u[at, :], up[:, cs])).astype(BF16)
        pl.when(t == nb // 2)(exchange.middle)

    each_tile(nb, gate_tile)
    gather.finish(3)
    out_weights = [mover.go(wo_h, wv.at[place(f, kw), :])]
    for j in range(1, nf):
        which = lax.rem(f + j, nf)
        out_weights.append(mover.go(woall_h.at[place(which, kw), :], wv.at[place(which, kw), :]))
    exchange.finish(run)
    late_cots.begin()
    for c in out_weights:
        c.wait()

    def out_tile(t):
        at = tile_rows(t)
        both = pairs(reaches[at, :])
        cm = act[at, INNER + STATE :]
        total = jnp.zeros((SPAN, LANES), F32)
        for cs in wide_chunks(INNER):
            now = run[:, cs]
            start = now.astype(BF16)
            states[t, :, cs] = start
            later = now * carry[t, 0:1, cs] + ls[t, :, cs]
            run[:, cs] = later
            mixed = y[at, cs].astype(F32) + nn(both, e[:, cs]) * nn(cm, start)
            mixed = mixed + skip_ref[:, cs] * act[at, cs].astype(F32)
            y[at, cs] = mixed.astype(BF16)
            z = raw[at, cs].astype(F32)
            gated = mixed * (z * sigmoid(z))
            wide[:, cs] = gated
            sq = gated * gated
            total = total + sq[:, :LANES] + sq[:, LANES:]
        rstd = lax.rsqrt(jnp.sum(total, 1, keepdims=True) * (1.0 / INNER) + EPS)
        small[at, RS] = jnp.broadcast_to(rstd, (SPAN, LANES))
        for cs in wide_chunks(INNER):
            nout[at, cs] = (wide[:, cs] * rstd * gate_ref[:, cs]).astype(BF16)
        pos = meta.cols(t)
        vt = (nt(nout[at, :], odown[...]) * meta.select(pos)).astype(BF16)
        v[at, :] = vt
        valid = meta.valid(pos)
        for cs in wide_chunks(width):
            branch = nn(nout[at, :], wv[:INNER, cs]) + nn(vt, oup[:, cs])
            got[at, cs] = ((x[at, cs].astype(F32) + branch) * valid).astype(BF16)

    each_tile(nb, out_tile)
    states[nb] = run[...].astype(BF16)
    sort_rows(where_ref[...], got, sorted_ref)
    soon, late = sets_of(n, OUT_LATE)
    results = Spread(sorted_ref, back_h, s_out, r_out, own_out, soon)
    late_results = Spread(sorted_ref, back_h, s_out, r_out, None, late)
    results.begin()
    cots.finish()
    late_cots.finish()
    hb_out.wait()

    def dout_tile(t):
        at = tile_rows(t)
        pos = meta.cols(t)
        hit = one_hot(iota((SPAN, rows), 0) + t * SPAN == slot_ref[...])
        valid = meta.valid(pos)
        for cs in wide_chunks(width):
            hb[at, cs] = (nn(hit, cot[:, cs]) * valid).astype(BF16)
        dv[at, :] = nt(hb[at, :], oup[...]).astype(BF16) * meta.select(pos).astype(BF16)

    each_tile(nb, dout_tile)
    done.append(mover.go(hb, dout_h))

    def down_grad(at):
        g_ref[:, at()] = tn(dv[...], nout[:, at()]).astype(BF16)

    def up_grad(at):
        g_ref[:, at(INNER)] = tn(v[...], hb[:, at()]).astype(BF16)

    each_chunk(INNER, down_grad)
    each_chunk(width, up_grad)
    run[...] = jnp.zeros_like(run)
    through[...] = jnp.ones_like(through)

    def back_tile(t):
        at = tile_rows(t)
        dout, dvt = hb[at, :], dv[at, :]
        rstd = small[at, RS][:, 0:1]
        cm = act[at, INNER + STATE :]
        total = jnp.zeros((SPAN, LANES), F32)
        for cs in wide_chunks(INNER):
            z = raw[at, cs].astype(F32)
            d = (nt(dout, wv[cs, :]) + nn(dvt, odown[:, cs])) * gate_ref[:, cs]
            wide[:, cs] = d
            g = d * (y[at, cs].astype(F32) * (z * sigmoid(z)))
            total = total + g[:, :LANES] + g[:, LANES:]
        back = jnp.sum(total, 1, keepdims=True) * (1.0 / INNER) * rstd * rstd
        both = pairs(reaches[at, :])
        dcm = jnp.zeros((SPAN, STATE), F32)
        for cs in wide_chunks(INNER):
            z = raw[at, cs].astype(F32)
            sg = sigmoid(z)
            silu = z * sg
            mixed = y[at, cs].astype(F32)
            dg = rstd * (wide[:, cs] - mixed * silu * back)
            dm = (dg * silu).astype(BF16)
            nout[at, cs] = dm
            raw[at, cs] = (dg * mixed * (sg + silu * (1.0 - sg))).astype(BF16)
            dm = dm.astype(F32)
            dp = (dm * nn(both, e[:, cs])).astype(BF16)
            prods[:, cs] = (dm * (mixed - skip_ref[:, cs] * act[at, cs].astype(F32))).astype(BF16)
            dcm = dcm + nt(dp, states[t, :, cs])
            dst = tn(cm, dp)
            ls[t, :, cs] = dst
            run[:, cs] += dst * through[0:1, cs]
        small[at, RS] = nt(prods[...], e[:LANES, :])
        small[at, DCM] = dcm
        through[...] = through[...] * carry[t]

    each_tile(nb, back_tile)
    third_weights = Resident(wall_h, wv, w_sem.at[2], 0, INNER, (wt_h, wzall_h))
    third_weights.begin()
    for j in range(parts2.shape[0]):
        parts2[j] = run[:, j * ow : (j + 1) * ow].astype(BF16)
    later.begin()
    done.append(mover.go(nout, dm_h))
    base = INNER + width

    def gate_grad(at):
        g_ref[:, at(base)] = tn(u[...], raw[:, at()]).astype(BF16)

    each_chunk(INNER, gate_grad)
    if g_ref.shape[1] > base + INNER:
        g_ref[:, base + INNER :] = jnp.zeros((LOW, g_ref.shape[1] - base - INNER), BF16)
    third_weights.finish()

    def dhz_tile(t):
        at = tile_rows(t)
        for cs in wide_chunks(width):
            cot[at, cs] = nn(raw[at, :INNER], wv[:INNER, cs]).astype(BF16)
        reaches[at, :] = nt(raw[at, :INNER], up[:, :INNER])

    each_tile(nb, dhz_tile)
    done += [mover.go(cot, dhz_h), mover.go(reaches, duz_h)]

    def mix_back_tile(t):
        at = tile_rows(t)
        bm, cm = act[at, INNER : INNER + STATE], act[at, INNER + STATE :]
        mask = block_mask(meta, t, True)
        sc[...] = jnp.where(mask, nt(bm, cm), 0.0)
        dsc[...] = jnp.zeros_like(dsc)
        both = pairs(small[at, DT])
        for cs in wide_chunks(INNER):
            dt = nn(both, e[:, cs])
            wide[:, cs] = dt
            low[:, cs] = (act[at, cs].astype(F32) * dt).astype(BF16)
        c2 = small[at, C2]
        top_rows, low_rows = pl.ds(pl.multiple_of(t * SPAN, HALF), HALF), pl.ds(pl.multiple_of(t * SPAN + HALF, HALF), HALF)

        def group(g, _):
            cols = pltpu.roll(c2, LANES - 4 * g, 1)
            rws = c2t[t, pl.ds(pl.multiple_of(8 * (g // 2), 8), 8), :]
            rws = pltpu.roll(rws, 4 * lax.rem(g, 2), 0)
            for q in range(2):
                lanes = pl.ds(pl.multiple_of(g * 256 + q * 128, 128), 128)
                dmt = nout[at, lanes]
                da, db = halves(dmt)
                mixes = []
                for h, xh in zip((2 * q, 2 * q + 1), halves(low[:, lanes])):
                    col, row = cols[:, h : h + 1], rws[h : h + 1, :]
                    top = nt(xh[:HALF], dmt)
                    bot = nt(xh[HALF:], dmt[HALF:])

                    def mix(i, j, d):
                        decay = jnp.exp2(jnp.minimum(row[:, j : j + HALF] - col[i : i + HALF], 0.0))
                        dsc[i : i + HALF, j : j + HALF] += d * decay
                        return (sc[i : i + HALF, j : j + HALF] * decay).astype(BF16)

                    mixes.append((mix(0, 0, top[:, :HALF]), mix(0, HALF, top[:, HALF:]), mix(HALF, HALF, bot)))
                (a00, a01, a11), (b00, b01, b11) = mixes
                g_top = nn(jnp.concatenate([a00, a01, b00, b01], 1), jnp.concatenate([da, db], 0))
                g_low = nn(jnp.concatenate([a11, b11], 1), jnp.concatenate([da[HALF:], db[HALF:]], 0))
                raw[top_rows, lanes] = (g_top * wide[:HALF, lanes]).astype(BF16)
                raw[low_rows, lanes] = (g_low * wide[HALF:, lanes]).astype(BF16)
            return 0

        lax.fori_loop(0, HEADS // 4, group, 0)
        ds = jnp.where(mask, dsc[...], 0.0).astype(BF16)
        small[at, DT] = nn(ds, cm)
        small[at, DCM] += tn(ds, bm)
        pl.when(t == nb // 2)(later.middle)
        pl.when(t == nb // 2)(late_results.begin)

    each_tile(nb, mix_back_tile)
    done += [mover.go(raw.at[:, 0:INNER], dxk_h), mover.go(small, small_h)]
    later.finish(run)
    for b in reversed(range(nb)):
        sums = []
        for cs in wide_chunks(INNER):
            a = run[:, cs]
            sums.append(jnp.sum(a * states[b + 1, :, cs].astype(F32), 0, keepdims=True))
            states[b + 1, :, cs] = a.astype(BF16)
            run[:, cs] = ls[b, :, cs] + carry[b, 0:1, cs] * a
        total = jnp.broadcast_to(jnp.concatenate(sums, 1), (16, INNER))
        dend_ref[b : b + 1, :] = sum(nt(p, e[:LANES, :]) for p in split(total, 3))[:1]
    done.append(mover.go(states.at[1 : nb + 1], dl_h))

    first_rows = slice(0, 16)
    both = pairs(small[first_rows, WTS])
    bm = act[first_rows, INNER : INNER + STATE]
    for cs in wide_chunks(INNER):
        w = nn(both, e[:, cs])
        dx = raw[first_rows, cs].astype(F32) + nn(bm, states[1, :, cs]) * w
        dx = dx + skip_ref[:, cs] * nout[first_rows, cs].astype(F32)
        edge[:, cs] = (dx * dact0[:, cs].astype(F32))[:8]
        low[first_rows, cs] = (act[first_rows, cs].astype(F32) * w).astype(BF16)
    bcols, ccols = slice(INNER, INNER + STATE), slice(INNER + STATE, CONV_CH)
    dbm = small[first_rows, DT] + nt(low[first_rows, :], states[1])
    edge[:, bcols] = (dbm * dact0[:, bcols].astype(F32))[:8]
    edge[:, ccols] = (small[first_rows, DCM] * dact0[:, ccols].astype(F32))[:8]
    pl.when(me > 0)(edge_copy.start)
    pl.when(me < n - 1)(halo.wait_send)
    results.finish()
    late_results.finish()
    pl.when(me > 0)(edge_copy.wait_send)
    pl.when(me < n - 1)(edge_copy.wait_recv)
    edge_ref[...] = landed2[...]
    for k, c in enumerate(done):
        if k != 1:
            c.wait()


def wait_all(copies):
    for c in copies:
        c.wait()


def back_kernel(
    len_ref, id_ref, where_ref, tok_ref, gain_ref, cw_ref, bias_ref, rate_ref, skip_ref, dend_ref, edge_ref, ga,
    wall_h, dall_h, uall_h, e_h, act_h, dact_h, small_h, dl_h, dm_h, dxk_h, hb_h, u_h, duz_h, dhz_h, x_h, dout_h, back_h,
    out_h, grad_h, indown_ref, inup_ref, outdown_ref, outup_ref, land_h,
    wv, down, up, e, act, dact, ddt, small, dl, dm, dxk, hb, u, du, duz, dhz, x, dout, gb, wide, low, prods, edge,
    move_sems, w_sem, s_grad, r_grad, *bufs,
):
    n, me = lax.axis_size("ctx"), lax.axis_index("ctx")
    rows, width = hb.shape
    nb = rows // SPAN
    mid, end = INNER + CONV_CH, INNER + CONV_CH + HEADS
    proj_w = uall_h.shape[1]
    meta = Meta(len_ref, id_ref, rows)
    targets = ctx_targets() + fsdp_targets()
    hail(targets)
    mover = Mover(move_sems)
    now = [mover.go(e_h, e), mover.go(dl_h, dl)]
    loads = {}
    for t in reversed(range(nb)):
        at = slice(t * SPAN, (t + 1) * SPAN)
        pairs_of = ((small_h, small), (act_h, act), (dxk_h, dxk), (dm_h, dm), (dact_h, dact))
        loads[t] = [mover.go(src.at[at, :], dst.at[at, :]) for src, dst in pairs_of]
        if t == nb - 1:
            now += [mover.go(uall_h, up), mover.go(duz_h, duz)]
    weights = Resident(wall_h, wv, w_sem, INNER, proj_w)
    weights.begin()
    for_grads = [mover.go(hb_h, hb), mover.go(u_h, u)]
    for_last = [mover.go(dall_h, down), mover.go(dhz_h, dhz), mover.go(x_h, x), mover.go(dout_h, dout)]
    count = len(bufs) // 2
    up_a, up_b = INNER + width, width + proj_w - INNER
    sum_a = Reduce(
        ga, [(outdown_ref, 0, 0, INNER), (outup_ref, 0, INNER, up_a), (inup_ref, 0, up_a, up_a + INNER)], bufs[:count]
    )
    sum_b = Reduce(gb, [(indown_ref, 0, 0, width), (inup_ref, INNER, width, up_b)], bufs[count:])
    edge[...] = edge_ref[...]
    wait_all(now)

    def edge_rows(k, t):
        at = pl.ds(pl.multiple_of(t * SPAN, SPAN), k)
        both = pairs(small[at, WTS])
        bm = act[at, INNER : INNER + STATE]
        for cs in wide_chunks(INNER):
            w = nn(both, e[:, cs])
            xs = act[at, cs].astype(F32)
            dx = dxk[at, cs].astype(F32) + nn(bm, dl[t, :, cs]) * w
            prods[:k, cs] = (xs * dx).astype(BF16)
            dx = dx + skip_ref[:, cs] * dm[at, cs].astype(F32)
            wide[:k, cs] = dx * dact[at, cs].astype(F32)
            low[:k, cs] = (xs * w).astype(BF16)
        bcols, ccols = slice(INNER, INNER + STATE), slice(INNER + STATE, CONV_CH)
        wide[:k, bcols] = (small[at, DT] + nt(low[:k, :], dl[t])) * dact[at, bcols].astype(F32)
        wide[:k, ccols] = small[at, DCM] * dact[at, ccols].astype(F32)

    def scan_tile(s):
        t = nb - 1 - s
        at = tile_rows(t)
        pl.when(s == 0)(lambda: wait_all(loads[nb - 1]))
        for k in range(1, nb):
            pl.when(s == k)(lambda k=k: wait_all(loads[nb - 1 - k]))
        ends = dend_ref[pl.ds(t, 1), :]
        edge_rows(SPAN, t)
        csum = nt(prods[...], e[:LANES, :])
        last = iota((SPAN, 1), 0) == SPAN - 1
        dcum = small[at, RS] - csum + jnp.where(last, ends, 0.0)
        tri = one_hot(iota((SPAN, SPAN), 0) <= iota((SPAN, SPAN), 1))
        dsteps = sum(nn(tri, p) for p in split(dcum, 3))
        val = small[at, DTR] + bias_ref[...]
        sg = 1.0 / (1.0 + jnp.exp(-val))
        ex = jnp.exp(jnp.minimum(val, 0.0))
        ratio = jnp.where(val < -12.0, 1.0 - 0.5 * ex, sg / jnp.maximum(softplus(val), 1e-7))
        steps = csum * ratio + dsteps * rate_ref[...] * sg
        ddt[at, :] = jnp.where(iota((SPAN, LANES), 1) < HEADS, steps, 0.0).astype(BF16)
        pos = meta.cols(t)
        around = meta.start + t * SPAN + iota((SPAN + 8, 1), 0)
        mask = (meta.seq(around + 1) == meta.seq(around)).astype(F32)
        for cs in wide_chunks(CONV_CH):
            ext = jnp.concatenate([wide[:, cs], edge[:, cs]], 0)
            total = cw_ref[0:1, cs] * ext
            for j in range(1, KERNEL):
                total = cw_ref[j : j + 1, cs] * ext + mask * pltpu.roll(total, SPAN + 7, 0)
            dact[at, cs] = total[:SPAN].astype(BF16)
        edge[...] = wide[:8, :]
        dut = duz[at, :] + nt(dact[at, :], up[:, INNER:mid]) + nt(ddt[at, :HEADS], up[:, mid:end])
        du[at, :] = dut.astype(BF16) * meta.select(pos).astype(BF16)

        @pl.when(s == 0)
        def _():
            hailed(targets)
            sum_a.begin()

        pl.when(s == 1)(sum_a.over_y)
        pl.when(s == nb - 1)(sum_a.scatter)

    each_tile(nb, scan_tile)
    wait_all(for_grads)

    def down_grad(at):
        gb[:, at()] = tn(du[...], hb[:, at()]).astype(BF16)

    def conv_grad(at):
        gb[:, at(width)] = tn(u[...], dact[:, at()]).astype(BF16)

    each_chunk(width, down_grad)
    each_chunk(CONV_CH, conv_grad)
    gb[:, width + CONV_CH :] = jnp.zeros((LOW, gb.shape[1] - width - CONV_CH), BF16)
    gb[:, width + CONV_CH : width + CONV_CH + HEADS] = tn(u[...], ddt[:, :HEADS]).astype(BF16)
    sum_b.begin()
    results = act.at[:, width : 2 * width]
    for_out = mover.go(back_h, results)
    weights.finish()
    wait_all(for_last)

    def last_tile(t):
        at = tile_rows(t)
        squares, crosses = jnp.zeros((SPAN, LANES), F32), jnp.zeros((SPAN, LANES), F32)
        for cs in wide_chunks(width):
            dh = (
                dhz[at, cs].astype(F32) + nn(dact[at, :], wv[:CONV_CH, cs]) + nn(ddt[at, :HEADS], wv[CONV_CH:, cs])
                + nn(du[at, :], down[:, cs])
            )
            g = dh * gain_ref[:, cs]
            wide[:, cs] = g
            xt = x[at, cs].astype(F32)
            sq, cross = xt * xt, g * xt
            squares = squares + sq[:, :LANES] + sq[:, LANES:]
            crosses = crosses + cross[:, :LANES] + cross[:, LANES:]
        rstd = lax.rsqrt(jnp.sum(squares, 1, keepdims=True) * (1.0 / width) + EPS)
        back = jnp.sum(crosses, 1, keepdims=True) * (1.0 / width) * rstd * rstd
        valid = meta.valid(meta.cols(t))
        for cs in wide_chunks(width):
            dx = rstd * (wide[:, cs] - x[at, cs].astype(F32) * back)
            douts = dout[at, cs].astype(F32)
            hb[at, cs] = ((douts + dx) * valid).astype(BF16)
        pl.when(t == 0)(sum_b.over_y)
        pl.when(t == nb - 2)(sum_a.gather)
        pl.when(t == nb - 1)(sum_b.scatter)

    each_tile(nb, last_tile)
    share = rows // n
    for_out.wait()
    sort_rows(where_ref[...], hb, act.at[:, 0:width])
    sum_b.gather()
    copies = [
        send(
            act.at[place(to, share), 0:width], land_h.at[place(me, share), :], s_grad.at[k - 1], r_grad.at[k - 1], ctx=to
        )
        for k, to, _ in peers("ctx")
    ]
    for c in copies:
        c.start()
    dhz[place(me, share), :] = act[place(me, share), 0:width]
    sort_rows(tok_ref[...], results, x)
    out_done = mover.go(x, out_h)
    sum_a.finish()
    sum_b.finish()
    arrived = []
    for c, (_, _, back) in zip(copies, peers("ctx")):
        c.wait_recv()
        arrived.append(mover.go(land_h.at[place(back, share), :], dhz.at[place(back, share), :]))
    wait_all(arrived)
    for c in copies:
        c.wait_send()
    tok, grads = tok_ref[...], []
    for t in range(0, rows, SPAN):
        hit = one_hot(iota((SPAN, rows), 0) + t == tok)
        for cs in wide_chunks(width):
            hb[t : t + SPAN, cs] = nn(hit, dhz[:, cs]).astype(BF16)
        grads.append(mover.go(hb.at[t : t + SPAN, :], grad_h.at[t : t + SPAN, :]))
    wait_all(grads + [out_done])


def shape(*dims, dtype=F32):
    return jax.ShapeDtypeStruct(dims, dtype)


def params(mib=60, remote=None):
    if remote is None:
        return pltpu.CompilerParams(vmem_limit_bytes=mib * MIB)
    return pltpu.CompilerParams(vmem_limit_bytes=mib * MIB, collective_id=remote, has_side_effects=True)


SMEM = pl.BlockSpec(memory_space=pltpu.SMEM)
VMEM = pl.BlockSpec(memory_space=pltpu.VMEM)
ANY = pl.BlockSpec(memory_space=pl.ANY)


def exchange_scratch(n, rows):
    owners = owners_of(n)
    w = INNER // owners
    return [
        pltpu.VMEM((n, rows, w), BF16), pltpu.VMEM((n, STATE, w), BF16), pltpu.VMEM((owners, STATE, w), BF16),
    ] + [pltpu.SemaphoreType.DMA((n - 1,))] * 4


def local(
    tokens, cotangent, order, lengths, adapter_ids, in_weight, out_weight, in_down, in_up, out_down, out_up,
    norm_gain, conv_weight, conv_bias, dt_bias, a_log, skip_gain, gate_gain,
):
    n, nf = lax.axis_size("ctx"), lax.axis_size("fsdp")
    rows, width = tokens.shape[1:]
    nb = rows // SPAN
    share = rows // n
    log_rows = rows.bit_length() - 1
    assert rows == 1 << log_rows and rows <= 1024 and rows % SPAN == 0 and nb >= 4
    assert nf % 2 == 0 and share % 16 == 0
    proj_w = in_weight.shape[1]
    rest = proj_w - INNER
    bf = lambda *dims: shape(*dims, dtype=BF16)
    vm = pltpu.VMEM
    dma = pltpu.SemaphoreType.DMA
    padded = lambda c: -(-c // (n * LANES)) * LANES * n
    owners = owners_of(n)
    ow = INNER // owners
    wt, in_down_t, out_down_t = in_weight.T, in_down.T, out_down.T
    kw, ko, ka = wt.shape[1], out_weight.shape[0], in_down_t.shape[0]
    idx = shape(1, rows, dtype=jnp.int32)
    gain, gate, cb = norm_gain[None], gate_gain[None], conv_bias[None]
    seqs = (lengths, adapter_ids)

    parts_w = len(chunks_of(proj_w - SPLIT, WEIGHT_PARTS))
    got, cot_sorted, slot, where, tok, w_in, a_in, b_in, e, skip, bias, rate = pl.pallas_call(
        partial(arrive_kernel, log_rows, share),
        in_specs=[VMEM] * 9,
        out_specs=[ANY, VMEM, VMEM, VMEM, VMEM, ANY, ANY, ANY, VMEM, VMEM, VMEM, VMEM],
        out_shape=(
            bf(rows, width), bf(rows, width), idx, idx, idx, bf(nf, proj_w - SPLIT, kw), bf(LOW, width), bf(LOW, proj_w),
            bf(2 * LANES, INNER), shape(1, INNER), shape(1, LANES), shape(1, LANES),
        ),
        scratch_shapes=[vm((rows, width), BF16)] + spread_sems(n) + gather_sems(nf, 2 + parts_w),
        compiler_params=params(remote=1),
        name="arrive",
    )(order, tokens[0], cotangent[0], wt, in_down_t, in_up, dt_bias[None], a_log[None], skip_gain[None])

    f32 = shape
    cols_a, cols_b = padded(2 * INNER + width), padded(width + rest)
    low = LOW // nf
    front_out = [
        bf(rows, width), bf(rows, width), bf(rows, LOW), bf(rows, CONV_CH), bf(rows, CONV_CH), f32(rows, SMALL),
        bf(nb, STATE, INNER), f32(nb, LANES), f32(8, CONV_CH), bf(rows, INNER), bf(rows, INNER), bf(rows, width),
        f32(rows, LOW), bf(rows, width), bf(LOW, cols_a), bf(rows, width), bf(INNER, width), bf(nf, SPLIT, kw),
    ]
    slot_buffers = [vm((n, STATE, ow), BF16), vm((n, STATE, ow), BF16), vm((owners, STATE, ow), BF16)]
    x, hb, u, act, dact, small, dl, dend, edge, dm, dxk, dhz, duz, dout, g_a, back_out, _, _ = pl.pallas_call(
        front_kernel,
        in_specs=[SMEM, SMEM] + [VMEM] * 11 + [ANY] * 8,
        out_specs=[ANY] * 7 + [VMEM, VMEM] + [ANY] * 5 + [VMEM] + [ANY] * 3,
        out_shape=front_out,
        scratch_shapes=[
            vm((rest, width), BF16), vm((LOW, width), BF16), vm((LOW, proj_w), BF16), vm((LOW, INNER), BF16),
            vm((LOW, width), BF16), vm((2 * LANES, INNER), BF16), vm((rows, width), BF16), vm((rows, width), BF16),
            vm((rows, width), BF16), vm((rows, LOW), BF16), vm((rows, LOW), BF16), vm((rows, LOW), BF16),
            vm((rows, CONV_CH), BF16), vm((rows, CONV_CH), BF16), vm((nb, STATE, INNER), F32), vm((rows, INNER), BF16),
            vm((rows, INNER), BF16), vm((nb + 1, STATE, INNER), BF16), vm((rows, width), BF16), vm((rows, width), BF16),
            vm((rows, SMALL), F32), vm((rows, LANES), F32), vm((nb, HEADS, SPAN), F32), vm((nb, 8, INNER), F32),
            vm((SPAN, INNER), F32), vm((SPAN, INNER), BF16), vm((SPAN, INNER), BF16), vm((STATE, INNER), F32),
            vm((8, INNER), F32), vm((SPAN, SPAN), F32), vm((SPAN, SPAN), F32), vm((nb + 1, 8, CONV_CH), F32),
            vm((8, CONV_CH), F32), vm((16, CONV_CH), BF16), vm((8, CONV_CH), F32), vm((8, CONV_CH), F32),
            vm((owners, STATE + 16, ow), BF16), vm((n, STATE + 16, ow), BF16), vm((n, STATE, ow), BF16),
            vm((owners, STATE, ow), BF16), vm((owners, STATE, ow), BF16),
        ] + slot_buffers + [dma((MOVES,)), dma((3, 2 * nf)), dma, dma] + spread_sems(n) + spread_sems(n) + [dma, dma]
        + [dma((n - 1,))] * 8 + gather_sems(nf, 4),
        compiler_params=params(63, remote=2),
        name="front",
    )(
        *seqs, slot, where, gain, conv_weight, cb, bias, rate, skip, gate, out_down_t, out_up, got, w_in, a_in, b_in, e,
        cot_sorted, out_weight, wt,
    )

    block_output, input_grad, g_in_down, g_in_up, g_out_down, g_out_up, _ = pl.pallas_call(
        back_kernel,
        in_specs=[SMEM, SMEM] + [VMEM] * 10 + [ANY] * 17,
        out_specs=[ANY, ANY, VMEM, VMEM, VMEM, VMEM, ANY],
        out_shape=(
            bf(rows, width), bf(rows, width), f32(low, width), f32(low, proj_w), f32(low, INNER), f32(low, width),
            bf(rows, width),
        ),
        scratch_shapes=[
            vm((rest, width), BF16), vm((LOW, width), BF16), vm((LOW, proj_w), BF16), vm((2 * LANES, INNER), BF16),
            vm((rows, CONV_CH), BF16), vm((rows, CONV_CH), BF16), vm((rows, LANES), BF16), vm((rows, SMALL), F32),
            vm((nb, STATE, INNER), BF16), vm((rows, INNER), BF16), vm((rows, INNER), BF16), vm((rows, width), BF16),
            vm((rows, LOW), BF16), vm((rows, LOW), BF16), vm((rows, LOW), F32), vm((rows, width), BF16),
            vm((rows, width), BF16), vm((rows, width), BF16), vm((LOW, cols_b), BF16),
            vm((SPAN, CONV_CH), F32), vm((SPAN, INNER), BF16), vm((SPAN, INNER), BF16), vm((8, CONV_CH), F32),
            dma((MOVES,)), dma((2 * nf,)),
        ] + [dma((n - 1,))] * 2 + reduce_scratch(n, nf, cols_a // n) + reduce_scratch(n, nf, cols_b // n),
        compiler_params=params(62, remote=3),
        name="back",
    )(
        *seqs, where, tok, gain, conv_weight, bias, rate, skip, dend, edge, g_a, w_in, a_in, b_in, e, act, dact, small, dl,
        dm, dxk, hb, u, duz, dhz, x, dout, back_out,
    )
    return block_output[None], input_grad[None], g_in_down.T, g_in_up, g_out_down.T, g_out_up


def solution(mesh):
    placed = (
        P("fsdp", "ctx", None),
        P("fsdp", "ctx", None),
        P("fsdp", None),
        P("fsdp", None),
        P("fsdp", None),
        P("fsdp", None),
        P("fsdp", None),
        P(None, "fsdp"),
        P("fsdp", None),
        P(None, "fsdp"),
        P("fsdp", None),
        P(),
        P(),
        P(),
        P(),
        P(),
        P(),
        P(),
    )
    return jax.shard_map(
        local,
        mesh=mesh,
        in_specs=placed,
        out_specs=(
            P("fsdp", "ctx", None),
            P("fsdp", "ctx", None),
            P(None, "fsdp"),
            P("fsdp", None),
            P(None, "fsdp"),
            P("fsdp", None),
        ),
        check_vma=False,
    )
```

```python
from functools import partial

import jax
import jax.numpy as jnp
from jax import lax
from jax.experimental import pallas as pl
from jax.experimental.pallas import tpu as pltpu
from jax.sharding import PartitionSpec as P

HEADS = 32
HEAD = 64
STATE = 128
KERNEL = 4
SPAN = 256
RANK = 16
ADAPTERS = 8
SEQS = 3
CONV_CH = 2304
INNER = HEADS * HEAD
LOW = ADAPTERS * RANK
LANES = 128
HALF = SPAN // 2
EPS = 1e-05
LOG2E = 1.4426950408889634

F32 = jnp.float32
BF16 = jnp.bfloat16
MIB = 1 << 20
MESH = pl.DeviceIdType.MESH


def nn(a, b):
    return jnp.dot(a, b, preferred_element_type=F32)


def nt(a, b):
    return lax.dot_general(a, b, (((1,), (1,)), ((), ())), preferred_element_type=F32)


def tn(a, b):
    return lax.dot_general(a, b, (((0,), (0,)), ((), ())), preferred_element_type=F32)


def iota(shape, dim):
    return lax.broadcasted_iota(jnp.int32, shape, dim)


def one_hot(cond):
    return jnp.where(cond, 1.0, 0.0).astype(BF16)


def split(v, parts):
    out = []
    for _ in range(parts):
        piece = v.astype(BF16)
        out.append(piece)
        v = v - piece.astype(F32)
    return out


def pairs(v):
    return jnp.concatenate(split(v, 2), 1)


class Meta:
    def __init__(self, len_ref, id_ref, rows):
        self.start = lax.axis_index("ctx") * rows
        self.ends = []
        for k in range(SEQS):
            self.ends.append(len_ref[0, k] + (self.ends[-1] if k else 0))
        self.ids = [id_ref[0, k] for k in range(SEQS)]

    def seq(self, pos):
        found = sum((pos >= end).astype(jnp.int32) for end in self.ends)
        return jnp.where(pos >= 0, found, -1)

    def valid(self, pos):
        return (pos < self.ends[-1]).astype(F32)

    def select(self, pos):
        seq = self.seq(pos)
        ids = sum(jnp.where(seq == k, self.ids[k], 0) for k in range(SEQS))
        shape = (pos.shape[0], LOW)
        return jnp.where(iota(shape, 1) // RANK == ids, 1.0, 0.0) * self.valid(pos)

    def cols(self, tile):
        return self.start + tile * SPAN + iota((SPAN, 1), 0)

    def rows(self, tile):
        return self.start + tile * SPAN + iota((1, SPAN), 1)


def sigmoid(v):
    return 0.5 * jnp.tanh(0.5 * v) + 0.5


def running_count(mask):
    width = mask.shape[1]
    tri = one_hot(iota((SPAN, SPAN), 0) <= iota((SPAN, SPAN), 1))
    pieces, before = [], jnp.zeros((mask.shape[0], 1), F32)
    for c in range(0, width, SPAN):
        part = mask[:, c : c + SPAN]
        pieces.append(nn(part.astype(BF16), tri) + before)
        before = before + jnp.sum(part, 1, keepdims=True)
    return jnp.concatenate(pieces, 1)


def two_rows(v):
    first = jnp.broadcast_to(v >> 5, (16, v.shape[1]))
    second = jnp.broadcast_to(v & 31, (16, v.shape[1]))
    row = iota((16, v.shape[1]), 0)
    return jnp.where(row == 0, first, jnp.where(row == 1, second, 0)).astype(F32).astype(BF16)


def from_two(r):
    return (r[0:1] * 32.0 + r[1:2]).astype(jnp.int32)


def invert(idx):
    width = idx.shape[1]
    values = two_rows(iota((1, width), 1))
    pieces = []
    for t in range(0, width, SPAN):
        hit = one_hot(iota((SPAN, width), 0) + t == idx)
        pieces.append(from_two(nt(values, hit)))
    return jnp.concatenate(pieces, 1)


def peers(axis):
    n, me = lax.axis_size(axis), lax.axis_index(axis)
    return [(k, lax.rem(me + k, n), lax.rem(me + n - k, n)) for k in range(1, n)]


def send(src, dst, send_sem, recv_sem, **where):
    return pltpu.make_async_remote_copy(
        src_ref=src, dst_ref=dst, send_sem=send_sem, recv_sem=recv_sem, device_id=where, device_id_type=MESH
    )


def hail(targets):
    barrier = pltpu.get_barrier_semaphore()
    for where in targets:
        pl.semaphore_signal(barrier, inc=1, device_id=where, device_id_type=MESH)


def hailed(targets):
    pl.semaphore_wait(pltpu.get_barrier_semaphore(), len(targets))


def place(which, share):
    return pl.ds(pl.multiple_of(which * share, share), share)


def sets_of(n, late):
    second = [k for k in range(1, n) if k % 8 in late]
    return [k for k in range(1, n) if k not in second], second


COT_LATE, OUT_LATE = (2, 6), (2, 6)


class Spread:
    def __init__(self, src, dst, send_sem, recv_sem, own_sem, steps):
        n, me = lax.axis_size("ctx"), lax.axis_index("ctx")
        share = src.shape[0] // n
        self.copies = [
            send(src.at[place(to, share), :], dst.at[place(me, share), :], send_sem.at[k - 1], recv_sem.at[k - 1], ctx=to)
            for k, to, _ in peers("ctx") if k in steps
        ]
        self.own = None
        if own_sem is not None:
            self.own = pltpu.make_async_copy(src.at[place(me, share), :], dst.at[place(me, share), :], own_sem)

    def begin(self):
        for c in self.copies:
            c.start()
        if self.own is not None:
            self.own.start()

    def finish(self):
        for c in self.copies:
            c.wait()
        if self.own is not None:
            self.own.wait()


def spread_sems(n):
    return [pltpu.SemaphoreType.DMA((n - 1,)), pltpu.SemaphoreType.DMA((n - 1,)), pltpu.SemaphoreType.DMA]


def ring_targets():
    n, me = lax.axis_size("ctx"), lax.axis_index("ctx")
    return [{"ctx": lax.rem(me + 1, n)}, {"ctx": lax.rem(me + n - 1, n)}]


def ctx_targets():
    return [{"ctx": p} for _, p, _ in peers("ctx")]


def fsdp_sides():
    nf, f = lax.axis_size("fsdp"), lax.axis_index("fsdp")
    sides = [lax.rem(f + 2 * k, nf) for k in range(1, nf // 2)]
    backs = [lax.rem(f + nf - 2 * k, nf) for k in range(1, nf // 2)]
    return f, f + 1 - 2 * lax.rem(f, 2), sides, backs


def fsdp_targets():
    _, pair, sides, _ = fsdp_sides()
    return [{"fsdp": p} for p in sides + [pair]]


class Gather:
    def __init__(self, pieces, sems, kept=None):
        s_y, r_y, s_c, r_c, keep = sems
        f, pair, sides, backs = fsdp_sides()
        self.across = [
            [send(src, dst(f), s_y.at[k, m], r_y.at[k, m], fsdp=side) for m, (src, dst) in enumerate(pieces)]
            for k, side in enumerate(sides)
        ]
        self.inside = [[send(src, dst(f), s_c.at[0, m], r_c.at[0, m], fsdp=pair) for m, (src, dst) in enumerate(pieces)]]
        self.inside += [
            [send(dst(back), dst(back), s_c.at[k + 1, m], r_c.at[k + 1, m], fsdp=pair) for m, (src, dst) in enumerate(pieces)]
            for k, back in enumerate(backs)
        ]
        self.keep = [pltpu.make_async_copy(src, dst(f), keep.at[m]) for m, (src, dst) in enumerate(pieces[:kept])]

    def begin(self):
        for group in self.across:
            for c in group:
                c.start()
        for c in self.inside[0] + self.keep:
            c.start()

    def relay(self, lo=0, hi=None):
        for k, group in enumerate(self.across):
            for c, forward in list(zip(group, self.inside[k + 1]))[lo:hi]:
                c.wait_recv()
                forward.start()

    def finish(self, lo=0, hi=None):
        for group in self.inside:
            for c in group[lo:hi]:
                c.wait()
        for group in self.across:
            for c in group[lo:hi]:
                c.wait_send()
        for c in self.keep[lo:hi]:
            c.wait()


def gather_sems(nf, pieces):
    dma = pltpu.SemaphoreType.DMA
    side = max(nf // 2 - 1, 1)
    return [dma((side, pieces)), dma((side, pieces)), dma((nf // 2, pieces)), dma((nf // 2, pieces)), dma((pieces,))]


def stacked(ref, h):
    return lambda which: ref.at[place(which, h), :]


def chunks_of(total, parts):
    step = -(-total // (16 * parts)) * 16
    return [(lo, min(lo + step, total)) for lo in range(0, total, step)]


WEIGHT_PARTS = 4
SPLIT = 1536


def arrive_kernel(
    log_rows, share, order_ref, x_ref, cot_ref, wt_ref, down_ref, up_ref, bias_in, log_in, skip_in,
    got_ref, cots_ref, slot_ref, where_ref, tok_ref, wall_ref, dall_ref, uall_ref, e_ref, skip_ref, bias_ref, rate_ref,
    sorted_ref, s_tok, r_tok, own_sem, *sems,
):
    n, me = lax.axis_size("ctx"), lax.axis_index("ctx")
    rows = x_ref.shape[0]
    targets = ctx_targets() + fsdp_targets()
    hail(targets)
    pieces = [(down_ref, stacked(dall_ref, down_ref.shape[0])), (up_ref, stacked(uall_ref, up_ref.shape[0]))]
    for lo, hi in chunks_of(wt_ref.shape[0] - SPLIT, WEIGHT_PARTS):
        pieces.append((wt_ref.at[SPLIT + lo : SPLIT + hi, :], lambda which, lo=lo, hi=hi: wall_ref.at[which, lo:hi, :]))
    gather = Gather(pieces, sems)

    own_order = order_ref[:, pl.ds(pl.multiple_of(me * rows, rows), rows)]
    dest = own_order >> log_rows
    hot = jnp.where(iota((max(n, 16), rows), 0) == dest, 1.0, 0.0)
    rank = jnp.sum(hot * (running_count(hot) - 1.0), axis=0, keepdims=True)
    spos = dest * share + rank.astype(jnp.int32)
    sort_rows(spos, x_ref, sorted_ref)
    hailed(targets)
    gather.begin()
    tokens = [
        send(
            sorted_ref.at[place(to, share), :], got_ref.at[place(me, share), :], s_tok.at[k - 1], r_tok.at[k - 1], ctx=to
        )
        for k, to, _ in peers("ctx")
    ]
    for c in tokens:
        c.start()
    own = pltpu.make_async_copy(sorted_ref.at[place(me, share), :], got_ref.at[place(me, share), :], own_sem)
    own.start()

    sort_rows(spos, cot_ref, cots_ref)
    by_source = [order_ref[:, s * rows : (s + 1) * rows] for s in range(n)]
    order = jnp.concatenate(by_source + [jnp.full((1, rows), -1, jnp.int32)] * (-n % 16), 0)
    mine = jnp.where(order >> log_rows == me, 1.0, 0.0)
    mark = jnp.where(mine > 0.0, running_count(mine) - 1.0, -1.0).astype(jnp.int32)
    for s in range(n):
        hit = one_hot(iota((share, rows), 0) == mark[s : s + 1, :])
        slot = by_source[s] & (rows - 1)
        slot_ref[:, s * share : (s + 1) * share] = from_two(nt(two_rows(slot), hit))
    where_ref[...] = invert(slot_ref[...])
    tok_ref[...] = invert(spos)
    e_ref[...] = one_hot((iota((2 * LANES, INNER), 0) & (LANES - 1)) == iota((2 * LANES, INNER), 1) // HEAD)
    pad = jnp.zeros((1, LANES - HEADS), F32)
    wide = jnp.broadcast_to(jnp.concatenate([skip_in[...], pad], 1), (16, LANES))
    skip_ref[...] = sum(nn(p, e_ref[:LANES, :]) for p in split(wide, 3))[0:1]
    bias_ref[...] = jnp.concatenate([bias_in[...], pad], 1)
    rate_ref[...] = jnp.concatenate([-jnp.exp(log_in[...]), pad], 1)

    gather.relay()
    gather.finish()
    for c in tokens:
        c.wait()
    own.wait()


def sort_rows(idx, src, dst):
    rows = src.shape[0]

    def body(t):
        hit = one_hot(iota((SPAN, rows), 0) + t * SPAN == idx)
        for cs in wide_chunks(src.shape[1]):
            dst[tile_rows(t), cs] = nn(hit, src[:, cs]).astype(BF16)

    each_tile(rows // SPAN, body)


def owners_of(n):
    return min(n, INNER // LANES)


def each_owner(n, which, act):
    if owners_of(n) == n:
        act()
    else:
        pl.when(which < owners_of(n))(act)


class Exchange:
    def __init__(self, parts, through, first, starts, landed, sems, reverse):
        self.parts, self.through, self.first, self.starts, self.landed = parts, through, first, starts, landed
        self.s1, self.r1, self.s2, self.r2 = sems
        self.reverse = reverse
        self.n, self.me = lax.axis_size("ctx"), lax.axis_index("ctx")

    def out(self, k, to):
        return send(self.parts.at[to], self.first.at[self.me], self.s1.at[k - 1], self.r1.at[k - 1], ctx=to)

    def back(self, k, to):
        return send(self.starts.at[to], self.landed.at[self.me], self.s2.at[k - 1], self.r2.at[k - 1], ctx=to)

    def begin(self):
        for k, to, _ in peers("ctx"):
            each_owner(self.n, to, lambda: self.out(k, to).start())

    def middle(self):
        n, me = self.n, self.me

        def act():
            self.first[me] = self.parts[me]
            for k, to, _ in peers("ctx"):
                self.out(k, to).wait_recv()

            def lap(t, running):
                j = n - 1 - t if self.reverse else t
                self.starts[j] = running.astype(BF16)
                part = self.first[j].astype(F32)
                through = self.through(self.first, j)
                return running * through + part[:STATE]

            lax.fori_loop(0, n, lap, jnp.zeros((STATE, self.first.shape[2]), F32))
            self.landed[me] = self.starts[me]
            for k, to, _ in peers("ctx"):
                self.back(k, to).start()

        each_owner(n, me, act)

    def finish(self, result):
        n, me = self.n, self.me
        for k, to, back in peers("ctx"):
            each_owner(n, back, lambda: self.back(k, to).wait_recv())
        w = self.landed.shape[2]
        for j in range(owners_of(n)):
            result[:, j * w : (j + 1) * w] = self.landed[j].astype(result.dtype)
        for k, to, _ in peers("ctx"):
            each_owner(n, to, lambda: self.out(k, to).wait_send())

        def act():
            for k, to, _ in peers("ctx"):
                self.back(k, to).wait_send()

        each_owner(n, me, act)


class Reduce:
    def __init__(self, g_ref, outs, bufs):
        self.g, self.outs = g_ref, outs
        self.pair_in, self.pair_sum, self.side_in, self.total, self.ctx_in, self.piece, self.all_in, sems = bufs
        self.n, self.me = lax.axis_size("ctx"), lax.axis_index("ctx")
        nf = lax.axis_size("fsdp")
        self.f, pair, sides, _ = fsdp_sides()
        self.core = lax.rem(self.f, 2)
        self.h, self.cw = g_ref.shape[0] // nf, g_ref.shape[1] // self.n
        self.first = [
            send(g_ref.at[place(2 * y + 1 - self.core, self.h), :], self.pair_in.at[y], sems.at[0, y], sems.at[1, y], fsdp=pair)
            for y in range(nf // 2)
        ]
        self.second = [
            send(self.pair_sum.at[side // 2], self.side_in.at[k], sems.at[2, k], sems.at[3, k], fsdp=side)
            for k, side in enumerate(sides)
        ]
        self.third = [
            send(self.total.at[to], self.ctx_in.at[k - 1], sems.at[4, k - 1], sems.at[5, k - 1], ctx=to)
            for k, to, _ in peers("ctx")
        ]
        self.fourth = [
            send(self.piece, self.all_in.at[self.me], sems.at[6, k - 1], sems.at[7, k - 1], ctx=to)
            for k, to, _ in peers("ctx")
        ]

    def parts(self, body):
        def step(j, _):
            body(pl.ds(pl.multiple_of(j * self.cw, LANES), self.cw), j)
            return 0

        lax.fori_loop(0, self.n, step, 0)

    def begin(self):
        for c in self.first:
            c.start()

    def over_y(self):
        for y, c in enumerate(self.first):
            c.wait_recv()

            def add(cs, j, y=y):
                both = self.g[place(2 * y + self.core, self.h), cs].astype(F32) + self.pair_in[y, :, cs].astype(F32)
                self.pair_sum[y, :, cs] = both.astype(BF16)

            self.parts(add)
        for c in self.second:
            c.start()

    def scatter(self):
        for c in self.second:
            c.wait_recv()

        def add(cs, j):
            mine = self.pair_sum[self.f // 2, :, cs].astype(F32)
            for k in range(len(self.second)):
                mine = mine + self.side_in[k, :, cs].astype(F32)
            self.total[j] = mine.astype(BF16)

        self.parts(add)
        for c in self.third:
            c.start()

    def gather(self):
        mine = self.total[self.me].astype(F32)
        for k, c in enumerate(self.third):
            c.wait_recv()
            mine = mine + self.ctx_in[k].astype(F32)
        self.piece[...] = mine.astype(BF16)
        for c in self.fourth:
            c.start()
        self.all_in[self.me] = self.piece[...]

    def finish(self):
        for c in self.fourth:
            c.wait_recv()

        for j in range(self.n):
            for ref, at, lo, hi in self.outs:
                a, b = max(lo, j * self.cw), min(hi, (j + 1) * self.cw)
                if a < b:
                    part = self.all_in[j, :, a - j * self.cw : b - j * self.cw]
                    ref[:, at + a - lo : at + b - lo] = part.astype(F32)
        for c in self.first + self.second + self.third + self.fourth:
            c.wait_send()


def reduce_scratch(n, nf, cw):
    half, low = nf // 2, LOW // nf
    return [
        pltpu.VMEM((half, low, n * cw), BF16), pltpu.VMEM((half, low, n * cw), BF16),
        pltpu.VMEM((max(half - 1, 1), low, n * cw), BF16), pltpu.VMEM((n, low, cw), BF16),
        pltpu.VMEM((n - 1, low, cw), BF16), pltpu.VMEM((low, cw), BF16), pltpu.VMEM((n, low, cw), BF16),
        pltpu.SemaphoreType.DMA((8, max(n, half))),
    ]


class Mover:
    def __init__(self, sems):
        self.sems, self.used = sems, 0

    def go(self, src, dst):
        c = pltpu.make_async_copy(src, dst, self.sems.at[self.used])
        self.used += 1
        c.start()
        return c

    def tiles(self, src, dst):
        return [self.go(src.at[t : t + SPAN, :], dst.at[t : t + SPAN, :]) for t in range(0, dst.shape[0], SPAN)]


MOVES = 96


def each_tile(n, body):
    def step(t, _):
        body(t)
        return 0

    lax.fori_loop(0, n, step, 0)


def tile_rows(t):
    return pl.ds(pl.multiple_of(t * SPAN, SPAN), SPAN)


def each_chunk(width, body, step=256):
    def run(c, _):
        body(lambda base=0: pl.ds(pl.multiple_of(base + c * step, LANES), step))
        return 0

    lax.fori_loop(0, width // step, run, 0)


def wide_chunks(width, step=256):
    return [slice(c, min(c + step, width)) for c in range(0, width, step)]


class Resident:
    def __init__(self, wall_ref, dst, sems, lo, hi, early=None):
        nf, _, kw = wall_ref.shape
        f = lax.axis_index("fsdp")
        self.copies, at = [], 0
        for j in range(nf):
            which = lax.rem(f + j, nf)
            cols = pl.ds(pl.multiple_of(which * kw, LANES), kw)
            if early is not None:
                own, others = early
                src = own.at[0:SPLIT, :] if j == 0 else others.at[which]
                self.copies.append(pltpu.make_async_copy(src, dst.at[0:SPLIT, cols], sems.at[nf + j]))
            start = max(lo, SPLIT)
            src = wall_ref.at[which, start - SPLIT : hi - SPLIT, :]
            self.copies.append(pltpu.make_async_copy(src, dst.at[start - lo : hi - lo, cols], sems.at[j]))

    def begin(self):
        for c in self.copies:
            c.start()

    def finish(self):
        for c in self.copies:
            c.wait()


def softplus(v):
    e = jnp.exp(-jnp.abs(v))
    series = e * (1.0 - e * (0.5 - e * (1.0 / 3.0 - 0.25 * e)))
    return jnp.maximum(v, 0.0) + jnp.where(e < 0.01, series, jnp.log(1.0 + e))


def block_mask(meta, t, transposed):
    col, row = meta.cols(t), meta.rows(t)
    return (meta.seq(col) == meta.seq(row)) & ((row >= col) if transposed else (col >= row))


def halves(x):
    lane = iota(x.shape, 1)
    zero = jnp.zeros_like(x)
    return jnp.where(lane < HEAD, x, zero), jnp.where(lane >= HEAD, x, zero)


DTR, DT, C2, WTS, RS, DCM = (slice(k * LANES, (k + 1) * LANES) for k in range(6))
SMALL = 6 * LANES


def front_kernel(
    len_ref, id_ref, slot_ref, where_ref, gain_ref, cw_ref, cb_ref, bias_ref, rate_ref, skip_ref, gate_ref, od_ref, ou_ref,
    got_h, wall_h, dall_h, uall_h, e_h, cots_h, wo_h, wt_h,
    x_h, hb_h, u_h, act_h, dact_h, small_h, dl_h, dend_ref, edge_ref, dm_h, dxk_h, dhz_h, duz_h, dout_h, g_ref,
    back_h, woall_h, wzall_h,
    wv, down, up, odown, oup, e, got, x, hb, u, v, dv, raw, act, ls, y, nout, states, sorted_ref, cot, small, reaches, c2t, carry,
    wide, prods, low, run, through, sc, dsc, tails, landed, dact0, edge, landed2, parts, first, starts, slices, parts2, first2, starts2, slices2,
    move_sems, w_sem, s_halo, r_halo, s_cot, r_cot, own_cot, s_out, r_out, own_out, s_edge, r_edge,
    s1, r1, s2, r2, s3, r3, s4, r4, *g_sems,
):
    n, me = lax.axis_size("ctx"), lax.axis_index("ctx")
    nf, f = lax.axis_size("fsdp"), lax.axis_index("fsdp")
    rows, width = x.shape
    nb = rows // SPAN
    mid = INNER + CONV_CH
    meta = Meta(len_ref, id_ref, rows)
    targets = ctx_targets() + fsdp_targets()
    landed[...] = jnp.zeros_like(landed)
    landed2[...] = jnp.zeros_like(landed2)
    hail(targets)
    mover = Mover(move_sems)
    in_got = mover.go(got_h, got)
    in_down = mover.go(dall_h, down)
    proj_w = wt_h.shape[0]
    first_weights = Resident(wall_h, wv, w_sem.at[0], INNER, proj_w)
    first_weights.begin()
    in_up = mover.go(uall_h, up)
    in_e = mover.go(e_h, e)
    halo = send(tails.at[nb, 5:8, :], landed.at[5:8, :], s_halo, r_halo, ctx=lax.rem(me + 1, n))
    soon, late = sets_of(n, COT_LATE)
    cots = Spread(cots_h, cot, s_cot, r_cot, own_cot, soon)
    late_cots = Spread(cots_h, cot, s_cot, r_cot, None, late)
    kw = wo_h.shape[0]
    pieces = [
        (od_ref, stacked(odown, od_ref.shape[0])), (ou_ref, stacked(oup, ou_ref.shape[0])),
        (wt_h.at[0:SPLIT, :], lambda which: wzall_h.at[which]), (wo_h, stacked(woall_h, kw)),
    ]
    gather = Gather(pieces, g_sems, kept=2)
    exchange = Exchange(
        parts, lambda first, j: first[j, STATE:].astype(F32)[0:1], first, starts, slices, (s1, r1, s2, r2), False
    )
    later = Exchange(
        parts2, lambda _, j: first[j, STATE:].astype(F32)[0:1], first2, starts2, slices2, (s3, r3, s4, r4), True
    )
    edge_copy = send(edge.at[0:3, :], landed2.at[0:3, :], s_edge, r_edge, ctx=lax.rem(me + n - 1, n))
    in_got.wait()
    in_down.wait()

    def norm(t):
        at = tile_rows(t)
        pos = meta.cols(t)
        hit = one_hot(iota((SPAN, rows), 0) + t * SPAN == slot_ref[...])
        valid = meta.valid(pos)
        total = jnp.zeros((SPAN, LANES), F32)
        for cs in wide_chunks(width):
            xt = nn(hit, got[:, cs]) * valid
            x[at, cs] = xt.astype(BF16)
            sq = xt * xt
            total = total + sq[:, :LANES] + sq[:, LANES:]
        rstd = lax.rsqrt(jnp.sum(total, 1, keepdims=True) * (1.0 / width) + EPS)
        for cs in wide_chunks(width):
            hb[at, cs] = (x[at, cs].astype(F32) * rstd * gain_ref[:, cs]).astype(BF16)
        u[at, :] = (nt(hb[at, :], down[...]) * meta.select(pos)).astype(BF16)

    in_up.wait()
    first_weights.finish()

    def project(s):
        t = nb - 1 - s
        norm(t)
        at = tile_rows(t)
        for cs in wide_chunks(CONV_CH):
            raw[at, cs] = (nt(hb[at, :], wv[cs, :]) + nn(u[at, :], up[:, INNER + cs.start : INNER + cs.stop])).astype(BF16)
        last = nt(hb[at, :], wv[CONV_CH:, :]) + nn(u[at, :], up[:, mid:])
        small[at, DTR] = jnp.concatenate([last, jnp.zeros((SPAN, LANES - HEADS), F32)], 1)
        tails[t + 1] = raw[pl.ds(pl.multiple_of(t * SPAN + SPAN - 16, 16), 16), :].astype(F32)[8:]

        @pl.when(t == nb - 1)
        def _():
            hailed(targets)
            pl.when(me < n - 1)(halo.start)
            gather.begin()
            cots.begin()

    each_tile(nb, project)
    done = [mover.go(x, x_h), mover.go(hb, hb_h), mover.go(u, u_h)]
    hb_out = done[1]
    in_e.wait()

    def conv(s):
        t = lax.rem(s + 1, nb)
        at = tile_rows(t)

        @pl.when(t == 0)
        def _():
            pl.when(me > 0)(halo.wait_recv)
            tails[0] = jnp.where(me > 0, landed[...], 0.0)

        pos = meta.cols(t)
        seq = meta.seq(pos)
        around = meta.start + t * SPAN - 8 + iota((SPAN + 8, 1), 0)
        mask = (meta.seq(around - 1) == meta.seq(around)).astype(F32)
        for cs in wide_chunks(CONV_CH):
            ext = jnp.concatenate([tails[t, :, cs], raw[at, cs].astype(F32)], 0)
            acc = cw_ref[0:1, cs] * ext
            for j in range(1, KERNEL):
                acc = cw_ref[j : j + 1, cs] * ext + mask * pltpu.roll(acc, 1, 0)
            acc = cb_ref[:, cs] + acc[8:]
            sg = sigmoid(acc)
            val = acc * sg
            raw[at, cs] = (sg + val * (1.0 - sg)).astype(BF16)
            act[at, cs] = val.astype(BF16)
        dt = softplus(small[at, DTR] + bias_ref[...])
        small[at, DT] = dt
        tri = one_hot(iota((SPAN, SPAN), 0) >= iota((SPAN, SPAN), 1))
        cum = sum(nn(tri, p) for p in split(dt * rate_ref[...], 3))
        start = meta.start + t * SPAN
        end_same = (seq == meta.seq(start + SPAN - 1)).astype(F32)
        passing = (seq == meta.seq(start - 1)).astype(F32)
        wts = jnp.exp(cum[SPAN - 1 : SPAN, :] - cum) * dt * end_same
        small[at, WTS] = wts
        reach = jnp.exp(cum) * passing
        reaches[at, :] = reach
        c2 = cum * LOG2E
        small[at, C2] = c2
        c2t[t] = c2.T[:HEADS]
        both = pairs(wts)
        bm = act[at, INNER : INNER + STATE]
        for cs in wide_chunks(INNER):
            weighted = (act[at, cs].astype(F32) * nn(both, e[:, cs])).astype(BF16)
            ls[t, :, cs] = tn(bm, weighted)
        ends = split(jnp.broadcast_to(reach[SPAN - 1 : SPAN, :], (16, LANES)), 3)
        carry[t] = sum(nn(p, e[:LANES, :]) for p in ends)[:8]

    each_tile(nb, conv)
    dact0[...] = raw[0:16, :]
    dact_out = mover.go(raw, dact_h)
    done += [mover.go(act, act_h)]
    ow = parts.shape[2]
    for j in range(parts.shape[0]):
        at = slice(j * ow, (j + 1) * ow)
        state, reached = ls[0, :, at], carry[0, 0:1, at]
        for b in range(1, nb):
            state = state * carry[b, 0:1, at] + ls[b, :, at]
            reached = reached * carry[b, 0:1, at]
        parts[j, :STATE] = state.astype(BF16)
        parts[j, STATE:] = jnp.broadcast_to(reached, (16, ow)).astype(BF16)
    exchange.begin()

    def mix_tile(t):
        at = tile_rows(t)
        bm, cm = act[at, INNER : INNER + STATE], act[at, INNER + STATE :]
        sc[...] = jnp.where(block_mask(meta, t, False), nt(cm, bm), 0.0)
        both = pairs(small[at, DT])
        for cs in wide_chunks(INNER):
            low[:, cs] = (act[at, cs].astype(F32) * nn(both, e[:, cs])).astype(BF16)
        c2 = small[at, C2]
        top_rows, low_rows = pl.ds(pl.multiple_of(t * SPAN, HALF), HALF), pl.ds(pl.multiple_of(t * SPAN + HALF, HALF), HALF)

        def group(g, _):
            cols = pltpu.roll(c2, LANES - 4 * g, 1)
            rws = c2t[t, pl.ds(pl.multiple_of(8 * (g // 2), 8), 8), :]
            rws = pltpu.roll(rws, 4 * lax.rem(g, 2), 0)
            for q in range(2):
                lanes = pl.ds(pl.multiple_of(g * 256 + q * 128, 128), 128)
                xa, xb = halves(low[:, lanes])
                mixes = []
                for h in (2 * q, 2 * q + 1):
                    col, row = cols[:, h : h + 1], rws[h : h + 1, :]

                    def mix(i, j):
                        decay = jnp.exp2(jnp.minimum(col[i : i + HALF] - row[:, j : j + HALF], 0.0))
                        return (sc[i : i + HALF, j : j + HALF] * decay).astype(BF16)

                    mixes.append((mix(0, 0), mix(HALF, 0), mix(HALF, HALF)))
                (a00, a10, a11), (b00, b10, b11) = mixes
                top = nn(jnp.concatenate([a00, b00], 1), jnp.concatenate([xa[:HALF], xb[:HALF]], 0))
                bot = nn(jnp.concatenate([a10, a11, b10, b11], 1), jnp.concatenate([xa, xb], 0))
                y[top_rows, lanes] = top.astype(BF16)
                y[low_rows, lanes] = bot.astype(BF16)
            return 0

        lax.fori_loop(0, HEADS // 4, group, 0)

    second_weights = Resident(wall_h, wv, w_sem.at[1], 0, INNER, (wt_h, wzall_h))

    def mix_and_load(t):
        mix_tile(t)
        pl.when(t == 0)(lambda: gather.relay(0, 3))

        @pl.when(t == nb // 2)
        def _():
            gather.finish(0, 3)
            second_weights.begin()

    each_tile(nb, mix_and_load)
    dact_out.wait()
    gather.relay(3)
    second_weights.finish()

    def gate_tile(t):
        at = tile_rows(t)
        for cs in wide_chunks(INNER):
            raw[at, cs] = (nt(hb[at, :], wv[cs, :]) + nn(u[at, :], up[:, cs])).astype(BF16)
        pl.when(t == nb // 2)(exchange.middle)

    each_tile(nb, gate_tile)
    gather.finish(3)
    out_weights = [mover.go(wo_h, wv.at[place(f, kw), :])]
    for j in range(1, nf):
        which = lax.rem(f + j, nf)
        out_weights.append(mover.go(woall_h.at[place(which, kw), :], wv.at[place(which, kw), :]))
    exchange.finish(run)
    late_cots.begin()
    for c in out_weights:
        c.wait()

    def out_tile(t):
        at = tile_rows(t)
        both = pairs(reaches[at, :])
        cm = act[at, INNER + STATE :]
        total = jnp.zeros((SPAN, LANES), F32)
        for cs in wide_chunks(INNER):
            now = run[:, cs]
            start = now.astype(BF16)
            states[t, :, cs] = start
            later = now * carry[t, 0:1, cs] + ls[t, :, cs]
            run[:, cs] = later
            mixed = y[at, cs].astype(F32) + nn(both, e[:, cs]) * nn(cm, start)
            mixed = mixed + skip_ref[:, cs] * act[at, cs].astype(F32)
            y[at, cs] = mixed.astype(BF16)
            z = raw[at, cs].astype(F32)
            gated = mixed * (z * sigmoid(z))
            wide[:, cs] = gated
            sq = gated * gated
            total = total + sq[:, :LANES] + sq[:, LANES:]
        rstd = lax.rsqrt(jnp.sum(total, 1, keepdims=True) * (1.0 / INNER) + EPS)
        small[at, RS] = jnp.broadcast_to(rstd, (SPAN, LANES))
        for cs in wide_chunks(INNER):
            nout[at, cs] = (wide[:, cs] * rstd * gate_ref[:, cs]).astype(BF16)
        pos = meta.cols(t)
        vt = (nt(nout[at, :], odown[...]) * meta.select(pos)).astype(BF16)
        v[at, :] = vt
        valid = meta.valid(pos)
        for cs in wide_chunks(width):
            branch = nn(nout[at, :], wv[:INNER, cs]) + nn(vt, oup[:, cs])
            got[at, cs] = ((x[at, cs].astype(F32) + branch) * valid).astype(BF16)

    each_tile(nb, out_tile)
    states[nb] = run[...].astype(BF16)
    sort_rows(where_ref[...], got, sorted_ref)
    soon, late = sets_of(n, OUT_LATE)
    results = Spread(sorted_ref, back_h, s_out, r_out, own_out, soon)
    late_results = Spread(sorted_ref, back_h, s_out, r_out, None, late)
    results.begin()
    cots.finish()
    late_cots.finish()
    hb_out.wait()

    def dout_tile(t):
        at = tile_rows(t)
        pos = meta.cols(t)
        hit = one_hot(iota((SPAN, rows), 0) + t * SPAN == slot_ref[...])
        valid = meta.valid(pos)
        for cs in wide_chunks(width):
            hb[at, cs] = (nn(hit, cot[:, cs]) * valid).astype(BF16)
        dv[at, :] = nt(hb[at, :], oup[...]).astype(BF16) * meta.select(pos).astype(BF16)

    each_tile(nb, dout_tile)
    done.append(mover.go(hb, dout_h))

    def down_grad(at):
        g_ref[:, at()] = tn(dv[...], nout[:, at()]).astype(BF16)

    def up_grad(at):
        g_ref[:, at(INNER)] = tn(v[...], hb[:, at()]).astype(BF16)

    each_chunk(INNER, down_grad)
    each_chunk(width, up_grad)
    run[...] = jnp.zeros_like(run)
    through[...] = jnp.ones_like(through)

    def back_tile(t):
        at = tile_rows(t)
        dout, dvt = hb[at, :], dv[at, :]
        rstd = small[at, RS][:, 0:1]
        cm = act[at, INNER + STATE :]
        total = jnp.zeros((SPAN, LANES), F32)
        for cs in wide_chunks(INNER):
            z = raw[at, cs].astype(F32)
            d = (nt(dout, wv[cs, :]) + nn(dvt, odown[:, cs])) * gate_ref[:, cs]
            wide[:, cs] = d
            g = d * (y[at, cs].astype(F32) * (z * sigmoid(z)))
            total = total + g[:, :LANES] + g[:, LANES:]
        back = jnp.sum(total, 1, keepdims=True) * (1.0 / INNER) * rstd * rstd
        both = pairs(reaches[at, :])
        dcm = jnp.zeros((SPAN, STATE), F32)
        for cs in wide_chunks(INNER):
            z = raw[at, cs].astype(F32)
            sg = sigmoid(z)
            silu = z * sg
            mixed = y[at, cs].astype(F32)
            dg = rstd * (wide[:, cs] - mixed * silu * back)
            dm = (dg * silu).astype(BF16)
            nout[at, cs] = dm
            raw[at, cs] = (dg * mixed * (sg + silu * (1.0 - sg))).astype(BF16)
            dm = dm.astype(F32)
            dp = (dm * nn(both, e[:, cs])).astype(BF16)
            prods[:, cs] = (dm * (mixed - skip_ref[:, cs] * act[at, cs].astype(F32))).astype(BF16)
            dcm = dcm + nt(dp, states[t, :, cs])
            dst = tn(cm, dp)
            ls[t, :, cs] = dst
            run[:, cs] += dst * through[0:1, cs]
        small[at, RS] = nt(prods[...], e[:LANES, :])
        small[at, DCM] = dcm
        through[...] = through[...] * carry[t]

    each_tile(nb, back_tile)
    third_weights = Resident(wall_h, wv, w_sem.at[2], 0, INNER, (wt_h, wzall_h))
    third_weights.begin()
    for j in range(parts2.shape[0]):
        parts2[j] = run[:, j * ow : (j + 1) * ow].astype(BF16)
    later.begin()
    done.append(mover.go(nout, dm_h))
    base = INNER + width

    def gate_grad(at):
        g_ref[:, at(base)] = tn(u[...], raw[:, at()]).astype(BF16)

    each_chunk(INNER, gate_grad)
    if g_ref.shape[1] > base + INNER:
        g_ref[:, base + INNER :] = jnp.zeros((LOW, g_ref.shape[1] - base - INNER), BF16)
    third_weights.finish()

    def dhz_tile(t):
        at = tile_rows(t)
        for cs in wide_chunks(width):
            cot[at, cs] = nn(raw[at, :INNER], wv[:INNER, cs]).astype(BF16)
        reaches[at, :] = nt(raw[at, :INNER], up[:, :INNER])

    each_tile(nb, dhz_tile)
    done += [mover.go(cot, dhz_h), mover.go(reaches, duz_h)]

    def mix_back_tile(t):
        at = tile_rows(t)
        bm, cm = act[at, INNER : INNER + STATE], act[at, INNER + STATE :]
        mask = block_mask(meta, t, True)
        sc[...] = jnp.where(mask, nt(bm, cm), 0.0)
        dsc[...] = jnp.zeros_like(dsc)
        both = pairs(small[at, DT])
        for cs in wide_chunks(INNER):
            dt = nn(both, e[:, cs])
            wide[:, cs] = dt
            low[:, cs] = (act[at, cs].astype(F32) * dt).astype(BF16)
        c2 = small[at, C2]
        top_rows, low_rows = pl.ds(pl.multiple_of(t * SPAN, HALF), HALF), pl.ds(pl.multiple_of(t * SPAN + HALF, HALF), HALF)

        def group(g, _):
            cols = pltpu.roll(c2, LANES - 4 * g, 1)
            rws = c2t[t, pl.ds(pl.multiple_of(8 * (g // 2), 8), 8), :]
            rws = pltpu.roll(rws, 4 * lax.rem(g, 2), 0)
            for q in range(2):
                lanes = pl.ds(pl.multiple_of(g * 256 + q * 128, 128), 128)
                dmt = nout[at, lanes]
                da, db = halves(dmt)
                mixes = []
                for h, xh in zip((2 * q, 2 * q + 1), halves(low[:, lanes])):
                    col, row = cols[:, h : h + 1], rws[h : h + 1, :]
                    top = nt(xh[:HALF], dmt)
                    bot = nt(xh[HALF:], dmt[HALF:])

                    def mix(i, j, d):
                        decay = jnp.exp2(jnp.minimum(row[:, j : j + HALF] - col[i : i + HALF], 0.0))
                        dsc[i : i + HALF, j : j + HALF] += d * decay
                        return (sc[i : i + HALF, j : j + HALF] * decay).astype(BF16)

                    mixes.append((mix(0, 0, top[:, :HALF]), mix(0, HALF, top[:, HALF:]), mix(HALF, HALF, bot)))
                (a00, a01, a11), (b00, b01, b11) = mixes
                g_top = nn(jnp.concatenate([a00, a01, b00, b01], 1), jnp.concatenate([da, db], 0))
                g_low = nn(jnp.concatenate([a11, b11], 1), jnp.concatenate([da[HALF:], db[HALF:]], 0))
                raw[top_rows, lanes] = (g_top * wide[:HALF, lanes]).astype(BF16)
                raw[low_rows, lanes] = (g_low * wide[HALF:, lanes]).astype(BF16)
            return 0

        lax.fori_loop(0, HEADS // 4, group, 0)
        ds = jnp.where(mask, dsc[...], 0.0).astype(BF16)
        small[at, DT] = nn(ds, cm)
        small[at, DCM] += tn(ds, bm)
        pl.when(t == nb // 2)(later.middle)
        pl.when(t == nb // 2)(late_results.begin)

    each_tile(nb, mix_back_tile)
    done += [mover.go(raw.at[:, 0:INNER], dxk_h), mover.go(small, small_h)]
    later.finish(run)
    for b in reversed(range(nb)):
        sums = []
        for cs in wide_chunks(INNER):
            a = run[:, cs]
            sums.append(jnp.sum(a * states[b + 1, :, cs].astype(F32), 0, keepdims=True))
            states[b + 1, :, cs] = a.astype(BF16)
            run[:, cs] = ls[b, :, cs] + carry[b, 0:1, cs] * a
        total = jnp.broadcast_to(jnp.concatenate(sums, 1), (16, INNER))
        dend_ref[b : b + 1, :] = sum(nt(p, e[:LANES, :]) for p in split(total, 3))[:1]
    done.append(mover.go(states.at[1 : nb + 1], dl_h))

    first_rows = slice(0, 16)
    both = pairs(small[first_rows, WTS])
    bm = act[first_rows, INNER : INNER + STATE]
    for cs in wide_chunks(INNER):
        w = nn(both, e[:, cs])
        dx = raw[first_rows, cs].astype(F32) + nn(bm, states[1, :, cs]) * w
        dx = dx + skip_ref[:, cs] * nout[first_rows, cs].astype(F32)
        edge[:, cs] = (dx * dact0[:, cs].astype(F32))[:8]
        low[first_rows, cs] = (act[first_rows, cs].astype(F32) * w).astype(BF16)
    bcols, ccols = slice(INNER, INNER + STATE), slice(INNER + STATE, CONV_CH)
    dbm = small[first_rows, DT] + nt(low[first_rows, :], states[1])
    edge[:, bcols] = (dbm * dact0[:, bcols].astype(F32))[:8]
    edge[:, ccols] = (small[first_rows, DCM] * dact0[:, ccols].astype(F32))[:8]
    pl.when(me > 0)(edge_copy.start)
    pl.when(me < n - 1)(halo.wait_send)
    results.finish()
    late_results.finish()
    pl.when(me > 0)(edge_copy.wait_send)
    pl.when(me < n - 1)(edge_copy.wait_recv)
    edge_ref[...] = landed2[...]
    for k, c in enumerate(done):
        if k != 1:
            c.wait()


def wait_all(copies):
    for c in copies:
        c.wait()


def back_kernel(
    len_ref, id_ref, where_ref, tok_ref, gain_ref, cw_ref, bias_ref, rate_ref, skip_ref, dend_ref, edge_ref, ga,
    wall_h, dall_h, uall_h, e_h, act_h, dact_h, small_h, dl_h, dm_h, dxk_h, hb_h, u_h, duz_h, dhz_h, x_h, dout_h, back_h,
    out_h, grad_h, indown_ref, inup_ref, outdown_ref, outup_ref, land_h,
    wv, down, up, e, act, dact, ddt, small, dl, dm, dxk, hb, u, du, duz, dhz, x, dout, gb, wide, low, prods, edge,
    move_sems, w_sem, s_grad, r_grad, *bufs,
):
    n, me = lax.axis_size("ctx"), lax.axis_index("ctx")
    rows, width = hb.shape
    nb = rows // SPAN
    mid, end = INNER + CONV_CH, INNER + CONV_CH + HEADS
    proj_w = uall_h.shape[1]
    meta = Meta(len_ref, id_ref, rows)
    targets = ctx_targets() + fsdp_targets()
    hail(targets)
    mover = Mover(move_sems)
    now = [mover.go(e_h, e), mover.go(dl_h, dl)]
    loads = {}
    for t in reversed(range(nb)):
        at = slice(t * SPAN, (t + 1) * SPAN)
        pairs_of = ((small_h, small), (act_h, act), (dxk_h, dxk), (dm_h, dm), (dact_h, dact))
        loads[t] = [mover.go(src.at[at, :], dst.at[at, :]) for src, dst in pairs_of]
        if t == nb - 1:
            now += [mover.go(uall_h, up), mover.go(duz_h, duz)]
    weights = Resident(wall_h, wv, w_sem, INNER, proj_w)
    weights.begin()
    for_grads = [mover.go(hb_h, hb), mover.go(u_h, u)]
    for_last = [mover.go(dall_h, down), mover.go(dhz_h, dhz), mover.go(x_h, x), mover.go(dout_h, dout)]
    count = len(bufs) // 2
    up_a, up_b = INNER + width, width + proj_w - INNER
    sum_a = Reduce(
        ga, [(outdown_ref, 0, 0, INNER), (outup_ref, 0, INNER, up_a), (inup_ref, 0, up_a, up_a + INNER)], bufs[:count]
    )
    sum_b = Reduce(gb, [(indown_ref, 0, 0, width), (inup_ref, INNER, width, up_b)], bufs[count:])
    edge[...] = edge_ref[...]
    wait_all(now)

    def edge_rows(k, t):
        at = pl.ds(pl.multiple_of(t * SPAN, SPAN), k)
        both = pairs(small[at, WTS])
        bm = act[at, INNER : INNER + STATE]
        for cs in wide_chunks(INNER):
            w = nn(both, e[:, cs])
            xs = act[at, cs].astype(F32)
            dx = dxk[at, cs].astype(F32) + nn(bm, dl[t, :, cs]) * w
            prods[:k, cs] = (xs * dx).astype(BF16)
            dx = dx + skip_ref[:, cs] * dm[at, cs].astype(F32)
            wide[:k, cs] = dx * dact[at, cs].astype(F32)
            low[:k, cs] = (xs * w).astype(BF16)
        bcols, ccols = slice(INNER, INNER + STATE), slice(INNER + STATE, CONV_CH)
        wide[:k, bcols] = (small[at, DT] + nt(low[:k, :], dl[t])) * dact[at, bcols].astype(F32)
        wide[:k, ccols] = small[at, DCM] * dact[at, ccols].astype(F32)

    def scan_tile(s):
        t = nb - 1 - s
        at = tile_rows(t)
        pl.when(s == 0)(lambda: wait_all(loads[nb - 1]))
        for k in range(1, nb):
            pl.when(s == k)(lambda k=k: wait_all(loads[nb - 1 - k]))
        ends = dend_ref[pl.ds(t, 1), :]
        edge_rows(SPAN, t)
        csum = nt(prods[...], e[:LANES, :])
        last = iota((SPAN, 1), 0) == SPAN - 1
        dcum = small[at, RS] - csum + jnp.where(last, ends, 0.0)
        tri = one_hot(iota((SPAN, SPAN), 0) <= iota((SPAN, SPAN), 1))
        dsteps = sum(nn(tri, p) for p in split(dcum, 3))
        val = small[at, DTR] + bias_ref[...]
        sg = 1.0 / (1.0 + jnp.exp(-val))
        ex = jnp.exp(jnp.minimum(val, 0.0))
        ratio = jnp.where(val < -12.0, 1.0 - 0.5 * ex, sg / jnp.maximum(softplus(val), 1e-7))
        steps = csum * ratio + dsteps * rate_ref[...] * sg
        ddt[at, :] = jnp.where(iota((SPAN, LANES), 1) < HEADS, steps, 0.0).astype(BF16)
        pos = meta.cols(t)
        around = meta.start + t * SPAN + iota((SPAN + 8, 1), 0)
        mask = (meta.seq(around + 1) == meta.seq(around)).astype(F32)
        for cs in wide_chunks(CONV_CH):
            ext = jnp.concatenate([wide[:, cs], edge[:, cs]], 0)
            total = cw_ref[0:1, cs] * ext
            for j in range(1, KERNEL):
                total = cw_ref[j : j + 1, cs] * ext + mask * pltpu.roll(total, SPAN + 7, 0)
            dact[at, cs] = total[:SPAN].astype(BF16)
        edge[...] = wide[:8, :]
        dut = duz[at, :] + nt(dact[at, :], up[:, INNER:mid]) + nt(ddt[at, :HEADS], up[:, mid:end])
        du[at, :] = dut.astype(BF16) * meta.select(pos).astype(BF16)

        @pl.when(s == 0)
        def _():
            hailed(targets)
            sum_a.begin()

        pl.when(s == 1)(sum_a.over_y)
        pl.when(s == nb - 1)(sum_a.scatter)

    each_tile(nb, scan_tile)
    wait_all(for_grads)

    def down_grad(at):
        gb[:, at()] = tn(du[...], hb[:, at()]).astype(BF16)

    def conv_grad(at):
        gb[:, at(width)] = tn(u[...], dact[:, at()]).astype(BF16)

    each_chunk(width, down_grad)
    each_chunk(CONV_CH, conv_grad)
    gb[:, width + CONV_CH :] = jnp.zeros((LOW, gb.shape[1] - width - CONV_CH), BF16)
    gb[:, width + CONV_CH : width + CONV_CH + HEADS] = tn(u[...], ddt[:, :HEADS]).astype(BF16)
    sum_b.begin()
    results = act.at[:, width : 2 * width]
    for_out = mover.go(back_h, results)
    weights.finish()
    wait_all(for_last)

    def last_tile(t):
        at = tile_rows(t)
        squares, crosses = jnp.zeros((SPAN, LANES), F32), jnp.zeros((SPAN, LANES), F32)
        for cs in wide_chunks(width):
            dh = (
                dhz[at, cs].astype(F32) + nn(dact[at, :], wv[:CONV_CH, cs]) + nn(ddt[at, :HEADS], wv[CONV_CH:, cs])
                + nn(du[at, :], down[:, cs])
            )
            g = dh * gain_ref[:, cs]
            wide[:, cs] = g
            xt = x[at, cs].astype(F32)
            sq, cross = xt * xt, g * xt
            squares = squares + sq[:, :LANES] + sq[:, LANES:]
            crosses = crosses + cross[:, :LANES] + cross[:, LANES:]
        rstd = lax.rsqrt(jnp.sum(squares, 1, keepdims=True) * (1.0 / width) + EPS)
        back = jnp.sum(crosses, 1, keepdims=True) * (1.0 / width) * rstd * rstd
        valid = meta.valid(meta.cols(t))
        for cs in wide_chunks(width):
            dx = rstd * (wide[:, cs] - x[at, cs].astype(F32) * back)
            douts = dout[at, cs].astype(F32)
            hb[at, cs] = ((douts + dx) * valid).astype(BF16)
        pl.when(t == 0)(sum_b.over_y)
        pl.when(t == nb - 2)(sum_a.gather)
        pl.when(t == nb - 1)(sum_b.scatter)

    each_tile(nb, last_tile)
    share = rows // n
    for_out.wait()
    sort_rows(where_ref[...], hb, act.at[:, 0:width])
    sum_b.gather()
    copies = [
        send(
            act.at[place(to, share), 0:width], land_h.at[place(me, share), :], s_grad.at[k - 1], r_grad.at[k - 1], ctx=to
        )
        for k, to, _ in peers("ctx")
    ]
    for c in copies:
        c.start()
    dhz[place(me, share), :] = act[place(me, share), 0:width]
    sort_rows(tok_ref[...], results, x)
    out_done = mover.go(x, out_h)
    sum_a.finish()
    sum_b.finish()
    arrived = []
    for c, (_, _, back) in zip(copies, peers("ctx")):
        c.wait_recv()
        arrived.append(mover.go(land_h.at[place(back, share), :], dhz.at[place(back, share), :]))
    wait_all(arrived)
    for c in copies:
        c.wait_send()
    tok, grads = tok_ref[...], []
    for t in range(0, rows, SPAN):
        hit = one_hot(iota((SPAN, rows), 0) + t == tok)
        for cs in wide_chunks(width):
            hb[t : t + SPAN, cs] = nn(hit, dhz[:, cs]).astype(BF16)
        grads.append(mover.go(hb.at[t : t + SPAN, :], grad_h.at[t : t + SPAN, :]))
    wait_all(grads + [out_done])


def shape(*dims, dtype=F32):
    return jax.ShapeDtypeStruct(dims, dtype)


def params(mib=60, remote=None):
    if remote is None:
        return pltpu.CompilerParams(vmem_limit_bytes=mib * MIB)
    return pltpu.CompilerParams(vmem_limit_bytes=mib * MIB, collective_id=remote, has_side_effects=True)


SMEM = pl.BlockSpec(memory_space=pltpu.SMEM)
VMEM = pl.BlockSpec(memory_space=pltpu.VMEM)
ANY = pl.BlockSpec(memory_space=pl.ANY)


def exchange_scratch(n, rows):
    owners = owners_of(n)
    w = INNER // owners
    return [
        pltpu.VMEM((n, rows, w), BF16), pltpu.VMEM((n, STATE, w), BF16), pltpu.VMEM((owners, STATE, w), BF16),
    ] + [pltpu.SemaphoreType.DMA((n - 1,))] * 4


def local(
    tokens, cotangent, order, lengths, adapter_ids, in_weight, out_weight, in_down, in_up, out_down, out_up,
    norm_gain, conv_weight, conv_bias, dt_bias, a_log, skip_gain, gate_gain,
):
    n, nf = lax.axis_size("ctx"), lax.axis_size("fsdp")
    rows, width = tokens.shape[1:]
    nb = rows // SPAN
    share = rows // n
    log_rows = rows.bit_length() - 1
    assert rows == 1 << log_rows and rows <= 1024 and rows % SPAN == 0 and nb >= 4
    assert nf % 2 == 0 and share % 16 == 0
    proj_w = in_weight.shape[1]
    rest = proj_w - INNER
    bf = lambda *dims: shape(*dims, dtype=BF16)
    vm = pltpu.VMEM
    dma = pltpu.SemaphoreType.DMA
    padded = lambda c: -(-c // (n * LANES)) * LANES * n
    owners = owners_of(n)
    ow = INNER // owners
    wt, in_down_t, out_down_t = in_weight.T, in_down.T, out_down.T
    kw, ko, ka = wt.shape[1], out_weight.shape[0], in_down_t.shape[0]
    idx = shape(1, rows, dtype=jnp.int32)
    gain, gate, cb = norm_gain[None], gate_gain[None], conv_bias[None]
    seqs = (lengths, adapter_ids)

    parts_w = len(chunks_of(proj_w - SPLIT, WEIGHT_PARTS))
    got, cot_sorted, slot, where, tok, w_in, a_in, b_in, e, skip, bias, rate = pl.pallas_call(
        partial(arrive_kernel, log_rows, share),
        in_specs=[VMEM] * 9,
        out_specs=[ANY, VMEM, VMEM, VMEM, VMEM, ANY, ANY, ANY, VMEM, VMEM, VMEM, VMEM],
        out_shape=(
            bf(rows, width), bf(rows, width), idx, idx, idx, bf(nf, proj_w - SPLIT, kw), bf(LOW, width), bf(LOW, proj_w),
            bf(2 * LANES, INNER), shape(1, INNER), shape(1, LANES), shape(1, LANES),
        ),
        scratch_shapes=[vm((rows, width), BF16)] + spread_sems(n) + gather_sems(nf, 2 + parts_w),
        compiler_params=params(remote=1),
        name="arrive",
    )(order, tokens[0], cotangent[0], wt, in_down_t, in_up, dt_bias[None], a_log[None], skip_gain[None])

    f32 = shape
    cols_a, cols_b = padded(2 * INNER + width), padded(width + rest)
    low = LOW // nf
    front_out = [
        bf(rows, width), bf(rows, width), bf(rows, LOW), bf(rows, CONV_CH), bf(rows, CONV_CH), f32(rows, SMALL),
        bf(nb, STATE, INNER), f32(nb, LANES), f32(8, CONV_CH), bf(rows, INNER), bf(rows, INNER), bf(rows, width),
        f32(rows, LOW), bf(rows, width), bf(LOW, cols_a), bf(rows, width), bf(INNER, width), bf(nf, SPLIT, kw),
    ]
    slot_buffers = [vm((n, STATE, ow), BF16), vm((n, STATE, ow), BF16), vm((owners, STATE, ow), BF16)]
    x, hb, u, act, dact, small, dl, dend, edge, dm, dxk, dhz, duz, dout, g_a, back_out, _, _ = pl.pallas_call(
        front_kernel,
        in_specs=[SMEM, SMEM] + [VMEM] * 11 + [ANY] * 8,
        out_specs=[ANY] * 7 + [VMEM, VMEM] + [ANY] * 5 + [VMEM] + [ANY] * 3,
        out_shape=front_out,
        scratch_shapes=[
            vm((rest, width), BF16), vm((LOW, width), BF16), vm((LOW, proj_w), BF16), vm((LOW, INNER), BF16),
            vm((LOW, width), BF16), vm((2 * LANES, INNER), BF16), vm((rows, width), BF16), vm((rows, width), BF16),
            vm((rows, width), BF16), vm((rows, LOW), BF16), vm((rows, LOW), BF16), vm((rows, LOW), BF16),
            vm((rows, CONV_CH), BF16), vm((rows, CONV_CH), BF16), vm((nb, STATE, INNER), F32), vm((rows, INNER), BF16),
            vm((rows, INNER), BF16), vm((nb + 1, STATE, INNER), BF16), vm((rows, width), BF16), vm((rows, width), BF16),
            vm((rows, SMALL), F32), vm((rows, LANES), F32), vm((nb, HEADS, SPAN), F32), vm((nb, 8, INNER), F32),
            vm((SPAN, INNER), F32), vm((SPAN, INNER), BF16), vm((SPAN, INNER), BF16), vm((STATE, INNER), F32),
            vm((8, INNER), F32), vm((SPAN, SPAN), F32), vm((SPAN, SPAN), F32), vm((nb + 1, 8, CONV_CH), F32),
            vm((8, CONV_CH), F32), vm((16, CONV_CH), BF16), vm((8, CONV_CH), F32), vm((8, CONV_CH), F32),
            vm((owners, STATE + 16, ow), BF16), vm((n, STATE + 16, ow), BF16), vm((n, STATE, ow), BF16),
            vm((owners, STATE, ow), BF16), vm((owners, STATE, ow), BF16),
        ] + slot_buffers + [dma((MOVES,)), dma((3, 2 * nf)), dma, dma] + spread_sems(n) + spread_sems(n) + [dma, dma]
        + [dma((n - 1,))] * 8 + gather_sems(nf, 4),
        compiler_params=params(63, remote=2),
        name="front",
    )(
        *seqs, slot, where, gain, conv_weight, cb, bias, rate, skip, gate, out_down_t, out_up, got, w_in, a_in, b_in, e,
        cot_sorted, out_weight, wt,
    )

    block_output, input_grad, g_in_down, g_in_up, g_out_down, g_out_up, _ = pl.pallas_call(
        back_kernel,
        in_specs=[SMEM, SMEM] + [VMEM] * 10 + [ANY] * 17,
        out_specs=[ANY, ANY, VMEM, VMEM, VMEM, VMEM, ANY],
        out_shape=(
            bf(rows, width), bf(rows, width), f32(low, width), f32(low, proj_w), f32(low, INNER), f32(low, width),
            bf(rows, width),
        ),
        scratch_shapes=[
            vm((rest, width), BF16), vm((LOW, width), BF16), vm((LOW, proj_w), BF16), vm((2 * LANES, INNER), BF16),
            vm((rows, CONV_CH), BF16), vm((rows, CONV_CH), BF16), vm((rows, LANES), BF16), vm((rows, SMALL), F32),
            vm((nb, STATE, INNER), BF16), vm((rows, INNER), BF16), vm((rows, INNER), BF16), vm((rows, width), BF16),
            vm((rows, LOW), BF16), vm((rows, LOW), BF16), vm((rows, LOW), F32), vm((rows, width), BF16),
            vm((rows, width), BF16), vm((rows, width), BF16), vm((LOW, cols_b), BF16),
            vm((SPAN, CONV_CH), F32), vm((SPAN, INNER), BF16), vm((SPAN, INNER), BF16), vm((8, CONV_CH), F32),
            dma((MOVES,)), dma((2 * nf,)),
        ] + [dma((n - 1,))] * 2 + reduce_scratch(n, nf, cols_a // n) + reduce_scratch(n, nf, cols_b // n),
        compiler_params=params(62, remote=3),
        name="back",
    )(
        *seqs, where, tok, gain, conv_weight, bias, rate, skip, dend, edge, g_a, w_in, a_in, b_in, e, act, dact, small, dl,
        dm, dxk, hb, u, duz, dhz, x, dout, back_out,
    )
    return block_output[None], input_grad[None], g_in_down.T, g_in_up, g_out_down.T, g_out_up


def solution(mesh):
    placed = (
        P("fsdp", "ctx", None),
        P("fsdp", "ctx", None),
        P("fsdp", None),
        P("fsdp", None),
        P("fsdp", None),
        P("fsdp", None),
        P("fsdp", None),
        P(None, "fsdp"),
        P("fsdp", None),
        P(None, "fsdp"),
        P("fsdp", None),
        P(),
        P(),
        P(),
        P(),
        P(),
        P(),
        P(),
    )
    return jax.shard_map(
        local,
        mesh=mesh,
        in_specs=placed,
        out_specs=(
            P("fsdp", "ctx", None),
            P("fsdp", "ctx", None),
            P(None, "fsdp"),
            P("fsdp", None),
            P(None, "fsdp"),
            P("fsdp", None),
        ),
        check_vma=False,
    )
```
